32 devices in a mesh: fsdp: 16 (over z, y, core), mp: 2 (over x).
Axes of the slice: x: 2, y: 2, z: 4, core: 2. Of those that a mesh axis runs over, the one named last changes fastest.
Arguments:
- inputs: bfloat16 [16, 1024, 1024], P('fsdp'), may hold values from -6 to 6
- doc_ids: int32 [16, 1024], P('fsdp'), may hold values from 0 to 3, never falling along the last dimension, each value on 1 to 512 neighbouring positions
- out_grad: bfloat16 [16, 1024, 1024], P('fsdp'), may hold values from -7 to 7
- attn_w: float32 [4, 1024, 1024], P(None, 'fsdp', 'mp'), may hold values from -7 to 7
- attn_mom: float32 [4, 1024, 1024], P(None, 'fsdp', 'mp'), may hold values from -3.2 to 3.2
- attn_avg: float32 [4, 1024, 1024], P(None, 'fsdp', 'mp'), may hold values from -7 to 7
- mlp_w: float32 [3, 1024, 4096], P(None, 'fsdp', 'mp'), may hold values from -7 to 7
- mlp_mom: float32 [3, 1024, 4096], P(None, 'fsdp', 'mp'), may hold values from -3.2 to 3.2
- mlp_avg: float32 [3, 1024, 4096], P(None, 'fsdp', 'mp'), may hold values from -7 to 7
- head_scale: float32 [1024], P('mp'), may hold values from 0.7 to 1.6
- head_mom: float32 [1024], P('mp'), may hold values from -153.6 to 153.6
- mix_rates: float32 [2, 1024], replicated, may hold values from 0.05 to 0.5
- mix_mom: float32 [2, 1024], replicated, may hold values from -512 to 512
- unit_scales: float32 [2, 4096], P(None, 'mp'), may hold values from 0.5 to 2
- unit_mom: float32 [2, 4096], P(None, 'mp'), may hold values from -153.6 to 153.6
Outputs:
- hidden_out: float32 [16, 1024, 1024], P('fsdp')
- input_grad: float32 [16, 1024, 1024], P('fsdp')
- attn_mom_new: float32 [4, 1024, 1024], P(None, 'fsdp', 'mp')
- attn_new: float32 [4, 1024, 1024], P(None, 'fsdp', 'mp')
- attn_avg_new: float32 [4, 1024, 1024], P(None, 'fsdp', 'mp')
- mlp_mom_new: float32 [3, 1024, 4096], P(None, 'fsdp', 'mp')
- mlp_new: float32 [3, 1024, 4096], P(None, 'fsdp', 'mp')
- mlp_avg_new: float32 [3, 1024, 4096], P(None, 'fsdp', 'mp')
- head_mom_new: float32 [1024], P('mp')
- head_new: float32 [1024], P('mp')
- mix_mom_new: float32 [2, 1024], replicated
- mix_new: float32 [2, 1024], replicated
- units_mom_new: float32 [2, 4096], P(None, 'mp')
- units_new: float32 [2, 4096], P(None, 'mp')
The draws below stay inside these ranges and needn't reach their ends.
Inputs may be any that keep to these rules, and one draw needn't show every extreme that they name: `doc_ids`: along a row the document number never falls; a document spans at most 512 positions.
All inputs are finite; a program needn't handle non-finite values.
Results may differ from the reference program's by a relative error of at most 0.014.
Values may be sent and summed in bfloat16 or wider, within the bound.
A program may use at most 256 MiB of HBM per device.

```python
import math
import jax
import jax.numpy as jnp
import numpy as np
from jax import lax

D = 1024
HEADS = 16
HD = 64
FF = 4096
SEQ = 1024
ROWS = 16
TOKENS = 16384


def rising(length, rise_ratio):
    fraction = jnp.arange(length, dtype=jnp.float32) / max(length - 1, 1)
    return jnp.exp(math.log(rise_ratio) * (fraction - 0.5))


def draw_out_grad(key, part):
    key = jax.random.fold_in(key, 1)
    out_shape = (ROWS, SEQ, D)
    base_vals = jnp.clip(jax.random.normal(key, out_shape, jnp.float32), -4.0, 4.0)
    rise_ratio = 3.0
    return (base_vals * rising(ROWS, rise_ratio)[:, None, None]).astype(jnp.bfloat16)


def weight_like(key, count, columns):
    out_shape = (count, D, columns)
    base_vals = jnp.clip(jax.random.normal(key, out_shape, jnp.float32), -4.0, 4.0)
    rise_ratio = 3.0
    return base_vals * rising(D, rise_ratio)[None, :, None]


def draw_attn_w(key, part):
    key = jax.random.fold_in(key, 2)
    return weight_like(key, 4, D)


def draw_attn_avg(key, part):
    key = jax.random.fold_in(key, 3)
    return weight_like(key, 4, D)


def draw_mlp_w(key, part):
    key = jax.random.fold_in(key, 4)
    return weight_like(key, 3, FF)


def draw_mlp_avg(key, part):
    key = jax.random.fold_in(key, 5)
    return weight_like(key, 3, FF)


def moment_like(key, out_shape, spread):
    base_vals = jnp.clip(jax.random.normal(key, out_shape, jnp.float32), -4.0, 4.0)
    return base_vals * spread


def draw_attn_mom(key, part):
    key = jax.random.fold_in(key, 6)
    return moment_like(key, (4, D, D), 0.2 * math.sqrt(TOKENS // D))


def draw_mlp_mom(key, part):
    key = jax.random.fold_in(key, 7)
    return moment_like(key, (3, D, FF), 0.2 * math.sqrt(TOKENS // D))


def draw_head_mom(key, part):
    key = jax.random.fold_in(key, 8)
    return moment_like(key, (D,), 0.3 * math.sqrt(TOKENS))


def draw_mix_mom(key, part):
    key = jax.random.fold_in(key, 9)
    return moment_like(key, (2, D), math.sqrt(TOKENS))


def draw_unit_mom(key, part):
    key = jax.random.fold_in(key, 10)
    return moment_like(key, (2, FF), 0.3 * math.sqrt(TOKENS))


def block_levels(stream_key, extent, pieces, smallest, high):
    level = 1.0
    for dim, parts in pieces:
        draws = jax.random.uniform(jax.random.fold_in(jax.random.fold_in(stream_key, 6), dim), (parts,), jnp.float32, smallest / len(pieces), high / len(pieces))
        level = level * jnp.repeat(jnp.exp(draws), extent[dim] // parts).reshape((-1,) + (1,) * (len(extent) - 1 - dim))
    return level


def split_up(count, total, limit, skew):
    weights = [(1 << 20) // math.isqrt(standing ** skew) + 1 for standing in range(2, count + 1)]
    rest, holding = total - limit - (count - 1), [1] * (count - 1)
    while rest > 0:
        movable = [i for i in range(count - 1) if holding[i] < limit]
        whole, left = sum([weights[i] for i in movable]), rest
        for i in movable:
            addition = min(limit - holding[i], max(1, left * weights[i] // whole), rest)
            holding[i] = holding[i] + addition
            rest = rest - addition
    return np.array([limit] + holding)


def uneven_parts(own_key, count, total, most, lean):
    if count == 2:
        one = jax.random.randint(own_key, (), max(1, total - most), min(most, total - 1) + 1)
        return jnp.stack([one, total - one])
    tallies = jnp.asarray(split_up(count, total, most, lean), jnp.int32)
    pairs = (count - 1) // 2
    source_of, taker = tallies[1:1 + 2 * pairs:2], tallies[2:2 + 2 * pairs:2]
    room = jnp.minimum(source_of - 1, most - taker)
    shifted = jax.random.randint(jax.random.fold_in(own_key, 1), (pairs,), 0, 1 << 20) % (room + 1)
    tallies = tallies.at[1:1 + 2 * pairs:2].set(source_of - shifted).at[2:2 + 2 * pairs:2].set(taker + shifted)
    return tallies[jax.random.permutation(jax.random.fold_in(own_key, 2), count)]


def noise(rng, dims, scale, most, cuts=(), kind=jnp.bfloat16):
    values = jax.random.normal(rng, dims, jnp.float32) * scale
    if len(cuts) > 0:
        values = block_levels(rng, dims, cuts, -0.22, 0.18) * values
    return jnp.clip(values, min=-most, max=most).astype(kind)


def setup_inputs(seed: int = 0) -> dict:
    keys = jax.random.split(jax.random.key(seed), 16)
    return {
        "inputs": noise(keys[0], (ROWS, SEQ, D), 1.0, 6.0, ((0, 16),)),
        "doc_ids": jax.vmap(lambda own: jnp.searchsorted(jnp.cumsum(uneven_parts(own, 4, SEQ, SEQ // 2, 2)), jnp.arange(SEQ), side="right"))(jax.random.split(keys[1], ROWS)).reshape((ROWS, SEQ)).astype(jnp.int32),
        "out_grad": draw_out_grad(jax.random.fold_in(keys[15], 71), 0),
        "attn_w": draw_attn_w(jax.random.fold_in(keys[15], 71), 0),
        "attn_mom": draw_attn_mom(jax.random.fold_in(keys[15], 71), 0),
        "attn_avg": draw_attn_avg(jax.random.fold_in(keys[15], 71), 0),
        "mlp_w": draw_mlp_w(jax.random.fold_in(keys[15], 71), 0),
        "mlp_mom": draw_mlp_mom(jax.random.fold_in(keys[15], 71), 0),
        "mlp_avg": draw_mlp_avg(jax.random.fold_in(keys[15], 71), 0),
        "head_scale": jnp.clip(jnp.exp(math.log(1.6) - 0.82667861 * jax.random.uniform(keys[9], (D,), jnp.float32) ** block_levels(keys[9], (D,), ((0, 2),), -0.2, 0.2)), 0.7, 1.6),
        "head_mom": draw_head_mom(jax.random.fold_in(keys[15], 71), 0),
        "mix_rates": jnp.clip(jnp.exp(jax.random.uniform(keys[11], (2, D), jnp.float32, math.log(0.05), math.log(0.5))), 0.05, 0.5),
        "mix_mom": draw_mix_mom(jax.random.fold_in(keys[15], 71), 0),
        "unit_scales": jnp.clip(jnp.exp(math.log(2.0) - 1.3862944 * jax.random.uniform(keys[13], (2, FF), jnp.float32) ** block_levels(keys[13], (2, FF), ((1, 2),), -0.2, 0.2)), 0.5, 2.0),
        "unit_mom": draw_unit_mom(jax.random.fold_in(keys[15], 71), 0),
    }


EPS = 1e-06
MOMENTUM = 0.9
AVERAGE = 0.9
NEG_FILL = -1e+30
THETA = 10000.0
RATE_WEIGHT = 50.0
RATE_HEAD = 0.08
RATE_MIX = 0.02
RATE_UNITS = 0.5
HIGH = lax.Precision.HIGHEST

@jax.custom_vjp
def low(v):
    return lax.optimization_barrier(v.astype(jnp.bfloat16)).astype(jnp.float32)

@jax.custom_vjp
def low_back(v):
    return v

def low_keep(v):
    return (low(v), None)

def low_pass(kept, grad):
    return (grad,)

def back_keep(v):
    return (v, None)

def back_low(kept, grad):
    return (low(grad),)
low.defvjp(low_keep, low_pass)
low_back.defvjp(back_keep, back_low)

def rms_unit(vector):
    return vector * lax.rsqrt(lax.optimization_barrier(jnp.mean(vector * vector, axis=-1, keepdims=True)) + EPS)

def rotary_tables(doc_row):
    length = doc_row.shape[0]
    position = jnp.arange(length, dtype=jnp.int32)
    boundary = jnp.concatenate([jnp.ones((1,), jnp.int32), (doc_row[1:] != doc_row[:-1]).astype(jnp.int32)])
    doc_start = lax.cummax(jnp.where(boundary > 0, position, 0), axis=0)
    offset = (position - doc_start).astype(jnp.float32)
    freq = THETA ** (-2.0 * jnp.arange(HD // 2, dtype=jnp.float32) / HD)
    angle = offset[:, None] * freq[None, :]
    return (jnp.cos(angle), jnp.sin(angle))

def rotate(vector, cos_table, sin_table):
    half_dim = vector.shape[-1] // 2
    lower_half = vector[..., :half_dim]
    upper_half = vector[..., half_dim:]
    cos_part = cos_table[:, None, :]
    sin_part = sin_table[:, None, :]
    return jnp.concatenate([lower_half * cos_part - upper_half * sin_part, lower_half * sin_part + upper_half * cos_part], axis=-1)

def layer_row(resid_in, doc_row, attn_all, mlp_all, head_all, mix_all, unit_all):
    length = resid_in.shape[0]
    cos_table, sin_table = rotary_tables(doc_row)
    input_low = low(resid_in)
    attn_low = low(attn_all)
    mlp_low = low(mlp_all)
    projected = jnp.einsum('sd,jdc->jsc', input_low, attn_low[:3], precision=HIGH)
    query = low_back(projected[0]).reshape(length, HEADS, HD)
    key_raw = low_back(projected[1]).reshape(length, HEADS, HD)
    value_low = low(low_back(projected[2])).reshape(length, HEADS, HD)
    head_gain = head_all.reshape(HEADS, HD)
    query_low = low(head_gain * rms_unit(rotate(query, cos_table, sin_table)))
    key_low = low(head_gain * rms_unit(rotate(key_raw, cos_table, sin_table)))
    raw_scores = low_back(jnp.einsum('qhe,khe->hqk', query_low, key_low, precision=HIGH))
    position = jnp.arange(length, dtype=jnp.int32)
    allowed = (doc_row[:, None] == doc_row[None, :]) & (position[None, :] <= position[:, None])
    scores = jnp.where(allowed[None], raw_scores * HD ** (-0.5), NEG_FILL)
    peak_val = lax.optimization_barrier(jnp.max(scores, axis=-1, keepdims=True))
    expo_vals = jnp.exp(scores - peak_val)
    attn_probs = expo_vals / lax.optimization_barrier(jnp.sum(expo_vals, axis=-1, keepdims=True))
    mixed = jnp.einsum('hqk,khe->qhe', low(attn_probs), value_low, precision=HIGH)
    mixed = low(low_back(mixed)).reshape(length, D)
    attn_out = low_back(jnp.einsum('sc,dc->sd', mixed, attn_low[3], precision=HIGH))
    resid_one = resid_in + mix_all[0] * (rms_unit(attn_out) - resid_in)
    hidden_one = rms_unit(resid_one)
    hidden_low = low(hidden_one)
    gates = jnp.einsum('sd,jdf->jsf', hidden_low, mlp_low[:2], precision=HIGH)
    up_proj = low_back(gates[0])
    gate_proj = low_back(gates[1])
    hidden_units = low(unit_all[0] * up_proj * jax.nn.silu(unit_all[1] * gate_proj * D ** (-0.5)))
    mlp_out = low_back(jnp.einsum('sf,df->sd', hidden_units, mlp_low[2], precision=HIGH))
    resid_two = hidden_one + mix_all[1] * (rms_unit(mlp_out) - hidden_one)
    return rms_unit(resid_two)

def nesterov(param, moment, grad, step_rate):
    moment_new = MOMENTUM * moment + grad
    return (moment_new, param - step_rate * (grad + MOMENTUM * moment_new))

def renorm(matrix):
    return matrix * lax.rsqrt(lax.optimization_barrier(jnp.mean(matrix * matrix, axis=1, keepdims=True)) + EPS)

def reference(inputs, doc_ids, out_grad, attn_w, attn_mom, attn_avg, mlp_w, mlp_mom, mlp_avg, head_scale, head_mom, mix_rates, mix_mom, unit_scales, unit_mom):
    resid_all = inputs.astype(jnp.float32)
    cotangent = out_grad.astype(jnp.float32)
    row_fn = jax.checkpoint(layer_row)

    def forward(states, attn_all, mlp_all, head_all, mix_all, unit_all):
        return lax.map(lambda item: row_fn(item[0], item[1], attn_all, mlp_all, head_all, mix_all, unit_all), (states, doc_ids))
    result, pull = jax.vjp(forward, resid_all, attn_w, mlp_w, head_scale, mix_rates, unit_scales)
    grad_in, grad_attn, grad_mlp, grad_head, grad_mix, grad_units = pull(cotangent)
    root_tokens = math.sqrt(TOKENS)
    weight_rate = RATE_WEIGHT / root_tokens
    attn_mom_new, attn_step = nesterov(attn_w, attn_mom, grad_attn, weight_rate)
    mlp_mom_new, mlp_step = nesterov(mlp_w, mlp_mom, grad_mlp, weight_rate)
    attn_new = renorm(attn_step)
    mlp_new = renorm(mlp_step)
    head_mom_new, head_new = nesterov(head_scale, head_mom, grad_head, RATE_HEAD / root_tokens)
    mix_mom_new, mix_new = nesterov(mix_rates, mix_mom, grad_mix, RATE_MIX / root_tokens)
    units_mom_new, units_new = nesterov(unit_scales, unit_mom, grad_units, RATE_UNITS / root_tokens)
    return (result, grad_in, attn_mom_new, attn_new, AVERAGE * attn_avg + (1.0 - AVERAGE) * attn_new, mlp_mom_new, mlp_new, AVERAGE * mlp_avg + (1.0 - AVERAGE) * mlp_new, head_mom_new, head_new, mix_mom_new, mix_new, units_mom_new, units_new)
```

```python
import functools
import math

import jax
import jax.numpy as jnp
from jax import lax
from jax.experimental import pallas as pl
from jax.experimental.pallas import tpu as pltpu
from jax.sharding import PartitionSpec as P

D = 1024
HD = 64


EPS = 1e-06
MOMENTUM = 0.9
AVERAGE = 0.9
NEG_FILL = -1e30
THETA = 10000.0
RATE_WEIGHT = 50.0
RATE_HEAD = 0.08
RATE_MIX = 0.02
RATE_UNITS = 0.5


def rms_unit(vector):
    return vector * lax.rsqrt(jnp.mean(vector * vector, axis=-1, keepdims=True) + EPS)


def rms_back(vector, grad):
    factor = lax.rsqrt(jnp.mean(vector * vector, axis=-1, keepdims=True) + EPS)
    unit_vec = vector * factor
    return factor * (grad - unit_vec * jnp.mean(grad * unit_vec, axis=-1, keepdims=True))


def rotary_tables(doc_row):
    length = doc_row.shape[0]
    position = jnp.arange(length, dtype=jnp.int32)
    boundary = jnp.concatenate(
        [jnp.ones((1,), jnp.int32), (doc_row[1:] != doc_row[:-1]).astype(jnp.int32)]
    )
    doc_start = lax.cummax(jnp.where(boundary > 0, position, 0), axis=0)
    offset = (position - doc_start).astype(jnp.float32)
    freq = THETA ** (-2.0 * jnp.arange(HD // 2, dtype=jnp.float32) / HD)
    angle = offset[:, None] * freq[None, :]
    return (jnp.cos(angle), jnp.sin(angle))


def rotate(vector, cos_table, sin_table):
    half_dim = vector.shape[-1] // 2
    lower_half = vector[..., :half_dim]
    upper_half = vector[..., half_dim:]
    cos_part = cos_table[:, None, :]
    sin_part = sin_table[:, None, :]
    return jnp.concatenate(
        [
            lower_half * cos_part - upper_half * sin_part,
            lower_half * sin_part + upper_half * cos_part,
        ],
        axis=-1,
    )


def rotate_back(grad, cos_table, sin_table):
    half_dim = grad.shape[-1] // 2
    lower_half = grad[..., :half_dim]
    upper_half = grad[..., half_dim:]
    cos_part = cos_table[:, None, :]
    sin_part = sin_table[:, None, :]
    return jnp.concatenate(
        [
            lower_half * cos_part + upper_half * sin_part,
            upper_half * cos_part - lower_half * sin_part,
        ],
        axis=-1,
    )


def nesterov(param, moment, grad, step_rate):
    moment_new = MOMENTUM * moment + grad
    return (moment_new, param - step_rate * (grad + MOMENTUM * moment_new))


BF = jnp.bfloat16
F32 = jnp.float32
MESH = pl.DeviceIdType.MESH
VM = pltpu.VMEM
MIB = 1 << 20


def dot_nn(a, b):
    return lax.dot_general(a, b, (((1,), (0,)), ((), ())), preferred_element_type=F32)


def dot_nt(a, b):
    return lax.dot_general(a, b, (((1,), (1,)), ((), ())), preferred_element_type=F32)


def dot_tn(a, b):
    return lax.dot_general(a, b, (((0,), (0,)), ((), ())), preferred_element_type=F32)


def split_dot(a, ones):
    high = a.astype(BF)
    return dot_nn(high, ones) + dot_nn((a - high.astype(F32)).astype(BF), ones)


def ring_place(index, chips):
    z, y = index // 4, (index // 2) % 2
    return z + y * (chips - 1 - 2 * z), index % 2


def ring_device(place, core, chips):
    y = place // (chips // 2)
    return ((place + y * (chips - 1 - 2 * place)) * 2 + y) * 2 + core


def greet(peers):
    barrier = pltpu.get_barrier_semaphore()
    for peer in peers:
        pl.semaphore_signal(barrier, inc=1, device_id=peer, device_id_type=MESH)
    pl.semaphore_wait(barrier, len(peers))


def remote(src, dst, send, recv, peer):
    return pltpu.make_async_remote_copy(
        src_ref=src, dst_ref=dst, send_sem=send, recv_sem=recv, device_id=peer, device_id_type=MESH
    )


GATHER_GROUPS = ((0, 0, 3), (0, 3, 1), (1, 0, 1), (1, 1, 1), (1, 2, 1))


def hops(group, chips):
    long, short = chips // 2, chips - 1 - chips // 2
    return (long, short) if group % 2 == 0 else (short, long)


def gather_kernel(
    chips, attn_ref, mlp_ref, attn_out, mlp_out, wo_out,
    ring_send, ring_recv, pair_send, pair_recv, own_sem, wo_send, wo_recv,
):
    index, x = lax.axis_index("fsdp"), lax.axis_index("mp")
    place, core = ring_place(index, chips)
    rows = attn_ref.shape[1]
    right = (ring_device((place + 1) % chips, core, chips), x)
    left = (ring_device((place + chips - 1) % chips, core, chips), x)
    pair = (index + 1 - 2 * core, x)
    across = (index, 1 - x)
    greet((right, left, pair, across))
    outs = (attn_out, mlp_out)
    ins = (attn_ref, mlp_ref)

    def block(group, dev):
        kind, first, count = GATHER_GROUPS[group]
        return outs[kind].at[pl.ds(first, count), pl.ds(pl.multiple_of(dev * rows, rows), rows), :]

    def own(group):
        kind, first, count = GATHER_GROUPS[group]
        return ins[kind].at[pl.ds(first, count)]

    def ring_copy(group, way, hop):
        origin = ring_device((place + chips - (hop - 1)) % chips if way == 0 else (place + hop - 1) % chips, core, chips)
        src = own(group) if hop == 1 else block(group, origin)
        return remote(
            src, block(group, origin), ring_send.at[group, way, hop - 1], ring_recv.at[group, way, hop - 1],
            right if way == 0 else left,
        )

    def arrived(group, way, hop):
        origin = (place + 2 * chips - hop) % chips if way == 0 else (place + hop) % chips
        return ring_device(origin, core, chips)

    def pair_copy(group, slot, dev, first):
        src = own(group) if first else block(group, dev)
        return remote(src, block(group, dev), pair_send.at[group, slot], pair_recv.at[group, slot], pair)

    def await_ring(group, way, hop):
        here = block(group, arrived(group, way, hop))
        remote(here, here, ring_send.at[group, way, hop - 1], ring_recv.at[group, way, hop - 1], right).wait_recv()

    def await_pair(group):
        counts = hops(group, chips)
        pair_copy(group, 0, pair_index, False).wait_recv()
        for way in (0, 1):
            for hop in range(1, counts[way] + 1):
                dev = arrived(group, way, hop) + 1 - 2 * core
                pair_copy(group, hop if way == 0 else counts[0] + hop, dev, False).wait_recv()

    pair_index = index + 1 - 2 * core
    sent = []
    groups = range(len(GATHER_GROUPS))
    for group in groups:
        for way in (0, 1):
            copy = ring_copy(group, way, 1)
            copy.start()
            sent.append(copy)
    for group in groups:
        copy = pltpu.make_async_copy(own(group), block(group, index), own_sem.at[group])
        copy.start()
        sent.append(("own", copy))
        copy = pair_copy(group, 0, index, True)
        copy.start()
        sent.append(copy)
    longest = chips // 2
    for hop in range(1, longest + 1):
        for group in groups:
            counts = hops(group, chips)
            for way in (0, 1):
                if hop > counts[way]:
                    continue
                await_ring(group, way, hop)
                dev = arrived(group, way, hop)
                if hop < counts[way]:
                    copy = ring_copy(group, way, hop + 1)
                    copy.start()
                    sent.append(copy)
                slot = hop if way == 0 else counts[0] + hop
                copy = pair_copy(group, slot, dev, False)
                copy.start()
                sent.append(copy)
            if group == 1 and hop == longest:
                await_pair(group)
                own_wait = [c for c in sent if isinstance(c, tuple)][1]
                own_wait[1].wait()
                sent = [c for c in sent if c is not own_wait]
                wo_copy = remote(attn_out.at[3], wo_out, wo_send, wo_recv, across)
                wo_copy.start()
    for group in groups:
        if group == 1:
            continue
        await_pair(group)
    for copy in sent:
        if isinstance(copy, tuple):
            copy[1].wait()
        else:
            copy.wait_send()
    wo_copy.wait()


def gather_weights(attn_low, mlp_low, fsdp):
    chips = fsdp // 2
    rows, cols = attn_low.shape[1:]
    units = mlp_low.shape[2]
    number = len(GATHER_GROUPS)
    anyspec = pl.BlockSpec(memory_space=pl.ANY)
    return pl.pallas_call(
        functools.partial(gather_kernel, chips),
        out_shape=(
            jax.ShapeDtypeStruct((4, rows * fsdp, cols), BF),
            jax.ShapeDtypeStruct((3, rows * fsdp, units), BF),
            jax.ShapeDtypeStruct((rows * fsdp, cols), BF),
        ),
        in_specs=[anyspec] * 2,
        out_specs=(anyspec,) * 3,
        scratch_shapes=[
            pltpu.SemaphoreType.DMA((number, 2, chips // 2)),
            pltpu.SemaphoreType.DMA((number, 2, chips // 2)),
            pltpu.SemaphoreType.DMA((number, chips)),
            pltpu.SemaphoreType.DMA((number, chips)),
            pltpu.SemaphoreType.DMA((number,)),
            pltpu.SemaphoreType.DMA,
            pltpu.SemaphoreType.DMA,
        ],
        compiler_params=pltpu.CompilerParams(collective_id=1, has_side_effects=True),
        name="gather_weights",
    )(attn_low, mlp_low)


def scatter_kernel(chips, attn_ref, wu_ref, wg_ref, wd_ref, attn_out, mlp_out, near_attn, near_mlp, first_attn, first_mlp, ring_attn, ring_mlp,
                   pair_send, pair_recv, ring_send, ring_recv):
    index, x = lax.axis_index("fsdp"), lax.axis_index("mp")
    place, core = ring_place(index, chips)
    right = (ring_device((place + 1) % chips, core, chips), x)
    left = (ring_device((place + chips - 1) % chips, core, chips), x)
    pair = (index + 1 - 2 * core, x)
    greet((right, left, pair))
    owns = (wu_ref, wg_ref, wd_ref, attn_ref)

    def mine(group, dev):
        if group == 3:
            return attn_ref.at[:, dev]
        return owns[group].at[dev]

    def near(group, chip):
        if group == 3:
            return near_attn.at[:, chip]
        return near_mlp.at[group, chip]

    def first(group, way):
        return first_attn.at[way] if group == 3 else first_mlp.at[group, way]

    def slot(group, way, hop):
        if group == 3:
            return ring_attn.at[way, hop - 1]
        return ring_mlp.at[group, way, hop - 1]

    order = (2, 0, 1, 3)
    pairs = {}
    for group in order:
        for chip in range(chips):
            dev = chip * 2 + 1 - core
            copy = remote(mine(group, dev), near(group, chip), pair_send.at[group, chip], pair_recv.at[group, chip], pair)
            copy.start()
            pairs[group, chip] = copy

    def add_into(group, dst, dev, extra):
        src_a, src_b = mine(group, dev), near(group, dev // 2)
        rows = src_a.shape[-2]
        if group == 3:
            for j in range(src_a.shape[0]):
                total = src_a[j].astype(F32) + src_b[j].astype(F32)
                for other in extra:
                    total = total + other[j].astype(F32)
                dst[j] = total.astype(dst.dtype)
        else:
            step = 16
            def body(i, _):
                r = pl.ds(pl.multiple_of(i * step, step), step)
                total = src_a[r].astype(F32) + src_b[r].astype(F32)
                for other in extra:
                    total = total + other[r].astype(F32)
                dst[r] = total.astype(dst.dtype)
                return 0
            lax.fori_loop(0, rows // step, body, 0)

    def target(way, count):
        return ring_device((place + count) % chips if way == 0 else (place + 2 * chips - count) % chips, core, chips)

    sends = []
    for group in order:
        counts = hops(group, chips)
        for chip in range(chips):
            pairs[group, chip].wait()
        for way in (0, 1):
            dev = target(way, counts[way])
            add_into(group, first(group, way), dev, ())
            copy = remote(first(group, way), slot(group, way, 1), ring_send.at[group, way, 0], ring_recv.at[group, way, 0], right if way == 0 else left)
            copy.start()
            sends.append(copy)
    for hop in range(1, chips // 2 + 1):
        for group in order:
            counts = hops(group, chips)
            for way in (0, 1):
                if hop > counts[way]:
                    continue
                here = slot(group, way, hop)
                remote(here, here, ring_send.at[group, way, hop - 1], ring_recv.at[group, way, hop - 1], right if way == 0 else left).wait_recv()
                if hop < counts[way]:
                    dev = target(way, counts[way] - hop)
                    add_into(group, here, dev, (here,))
                    copy = remote(here, slot(group, way, hop + 1), ring_send.at[group, way, hop], ring_recv.at[group, way, hop], right if way == 0 else left)
                    copy.start()
                    sends.append(copy)
            if hop == chips // 2:
                extra = (slot(group, 0, counts[0]), slot(group, 1, counts[1]))
                dst = attn_out if group == 3 else mlp_out.at[group]
                add_into(group, dst, index, extra)
    for copy in sends:
        copy.wait_send()


def scatter_grads(attn_grad, wu, wg, wd, fsdp):
    chips = fsdp // 2
    number, width, cols = attn_grad.shape
    rows, units = width // fsdp, wu.shape[1]
    vspec = pl.BlockSpec(memory_space=VM)
    return pl.pallas_call(
        functools.partial(scatter_kernel, chips),
        out_shape=(
            jax.ShapeDtypeStruct((number, rows, cols), F32),
            jax.ShapeDtypeStruct((3, rows, units), F32),
        ),
        in_specs=[vspec] * 4,
        out_specs=(vspec,) * 2,
        scratch_shapes=[
            VM((number, chips, rows, cols), BF),
            VM((3, chips, rows, units), BF),
            VM((2, number, rows, cols), BF),
            VM((3, 2, rows, units), BF),
            VM((2, chips // 2, number, rows, cols), BF),
            VM((3, 2, chips // 2, rows, units), BF),
            pltpu.SemaphoreType.DMA((4, chips)),
            pltpu.SemaphoreType.DMA((4, chips)),
            pltpu.SemaphoreType.DMA((4, 2, chips // 2)),
            pltpu.SemaphoreType.DMA((4, 2, chips // 2)),
        ],
        compiler_params=pltpu.CompilerParams(collective_id=2, has_side_effects=True, vmem_limit_bytes=60 * MIB),
        name="scatter_grads",
    )(
        attn_grad.reshape(number, fsdp, rows, cols),
        *(w.reshape(fsdp, rows, units) for w in (wu, wg, wd)),
    )


def update_kernel(stages, rate, width, ga, gm, small, wa, ma, aa, wm, mm, am, ma_o, wa_o, aa_o, mm_o, wm_o, am_o, small_o, mine, got, send, recv):
    index, x = lax.axis_index("fsdp"), lax.axis_index("mp")
    peers = [(index + (1 << s) * (1 - 2 * ((index // (1 << s)) % 2)), x) for s in range(stages)]
    greet(peers)
    rows = ga.shape[1]
    cols, units = ga.shape[2], gm.shape[2]

    def step(j, r, g, w, m, m_o, w_o):
        grad = g[j, r]
        moment = MOMENTUM * m[j, r] + grad
        stepped = w[j, r] - rate * (grad + MOMENTUM * moment)
        m_o[j, r] = moment
        w_o[j, r] = stepped
        return stepped * stepped

    lanes = mine.shape[2]

    def spots(base, count):
        size = min(count, lanes)
        return [((base + k) // lanes, (base + k) % lanes, k, size) for k in range(0, count, size)]

    def pack(refs, j, count, base):
        def body(i, total):
            r = pl.ds(pl.multiple_of(i * 8, 8), 8)
            return total + step(j, r, *refs)

        total = jnp.sum(lax.fori_loop(0, rows // 8, body, jnp.zeros((8, count), F32)), axis=0, keepdims=True)
        for row, lane, k, size in spots(base, count):
            mine[0, row : row + 1, lane : lane + size] = total[:, k : k + size]

    for j in range(4):
        pack((ga, wa, ma, ma_o, wa_o), j, cols, j * cols)
    for j in range(3):
        pack((gm, wm, mm, mm_o, wm_o), j, units, 4 * cols + j * units)
    squares = (4 * cols + 3 * units) // lanes
    mine[0, squares:] = small[...]
    for s in range(stages):
        copy = remote(mine.at[s], got.at[s], send.at[s], recv.at[s], peers[s])
        copy.start()
        copy.wait()
        mine[s + 1] = mine[s] + got[s]
    small_o[...] = mine[stages, squares:]

    def finish(j, count, base, a, a_o, w_o):
        for row, lane, k, size in spots(base, count):
            c = slice(k, k + size)
            scale = lax.rsqrt(mine[stages, row : row + 1, lane : lane + size] / width + EPS)

            def body(i, _):
                r = pl.ds(pl.multiple_of(i * 8, 8), 8)
                new = w_o[j, r, c] * scale
                w_o[j, r, c] = new
                a_o[j, r, c] = AVERAGE * a[j, r, c] + (1.0 - AVERAGE) * new
                return 0

            lax.fori_loop(0, rows // 8, body, 0)

    for j in range(4):
        finish(j, cols, j * cols, aa, aa_o, wa_o)
    for j in range(3):
        finish(j, units, 4 * cols + j * units, am, am_o, wm_o)


def update(ga, gm, small, wa, ma, aa, wm, mm, am, rate, width, fsdp):
    stages = fsdp.bit_length() - 1
    lanes = small.shape[1]
    squares = (4 * wa.shape[2] + 3 * wm.shape[2]) // lanes
    total = squares + small.shape[0]
    vspec = pl.BlockSpec(memory_space=VM)
    a_shape, m_shape = jax.ShapeDtypeStruct(wa.shape, F32), jax.ShapeDtypeStruct(wm.shape, F32)
    return pl.pallas_call(
        functools.partial(update_kernel, stages, rate, width),
        out_shape=(a_shape, a_shape, a_shape, m_shape, m_shape, m_shape, jax.ShapeDtypeStruct(small.shape, F32)),
        in_specs=[vspec] * 9,
        out_specs=(vspec,) * 7,
        scratch_shapes=[
            VM((stages + 1, total, lanes), F32),
            VM((stages, total, lanes), F32),
            pltpu.SemaphoreType.DMA((stages,)),
            pltpu.SemaphoreType.DMA((stages,)),
        ],
        compiler_params=pltpu.CompilerParams(collective_id=3, has_side_effects=True, vmem_limit_bytes=60 * MIB),
        name="update_weights",
    )(ga, gm, small, wa, ma, aa, wm, mm, am)


def local(
    inputs,
    doc_ids,
    out_grad,
    attn_w,
    attn_mom,
    attn_avg,
    mlp_w,
    mlp_mom,
    mlp_avg,
    head_scale,
    head_mom,
    mix_rates,
    mix_mom,
    unit_scales,
    unit_mom,
):
    length = inputs.shape[1]
    model_width = inputs.shape[2]
    head_count = head_scale.shape[0] // HD
    block_rows = min(512, length)
    block_count = length // block_rows
    tokens = inputs.shape[0] * lax.axis_size("fsdp") * length
    doc_row = doc_ids[0]
    input_low = inputs[0]
    resid_in = input_low.astype(jnp.float32)
    cos_table, sin_table = rotary_tables(doc_row)
    position = jnp.arange(length, dtype=jnp.int32)
    attn_full = lax.all_gather(attn_w.astype(jnp.bfloat16), "fsdp", axis=1, tiled=True)
    projected = jnp.einsum(
        "sd,jdc->jsc", input_low, attn_full[:3], preferred_element_type=jnp.float32
    )
    head_gain = head_scale.reshape(head_count, HD)
    q_rot = rotate(projected[0].reshape(length, head_count, HD), cos_table, sin_table)
    k_rot = rotate(projected[1].reshape(length, head_count, HD), cos_table, sin_table)
    q_unit = rms_unit(q_rot)
    k_unit = rms_unit(k_rot)
    query_low = (head_gain * q_unit).astype(jnp.bfloat16)
    key_low = (head_gain * k_unit).astype(jnp.bfloat16)
    value_low = projected[2].reshape(length, head_count, HD).astype(jnp.bfloat16)

    def scores_of(row_first):
        query_blk = lax.dynamic_slice_in_dim(query_low, row_first, block_rows, 0)
        raw_scores = jnp.einsum(
            "qhe,khe->hqk", query_blk, key_low, preferred_element_type=jnp.float32
        )
        row_pos = lax.dynamic_slice_in_dim(position, row_first, block_rows, 0)
        row_docs = lax.dynamic_slice_in_dim(doc_row, row_first, block_rows, 0)
        allowed = (row_docs[:, None] == doc_row[None, :]) & (position[None, :] <= row_pos[:, None])
        return (jnp.where(allowed[None], raw_scores * HD ** (-0.5), NEG_FILL), query_blk)

    def attend(accums, blk_index):
        scores, query_blk = scores_of(blk_index * block_rows)
        peak_val = jnp.max(scores, axis=-1, keepdims=True)
        expo_vals = jnp.exp(scores - peak_val)
        row_total = jnp.sum(expo_vals, axis=-1, keepdims=True)
        probs_low = (expo_vals / row_total).astype(jnp.bfloat16)
        blk_out = jnp.einsum(
            "hqk,khe->qhe", probs_low, value_low, preferred_element_type=jnp.float32
        )
        return (accums, (blk_out, (peak_val + jnp.log(row_total))[..., 0]))

    _, (mixed_blocks, log_totals) = lax.scan(attend, None, jnp.arange(block_count))
    mixed_low = mixed_blocks.reshape(length, head_count * HD).astype(jnp.bfloat16)
    attn_part = jnp.einsum("sc,dc->sd", mixed_low, attn_full[3], preferred_element_type=jnp.float32)
    attn_out = lax.psum(attn_part, "mp")
    attn_unit = rms_unit(attn_out)
    resid_one = resid_in + mix_rates[0] * (attn_unit - resid_in)
    hidden_one = rms_unit(resid_one)
    hidden_low = hidden_one.astype(jnp.bfloat16)
    mlp_full = lax.all_gather(mlp_w.astype(jnp.bfloat16), "fsdp", axis=1, tiled=True)
    gates = jnp.einsum("sd,jdf->jsf", hidden_low, mlp_full[:2], preferred_element_type=jnp.float32)
    up_proj = gates[0]
    gate_proj = gates[1]
    gate_arg = unit_scales[1] * gate_proj * D ** (-0.5)
    gate_sig = jax.nn.sigmoid(gate_arg)
    gate_act = gate_arg * gate_sig
    units_low = (unit_scales[0] * up_proj * gate_act).astype(jnp.bfloat16)
    mlp_part = jnp.einsum("sf,df->sd", units_low, mlp_full[2], preferred_element_type=jnp.float32)
    mlp_out = lax.psum(mlp_part, "mp")
    mlp_unit = rms_unit(mlp_out)
    resid_two = hidden_one + mix_rates[1] * (mlp_unit - hidden_one)
    result = rms_unit(resid_two)
    cotangent = out_grad[0].astype(jnp.float32)
    d_resid_two = rms_back(resid_two, cotangent)
    grad_mix_mlp = jnp.sum(d_resid_two * (mlp_unit - hidden_one), axis=0)
    d_hidden_one = d_resid_two * (1.0 - mix_rates[1])
    d_mlp_low = rms_back(mlp_out, mix_rates[1] * d_resid_two).astype(jnp.bfloat16)
    mlp_back = lax.all_gather(mlp_w.astype(jnp.bfloat16), "fsdp", axis=1, tiled=True)
    d_units = jnp.einsum("sd,df->sf", d_mlp_low, mlp_back[2], preferred_element_type=jnp.float32)
    d_up = d_units * unit_scales[0] * gate_act
    d_arg = d_units * unit_scales[0] * up_proj * gate_sig * (1.0 + gate_arg * (1.0 - gate_sig))
    d_gate = d_arg * unit_scales[1] * D ** (-0.5)
    grad_units = jnp.stack(
        [
            jnp.sum(d_units * up_proj * gate_act, axis=0),
            jnp.sum(d_arg * gate_proj * D ** (-0.5), axis=0),
        ]
    )
    d_gates_low = jnp.stack([d_up, d_gate]).astype(jnp.bfloat16)
    mlp_back_part = jnp.einsum(
        "jsf,jdf->sd", d_gates_low, mlp_back[:2], preferred_element_type=jnp.float32
    )
    d_hidden_one = d_hidden_one + lax.psum(mlp_back_part, "mp")
    right_cols = d_mlp_low
    left_cols = hidden_low
    grad_mlp = jnp.transpose(
        lax.psum_scatter(
            jnp.concatenate(
                [
                    jnp.einsum(
                        "sd,jsf->djf", left_cols, d_gates_low, preferred_element_type=jnp.float32
                    ),
                    jnp.einsum(
                        "sd,sf->df", right_cols, units_low, preferred_element_type=jnp.float32
                    )[:, None, :],
                ],
                axis=1,
            ),
            "fsdp",
            scatter_dimension=0,
            tiled=True,
        ),
        (1, 0, 2),
    )
    d_resid_one = rms_back(resid_one, d_hidden_one)
    grad_mix_attn = jnp.sum(d_resid_one * (attn_unit - resid_in), axis=0)
    d_resid_in = d_resid_one * (1.0 - mix_rates[0])
    d_attn_low = rms_back(attn_out, mix_rates[0] * d_resid_one).astype(jnp.bfloat16)
    attn_back = lax.all_gather(attn_w.astype(jnp.bfloat16), "fsdp", axis=1, tiled=True)
    d_mixed = jnp.einsum("sd,dc->sc", d_attn_low, attn_back[3], preferred_element_type=jnp.float32)
    d_mixed = d_mixed.astype(jnp.bfloat16).reshape(length, head_count, HD)

    def attend_back(accums, blk_index):
        d_key, d_value = accums
        row_first = blk_index * block_rows
        scores, query_blk = scores_of(row_first)
        blk_total = lax.dynamic_index_in_dim(log_totals, blk_index, 0, keepdims=False)
        attn_probs = jnp.exp(scores - blk_total[..., None])
        d_out_blk = lax.dynamic_slice_in_dim(d_mixed, row_first, block_rows, 0)
        d_probs = jnp.einsum(
            "qhe,khe->hqk", d_out_blk, value_low, preferred_element_type=jnp.float32
        )
        d_scores = attn_probs * (d_probs - jnp.sum(attn_probs * d_probs, axis=-1, keepdims=True))
        d_raw_low = (d_scores * HD ** (-0.5)).astype(jnp.bfloat16)
        d_query = jnp.einsum("hqk,khe->qhe", d_raw_low, key_low, preferred_element_type=jnp.float32)
        d_key = d_key + jnp.einsum(
            "hqk,qhe->khe", d_raw_low, query_blk, preferred_element_type=jnp.float32
        )
        d_value = d_value + jnp.einsum(
            "hqk,qhe->khe",
            attn_probs.astype(jnp.bfloat16),
            d_out_blk,
            preferred_element_type=jnp.float32,
        )
        return ((d_key, d_value), d_query)

    zero_heads = jnp.zeros((length, head_count, HD), jnp.float32)
    (d_key_all, d_value_all), d_query_blocks = lax.scan(
        attend_back, (zero_heads, zero_heads), jnp.arange(block_count)
    )
    d_query_all = d_query_blocks.reshape(length, head_count, HD)
    grad_head = jnp.sum(d_query_all * q_unit + d_key_all * k_unit, axis=0).reshape(-1)
    d_query_raw = rotate_back(rms_back(q_rot, head_gain * d_query_all), cos_table, sin_table)
    d_key_raw = rotate_back(rms_back(k_rot, head_gain * d_key_all), cos_table, sin_table)
    d_proj_low = jnp.stack(
        [
            d_query_raw.reshape(length, -1),
            d_key_raw.reshape(length, -1),
            d_value_all.reshape(length, -1),
        ]
    ).astype(jnp.bfloat16)
    grad_mix = jnp.stack([grad_mix_attn, grad_mix_mlp])
    grad_head, grad_mix, grad_units = lax.psum((grad_head, grad_mix, grad_units), "fsdp")
    attn_back_part = jnp.einsum(
        "jsc,jdc->sd", d_proj_low, attn_back[:3], preferred_element_type=jnp.float32
    )
    input_grad = d_resid_in + lax.psum(attn_back_part.astype(jnp.bfloat16), "mp").astype(
        jnp.float32
    )
    left_cols = input_low
    right_cols = d_attn_low
    in_terms = jnp.einsum("sd,jsc->djc", left_cols, d_proj_low, preferred_element_type=jnp.float32)
    out_terms = jnp.einsum("sd,sc->dc", right_cols, mixed_low, preferred_element_type=jnp.float32)
    grad_attn = jnp.transpose(
        lax.psum_scatter(
            jnp.concatenate([in_terms, out_terms[:, None, :]], axis=1),
            "fsdp",
            scatter_dimension=0,
            tiled=True,
        ),
        (1, 0, 2),
    )
    root_tokens = math.sqrt(tokens)
    weight_rate = RATE_WEIGHT / root_tokens
    attn_mom_new, attn_step = nesterov(attn_w, attn_mom, grad_attn, weight_rate)
    mlp_mom_new, mlp_step = nesterov(mlp_w, mlp_mom, grad_mlp, weight_rate)
    attn_squares = jnp.sum(attn_step * attn_step, axis=1)
    mlp_squares = jnp.sum(mlp_step * mlp_step, axis=1)
    attn_squares, mlp_squares = lax.psum((attn_squares, mlp_squares), "fsdp")
    attn_new = attn_step * lax.rsqrt(attn_squares[:, None, :] / model_width + EPS)
    mlp_new = mlp_step * lax.rsqrt(mlp_squares[:, None, :] / model_width + EPS)
    head_mom_new, head_new = nesterov(head_scale, head_mom, grad_head, RATE_HEAD / root_tokens)
    mix_mom_new, mix_new = nesterov(mix_rates, mix_mom, grad_mix, RATE_MIX / root_tokens)
    units_mom_new, units_new = nesterov(unit_scales, unit_mom, grad_units, RATE_UNITS / root_tokens)
    return (
        result[None],
        input_grad[None],
        attn_mom_new,
        attn_new,
        AVERAGE * attn_avg + (1.0 - AVERAGE) * attn_new,
        mlp_mom_new,
        mlp_new,
        AVERAGE * mlp_avg + (1.0 - AVERAGE) * mlp_new,
        head_mom_new,
        head_new,
        mix_mom_new,
        mix_new,
        units_mom_new,
        units_new,
    )


def local_fast(
    inputs,
    doc_ids,
    out_grad,
    attn_w,
    attn_mom,
    attn_avg,
    mlp_w,
    mlp_mom,
    mlp_avg,
    head_scale,
    head_mom,
    mix_rates,
    mix_mom,
    unit_scales,
    unit_mom,
):
    length = inputs.shape[1]
    model_width = inputs.shape[2]
    head_count = head_scale.shape[0] // HD
    block_rows = min(512, length)
    block_count = length // block_rows
    tokens = inputs.shape[0] * lax.axis_size("fsdp") * length
    doc_row = doc_ids[0]
    input_low = inputs[0]
    resid_in = input_low.astype(jnp.float32)
    cos_table, sin_table = rotary_tables(doc_row)
    position = jnp.arange(length, dtype=jnp.int32)
    fsdp = lax.axis_size("fsdp")
    attn_full, mlp_full, _ = gather_weights(attn_w.astype(BF), mlp_w.astype(BF), fsdp)
    attn_back, mlp_back = attn_full, mlp_full
    projected = jnp.einsum(
        "sd,jdc->jsc", input_low, attn_full[:3], preferred_element_type=jnp.float32
    )
    head_gain = head_scale.reshape(head_count, HD)
    q_rot = rotate(projected[0].reshape(length, head_count, HD), cos_table, sin_table)
    k_rot = rotate(projected[1].reshape(length, head_count, HD), cos_table, sin_table)
    q_unit = rms_unit(q_rot)
    k_unit = rms_unit(k_rot)
    query_low = (head_gain * q_unit).astype(jnp.bfloat16)
    key_low = (head_gain * k_unit).astype(jnp.bfloat16)
    value_low = projected[2].reshape(length, head_count, HD).astype(jnp.bfloat16)

    def scores_of(row_first):
        query_blk = lax.dynamic_slice_in_dim(query_low, row_first, block_rows, 0)
        raw_scores = jnp.einsum(
            "qhe,khe->hqk", query_blk, key_low, preferred_element_type=jnp.float32
        )
        row_pos = lax.dynamic_slice_in_dim(position, row_first, block_rows, 0)
        row_docs = lax.dynamic_slice_in_dim(doc_row, row_first, block_rows, 0)
        allowed = (row_docs[:, None] == doc_row[None, :]) & (position[None, :] <= row_pos[:, None])
        return (jnp.where(allowed[None], raw_scores * HD ** (-0.5), NEG_FILL), query_blk)

    def attend(accums, blk_index):
        scores, query_blk = scores_of(blk_index * block_rows)
        peak_val = jnp.max(scores, axis=-1, keepdims=True)
        expo_vals = jnp.exp(scores - peak_val)
        row_total = jnp.sum(expo_vals, axis=-1, keepdims=True)
        probs_low = (expo_vals / row_total).astype(jnp.bfloat16)
        blk_out = jnp.einsum(
            "hqk,khe->qhe", probs_low, value_low, preferred_element_type=jnp.float32
        )
        return (accums, (blk_out, (peak_val + jnp.log(row_total))[..., 0]))

    _, (mixed_blocks, log_totals) = lax.scan(attend, None, jnp.arange(block_count))
    mixed_low = mixed_blocks.reshape(length, head_count * HD).astype(jnp.bfloat16)
    attn_part = jnp.einsum("sc,dc->sd", mixed_low, attn_full[3], preferred_element_type=jnp.float32)
    attn_out = lax.psum(attn_part, "mp")
    attn_unit = rms_unit(attn_out)
    resid_one = resid_in + mix_rates[0] * (attn_unit - resid_in)
    hidden_one = rms_unit(resid_one)
    hidden_low = hidden_one.astype(jnp.bfloat16)
    gates = jnp.einsum("sd,jdf->jsf", hidden_low, mlp_full[:2], preferred_element_type=jnp.float32)
    up_proj = gates[0]
    gate_proj = gates[1]
    gate_arg = unit_scales[1] * gate_proj * D ** (-0.5)
    gate_sig = jax.nn.sigmoid(gate_arg)
    gate_act = gate_arg * gate_sig
    units_low = (unit_scales[0] * up_proj * gate_act).astype(jnp.bfloat16)
    mlp_part = jnp.einsum("sf,df->sd", units_low, mlp_full[2], preferred_element_type=jnp.float32)
    mlp_out = lax.psum(mlp_part, "mp")
    mlp_unit = rms_unit(mlp_out)
    resid_two = hidden_one + mix_rates[1] * (mlp_unit - hidden_one)
    result = rms_unit(resid_two)
    cotangent = out_grad[0].astype(jnp.float32)
    d_resid_two = rms_back(resid_two, cotangent)
    grad_mix_mlp = jnp.sum(d_resid_two * (mlp_unit - hidden_one), axis=0)
    d_hidden_one = d_resid_two * (1.0 - mix_rates[1])
    d_mlp_low = rms_back(mlp_out, mix_rates[1] * d_resid_two).astype(jnp.bfloat16)
    d_units = jnp.einsum("sd,df->sf", d_mlp_low, mlp_back[2], preferred_element_type=jnp.float32)
    d_up = d_units * unit_scales[0] * gate_act
    d_arg = d_units * unit_scales[0] * up_proj * gate_sig * (1.0 + gate_arg * (1.0 - gate_sig))
    d_gate = d_arg * unit_scales[1] * D ** (-0.5)
    grad_units = jnp.stack(
        [
            jnp.sum(d_units * up_proj * gate_act, axis=0),
            jnp.sum(d_arg * gate_proj * D ** (-0.5), axis=0),
        ]
    )
    d_gates_low = jnp.stack([d_up, d_gate]).astype(jnp.bfloat16)
    mlp_back_part = jnp.einsum(
        "jsf,jdf->sd", d_gates_low, mlp_back[:2], preferred_element_type=jnp.float32
    )
    d_hidden_one = d_hidden_one + lax.psum(mlp_back_part, "mp")
    w_u = jnp.einsum("sd,sf->df", hidden_low, d_gates_low[0], preferred_element_type=jnp.float32).astype(BF)
    w_g = jnp.einsum("sd,sf->df", hidden_low, d_gates_low[1], preferred_element_type=jnp.float32).astype(BF)
    w_d = jnp.einsum("sd,sf->df", d_mlp_low, units_low, preferred_element_type=jnp.float32).astype(BF)
    d_resid_one = rms_back(resid_one, d_hidden_one)
    grad_mix_attn = jnp.sum(d_resid_one * (attn_unit - resid_in), axis=0)
    d_resid_in = d_resid_one * (1.0 - mix_rates[0])
    d_attn_low = rms_back(attn_out, mix_rates[0] * d_resid_one).astype(jnp.bfloat16)
    d_mixed = jnp.einsum("sd,dc->sc", d_attn_low, attn_back[3], preferred_element_type=jnp.float32)
    d_mixed = d_mixed.astype(jnp.bfloat16).reshape(length, head_count, HD)

    def attend_back(accums, blk_index):
        d_key, d_value = accums
        row_first = blk_index * block_rows
        scores, query_blk = scores_of(row_first)
        blk_total = lax.dynamic_index_in_dim(log_totals, blk_index, 0, keepdims=False)
        attn_probs = jnp.exp(scores - blk_total[..., None])
        d_out_blk = lax.dynamic_slice_in_dim(d_mixed, row_first, block_rows, 0)
        d_probs = jnp.einsum(
            "qhe,khe->hqk", d_out_blk, value_low, preferred_element_type=jnp.float32
        )
        d_scores = attn_probs * (d_probs - jnp.sum(attn_probs * d_probs, axis=-1, keepdims=True))
        d_raw_low = (d_scores * HD ** (-0.5)).astype(jnp.bfloat16)
        d_query = jnp.einsum("hqk,khe->qhe", d_raw_low, key_low, preferred_element_type=jnp.float32)
        d_key = d_key + jnp.einsum(
            "hqk,qhe->khe", d_raw_low, query_blk, preferred_element_type=jnp.float32
        )
        d_value = d_value + jnp.einsum(
            "hqk,qhe->khe",
            attn_probs.astype(jnp.bfloat16),
            d_out_blk,
            preferred_element_type=jnp.float32,
        )
        return ((d_key, d_value), d_query)

    zero_heads = jnp.zeros((length, head_count, HD), jnp.float32)
    (d_key_all, d_value_all), d_query_blocks = lax.scan(
        attend_back, (zero_heads, zero_heads), jnp.arange(block_count)
    )
    d_query_all = d_query_blocks.reshape(length, head_count, HD)
    grad_head = jnp.sum(d_query_all * q_unit + d_key_all * k_unit, axis=0).reshape(-1)
    d_query_raw = rotate_back(rms_back(q_rot, head_gain * d_query_all), cos_table, sin_table)
    d_key_raw = rotate_back(rms_back(k_rot, head_gain * d_key_all), cos_table, sin_table)
    d_proj_low = jnp.stack(
        [
            d_query_raw.reshape(length, -1),
            d_key_raw.reshape(length, -1),
            d_value_all.reshape(length, -1),
        ]
    ).astype(jnp.bfloat16)
    grad_mix = jnp.stack([grad_mix_attn, grad_mix_mlp])
    attn_back_part = jnp.einsum(
        "jsc,jdc->sd", d_proj_low, attn_back[:3], preferred_element_type=jnp.float32
    )
    input_grad = d_resid_in + lax.psum(attn_back_part.astype(jnp.bfloat16), "mp").astype(
        jnp.float32
    )
    in_terms = jnp.einsum("sd,jsc->jdc", input_low, d_proj_low, preferred_element_type=jnp.float32)
    out_terms = jnp.einsum("sd,sc->dc", d_attn_low, mixed_low, preferred_element_type=jnp.float32)
    w_a = jnp.concatenate([in_terms, out_terms[None]], 0).astype(BF)
    grad_attn, grad_mlp = scatter_grads(w_a, w_u, w_g, w_d, fsdp)
    root_tokens = math.sqrt(tokens)
    weight_rate = RATE_WEIGHT / root_tokens
    small = jnp.concatenate([jnp.pad(grad_head, (0, D - grad_head.shape[0])), grad_mix.reshape(-1), grad_units.reshape(-1), jnp.zeros((D,), F32)]).reshape(8, D)
    attn_mom_new, attn_new, attn_avg_new, mlp_mom_new, mlp_new, mlp_avg_new, small = update(
        grad_attn, grad_mlp, small, attn_w, attn_mom, attn_avg, mlp_w, mlp_mom, mlp_avg, weight_rate, model_width, fsdp)
    grad_head, grad_mix, grad_units = small[0, : grad_head.shape[0]], small[1:3], small[3:7].reshape(2, -1)
    head_mom_new, head_new = nesterov(head_scale, head_mom, grad_head, RATE_HEAD / root_tokens)
    mix_mom_new, mix_new = nesterov(mix_rates, mix_mom, grad_mix, RATE_MIX / root_tokens)
    units_mom_new, units_new = nesterov(unit_scales, unit_mom, grad_units, RATE_UNITS / root_tokens)
    return (
        result[None],
        input_grad[None],
        attn_mom_new,
        attn_new,
        attn_avg_new,
        mlp_mom_new,
        mlp_new,
        mlp_avg_new,
        head_mom_new,
        head_new,
        mix_mom_new,
        mix_new,
        units_mom_new,
        units_new,
    )


def solution(mesh):
    fast = D // mesh.shape["fsdp"] % 16 == 0 and mesh.shape["fsdp"] % 8 == 0
    placed = (
        P("fsdp", None, None),
        P("fsdp", None),
        P("fsdp", None, None),
        P(None, "fsdp", "mp"),
        P(None, "fsdp", "mp"),
        P(None, "fsdp", "mp"),
        P(None, "fsdp", "mp"),
        P(None, "fsdp", "mp"),
        P(None, "fsdp", "mp"),
        P("mp"),
        P("mp"),
        P(),
        P(),
        P(None, "mp"),
        P(None, "mp"),
    )
    return jax.shard_map(
        local_fast if fast else local,
        mesh=mesh,
        in_specs=placed,
        out_specs=(
            P("fsdp", None, None),
            P("fsdp", None, None),
            P(None, "fsdp", "mp"),
            P(None, "fsdp", "mp"),
            P(None, "fsdp", "mp"),
            P(None, "fsdp", "mp"),
            P(None, "fsdp", "mp"),
            P(None, "fsdp", "mp"),
            P("mp"),
            P("mp"),
            P(),
            P(),
            P(None, "mp"),
            P(None, "mp"),
        ),
        check_vma=False,
    )
```

```python
import functools
import math

import jax
import jax.numpy as jnp
from jax import lax
from jax.experimental import pallas as pl
from jax.experimental.pallas import tpu as pltpu
from jax.sharding import PartitionSpec as P

D = 1024
HD = 64


EPS = 1e-06
MOMENTUM = 0.9
AVERAGE = 0.9
NEG_FILL = -1e30
THETA = 10000.0
RATE_WEIGHT = 50.0
RATE_HEAD = 0.08
RATE_MIX = 0.02
RATE_UNITS = 0.5


def rms_unit(vector):
    return vector * lax.rsqrt(jnp.mean(vector * vector, axis=-1, keepdims=True) + EPS)


def rms_back(vector, grad):
    factor = lax.rsqrt(jnp.mean(vector * vector, axis=-1, keepdims=True) + EPS)
    unit_vec = vector * factor
    return factor * (grad - unit_vec * jnp.mean(grad * unit_vec, axis=-1, keepdims=True))


def rotary_tables(doc_row):
    length = doc_row.shape[0]
    position = jnp.arange(length, dtype=jnp.int32)
    boundary = jnp.concatenate(
        [jnp.ones((1,), jnp.int32), (doc_row[1:] != doc_row[:-1]).astype(jnp.int32)]
    )
    doc_start = lax.cummax(jnp.where(boundary > 0, position, 0), axis=0)
    offset = (position - doc_start).astype(jnp.float32)
    freq = THETA ** (-2.0 * jnp.arange(HD // 2, dtype=jnp.float32) / HD)
    angle = offset[:, None] * freq[None, :]
    return (jnp.cos(angle), jnp.sin(angle))


def rotate(vector, cos_table, sin_table):
    half_dim = vector.shape[-1] // 2
    lower_half = vector[..., :half_dim]
    upper_half = vector[..., half_dim:]
    cos_part = cos_table[:, None, :]
    sin_part = sin_table[:, None, :]
    return jnp.concatenate(
        [
            lower_half * cos_part - upper_half * sin_part,
            lower_half * sin_part + upper_half * cos_part,
        ],
        axis=-1,
    )


def rotate_back(grad, cos_table, sin_table):
    half_dim = grad.shape[-1] // 2
    lower_half = grad[..., :half_dim]
    upper_half = grad[..., half_dim:]
    cos_part = cos_table[:, None, :]
    sin_part = sin_table[:, None, :]
    return jnp.concatenate(
        [
            lower_half * cos_part + upper_half * sin_part,
            upper_half * cos_part - lower_half * sin_part,
        ],
        axis=-1,
    )


def nesterov(param, moment, grad, step_rate):
    moment_new = MOMENTUM * moment + grad
    return (moment_new, param - step_rate * (grad + MOMENTUM * moment_new))


BF = jnp.bfloat16
F32 = jnp.float32
MESH = pl.DeviceIdType.MESH
VM = pltpu.VMEM
MIB = 1 << 20


def dot_nn(a, b):
    return lax.dot_general(a, b, (((1,), (0,)), ((), ())), preferred_element_type=F32)


def dot_nt(a, b):
    return lax.dot_general(a, b, (((1,), (1,)), ((), ())), preferred_element_type=F32)


def dot_tn(a, b):
    return lax.dot_general(a, b, (((0,), (0,)), ((), ())), preferred_element_type=F32)


def split_dot(a, ones):
    high = a.astype(BF)
    return dot_nn(high, ones) + dot_nn((a - high.astype(F32)).astype(BF), ones)


def ring_place(index, chips):
    z, y = index // 4, (index // 2) % 2
    return z + y * (chips - 1 - 2 * z), index % 2


def ring_device(place, core, chips):
    y = place // (chips // 2)
    return ((place + y * (chips - 1 - 2 * place)) * 2 + y) * 2 + core


def greet(peers):
    barrier = pltpu.get_barrier_semaphore()
    for peer in peers:
        pl.semaphore_signal(barrier, inc=1, device_id=peer, device_id_type=MESH)
    pl.semaphore_wait(barrier, len(peers))


def remote(src, dst, send, recv, peer):
    return pltpu.make_async_remote_copy(
        src_ref=src, dst_ref=dst, send_sem=send, recv_sem=recv, device_id=peer, device_id_type=MESH
    )


GATHER_GROUPS = ((0, 0, 3), (0, 3, 1), (1, 0, 1), (1, 1, 1), (1, 2, 1))


def hops(group, chips):
    long, short = chips // 2, chips - 1 - chips // 2
    return (long, short) if group % 2 == 0 else (short, long)


def gather_kernel(
    chips, attn_ref, mlp_ref, attn_out, mlp_out, wo_out,
    ring_send, ring_recv, pair_send, pair_recv, own_sem, wo_send, wo_recv,
):
    index, x = lax.axis_index("fsdp"), lax.axis_index("mp")
    place, core = ring_place(index, chips)
    rows = attn_ref.shape[1]
    right = (ring_device((place + 1) % chips, core, chips), x)
    left = (ring_device((place + chips - 1) % chips, core, chips), x)
    pair = (index + 1 - 2 * core, x)
    across = (index, 1 - x)
    greet((right, left, pair, across))
    outs = (attn_out, mlp_out)
    ins = (attn_ref, mlp_ref)

    def block(group, dev):
        kind, first, count = GATHER_GROUPS[group]
        return outs[kind].at[pl.ds(first, count), pl.ds(pl.multiple_of(dev * rows, rows), rows), :]

    def own(group):
        kind, first, count = GATHER_GROUPS[group]
        return ins[kind].at[pl.ds(first, count)]

    def ring_copy(group, way, hop):
        origin = ring_device((place + chips - (hop - 1)) % chips if way == 0 else (place + hop - 1) % chips, core, chips)
        src = own(group) if hop == 1 else block(group, origin)
        return remote(
            src, block(group, origin), ring_send.at[group, way, hop - 1], ring_recv.at[group, way, hop - 1],
            right if way == 0 else left,
        )

    def arrived(group, way, hop):
        origin = (place + 2 * chips - hop) % chips if way == 0 else (place + hop) % chips
        return ring_device(origin, core, chips)

    def pair_copy(group, slot, dev, first):
        src = own(group) if first else block(group, dev)
        return remote(src, block(group, dev), pair_send.at[group, slot], pair_recv.at[group, slot], pair)

    def await_ring(group, way, hop):
        here = block(group, arrived(group, way, hop))
        remote(here, here, ring_send.at[group, way, hop - 1], ring_recv.at[group, way, hop - 1], right).wait_recv()

    def await_pair(group):
        counts = hops(group, chips)
        pair_copy(group, 0, pair_index, False).wait_recv()
        for way in (0, 1):
            for hop in range(1, counts[way] + 1):
                dev = arrived(group, way, hop) + 1 - 2 * core
                pair_copy(group, hop if way == 0 else counts[0] + hop, dev, False).wait_recv()

    pair_index = index + 1 - 2 * core
    sent = []
    groups = range(len(GATHER_GROUPS))
    for group in groups:
        for way in (0, 1):
            copy = ring_copy(group, way, 1)
            copy.start()
            sent.append(copy)
    for group in groups:
        copy = pltpu.make_async_copy(own(group), block(group, index), own_sem.at[group])
        copy.start()
        sent.append(("own", copy))
        copy = pair_copy(group, 0, index, True)
        copy.start()
        sent.append(copy)
    longest = chips // 2
    for hop in range(1, longest + 1):
        for group in groups:
            counts = hops(group, chips)
            for way in (0, 1):
                if hop > counts[way]:
                    continue
                await_ring(group, way, hop)
                dev = arrived(group, way, hop)
                if hop < counts[way]:
                    copy = ring_copy(group, way, hop + 1)
                    copy.start()
                    sent.append(copy)
                slot = hop if way == 0 else counts[0] + hop
                copy = pair_copy(group, slot, dev, False)
                copy.start()
                sent.append(copy)
            if group == 1 and hop == longest:
                await_pair(group)
                own_wait = [c for c in sent if isinstance(c, tuple)][1]
                own_wait[1].wait()
                sent = [c for c in sent if c is not own_wait]
                wo_copy = remote(attn_out.at[3], wo_out, wo_send, wo_recv, across)
                wo_copy.start()
    for group in groups:
        if group == 1:
            continue
        await_pair(group)
    for copy in sent:
        if isinstance(copy, tuple):
            copy[1].wait()
        else:
            copy.wait_send()
    wo_copy.wait()


def gather_weights(attn_low, mlp_low, fsdp):
    chips = fsdp // 2
    rows, cols = attn_low.shape[1:]
    units = mlp_low.shape[2]
    number = len(GATHER_GROUPS)
    anyspec = pl.BlockSpec(memory_space=pl.ANY)
    return pl.pallas_call(
        functools.partial(gather_kernel, chips),
        out_shape=(
            jax.ShapeDtypeStruct((4, rows * fsdp, cols), BF),
            jax.ShapeDtypeStruct((3, rows * fsdp, units), BF),
            jax.ShapeDtypeStruct((rows * fsdp, cols), BF),
        ),
        in_specs=[anyspec] * 2,
        out_specs=(anyspec,) * 3,
        scratch_shapes=[
            pltpu.SemaphoreType.DMA((number, 2, chips // 2)),
            pltpu.SemaphoreType.DMA((number, 2, chips // 2)),
            pltpu.SemaphoreType.DMA((number, chips)),
            pltpu.SemaphoreType.DMA((number, chips)),
            pltpu.SemaphoreType.DMA((number,)),
            pltpu.SemaphoreType.DMA,
            pltpu.SemaphoreType.DMA,
        ],
        compiler_params=pltpu.CompilerParams(collective_id=1, has_side_effects=True),
        name="gather_weights",
    )(attn_low, mlp_low)


def scatter_kernel(chips, attn_ref, wu_ref, wg_ref, wd_ref, attn_out, mlp_out, near_attn, near_mlp, first_attn, first_mlp, ring_attn, ring_mlp,
                   pair_send, pair_recv, ring_send, ring_recv):
    index, x = lax.axis_index("fsdp"), lax.axis_index("mp")
    place, core = ring_place(index, chips)
    right = (ring_device((place + 1) % chips, core, chips), x)
    left = (ring_device((place + chips - 1) % chips, core, chips), x)
    pair = (index + 1 - 2 * core, x)
    greet((right, left, pair))
    owns = (wu_ref, wg_ref, wd_ref, attn_ref)

    def mine(group, dev):
        if group == 3:
            return attn_ref.at[:, dev]
        return owns[group].at[dev]

    def near(group, chip):
        if group == 3:
            return near_attn.at[:, chip]
        return near_mlp.at[group, chip]

    def first(group, way):
        return first_attn.at[way] if group == 3 else first_mlp.at[group, way]

    def slot(group, way, hop):
        if group == 3:
            return ring_attn.at[way, hop - 1]
        return ring_mlp.at[group, way, hop - 1]

    order = (2, 0, 1, 3)
    pairs = {}
    for group in order:
        for chip in range(chips):
            dev = chip * 2 + 1 - core
            copy = remote(mine(group, dev), near(group, chip), pair_send.at[group, chip], pair_recv.at[group, chip], pair)
            copy.start()
            pairs[group, chip] = copy

    def add_into(group, dst, dev, extra):
        src_a, src_b = mine(group, dev), near(group, dev // 2)
        rows = src_a.shape[-2]
        if group == 3:
            for j in range(src_a.shape[0]):
                total = src_a[j].astype(F32) + src_b[j].astype(F32)
                for other in extra:
                    total = total + other[j].astype(F32)
                dst[j] = total.astype(dst.dtype)
        else:
            step = 16
            def body(i, _):
                r = pl.ds(pl.multiple_of(i * step, step), step)
                total = src_a[r].astype(F32) + src_b[r].astype(F32)
                for other in extra:
                    total = total + other[r].astype(F32)
                dst[r] = total.astype(dst.dtype)
                return 0
            lax.fori_loop(0, rows // step, body, 0)

    def target(way, count):
        return ring_device((place + count) % chips if way == 0 else (place + 2 * chips - count) % chips, core, chips)

    sends = []
    for group in order:
        counts = hops(group, chips)
        for chip in range(chips):
            pairs[group, chip].wait()
        for way in (0, 1):
            dev = target(way, counts[way])
            add_into(group, first(group, way), dev, ())
            copy = remote(first(group, way), slot(group, way, 1), ring_send.at[group, way, 0], ring_recv.at[group, way, 0], right if way == 0 else left)
            copy.start()
            sends.append(copy)
    for hop in range(1, chips // 2 + 1):
        for group in order:
            counts = hops(group, chips)
            for way in (0, 1):
                if hop > counts[way]:
                    continue
                here = slot(group, way, hop)
                remote(here, here, ring_send.at[group, way, hop - 1], ring_recv.at[group, way, hop - 1], right if way == 0 else left).wait_recv()
                if hop < counts[way]:
                    dev = target(way, counts[way] - hop)
                    add_into(group, here, dev, (here,))
                    copy = remote(here, slot(group, way, hop + 1), ring_send.at[group, way, hop], ring_recv.at[group, way, hop], right if way == 0 else left)
                    copy.start()
                    sends.append(copy)
            if hop == chips // 2:
                extra = (slot(group, 0, counts[0]), slot(group, 1, counts[1]))
                dst = attn_out if group == 3 else mlp_out.at[group]
                add_into(group, dst, index, extra)
    for copy in sends:
        copy.wait_send()


def scatter_grads(attn_grad, wu, wg, wd, fsdp):
    chips = fsdp // 2
    number, width, cols = attn_grad.shape
    rows, units = width // fsdp, wu.shape[1]
    vspec = pl.BlockSpec(memory_space=VM)
    return pl.pallas_call(
        functools.partial(scatter_kernel, chips),
        out_shape=(
            jax.ShapeDtypeStruct((number, rows, cols), F32),
            jax.ShapeDtypeStruct((3, rows, units), F32),
        ),
        in_specs=[vspec] * 4,
        out_specs=(vspec,) * 2,
        scratch_shapes=[
            VM((number, chips, rows, cols), BF),
            VM((3, chips, rows, units), BF),
            VM((2, number, rows, cols), BF),
            VM((3, 2, rows, units), BF),
            VM((2, chips // 2, number, rows, cols), BF),
            VM((3, 2, chips // 2, rows, units), BF),
            pltpu.SemaphoreType.DMA((4, chips)),
            pltpu.SemaphoreType.DMA((4, chips)),
            pltpu.SemaphoreType.DMA((4, 2, chips // 2)),
            pltpu.SemaphoreType.DMA((4, 2, chips // 2)),
        ],
        compiler_params=pltpu.CompilerParams(collective_id=2, has_side_effects=True, vmem_limit_bytes=60 * MIB),
        name="scatter_grads",
    )(
        attn_grad.reshape(number, fsdp, rows, cols),
        *(w.reshape(fsdp, rows, units) for w in (wu, wg, wd)),
    )


def update_kernel(stages, rate, width, ga, gm, small, wa, ma, aa, wm, mm, am, ma_o, wa_o, aa_o, mm_o, wm_o, am_o, small_o, mine, got, send, recv):
    index, x = lax.axis_index("fsdp"), lax.axis_index("mp")
    peers = [(index + (1 << s) * (1 - 2 * ((index // (1 << s)) % 2)), x) for s in range(stages)]
    greet(peers)
    rows = ga.shape[1]
    cols, units = ga.shape[2], gm.shape[2]

    def step(j, r, g, w, m, m_o, w_o):
        grad = g[j, r]
        moment = MOMENTUM * m[j, r] + grad
        stepped = w[j, r] - rate * (grad + MOMENTUM * moment)
        m_o[j, r] = moment
        w_o[j, r] = stepped
        return stepped * stepped

    lanes = mine.shape[2]

    def spots(base, count):
        size = min(count, lanes)
        return [((base + k) // lanes, (base + k) % lanes, k, size) for k in range(0, count, size)]

    def pack(refs, j, count, base):
        def body(i, total):
            r = pl.ds(pl.multiple_of(i * 8, 8), 8)
            return total + step(j, r, *refs)

        total = jnp.sum(lax.fori_loop(0, rows // 8, body, jnp.zeros((8, count), F32)), axis=0, keepdims=True)
        for row, lane, k, size in spots(base, count):
            mine[0, row : row + 1, lane : lane + size] = total[:, k : k + size]

    for j in range(4):
        pack((ga, wa, ma, ma_o, wa_o), j, cols, j * cols)
    for j in range(3):
        pack((gm, wm, mm, mm_o, wm_o), j, units, 4 * cols + j * units)
    squares = (4 * cols + 3 * units) // lanes
    mine[0, squares:] = small[...]
    for s in range(stages):
        copy = remote(mine.at[s], got.at[s], send.at[s], recv.at[s], peers[s])
        copy.start()
        copy.wait()
        mine[s + 1] = mine[s] + got[s]
    small_o[...] = mine[stages, squares:]

    def finish(j, count, base, a, a_o, w_o):
        for row, lane, k, size in spots(base, count):
            c = slice(k, k + size)
            scale = lax.rsqrt(mine[stages, row : row + 1, lane : lane + size] / width + EPS)

            def body(i, _):
                r = pl.ds(pl.multiple_of(i * 8, 8), 8)
                new = w_o[j, r, c] * scale
                w_o[j, r, c] = new
                a_o[j, r, c] = AVERAGE * a[j, r, c] + (1.0 - AVERAGE) * new
                return 0

            lax.fori_loop(0, rows // 8, body, 0)

    for j in range(4):
        finish(j, cols, j * cols, aa, aa_o, wa_o)
    for j in range(3):
        finish(j, units, 4 * cols + j * units, am, am_o, wm_o)


def update(ga, gm, small, wa, ma, aa, wm, mm, am, rate, width, fsdp):
    stages = fsdp.bit_length() - 1
    lanes = small.shape[1]
    squares = (4 * wa.shape[2] + 3 * wm.shape[2]) // lanes
    total = squares + small.shape[0]
    vspec = pl.BlockSpec(memory_space=VM)
    a_shape, m_shape = jax.ShapeDtypeStruct(wa.shape, F32), jax.ShapeDtypeStruct(wm.shape, F32)
    return pl.pallas_call(
        functools.partial(update_kernel, stages, rate, width),
        out_shape=(a_shape, a_shape, a_shape, m_shape, m_shape, m_shape, jax.ShapeDtypeStruct(small.shape, F32)),
        in_specs=[vspec] * 9,
        out_specs=(vspec,) * 7,
        scratch_shapes=[
            VM((stages + 1, total, lanes), F32),
            VM((stages, total, lanes), F32),
            pltpu.SemaphoreType.DMA((stages,)),
            pltpu.SemaphoreType.DMA((stages,)),
        ],
        compiler_params=pltpu.CompilerParams(collective_id=3, has_side_effects=True, vmem_limit_bytes=60 * MIB),
        name="update_weights",
    )(ga, gm, small, wa, ma, aa, wm, mm, am)


BLOCK = 256
SPAN = 512


def head_ones():
    row = lax.broadcasted_iota(jnp.int32, (128, 128), 0) // HD
    col = lax.broadcasted_iota(jnp.int32, (128, 128), 1) // HD
    return jnp.where(row == col, 1.0, 0.0).astype(BF)


def half_of(rows, half):
    lane = lax.broadcasted_iota(jnp.int32, (rows, 128), 1)
    return jnp.where((lane < HD) == (half == 0), 1.0, 0.0).astype(BF)


def other_half(v):
    lane = lax.broadcasted_iota(jnp.int32, v.shape, 1)
    return jnp.where(lane % HD < HD // 2, pltpu.roll(v, 128 - HD // 2, 1), pltpu.roll(v, HD // 2, 1))


def first_key(block):
    return max(0, block * BLOCK - SPAN)


def forward_kernel(x_ref, w_ref, cos_ref, sin_ref, gain_ref, start_ref, q_o, k_o, v_o, rq_o, rk_o, y_o, bias, send, recv):
    index, x = lax.axis_index("fsdp"), lax.axis_index("mp")
    across = (index, 1 - x)
    greet((across,))
    length, cols = q_o.shape
    ones = head_ones()

    def project(i, _):
        rows = pl.ds(pl.multiple_of(i * BLOCK, BLOCK), BLOCK)
        states = x_ref[rows]
        cos, sin = cos_ref[rows], sin_ref[rows]
        for j, (out, factor_o, scale) in enumerate(((q_o, rq_o, HD**-0.5), (k_o, rk_o, 1.0))):
            raw = dot_nn(states, w_ref[j])
            for c in range(0, cols, 128):
                part = raw[:, c : c + 128]
                factor = lax.rsqrt(split_dot(part * part, ones) * (1.0 / HD) + EPS)
                unit = (part * cos + other_half(part) * sin) * factor
                out[rows, c : c + 128] = ((gain_ref[:, c : c + 128] * unit).astype(BF).astype(F32) * scale).astype(BF)
                factor_o[rows, c : c + 128] = factor
        v_o[rows] = dot_nn(states, w_ref[2]).astype(BF)
        return 0

    lax.fori_loop(0, length // BLOCK, project, 0)
    copies = []
    for block in range(length // BLOCK):
        low = first_key(block)
        keys = (block + 1) * BLOCK - low
        rows = pl.ds(block * BLOCK, BLOCK)
        span = pl.ds(low, keys)
        kpos = lax.broadcasted_iota(jnp.int32, (BLOCK, keys), 1) + low
        qpos = lax.broadcasted_iota(jnp.int32, (BLOCK, keys), 0) + block * BLOCK
        allowed = (kpos >= start_ref[rows]) & (kpos <= qpos)
        bias[:, :keys] = jnp.where(allowed, 0.0, NEG_FILL)

        def heads(pair, _):
            c = pl.ds(pl.multiple_of(pair * 128, 128), 128)
            q, k, v = q_o[rows, c], k_o[span, c], v_o[span, c]
            outs = []
            for half in (0, 1):
                scores = dot_nt(q * half_of(BLOCK, half), k)
                probs = jnp.exp(scores + bias[:, :keys]).astype(BF)
                outs.append(dot_nn(probs, v * half_of(keys, half) + half_of(keys, 1 - half)))
            lane = lax.broadcasted_iota(jnp.int32, (BLOCK, 128), 1)
            total = pltpu.roll(jnp.where(lane < HD, outs[1], outs[0]), HD, 1)
            y_o[x, rows, c] = (jnp.where(lane < HD, outs[0], outs[1]) / total).astype(BF)
            return 0

        lax.fori_loop(0, cols // 128, heads, 0)
        copy = remote(y_o.at[x, rows], y_o.at[x, rows], send.at[block], recv.at[block], across)
        copy.start()
        copies.append(copy)
    for copy in copies:
        copy.wait_send()
    for block in range(length // BLOCK):
        there = y_o.at[1 - x, pl.ds(block * BLOCK, BLOCK)]
        remote(there, there, send.at[block], recv.at[block], across).wait_recv()


def attention_forward(states, weights, cos, sin, gain, start):
    length, cols = states.shape[0], gain.shape[1]
    vspec = pl.BlockSpec(memory_space=VM)
    blocks = length // BLOCK
    low = jax.ShapeDtypeStruct((length, cols), BF)
    full = jax.ShapeDtypeStruct((length, cols), F32)
    return pl.pallas_call(
        forward_kernel,
        out_shape=(low, low, low, full, full, jax.ShapeDtypeStruct((2, length, cols), BF)),
        in_specs=[vspec] * 6,
        out_specs=(vspec,) * 6,
        scratch_shapes=[
            VM((BLOCK, BLOCK + SPAN), F32),
            pltpu.SemaphoreType.DMA((blocks,)),
            pltpu.SemaphoreType.DMA((blocks,)),
        ],
        compiler_params=pltpu.CompilerParams(collective_id=4, has_side_effects=True, vmem_limit_bytes=60 * MIB),
        name="attention_forward",
    )(states, weights, cos, sin, gain, start)


def backward_kernel(
    x_ref, w_ref, q_ref, k_ref, v_ref, rq_ref, rk_ref, y_ref, dy_ref, do_ref, dri_ref, cos_ref, sin_ref, gain_ref, start_ref,
    ig_o, head_o, dw_o, bias, dq_s, dk_s, dv_s, low_s, out_s, in_s, send, recv,
):
    index, x = lax.axis_index("fsdp"), lax.axis_index("mp")
    across = (index, 1 - x)
    greet((across,))
    length, cols = q_ref.shape
    width = x_ref.shape[1]
    ones = head_ones()
    dk_s[...] = jnp.zeros_like(dk_s)
    dv_s[...] = jnp.zeros_like(dv_s)
    head_o[...] = jnp.zeros_like(head_o)
    copies = {}
    for block in reversed(range(length // BLOCK)):
        low = first_key(block)
        keys = (block + 1) * BLOCK - low
        rows = pl.ds(block * BLOCK, BLOCK)
        span = pl.ds(low, keys)
        kpos = lax.broadcasted_iota(jnp.int32, (keys, BLOCK), 0) + low
        qpos = lax.broadcasted_iota(jnp.int32, (keys, BLOCK), 1) + block * BLOCK
        allowed = (kpos >= start_ref[:, block * BLOCK : (block + 1) * BLOCK]) & (kpos <= qpos)
        bias[:keys] = jnp.where(allowed, 0.0, NEG_FILL)

        def heads(pair, _):
            c = pl.ds(pl.multiple_of(pair * 128, 128), 128)
            q, k, v, dy = q_ref[rows, c], k_ref[span, c], v_ref[span, c], dy_ref[rows, c]
            prod = dy.astype(F32) * y_ref[x, rows, c].astype(F32)
            prod_high = prod.astype(BF)
            prod_low = (prod - prod_high.astype(F32)).astype(BF)
            dq = jnp.zeros((BLOCK, 128), F32)
            dk = jnp.zeros((keys, 128), F32)
            dv = jnp.zeros((keys, 128), F32)
            for half in (0, 1):
                mask, row = half_of(BLOCK, half), half_of(8, half)
                qm, dym, km = q * mask, dy * mask, k * half_of(keys, half)
                expo = jnp.exp(dot_nt(k, qm) + bias[:keys])
                probs = expo * (1.0 / jnp.sum(expo, axis=0, keepdims=True))
                delta = (dot_nt(row, prod_high) + dot_nt(row, prod_low))[0:1]
                dz = (probs * (dot_nt(v, dym) - delta)).astype(BF)
                dk = dk + dot_nn(dz, qm)
                dv = dv + dot_nn(probs.astype(BF), dym)
                dq = dq + dot_tn(dz, km)
            dq_s[rows, c] = dq * HD**-0.5
            dk_s[span, c] = dk_s[span, c] + dk
            dv_s[span, c] = dv_s[span, c] + dv
            return 0

        lax.fori_loop(0, cols // 128, heads, 0)
        cos, sin = cos_ref[rows], sin_ref[rows]
        for c in range(0, cols, 128):
            s = slice(c, c + 128)
            gain = gain_ref[:, s]
            head = jnp.zeros((BLOCK, 128), F32)
            for j, (grad_s, low_ref, factor_ref, scale) in enumerate(
                ((dq_s, q_ref, rq_ref, HD**0.5), (dk_s, k_ref, rk_ref, 1.0))
            ):
                grad = grad_s[rows, s]
                unit = low_ref[rows, s].astype(F32) * (scale / gain)
                head = head + grad * unit
                grad = grad * gain
                turned = factor_ref[rows, s] * (grad - unit * (split_dot(grad * unit, ones) * (1.0 / HD)))
                low_s[j, rows, s] = (turned * cos - other_half(turned) * sin).astype(BF)
            head_o[:, s] = head_o[:, s] + jnp.sum(head, axis=0, keepdims=True)
            low_s[2, rows, s] = dv_s[rows, s].astype(BF)
        for c in range(0, width, 512):
            part = sum(dot_nt(low_s[j, rows], w_ref[j, c : c + 512]) for j in range(3))
            out_s[rows, c : c + 512] = part.astype(BF)
        copy = remote(out_s.at[rows], in_s.at[rows], send.at[block], recv.at[block], across)
        copy.start()
        copies[block] = copy

    def grads(i, _):
        d = pl.ds(pl.multiple_of(i * BLOCK, BLOCK), BLOCK)
        for j in range(3):
            dw_o[j, d] = dot_tn(x_ref[:, d], low_s[j]).astype(BF)
        dw_o[3, d] = dot_tn(do_ref[:, d], y_ref[x]).astype(BF)
        return 0

    lax.fori_loop(0, width // BLOCK, grads, 0)
    for block in reversed(range(length // BLOCK)):
        copies[block].wait()

        def finish(i, _):
            r = pl.ds(pl.multiple_of(block * BLOCK + i * 32, 32), 32)
            ig_o[r] = dri_ref[r] + (out_s[r].astype(F32) + in_s[r].astype(F32))
            return 0

        lax.fori_loop(0, BLOCK // 32, finish, 0)


def attention_backward(states, weights, q, k, v, rq, rk, y, dy, do, dri, cos, sin, gain, start):
    length, width = states.shape
    cols = gain.shape[1]
    vspec = pl.BlockSpec(memory_space=VM)
    blocks = length // BLOCK
    return pl.pallas_call(
        backward_kernel,
        out_shape=(
            jax.ShapeDtypeStruct((length, width), F32),
            jax.ShapeDtypeStruct((1, cols), F32),
            jax.ShapeDtypeStruct((4, width, cols), BF),
        ),
        in_specs=[vspec] * 15,
        out_specs=(vspec,) * 3,
        scratch_shapes=[
            VM((BLOCK + SPAN, BLOCK), F32),
            VM((length, cols), F32),
            VM((length, cols), F32),
            VM((length, cols), F32),
            VM((3, length, cols), BF),
            VM((length, width), BF),
            VM((length, width), BF),
            pltpu.SemaphoreType.DMA((blocks,)),
            pltpu.SemaphoreType.DMA((blocks,)),
        ],
        compiler_params=pltpu.CompilerParams(collective_id=5, has_side_effects=True, vmem_limit_bytes=60 * MIB),
        name="attention_backward",
    )(states, weights, q, k, v, rq, rk, y, dy, do, dri, cos, sin, gain, start)


ROWS_STEP = 32
UNIT_STEP = 512


def row_factor(v):
    return lax.rsqrt(jnp.mean(v * v, axis=-1, keepdims=True) + EPS)


def unit_back(factor, unit, grad):
    return factor * (grad - unit * jnp.mean(grad * unit, axis=-1, keepdims=True))


def fold(v):
    return jnp.sum(v.reshape(v.shape[0] // 8, 8, v.shape[1]), axis=0)


def feed_kernel(
    x_ref, y_ref, og_ref, mix_ref, us_ref, wo_own, wo_peer, w_ref,
    out_o, dri_o, do_o, dy_o, mix_o, us_o, dwu_o, dwg_o, dwd_o,
    wo_s, wu_s, wg_s, wd_s, o_s, hb_s, u_s, g_s, hid_s, dm_s, dh_s, own_s, got_m, got_d, hout_s,
    load, store, send_m, recv_m, send_d, recv_d,
):
    index, x = lax.axis_index("fsdp"), lax.axis_index("mp")
    across = (index, 1 - x)
    length, width = x_ref.shape
    cols, units = wo_own.shape[2], us_ref.shape[1]
    loads = [
        pltpu.make_async_copy(wo_own.at[3], wo_s.at[x], load.at[0]),
        pltpu.make_async_copy(wo_peer, wo_s.at[1 - x], load.at[1]),
        pltpu.make_async_copy(w_ref.at[0], wu_s, load.at[2]),
        pltpu.make_async_copy(w_ref.at[1], wg_s, load.at[3]),
        pltpu.make_async_copy(w_ref.at[2], wd_s, load.at[4]),
    ]
    for copy in loads:
        copy.start()
    greet((across,))
    blocks = length // BLOCK
    copies_m, copies_d = [], []

    def first_half(r):
        states = x_ref[r].astype(F32)
        o = o_s[r]
        ro = row_factor(o)
        uo = o * ro
        mix = mix_ref[0:1]
        r1 = states + mix * (uo - states)
        rr = row_factor(r1)
        return states, ro, uo, rr, r1 * rr

    def by_rows(block, body, init):
        def run(i, carry):
            return body(pl.ds(pl.multiple_of(block * BLOCK + i * ROWS_STEP, ROWS_STEP), ROWS_STEP), i, carry)

        return lax.fori_loop(0, BLOCK // ROWS_STEP, run, init)

    def by_cols(total, step, body):
        def run(i, _):
            body(pl.ds(pl.multiple_of(i * step, step), step))
            return 0

        lax.fori_loop(0, total // step, run, 0)

    for block in range(blocks):
        rows = pl.ds(block * BLOCK, BLOCK)
        if block == 0:
            loads[0].wait()
            loads[1].wait()

        def out_proj(c):
            o_s[rows, c] = dot_nt(y_ref[0, rows], wo_s[0, c]) + dot_nt(y_ref[1, rows], wo_s[1, c])

        by_cols(width, 512, out_proj)

        def hidden(r, i, _):
            hb_s[r] = first_half(r)[4].astype(BF)
            return 0

        by_rows(block, hidden, 0)
        if block == 0:
            loads[2].wait()
            loads[3].wait()

        def gate(f):
            up = dot_nn(hb_s[rows], wu_s[:, f])
            gt = dot_nn(hb_s[rows], wg_s[:, f])
            arg = us_ref[1:2, f] * gt * D**-0.5
            sig = 1.0 / (1.0 + jnp.exp(-arg))
            u_s[rows, f] = up.astype(BF)
            g_s[rows, f] = gt.astype(BF)
            hid_s[rows, f] = (us_ref[0:1, f] * up * (arg * sig)).astype(BF)

        by_cols(units, UNIT_STEP, gate)
        if block == 0:
            loads[4].wait()

        def down(c):
            own_s[rows, c] = dot_nt(hid_s[rows], wd_s[c]).astype(BF)

        by_cols(width, 512, down)
        copy = remote(own_s.at[rows], got_m.at[rows], send_m.at[block], recv_m.at[block], across)
        copy.start()
        copies_m.append(copy)

    mix_m = jnp.zeros((8, width), F32)
    us_o[...] = jnp.zeros_like(us_o)
    outs = []
    for block in range(blocks):
        rows = pl.ds(block * BLOCK, BLOCK)
        copies_m[block].wait()
        if block >= 2:
            outs[block - 2].wait()

        def middle(r, i, total):
            h1 = first_half(r)[4]
            m = own_s[r].astype(F32) + got_m[r].astype(F32)
            rm = row_factor(m)
            um = m * rm
            mix = mix_ref[1:2]
            r2 = h1 + mix * (um - h1)
            rr = row_factor(r2)
            out = r2 * rr
            hout_s[block % 2, pl.ds(pl.multiple_of(i * ROWS_STEP, ROWS_STEP), ROWS_STEP)] = out
            dr2 = unit_back(rr, out, og_ref[r].astype(F32))
            dm_s[r] = unit_back(rm, um, mix * dr2).astype(BF)
            dh_s[r] = dr2 * (1.0 - mix)
            return total + fold(dr2 * (um - h1))

        mix_m = by_rows(block, middle, mix_m)
        copy = pltpu.make_async_copy(hout_s.at[block % 2], out_o.at[rows], store.at[block])
        copy.start()
        outs.append(copy)

        def gate_back(f):
            dhid = dot_nn(dm_s[rows], wd_s[:, f])
            up, gt = u_s[rows, f].astype(F32), g_s[rows, f].astype(F32)
            su, sv = us_ref[0:1, f], us_ref[1:2, f]
            arg = sv * gt * D**-0.5
            sig = 1.0 / (1.0 + jnp.exp(-arg))
            act = dhid * (arg * sig)
            darg = dhid * su * up * sig * (1.0 + arg * (1.0 - sig))
            us_o[0:1, f] = us_o[0:1, f] + jnp.sum(act * up, axis=0, keepdims=True)
            us_o[1:2, f] = us_o[1:2, f] + jnp.sum(darg * gt, axis=0, keepdims=True) * D**-0.5
            u_s[rows, f] = (act * su).astype(BF)
            g_s[rows, f] = (darg * sv * D**-0.5).astype(BF)

        by_cols(units, UNIT_STEP, gate_back)

        def up_back(c):
            own_s[rows, c] = (dot_nt(u_s[rows], wu_s[c]) + dot_nt(g_s[rows], wg_s[c])).astype(BF)

        by_cols(width, 512, up_back)
        copy = remote(own_s.at[rows], got_d.at[rows], send_d.at[block], recv_d.at[block], across)
        copy.start()
        copies_d.append(copy)

    def grads(d):
        for u in range(0, units, 1024):
            f = pl.ds(u, 1024)
            wu_s[d, f] = dot_tn(hb_s[:, d], u_s[:, f]).astype(BF)
            wg_s[d, f] = dot_tn(hb_s[:, d], g_s[:, f]).astype(BF)
            wd_s[d, f] = dot_tn(dm_s[:, d], hid_s[:, f]).astype(BF)

    by_cols(width, BLOCK, grads)
    saves = [
        pltpu.make_async_copy(src, dst, load.at[j])
        for j, (src, dst) in enumerate(((wu_s, dwu_o), (wg_s, dwg_o), (wd_s, dwd_o)))
    ]
    for copy in saves:
        copy.start()

    mix_a = jnp.zeros((8, width), F32)
    for block in range(blocks):
        rows = pl.ds(block * BLOCK, BLOCK)
        copies_d[block].wait()

        def last(r, i, total):
            states, ro, uo, rr, h1 = first_half(r)
            mix = mix_ref[0:1]
            dr1 = unit_back(rr, h1, dh_s[r] + (own_s[r].astype(F32) + got_d[r].astype(F32)))
            dh_s[r] = dr1 * (1.0 - mix)
            dm_s[r] = unit_back(ro, uo, mix * dr1).astype(BF)
            return total + fold(dr1 * (uo - states))

        mix_a = by_rows(block, last, mix_a)
        dy_o[rows] = dot_nn(dm_s[rows], wo_s[x]).astype(BF)
    ends = [
        pltpu.make_async_copy(dh_s, dri_o, load.at[3]),
        pltpu.make_async_copy(dm_s, do_o, load.at[4]),
    ]
    for copy in ends:
        copy.start()
    mix_o[0:1] = jnp.sum(mix_a, axis=0, keepdims=True)
    mix_o[1:2] = jnp.sum(mix_m, axis=0, keepdims=True)
    for copy in outs[-2:] + saves + ends:
        copy.wait()


def feed_forward(states, y, out_grad, mix, scales, attn_full, wo_peer, mlp_full):
    length, width = states.shape
    cols, units = y.shape[2], scales.shape[1]
    vspec, anyspec = pl.BlockSpec(memory_space=VM), pl.BlockSpec(memory_space=pl.ANY)
    blocks = length // BLOCK
    sem = pltpu.SemaphoreType.DMA

    def low(*shape):
        return jax.ShapeDtypeStruct(shape, BF)

    def full(*shape):
        return jax.ShapeDtypeStruct(shape, F32)

    return pl.pallas_call(
        feed_kernel,
        out_shape=(
            full(length, width), full(length, width), low(length, width), low(length, cols),
            full(2, width), full(2, units), low(width, units), low(width, units), low(width, units),
        ),
        in_specs=[vspec] * 5 + [anyspec] * 3,
        out_specs=(anyspec, anyspec, anyspec, vspec, vspec, vspec, anyspec, anyspec, anyspec),
        scratch_shapes=[
            VM((2, width, cols), BF),
            VM((width, units), BF), VM((width, units), BF), VM((width, units), BF),
            VM((length, width), F32), VM((length, width), BF),
            VM((length, units), BF), VM((length, units), BF), VM((length, units), BF),
            VM((length, width), BF), VM((length, width), F32),
            VM((length, width), BF), VM((length, width), BF), VM((length, width), BF),
            VM((2, BLOCK, width), F32),
            sem((5,)), sem((blocks,)), sem((blocks,)), sem((blocks,)), sem((blocks,)), sem((blocks,)),
        ],
        compiler_params=pltpu.CompilerParams(collective_id=6, has_side_effects=True, vmem_limit_bytes=63 * MIB),
        name="feed_forward",
    )(states, y, out_grad, mix, scales, attn_full, wo_peer, mlp_full)


def rotary_rows(doc_row, lanes):
    length = doc_row.shape[0]
    start = jnp.sum((doc_row[None, :] < doc_row[:, None]).astype(jnp.int32), axis=1)
    offset = (jnp.arange(length, dtype=jnp.int32) - start).astype(F32)
    freq = THETA ** (-2.0 * jnp.arange(HD // 2, dtype=F32) / HD)
    angle = offset[:, None] * freq[None, :]
    cos, sin = jnp.cos(angle), jnp.sin(angle)
    repeat = lanes // HD
    return start, jnp.tile(jnp.concatenate([cos, cos], 1), (1, repeat)), jnp.tile(jnp.concatenate([-sin, sin], 1), (1, repeat))


def local_fast(
    inputs, doc_ids, out_grad, attn_w, attn_mom, attn_avg, mlp_w, mlp_mom, mlp_avg,
    head_scale, head_mom, mix_rates, mix_mom, unit_scales, unit_mom,
):
    fsdp = lax.axis_size("fsdp")
    tokens = inputs.shape[0] * fsdp * inputs.shape[1]
    root_tokens = math.sqrt(tokens)
    width = inputs.shape[2]
    states = inputs[0]
    start, cos, sin = rotary_rows(doc_ids[0], 128)
    gain = head_scale[None]
    attn_full, mlp_full, wo_peer = gather_weights(attn_w.astype(BF), mlp_w.astype(BF), fsdp)
    q, k, v, rq, rk, y = attention_forward(states, attn_full, cos, sin, gain, start[:, None])
    result, dri, do, dy, grad_mix, grad_units, dwu, dwg, dwd = feed_forward(
        states, y, out_grad[0], mix_rates, unit_scales, attn_full, wo_peer, mlp_full
    )
    input_grad, grad_head, dwa = attention_backward(
        states, attn_full, q, k, v, rq, rk, y, dy, do, dri, cos, sin, gain, start[None]
    )
    grad_head = grad_head[0]
    grad_attn, grad_mlp = scatter_grads(dwa, dwu, dwg, dwd, fsdp)
    small = jnp.concatenate(
        [
            jnp.pad(grad_head, (0, D - grad_head.shape[0])),
            grad_mix.reshape(-1),
            grad_units.reshape(-1),
            jnp.zeros((D,), F32),
        ]
    ).reshape(8, D)
    attn_mom_new, attn_new, attn_avg_new, mlp_mom_new, mlp_new, mlp_avg_new, small = update(
        grad_attn, grad_mlp, small, attn_w, attn_mom, attn_avg, mlp_w, mlp_mom, mlp_avg,
        RATE_WEIGHT / root_tokens, width, fsdp,
    )
    grad_head, grad_mix, grad_units = small[0, : grad_head.shape[0]], small[1:3], small[3:7].reshape(2, -1)
    head_mom_new, head_new = nesterov(head_scale, head_mom, grad_head, RATE_HEAD / root_tokens)
    mix_mom_new, mix_new = nesterov(mix_rates, mix_mom, grad_mix, RATE_MIX / root_tokens)
    units_mom_new, units_new = nesterov(unit_scales, unit_mom, grad_units, RATE_UNITS / root_tokens)
    return (
        result[None], input_grad[None], attn_mom_new, attn_new, attn_avg_new, mlp_mom_new, mlp_new, mlp_avg_new,
        head_mom_new, head_new, mix_mom_new, mix_new, units_mom_new, units_new,
    )


def local(
    inputs,
    doc_ids,
    out_grad,
    attn_w,
    attn_mom,
    attn_avg,
    mlp_w,
    mlp_mom,
    mlp_avg,
    head_scale,
    head_mom,
    mix_rates,
    mix_mom,
    unit_scales,
    unit_mom,
):
    length = inputs.shape[1]
    model_width = inputs.shape[2]
    head_count = head_scale.shape[0] // HD
    block_rows = min(512, length)
    block_count = length // block_rows
    tokens = inputs.shape[0] * lax.axis_size("fsdp") * length
    doc_row = doc_ids[0]
    input_low = inputs[0]
    resid_in = input_low.astype(jnp.float32)
    cos_table, sin_table = rotary_tables(doc_row)
    position = jnp.arange(length, dtype=jnp.int32)
    attn_full = lax.all_gather(attn_w.astype(jnp.bfloat16), "fsdp", axis=1, tiled=True)
    projected = jnp.einsum(
        "sd,jdc->jsc", input_low, attn_full[:3], preferred_element_type=jnp.float32
    )
    head_gain = head_scale.reshape(head_count, HD)
    q_rot = rotate(projected[0].reshape(length, head_count, HD), cos_table, sin_table)
    k_rot = rotate(projected[1].reshape(length, head_count, HD), cos_table, sin_table)
    q_unit = rms_unit(q_rot)
    k_unit = rms_unit(k_rot)
    query_low = (head_gain * q_unit).astype(jnp.bfloat16)
    key_low = (head_gain * k_unit).astype(jnp.bfloat16)
    value_low = projected[2].reshape(length, head_count, HD).astype(jnp.bfloat16)

    def scores_of(row_first):
        query_blk = lax.dynamic_slice_in_dim(query_low, row_first, block_rows, 0)
        raw_scores = jnp.einsum(
            "qhe,khe->hqk", query_blk, key_low, preferred_element_type=jnp.float32
        )
        row_pos = lax.dynamic_slice_in_dim(position, row_first, block_rows, 0)
        row_docs = lax.dynamic_slice_in_dim(doc_row, row_first, block_rows, 0)
        allowed = (row_docs[:, None] == doc_row[None, :]) & (position[None, :] <= row_pos[:, None])
        return (jnp.where(allowed[None], raw_scores * HD ** (-0.5), NEG_FILL), query_blk)

    def attend(accums, blk_index):
        scores, query_blk = scores_of(blk_index * block_rows)
        peak_val = jnp.max(scores, axis=-1, keepdims=True)
        expo_vals = jnp.exp(scores - peak_val)
        row_total = jnp.sum(expo_vals, axis=-1, keepdims=True)
        probs_low = (expo_vals / row_total).astype(jnp.bfloat16)
        blk_out = jnp.einsum(
            "hqk,khe->qhe", probs_low, value_low, preferred_element_type=jnp.float32
        )
        return (accums, (blk_out, (peak_val + jnp.log(row_total))[..., 0]))

    _, (mixed_blocks, log_totals) = lax.scan(attend, None, jnp.arange(block_count))
    mixed_low = mixed_blocks.reshape(length, head_count * HD).astype(jnp.bfloat16)
    attn_part = jnp.einsum("sc,dc->sd", mixed_low, attn_full[3], preferred_element_type=jnp.float32)
    attn_out = lax.psum(attn_part, "mp")
    attn_unit = rms_unit(attn_out)
    resid_one = resid_in + mix_rates[0] * (attn_unit - resid_in)
    hidden_one = rms_unit(resid_one)
    hidden_low = hidden_one.astype(jnp.bfloat16)
    mlp_full = lax.all_gather(mlp_w.astype(jnp.bfloat16), "fsdp", axis=1, tiled=True)
    gates = jnp.einsum("sd,jdf->jsf", hidden_low, mlp_full[:2], preferred_element_type=jnp.float32)
    up_proj = gates[0]
    gate_proj = gates[1]
    gate_arg = unit_scales[1] * gate_proj * D ** (-0.5)
    gate_sig = jax.nn.sigmoid(gate_arg)
    gate_act = gate_arg * gate_sig
    units_low = (unit_scales[0] * up_proj * gate_act).astype(jnp.bfloat16)
    mlp_part = jnp.einsum("sf,df->sd", units_low, mlp_full[2], preferred_element_type=jnp.float32)
    mlp_out = lax.psum(mlp_part, "mp")
    mlp_unit = rms_unit(mlp_out)
    resid_two = hidden_one + mix_rates[1] * (mlp_unit - hidden_one)
    result = rms_unit(resid_two)
    cotangent = out_grad[0].astype(jnp.float32)
    d_resid_two = rms_back(resid_two, cotangent)
    grad_mix_mlp = jnp.sum(d_resid_two * (mlp_unit - hidden_one), axis=0)
    d_hidden_one = d_resid_two * (1.0 - mix_rates[1])
    d_mlp_low = rms_back(mlp_out, mix_rates[1] * d_resid_two).astype(jnp.bfloat16)
    mlp_back = lax.all_gather(mlp_w.astype(jnp.bfloat16), "fsdp", axis=1, tiled=True)
    d_units = jnp.einsum("sd,df->sf", d_mlp_low, mlp_back[2], preferred_element_type=jnp.float32)
    d_up = d_units * unit_scales[0] * gate_act
    d_arg = d_units * unit_scales[0] * up_proj * gate_sig * (1.0 + gate_arg * (1.0 - gate_sig))
    d_gate = d_arg * unit_scales[1] * D ** (-0.5)
    grad_units = jnp.stack(
        [
            jnp.sum(d_units * up_proj * gate_act, axis=0),
            jnp.sum(d_arg * gate_proj * D ** (-0.5), axis=0),
        ]
    )
    d_gates_low = jnp.stack([d_up, d_gate]).astype(jnp.bfloat16)
    mlp_back_part = jnp.einsum(
        "jsf,jdf->sd", d_gates_low, mlp_back[:2], preferred_element_type=jnp.float32
    )
    d_hidden_one = d_hidden_one + lax.psum(mlp_back_part, "mp")
    right_cols = d_mlp_low
    left_cols = hidden_low
    grad_mlp = jnp.transpose(
        lax.psum_scatter(
            jnp.concatenate(
                [
                    jnp.einsum(
                        "sd,jsf->djf", left_cols, d_gates_low, preferred_element_type=jnp.float32
                    ),
                    jnp.einsum(
                        "sd,sf->df", right_cols, units_low, preferred_element_type=jnp.float32
                    )[:, None, :],
                ],
                axis=1,
            ),
            "fsdp",
            scatter_dimension=0,
            tiled=True,
        ),
        (1, 0, 2),
    )
    d_resid_one = rms_back(resid_one, d_hidden_one)
    grad_mix_attn = jnp.sum(d_resid_one * (attn_unit - resid_in), axis=0)
    d_resid_in = d_resid_one * (1.0 - mix_rates[0])
    d_attn_low = rms_back(attn_out, mix_rates[0] * d_resid_one).astype(jnp.bfloat16)
    attn_back = lax.all_gather(attn_w.astype(jnp.bfloat16), "fsdp", axis=1, tiled=True)
    d_mixed = jnp.einsum("sd,dc->sc", d_attn_low, attn_back[3], preferred_element_type=jnp.float32)
    d_mixed = d_mixed.astype(jnp.bfloat16).reshape(length, head_count, HD)

    def attend_back(accums, blk_index):
        d_key, d_value = accums
        row_first = blk_index * block_rows
        scores, query_blk = scores_of(row_first)
        blk_total = lax.dynamic_index_in_dim(log_totals, blk_index, 0, keepdims=False)
        attn_probs = jnp.exp(scores - blk_total[..., None])
        d_out_blk = lax.dynamic_slice_in_dim(d_mixed, row_first, block_rows, 0)
        d_probs = jnp.einsum(
            "qhe,khe->hqk", d_out_blk, value_low, preferred_element_type=jnp.float32
        )
        d_scores = attn_probs * (d_probs - jnp.sum(attn_probs * d_probs, axis=-1, keepdims=True))
        d_raw_low = (d_scores * HD ** (-0.5)).astype(jnp.bfloat16)
        d_query = jnp.einsum("hqk,khe->qhe", d_raw_low, key_low, preferred_element_type=jnp.float32)
        d_key = d_key + jnp.einsum(
            "hqk,qhe->khe", d_raw_low, query_blk, preferred_element_type=jnp.float32
        )
        d_value = d_value + jnp.einsum(
            "hqk,qhe->khe",
            attn_probs.astype(jnp.bfloat16),
            d_out_blk,
            preferred_element_type=jnp.float32,
        )
        return ((d_key, d_value), d_query)

    zero_heads = jnp.zeros((length, head_count, HD), jnp.float32)
    (d_key_all, d_value_all), d_query_blocks = lax.scan(
        attend_back, (zero_heads, zero_heads), jnp.arange(block_count)
    )
    d_query_all = d_query_blocks.reshape(length, head_count, HD)
    grad_head = jnp.sum(d_query_all * q_unit + d_key_all * k_unit, axis=0).reshape(-1)
    d_query_raw = rotate_back(rms_back(q_rot, head_gain * d_query_all), cos_table, sin_table)
    d_key_raw = rotate_back(rms_back(k_rot, head_gain * d_key_all), cos_table, sin_table)
    d_proj_low = jnp.stack(
        [
            d_query_raw.reshape(length, -1),
            d_key_raw.reshape(length, -1),
            d_value_all.reshape(length, -1),
        ]
    ).astype(jnp.bfloat16)
    grad_mix = jnp.stack([grad_mix_attn, grad_mix_mlp])
    grad_head, grad_mix, grad_units = lax.psum((grad_head, grad_mix, grad_units), "fsdp")
    attn_back_part = jnp.einsum(
        "jsc,jdc->sd", d_proj_low, attn_back[:3], preferred_element_type=jnp.float32
    )
    input_grad = d_resid_in + lax.psum(attn_back_part.astype(jnp.bfloat16), "mp").astype(
        jnp.float32
    )
    left_cols = input_low
    right_cols = d_attn_low
    in_terms = jnp.einsum("sd,jsc->djc", left_cols, d_proj_low, preferred_element_type=jnp.float32)
    out_terms = jnp.einsum("sd,sc->dc", right_cols, mixed_low, preferred_element_type=jnp.float32)
    grad_attn = jnp.transpose(
        lax.psum_scatter(
            jnp.concatenate([in_terms, out_terms[:, None, :]], axis=1),
            "fsdp",
            scatter_dimension=0,
            tiled=True,
        ),
        (1, 0, 2),
    )
    root_tokens = math.sqrt(tokens)
    weight_rate = RATE_WEIGHT / root_tokens
    attn_mom_new, attn_step = nesterov(attn_w, attn_mom, grad_attn, weight_rate)
    mlp_mom_new, mlp_step = nesterov(mlp_w, mlp_mom, grad_mlp, weight_rate)
    attn_squares = jnp.sum(attn_step * attn_step, axis=1)
    mlp_squares = jnp.sum(mlp_step * mlp_step, axis=1)
    attn_squares, mlp_squares = lax.psum((attn_squares, mlp_squares), "fsdp")
    attn_new = attn_step * lax.rsqrt(attn_squares[:, None, :] / model_width + EPS)
    mlp_new = mlp_step * lax.rsqrt(mlp_squares[:, None, :] / model_width + EPS)
    head_mom_new, head_new = nesterov(head_scale, head_mom, grad_head, RATE_HEAD / root_tokens)
    mix_mom_new, mix_new = nesterov(mix_rates, mix_mom, grad_mix, RATE_MIX / root_tokens)
    units_mom_new, units_new = nesterov(unit_scales, unit_mom, grad_units, RATE_UNITS / root_tokens)
    return (
        result[None],
        input_grad[None],
        attn_mom_new,
        attn_new,
        AVERAGE * attn_avg + (1.0 - AVERAGE) * attn_new,
        mlp_mom_new,
        mlp_new,
        AVERAGE * mlp_avg + (1.0 - AVERAGE) * mlp_new,
        head_mom_new,
        head_new,
        mix_mom_new,
        mix_new,
        units_mom_new,
        units_new,
    )


def solution(mesh):
    fast = D // mesh.shape["fsdp"] % 16 == 0 and mesh.shape["fsdp"] % 8 == 0
    placed = (
        P("fsdp", None, None),
        P("fsdp", None),
        P("fsdp", None, None),
        P(None, "fsdp", "mp"),
        P(None, "fsdp", "mp"),
        P(None, "fsdp", "mp"),
        P(None, "fsdp", "mp"),
        P(None, "fsdp", "mp"),
        P(None, "fsdp", "mp"),
        P("mp"),
        P("mp"),
        P(),
        P(),
        P(None, "mp"),
        P(None, "mp"),
    )
    return jax.shard_map(
        local_fast if fast else local,
        mesh=mesh,
        in_specs=placed,
        out_specs=(
            P("fsdp", None, None),
            P("fsdp", None, None),
            P(None, "fsdp", "mp"),
            P(None, "fsdp", "mp"),
            P(None, "fsdp", "mp"),
            P(None, "fsdp", "mp"),
            P(None, "fsdp", "mp"),
            P(None, "fsdp", "mp"),
            P("mp"),
            P("mp"),
            P(),
            P(),
            P(None, "mp"),
            P(None, "mp"),
        ),
        check_vma=False,
    )
```

```python
import functools
import math

import jax
import jax.numpy as jnp
from jax import lax
from jax.experimental import pallas as pl
from jax.experimental.pallas import tpu as pltpu
from jax.sharding import PartitionSpec as P

D = 1024
HD = 64


EPS = 1e-06
MOMENTUM = 0.9
AVERAGE = 0.9
NEG_FILL = -1e30
THETA = 10000.0
RATE_WEIGHT = 50.0
RATE_HEAD = 0.08
RATE_MIX = 0.02
RATE_UNITS = 0.5


def rms_unit(vector):
    return vector * lax.rsqrt(jnp.mean(vector * vector, axis=-1, keepdims=True) + EPS)


def rms_back(vector, grad):
    factor = lax.rsqrt(jnp.mean(vector * vector, axis=-1, keepdims=True) + EPS)
    unit_vec = vector * factor
    return factor * (grad - unit_vec * jnp.mean(grad * unit_vec, axis=-1, keepdims=True))


def rotary_tables(doc_row):
    length = doc_row.shape[0]
    position = jnp.arange(length, dtype=jnp.int32)
    boundary = jnp.concatenate(
        [jnp.ones((1,), jnp.int32), (doc_row[1:] != doc_row[:-1]).astype(jnp.int32)]
    )
    doc_start = lax.cummax(jnp.where(boundary > 0, position, 0), axis=0)
    offset = (position - doc_start).astype(jnp.float32)
    freq = THETA ** (-2.0 * jnp.arange(HD // 2, dtype=jnp.float32) / HD)
    angle = offset[:, None] * freq[None, :]
    return (jnp.cos(angle), jnp.sin(angle))


def rotate(vector, cos_table, sin_table):
    half_dim = vector.shape[-1] // 2
    lower_half = vector[..., :half_dim]
    upper_half = vector[..., half_dim:]
    cos_part = cos_table[:, None, :]
    sin_part = sin_table[:, None, :]
    return jnp.concatenate(
        [
            lower_half * cos_part - upper_half * sin_part,
            lower_half * sin_part + upper_half * cos_part,
        ],
        axis=-1,
    )


def rotate_back(grad, cos_table, sin_table):
    half_dim = grad.shape[-1] // 2
    lower_half = grad[..., :half_dim]
    upper_half = grad[..., half_dim:]
    cos_part = cos_table[:, None, :]
    sin_part = sin_table[:, None, :]
    return jnp.concatenate(
        [
            lower_half * cos_part + upper_half * sin_part,
            upper_half * cos_part - lower_half * sin_part,
        ],
        axis=-1,
    )


def nesterov(param, moment, grad, step_rate):
    moment_new = MOMENTUM * moment + grad
    return (moment_new, param - step_rate * (grad + MOMENTUM * moment_new))


BF = jnp.bfloat16
F32 = jnp.float32
MESH = pl.DeviceIdType.MESH
VM = pltpu.VMEM
MIB = 1 << 20


def dot_nn(a, b):
    return lax.dot_general(a, b, (((1,), (0,)), ((), ())), preferred_element_type=F32)


def dot_nt(a, b):
    return lax.dot_general(a, b, (((1,), (1,)), ((), ())), preferred_element_type=F32)


def dot_tn(a, b):
    return lax.dot_general(a, b, (((0,), (0,)), ((), ())), preferred_element_type=F32)


def split_dot(a, ones):
    high = a.astype(BF)
    return dot_nn(high, ones) + dot_nn((a - high.astype(F32)).astype(BF), ones)


def ring_place(index, chips):
    z, y = index // 4, (index // 2) % 2
    return z + y * (chips - 1 - 2 * z), index % 2


def ring_device(place, core, chips):
    y = place // (chips // 2)
    return ((place + y * (chips - 1 - 2 * place)) * 2 + y) * 2 + core


def greet(peers):
    barrier = pltpu.get_barrier_semaphore()
    for peer in peers:
        pl.semaphore_signal(barrier, inc=1, device_id=peer, device_id_type=MESH)
    pl.semaphore_wait(barrier, len(peers))


def remote(src, dst, send, recv, peer):
    return pltpu.make_async_remote_copy(
        src_ref=src, dst_ref=dst, send_sem=send, recv_sem=recv, device_id=peer, device_id_type=MESH
    )


def update_kernel(stages, rate, width, ga, gm, small, wa, ma, aa, wm, mm, am, ma_o, wa_o, aa_o, mm_o, wm_o, am_o, small_o, mine, got, send, recv):
    index, x = lax.axis_index("fsdp"), lax.axis_index("mp")
    peers = [(index + (1 << s) * (1 - 2 * ((index // (1 << s)) % 2)), x) for s in range(stages)]
    greet(peers)
    rows = ga.shape[1]
    cols, units = ga.shape[2], gm.shape[2]

    def step(j, r, g, w, m, m_o, w_o):
        grad = g[j, r]
        moment = MOMENTUM * m[j, r] + grad
        stepped = w[j, r] - rate * (grad + MOMENTUM * moment)
        m_o[j, r] = moment
        w_o[j, r] = stepped
        return stepped * stepped

    lanes = mine.shape[2]

    def spots(base, count):
        size = min(count, lanes)
        return [((base + k) // lanes, (base + k) % lanes, k, size) for k in range(0, count, size)]

    def pack(refs, j, count, base):
        def body(i, total):
            r = pl.ds(pl.multiple_of(i * 8, 8), 8)
            return total + step(j, r, *refs)

        total = jnp.sum(lax.fori_loop(0, rows // 8, body, jnp.zeros((8, count), F32)), axis=0, keepdims=True)
        for row, lane, k, size in spots(base, count):
            mine[0, row : row + 1, lane : lane + size] = total[:, k : k + size]

    for j in range(4):
        pack((ga, wa, ma, ma_o, wa_o), j, cols, j * cols)
    for j in range(3):
        pack((gm, wm, mm, mm_o, wm_o), j, units, 4 * cols + j * units)
    squares = (4 * cols + 3 * units) // lanes
    mine[0, squares:] = small[...]
    for s in range(stages):
        copy = remote(mine.at[s], got.at[s], send.at[s], recv.at[s], peers[s])
        copy.start()
        copy.wait()
        mine[s + 1] = mine[s] + got[s]
    small_o[...] = mine[stages, squares:]

    def finish(j, count, base, a, a_o, w_o):
        for row, lane, k, size in spots(base, count):
            c = slice(k, k + size)
            scale = lax.rsqrt(mine[stages, row : row + 1, lane : lane + size] / width + EPS)

            def body(i, _):
                r = pl.ds(pl.multiple_of(i * 8, 8), 8)
                new = w_o[j, r, c] * scale
                w_o[j, r, c] = new
                a_o[j, r, c] = AVERAGE * a[j, r, c] + (1.0 - AVERAGE) * new
                return 0

            lax.fori_loop(0, rows // 8, body, 0)

    for j in range(4):
        finish(j, cols, j * cols, aa, aa_o, wa_o)
    for j in range(3):
        finish(j, units, 4 * cols + j * units, am, am_o, wm_o)


def update(ga, gm, small, wa, ma, aa, wm, mm, am, rate, width, fsdp):
    stages = fsdp.bit_length() - 1
    lanes = small.shape[1]
    squares = (4 * wa.shape[2] + 3 * wm.shape[2]) // lanes
    total = squares + small.shape[0]
    vspec = pl.BlockSpec(memory_space=VM)
    a_shape, m_shape = jax.ShapeDtypeStruct(wa.shape, F32), jax.ShapeDtypeStruct(wm.shape, F32)
    return pl.pallas_call(
        functools.partial(update_kernel, stages, rate, width),
        out_shape=(a_shape, a_shape, a_shape, m_shape, m_shape, m_shape, jax.ShapeDtypeStruct(small.shape, F32)),
        in_specs=[vspec] * 9,
        out_specs=(vspec,) * 7,
        scratch_shapes=[
            VM((stages + 1, total, lanes), F32),
            VM((stages, total, lanes), F32),
            pltpu.SemaphoreType.DMA((stages,)),
            pltpu.SemaphoreType.DMA((stages,)),
        ],
        compiler_params=pltpu.CompilerParams(collective_id=3, has_side_effects=True, vmem_limit_bytes=60 * MIB),
        name="update_weights",
    )(ga, gm, small, wa, ma, aa, wm, mm, am)


BLOCK = 256
SPAN = 512
GATHER_GROUPS = ((0, 0, 3), (0, 3, 1), (1, 0, 1), (1, 1, 1), (1, 2, 1))
GATHER_LONG = (0, 2, 4)


def head_ones():
    row = lax.broadcasted_iota(jnp.int32, (128, 128), 0) // HD
    col = lax.broadcasted_iota(jnp.int32, (128, 128), 1) // HD
    return jnp.where(row == col, 1.0, 0.0).astype(BF)


def half_of(rows, half):
    lane = lax.broadcasted_iota(jnp.int32, (rows, 128), 1)
    return jnp.where((lane < HD) == (half == 0), 1.0, 0.0).astype(BF)


def other_half(v):
    lane = lax.broadcasted_iota(jnp.int32, v.shape, 1)
    return jnp.where(lane % HD < HD // 2, pltpu.roll(v, 128 - HD // 2, 1), pltpu.roll(v, HD // 2, 1))


def first_key(block):
    return max(0, block * BLOCK - SPAN)


def forward_kernel(
    chips, attn_ref, mlp_ref, x_hbm, doc_ref, gain_ref, freq_ref,
    attn_o, mlp_o, wo_o, q_o, k_o, v_o, rq_o, rk_o, y_o, start_o, cos_o, sin_o,
    attn_s, mlp_s, w_s, x_ref, start_s, bias,
    load, send, recv, ring_send, ring_recv, pair_send, pair_recv, own_sem, wo_send, wo_recv,
):
    index, x = lax.axis_index("fsdp"), lax.axis_index("mp")
    place, core = ring_place(index, chips)
    rows_own = attn_ref.shape[1]
    length, cols = q_o.shape
    blocks = length // BLOCK
    right = (ring_device((place + 1) % chips, core, chips), x)
    left = (ring_device((place + chips - 1) % chips, core, chips), x)
    pair_index = index + 1 - 2 * core
    pair = (pair_index, x)
    across = (index, 1 - x)
    load_x = pltpu.make_async_copy(x_hbm, x_ref, load.at[0])
    load_x.start()
    ins, outs = (attn_s, mlp_s), (w_s, mlp_o)

    def own(group):
        kind, first, count = GATHER_GROUPS[group]
        return ins[kind].at[pl.ds(first, count)]

    def block_of(group, dev):
        kind, first, count = GATHER_GROUPS[group]
        return outs[kind].at[pl.ds(first, count), pl.ds(pl.multiple_of(dev * rows_own, rows_own), rows_own)]

    def counts(group):
        pair_of = (chips // 2, chips - 1 - chips // 2)
        return pair_of if group in GATHER_LONG else pair_of[::-1]

    def origin(way, hop):
        there = (place + chips - hop) % chips if way == 0 else (place + hop) % chips
        return ring_device(there, core, chips)

    def ring_copy(group, way, hop, src, dst):
        return remote(
            src, dst, ring_send.at[group, way, hop - 1], ring_recv.at[group, way, hop - 1], right if way == 0 else left
        )

    def pair_copy(group, at, src, dev):
        return remote(src, block_of(group, dev), pair_send.at[group, at], pair_recv.at[group, at], pair)

    sends, owns = [], []

    def launch(group):
        for way in (0, 1):
            copy = ring_copy(group, way, 1, own(group), block_of(group, index))
            copy.start()
            sends.append(copy)
        copy = pair_copy(group, 0, own(group), index)
        copy.start()
        sends.append(copy)
        copy = pltpu.make_async_copy(own(group), block_of(group, index), own_sem.at[group])
        copy.start()
        owns.append(copy)

    def tick(group, hop):
        for way in (0, 1):
            if hop > counts(group)[way]:
                continue
            dev = origin(way, hop)
            here = block_of(group, dev)
            ring_copy(group, way, hop, here, here).wait_recv()
            if hop < counts(group)[way]:
                copy = ring_copy(group, way, hop + 1, here, here)
                copy.start()
                sends.append(copy)
            copy = pair_copy(group, hop if way == 0 else counts(group)[0] + hop, here, dev)
            copy.start()
            sends.append(copy)

    def await_pair(group):
        here = block_of(group, pair_index)
        pair_copy(group, 0, here, pair_index).wait_recv()
        for way in (0, 1):
            for hop in range(1, counts(group)[way] + 1):
                dev = origin(way, hop) + 1 - 2 * core
                here = block_of(group, dev)
                pair_copy(group, hop if way == 0 else counts(group)[0] + hop, here, dev).wait_recv()

    attn_s[...] = attn_ref[...].astype(BF)
    greet((right, left, pair, across))
    launch(0)
    launch(1)
    mlp_s[...] = mlp_ref[...].astype(BF)
    doc = doc_ref[...]
    start = jnp.zeros(doc.shape, F32)
    for number in range(3):
        count = jnp.sum(jnp.where(doc == number, 1.0, 0.0), axis=1, keepdims=True)
        start = start + jnp.where(doc > number, count, 0.0)
    start_o[...] = start.astype(jnp.int32)
    start_s[...] = jnp.transpose(jnp.broadcast_to(start, (128, length)))
    tick(0, 1)

    def tables(i, _):
        rows = pl.ds(pl.multiple_of(i * BLOCK, BLOCK), BLOCK)
        position = (lax.broadcasted_iota(jnp.int32, (BLOCK, 128), 0) + i * BLOCK).astype(F32)
        angle = (position - start_s[rows]) * freq_ref[...]
        lane = lax.broadcasted_iota(jnp.int32, (BLOCK, 128), 1)
        cos_o[rows] = jnp.cos(angle)
        sin_o[rows] = jnp.where(lane % HD < HD // 2, -1.0, 1.0) * jnp.sin(angle)
        return 0

    lax.fori_loop(0, blocks // 2, tables, 0)
    tick(0, 2)
    lax.fori_loop(blocks // 2, blocks, tables, 0)
    tick(1, 1)
    tick(0, 3)
    for group in (2, 3, 4):
        launch(group)
    tick(1, 2)
    tick(0, 4)
    tick(1, 3)
    pending = [(group, hop) for hop in range(1, chips // 2 + 1) for group in (2, 3, 4)]
    ones = head_ones()
    load_x.wait()
    owns[0].wait()
    await_pair(0)
    keep = [pltpu.make_async_copy(w_s.at[pl.ds(0, 3)], attn_o.at[pl.ds(0, 3)], load.at[1])]
    keep[0].start()

    def project(i, _):
        rows = pl.ds(pl.multiple_of(i * BLOCK, BLOCK), BLOCK)
        states = x_ref[rows]
        cos, sin = cos_o[rows], sin_o[rows]
        for j, (out, factor_o, scale) in enumerate(((q_o, rq_o, HD**-0.5), (k_o, rk_o, 1.0))):
            raw = dot_nn(states, w_s[j])
            for c in range(0, cols, 128):
                part = raw[:, c : c + 128]
                factor = lax.rsqrt(split_dot(part * part, ones) * (1.0 / HD) + EPS)
                unit = (part * cos + other_half(part) * sin) * factor
                out[rows, c : c + 128] = ((gain_ref[:, c : c + 128] * unit).astype(BF).astype(F32) * scale).astype(BF)
                factor_o[rows, c : c + 128] = factor.astype(BF)
        v_o[rows] = dot_nn(states, w_s[2]).astype(BF)
        return 0

    lax.fori_loop(0, blocks // 2, project, 0)
    tick(1, 4)
    owns[1].wait()
    await_pair(1)
    wo_copy = remote(w_s.at[3], wo_o, wo_send, wo_recv, across)
    wo_copy.start()
    keep.append(pltpu.make_async_copy(w_s.at[3], attn_o.at[3], load.at[2]))
    keep[1].start()
    tick(*pending.pop(0))
    lax.fori_loop(blocks // 2, blocks, project, 0)
    tick(*pending.pop(0))
    copies = []
    for block in range(blocks):
        low = first_key(block)
        keys = (block + 1) * BLOCK - low
        rows = pl.ds(block * BLOCK, BLOCK)
        span = pl.ds(low, keys)
        kpos = (lax.broadcasted_iota(jnp.int32, (BLOCK, keys), 1) + low).astype(F32)
        qpos = (lax.broadcasted_iota(jnp.int32, (BLOCK, keys), 0) + block * BLOCK).astype(F32)
        allowed = (kpos >= start_s[rows, 0:1]) & (kpos <= qpos)
        bias[:, :keys] = jnp.where(allowed, 0.0, NEG_FILL)

        def heads(pair_of, _):
            c = pl.ds(pl.multiple_of(pair_of * 128, 128), 128)
            q, k, v = q_o[rows, c], k_o[span, c], v_o[span, c]
            results = []
            for half in (0, 1):
                scores = dot_nt(q * half_of(BLOCK, half), k)
                probs = jnp.exp(scores + bias[:, :keys]).astype(BF)
                results.append(dot_nn(probs, v * half_of(keys, half) + half_of(keys, 1 - half)))
            lane = lax.broadcasted_iota(jnp.int32, (BLOCK, 128), 1)
            total = pltpu.roll(jnp.where(lane < HD, results[1], results[0]), HD, 1)
            y_o[x, rows, c] = (jnp.where(lane < HD, results[0], results[1]) / total).astype(BF)
            return 0

        lax.fori_loop(0, cols // 128, heads, 0)
        copy = remote(y_o.at[x, rows], y_o.at[x, rows], send.at[block], recv.at[block], across)
        copy.start()
        copies.append(copy)
        tick(*pending.pop(0))
    while pending:
        tick(*pending.pop(0))
    for group in (2, 3, 4):
        await_pair(group)
    for copy in owns[2:] + keep:
        copy.wait()
    for copy in sends + copies:
        copy.wait_send()
    for block in range(blocks):
        there = y_o.at[1 - x, pl.ds(block * BLOCK, BLOCK)]
        remote(there, there, send.at[block], recv.at[block], across).wait_recv()
    wo_copy.wait()


def attention_forward(attn_w, mlp_w, states, doc, gain, fsdp):
    chips = fsdp // 2
    length, width = states.shape
    cols, units, rows = attn_w.shape[2], mlp_w.shape[2], attn_w.shape[1]
    vspec, anyspec = pl.BlockSpec(memory_space=VM), pl.BlockSpec(memory_space=pl.ANY)
    blocks = length // BLOCK
    low = jax.ShapeDtypeStruct((length, cols), BF)
    sem = pltpu.SemaphoreType.DMA
    number = len(GATHER_GROUPS)
    freq = THETA ** (-2.0 * (jnp.arange(128, dtype=F32) % (HD // 2)) / HD)
    return pl.pallas_call(
        functools.partial(forward_kernel, chips),
        out_shape=(
            jax.ShapeDtypeStruct((4, width, cols), BF),
            jax.ShapeDtypeStruct((3, width, units), BF),
            jax.ShapeDtypeStruct((width, cols), BF),
            low, low, low, low, low,
            jax.ShapeDtypeStruct((2, length, cols), BF),
            jax.ShapeDtypeStruct((1, length), jnp.int32),
            jax.ShapeDtypeStruct((length, 128), F32),
            jax.ShapeDtypeStruct((length, 128), F32),
        ),
        in_specs=[vspec, vspec, anyspec, vspec, vspec, vspec],
        out_specs=(anyspec,) * 3 + (vspec,) * 9,
        scratch_shapes=[
            VM((4, rows, cols), BF), VM((3, rows, units), BF), VM((4, width, cols), BF), VM((length, width), BF),
            VM((length, 128), F32), VM((BLOCK, BLOCK + SPAN), F32),
            sem((3,)), sem((blocks,)), sem((blocks,)), sem((number, 2, chips // 2)), sem((number, 2, chips // 2)),
            sem((number, chips)), sem((number, chips)), sem((number,)), sem, sem,
        ],
        compiler_params=pltpu.CompilerParams(collective_id=4, has_side_effects=True, vmem_limit_bytes=60 * MIB),
        name="attention_forward",
    )(attn_w, mlp_w, states, doc, gain, freq[None])


def add_all(dst, refs):
    if len(dst.shape) == 3:
        for j in range(dst.shape[0]):
            add_all(dst.at[j], [ref.at[j] for ref in refs])
        return

    def body(i, _):
        r = pl.ds(pl.multiple_of(i * 16, 16), 16)
        total = refs[0][r].astype(F32)
        for ref in refs[1:]:
            total = total + ref[r].astype(F32)
        dst[r] = total.astype(dst.dtype)
        return 0

    lax.fori_loop(0, dst.shape[0] // 16, body, 0)


SCATTER_LONG = (0, 2)


def backward_kernel(
    x_hbm, w_hbm, q_hbm, k_hbm, v_hbm, rq_hbm, rk_hbm, y_hbm, dy_hbm, do_hbm, dri_hbm, sums_hbm, cos_hbm, sin_hbm,
    gain_ref, start_ref,
    ig_o, head_o, ga_o, gm_o,
    x_ref, w_ref, q_ref, k_ref, v_ref, rq_ref, rk_ref, y_ref, dy_ref, do_ref, sums, cos_ref, sin_ref, dri_s,
    bias, dq_s, dk_s, dv_s, low_s, out_s, in_s, dw_s, near, ring_a, ring_m,
    load, load_dri, store, send, recv, pair_send, pair_recv, ring_send, ring_recv,
):
    index, x = lax.axis_index("fsdp"), lax.axis_index("mp")
    length, cols = q_ref.shape
    width = x_ref.shape[1]
    chips, rows_own = sums.shape[1:3]
    place, core = ring_place(index, chips)
    right = (ring_device((place + 1) % chips, core, chips), x)
    left = (ring_device((place + chips - 1) % chips, core, chips), x)
    pair = (index + 1 - 2 * core, x)
    across = (index, 1 - x)
    blocks = length // BLOCK
    pieces = (
        (q_hbm, q_ref), (k_hbm, k_ref), (v_hbm, v_ref), (dy_hbm, dy_ref), (y_hbm.at[x], y_ref),
        (cos_hbm, cos_ref), (sin_hbm, sin_ref), (rq_hbm, rq_ref), (rk_hbm, rk_ref), (w_hbm.at[pl.ds(0, 3)], w_ref),
        (sums_hbm, sums), (do_hbm, do_ref), (x_hbm, x_ref),
    )
    loads = [pltpu.make_async_copy(src, dst, load.at[i]) for i, (src, dst) in enumerate(pieces)]
    for copy in loads:
        copy.start()
    dk_s[...] = jnp.zeros_like(dk_s)
    dv_s[...] = jnp.zeros_like(dv_s)
    head_o[...] = jnp.zeros_like(head_o)
    ones = head_ones()
    greet((right, left, pair, across))

    def counts(group):
        pair_of = (chips // 2, chips - 1 - chips // 2)
        return pair_of if group in SCATTER_LONG else pair_of[::-1]

    def mine(group, chip):
        if group < 3:
            return sums.at[group, chip]
        return near.at[3, chip] if group == 3 else near.at[pl.ds(0, 3), chip]

    def slot(group, way, hop):
        at = hop - 1 if way == 0 else counts(group)[0] + hop - 1
        if group < 3:
            return ring_m.at[group, at]
        return ring_a.at[at, 3] if group == 3 else ring_a.at[at, pl.ds(0, 3)]

    def chip_at(way, count):
        there = ring_device((place + count) % chips if way == 0 else (place + chips - count) % chips, core, chips)
        return there // 2

    def ring_copy(group, way, hop, src):
        at = hop - 1 if way == 0 else counts(group)[0] + hop - 1
        return remote(
            src, slot(group, way, hop), ring_send.at[group, at], ring_recv.at[group, at], right if way == 0 else left
        )

    sends = []

    def launch(group):
        for way in (0, 1):
            src = mine(group, chip_at(way, counts(group)[way]))
            copy = ring_copy(group, way, 1, src)
            copy.start()
            sends.append(copy)

    def tick(group, hop):
        for way in (0, 1):
            if hop > counts(group)[way]:
                continue
            here = slot(group, way, hop)
            ring_copy(group, way, hop, here).wait_recv()
            to_go = counts(group)[way] - hop
            if to_go:
                add_all(here, [here, mine(group, chip_at(way, to_go))])
                copy = ring_copy(group, way, hop + 1, here)
                copy.start()
                sends.append(copy)
        if hop == chips // 2:
            ends = [slot(group, way, counts(group)[way]) for way in (0, 1)]
            dst = gm_o.at[group] if group < 3 else ga_o.at[3] if group == 3 else ga_o.at[pl.ds(0, 3)]
            add_all(dst, [mine(group, index // 2)] + ends)

    def send_pair(matrices, at):
        copies = []
        for chip in range(chips):
            there = pl.multiple_of((chip * 2 + 1 - core) * rows_own, rows_own)
            copy = remote(
                dw_s.at[matrices, pl.ds(there, rows_own)], near.at[matrices, chip],
                pair_send.at[at, chip], pair_recv.at[at, chip], pair,
            )
            copy.start()
            copies.append(copy)
        return copies

    def sum_pair(copies, matrices):
        for chip, copy in enumerate(copies):
            copy.wait()
            own = pl.ds(pl.multiple_of((chip * 2 + core) * rows_own, rows_own), rows_own)
            here = near.at[matrices, chip]
            add_all(here, [here, dw_s.at[matrices, own]])

    loads[10].wait()
    for group in (2, 0, 1):
        launch(group)
    pending = [(group, hop) for hop in range(1, chips // 2 + 1) for group in (2, 0, 1)]
    for copy in loads[:10]:
        copy.wait()
    copies = {}

    def finish_input(block):
        rows = pl.ds(block * BLOCK, BLOCK)
        copies[block].wait()
        pltpu.make_async_copy(dri_hbm.at[rows], dri_s.at[block % 2], load_dri.at[block]).wait()

        def body(i, _):
            r = pl.ds(pl.multiple_of(block * BLOCK + i * 16, 16), 16)
            total = out_s[r].astype(F32) + in_s[r].astype(F32)
            out_s[r] = (dri_s[block % 2, pl.ds(pl.multiple_of(i * 16, 16), 16)] + total).astype(BF)
            return 0

        lax.fori_loop(0, BLOCK // 16, body, 0)
        copy = pltpu.make_async_copy(out_s.at[rows], ig_o.at[rows], store.at[block])
        copy.start()
        if block >= 2:
            fetch_dri(block - 2)
        return copy

    def fetch_dri(block):
        rows = pl.ds(block * BLOCK, BLOCK)
        pltpu.make_async_copy(dri_hbm.at[rows], dri_s.at[block % 2], load_dri.at[block]).start()

    fetch_dri(blocks - 1)
    fetch_dri(blocks - 2)
    for block in reversed(range(blocks)):
        low = first_key(block)
        keys = (block + 1) * BLOCK - low
        rows = pl.ds(block * BLOCK, BLOCK)
        span = pl.ds(low, keys)
        kpos = lax.broadcasted_iota(jnp.int32, (keys, BLOCK), 0) + low
        qpos = lax.broadcasted_iota(jnp.int32, (keys, BLOCK), 1) + block * BLOCK
        allowed = (kpos >= start_ref[:, block * BLOCK : (block + 1) * BLOCK]) & (kpos <= qpos)
        bias[:keys] = jnp.where(allowed, 0.0, NEG_FILL)

        def heads(pair_of, _):
            c = pl.ds(pl.multiple_of(pair_of * 128, 128), 128)
            q, k, v, dy = q_ref[rows, c], k_ref[span, c], v_ref[span, c], dy_ref[rows, c]
            prod = dy.astype(F32) * y_ref[rows, c].astype(F32)
            prod_high = prod.astype(BF)
            prod_low = (prod - prod_high.astype(F32)).astype(BF)
            dq = jnp.zeros((BLOCK, 128), F32)
            dk = jnp.zeros((keys, 128), F32)
            dv = jnp.zeros((keys, 128), F32)
            for half in (0, 1):
                mask, row = half_of(BLOCK, half), half_of(8, half)
                qm, dym, km = q * mask, dy * mask, k * half_of(keys, half)
                expo = jnp.exp(dot_nt(k, qm) + bias[:keys])
                probs = expo * (1.0 / jnp.sum(expo, axis=0, keepdims=True))
                delta = (dot_nt(row, prod_high) + dot_nt(row, prod_low))[0:1]
                dz = (probs * (dot_nt(v, dym) - delta)).astype(BF)
                dk = dk + dot_nn(dz, qm)
                dv = dv + dot_nn(probs.astype(BF), dym)
                dq = dq + dot_tn(dz, km)
            dq_s[rows, c] = dq * HD**-0.5
            dk_s[span, c] = dk_s[span, c] + dk
            dv_s[span, c] = dv_s[span, c] + dv
            return 0

        for part in (0, 1):
            lax.fori_loop(part * (cols // 256), (part + 1) * (cols // 256), heads, 0)
            if part == 0:
                tick(*pending.pop(0))
        cos, sin = cos_ref[rows], sin_ref[rows]
        for c in range(0, cols, 128):
            s = slice(c, c + 128)
            gain = gain_ref[:, s]
            head = jnp.zeros((BLOCK, 128), F32)
            for j, (grad_s, low_ref, factor_ref, scale) in enumerate(
                ((dq_s, q_ref, rq_ref, HD**0.5), (dk_s, k_ref, rk_ref, 1.0))
            ):
                grad = grad_s[rows, s]
                unit = low_ref[rows, s].astype(F32) * (scale / gain)
                head = head + grad * unit
                grad = grad * gain
                turned = factor_ref[rows, s].astype(F32) * (grad - unit * (split_dot(grad * unit, ones) * (1.0 / HD)))
                low_s[j, rows, s] = (turned * cos - other_half(turned) * sin).astype(BF)
            head_o[:, s] = head_o[:, s] + jnp.sum(head, axis=0, keepdims=True)
            low_s[2, rows, s] = dv_s[rows, s].astype(BF)
        for c in range(0, width, 512):
            part = sum(dot_nt(low_s[j, rows], w_ref[j, c : c + 512]) for j in range(3))
            out_s[rows, c : c + 512] = part.astype(BF)
        copy = remote(out_s.at[rows], in_s.at[rows], send.at[block], recv.at[block], across)
        copy.start()
        copies[block] = copy
        tick(*pending.pop(0))
        if block == blocks - 1:
            for copy in loads[11:]:
                copy.wait()

            def out_grad(i, _):
                d = pl.ds(pl.multiple_of(i * BLOCK, BLOCK), BLOCK)
                dw_s[3, d] = dot_tn(do_ref[:, d], y_ref[...]).astype(BF)
                return 0

            lax.fori_loop(0, width // BLOCK, out_grad, 0)
            pair_out = send_pair(3, 0)
        if block == blocks - 2:
            sum_pair(pair_out, 3)
            launch(3)
    stores = [finish_input(blocks - 1)]

    def in_grads(i, _):
        d = pl.ds(pl.multiple_of(i * BLOCK, BLOCK), BLOCK)
        for j in range(3):
            dw_s[j, d] = dot_tn(x_ref[:, d], low_s[j]).astype(BF)
        return 0

    lax.fori_loop(0, width // BLOCK, in_grads, 0)
    pair_in = send_pair(pl.ds(0, 3), 1)
    tick(3, 1)
    tick(3, 2)
    tick(*pending.pop(0))
    sum_pair(pair_in, pl.ds(0, 3))
    launch(4)
    tick(3, 3)
    tick(3, 4)
    for hop in range(1, chips // 2 + 1):
        if pending:
            tick(*pending.pop(0))
        if hop == 1:
            stores.append(finish_input(blocks - 2))
        tick(4, hop)
    while pending:
        tick(*pending.pop(0))
    for block in reversed(range(blocks - 2)):
        stores.append(finish_input(block))
    for copy in stores:
        copy.wait()
    for copy in sends:
        copy.wait_send()


def attention_backward(states, weights, q, k, v, rq, rk, y, dy, do, dri, sums, cos, sin, gain, start, fsdp):
    length, width = states.shape
    cols = gain.shape[1]
    chips = fsdp // 2
    rows, units = sums.shape[2:]
    vspec, anyspec = pl.BlockSpec(memory_space=VM), pl.BlockSpec(memory_space=pl.ANY)
    blocks = length // BLOCK
    sem = pltpu.SemaphoreType.DMA
    square = VM((length, cols), BF)
    return pl.pallas_call(
        backward_kernel,
        out_shape=(
            jax.ShapeDtypeStruct((length, width), BF),
            jax.ShapeDtypeStruct((1, cols), F32),
            jax.ShapeDtypeStruct((4, rows, cols), F32),
            jax.ShapeDtypeStruct((3, rows, units), F32),
        ),
        in_specs=[anyspec] * 14 + [vspec] * 2,
        out_specs=(anyspec, vspec, vspec, vspec),
        scratch_shapes=[
            VM((length, width), BF), VM((3, width, cols), BF), square, square, square, square, square, square, square,
            VM((length, width), BF), VM(sums.shape, BF), VM((length, 128), F32), VM((length, 128), F32),
            VM((2, BLOCK, width), F32),
            VM((BLOCK + SPAN, BLOCK), F32),
            VM((length, cols), F32), VM((length, cols), F32), VM((length, cols), F32),
            VM((3, length, cols), BF), VM((length, width), BF), VM((length, width), BF),
            VM((4, width, cols), BF), VM((4, chips, rows, cols), BF),
            VM((chips - 1, 4, rows, cols), BF), VM((3, chips - 1, rows, units), BF),
            sem((13,)), sem((blocks,)), sem((blocks,)), sem((blocks,)), sem((blocks,)),
            sem((2, chips)), sem((2, chips)), sem((5, chips - 1)), sem((5, chips - 1)),
        ],
        compiler_params=pltpu.CompilerParams(collective_id=5, has_side_effects=True, vmem_limit_bytes=63 * MIB),
        name="attention_backward",
    )(states, weights, q, k, v, rq, rk, y, dy, do, dri, sums, cos, sin, gain, start)


ROWS_STEP = 32
UNIT_STEP = 512


def row_factor(v):
    return lax.rsqrt(jnp.mean(v * v, axis=-1, keepdims=True) + EPS)


def unit_back(factor, unit, grad):
    return factor * (grad - unit * jnp.mean(grad * unit, axis=-1, keepdims=True))


def fold(v):
    return jnp.sum(v.reshape(v.shape[0] // 8, 8, v.shape[1]), axis=0)


def feed_kernel(
    x_ref, y_ref, og_ref, mix_ref, us_ref, wo_own, wo_peer, w_ref,
    out_o, dri_o, do_o, dy_o, mix_o, us_o, sum_o,
    wo_s, wu_s, wg_s, wd_s, o_s, hb_s, u_s, g_s, hid_s, dm_s, dh_s, own_s, got_m, got_d, hout_s,
    load, store, send_m, recv_m, send_d, recv_d, pair_free, pair_send, pair_recv, pair_save,
):
    index, x = lax.axis_index("fsdp"), lax.axis_index("mp")
    across = (index, 1 - x)
    core = index % 2
    pair = (index + 1 - 2 * core, x)
    length, width = x_ref.shape
    cols, units = wo_own.shape[2], us_ref.shape[1]
    chips, rows_own = sum_o.shape[1:3]
    loads = [
        pltpu.make_async_copy(wo_own.at[3], wo_s.at[x], load.at[0]),
        pltpu.make_async_copy(wo_peer, wo_s.at[1 - x], load.at[1]),
        pltpu.make_async_copy(w_ref.at[0], wu_s, load.at[2]),
        pltpu.make_async_copy(w_ref.at[1], wg_s, load.at[3]),
        pltpu.make_async_copy(w_ref.at[2], wd_s, load.at[4]),
    ]
    for copy in loads:
        copy.start()
    greet((across, pair))
    blocks = length // BLOCK
    copies_m, copies_d = [], []

    def first_half(r):
        states = x_ref[r].astype(F32)
        o = o_s[r]
        ro = row_factor(o)
        uo = o * ro
        mix = mix_ref[0:1]
        r1 = states + mix * (uo - states)
        rr = row_factor(r1)
        return states, ro, uo, rr, r1 * rr

    def by_rows(block, body, init):
        def run(i, carry):
            return body(pl.ds(pl.multiple_of(block * BLOCK + i * ROWS_STEP, ROWS_STEP), ROWS_STEP), i, carry)

        return lax.fori_loop(0, BLOCK // ROWS_STEP, run, init)

    def by_cols(total, step, body):
        def run(i, _):
            body(pl.ds(pl.multiple_of(i * step, step), step))
            return 0

        lax.fori_loop(0, total // step, run, 0)

    for block in range(blocks):
        rows = pl.ds(block * BLOCK, BLOCK)
        if block == 0:
            loads[0].wait()
            loads[1].wait()

        def out_proj(c):
            o_s[rows, c] = dot_nt(y_ref[0, rows], wo_s[0, c]) + dot_nt(y_ref[1, rows], wo_s[1, c])

        by_cols(width, 512, out_proj)

        def hidden(r, i, _):
            hb_s[r] = first_half(r)[4].astype(BF)
            return 0

        by_rows(block, hidden, 0)
        if block == 0:
            loads[2].wait()
            loads[3].wait()

        def gate(f):
            up = dot_nn(hb_s[rows], wu_s[:, f])
            gt = dot_nn(hb_s[rows], wg_s[:, f])
            arg = us_ref[1:2, f] * gt * D**-0.5
            sig = 1.0 / (1.0 + jnp.exp(-arg))
            u_s[rows, f] = up.astype(BF)
            g_s[rows, f] = gt.astype(BF)
            hid_s[rows, f] = (us_ref[0:1, f] * up * (arg * sig)).astype(BF)

        by_cols(units, UNIT_STEP, gate)
        if block == 0:
            loads[4].wait()

        def down(c):
            own_s[rows, c] = dot_nt(hid_s[rows], wd_s[c]).astype(BF)

        by_cols(width, 512, down)
        copy = remote(own_s.at[rows], got_m.at[rows], send_m.at[block], recv_m.at[block], across)
        copy.start()
        copies_m.append(copy)

    mix_m = jnp.zeros((8, width), F32)
    us_o[...] = jnp.zeros_like(us_o)
    outs = []
    for block in range(blocks):
        rows = pl.ds(block * BLOCK, BLOCK)
        copies_m[block].wait()
        if block >= 2:
            outs[block - 2].wait()

        def middle(r, i, total):
            h1 = first_half(r)[4]
            m = own_s[r].astype(F32) + got_m[r].astype(F32)
            rm = row_factor(m)
            um = m * rm
            mix = mix_ref[1:2]
            r2 = h1 + mix * (um - h1)
            rr = row_factor(r2)
            out = r2 * rr
            hout_s[block % 2, pl.ds(pl.multiple_of(i * ROWS_STEP, ROWS_STEP), ROWS_STEP)] = out
            dr2 = unit_back(rr, out, og_ref[r].astype(F32))
            dm_s[r] = unit_back(rm, um, mix * dr2).astype(BF)
            dh_s[r] = dr2 * (1.0 - mix)
            return total + fold(dr2 * (um - h1))

        mix_m = by_rows(block, middle, mix_m)
        copy = pltpu.make_async_copy(hout_s.at[block % 2], out_o.at[rows], store.at[block])
        copy.start()
        outs.append(copy)

        def gate_back(f):
            dhid = dot_nn(dm_s[rows], wd_s[:, f])
            up, gt = u_s[rows, f].astype(F32), g_s[rows, f].astype(F32)
            su, sv = us_ref[0:1, f], us_ref[1:2, f]
            arg = sv * gt * D**-0.5
            sig = 1.0 / (1.0 + jnp.exp(-arg))
            act = dhid * (arg * sig)
            darg = dhid * su * up * sig * (1.0 + arg * (1.0 - sig))
            us_o[0:1, f] = us_o[0:1, f] + jnp.sum(act * up, axis=0, keepdims=True)
            us_o[1:2, f] = us_o[1:2, f] + jnp.sum(darg * gt, axis=0, keepdims=True) * D**-0.5
            u_s[rows, f] = (act * su).astype(BF)
            g_s[rows, f] = (darg * sv * D**-0.5).astype(BF)

        by_cols(units, UNIT_STEP, gate_back)

        def up_back(c):
            own_s[rows, c] = (dot_nt(u_s[rows], wu_s[c]) + dot_nt(g_s[rows], wg_s[c])).astype(BF)

        by_cols(width, 512, up_back)
        copy = remote(own_s.at[rows], got_d.at[rows], send_d.at[block], recv_d.at[block], across)
        copy.start()
        copies_d.append(copy)

    jobs = ((wd_s, dm_s, hid_s), (wu_s, hb_s, u_s), (wg_s, hb_s, g_s))
    pairs = []
    for j, (weight_s, left_s, right_s) in enumerate(jobs):

        def grads(d):
            for u in range(0, units, 1024):
                f = pl.ds(u, 1024)
                weight_s[d, f] = dot_tn(left_s[:, d], right_s[:, f]).astype(BF)

        by_cols(width, BLOCK, grads)
        pl.semaphore_signal(pair_free.at[j], inc=1, device_id=pair, device_id_type=MESH)
        pl.semaphore_wait(pair_free.at[j], 1)
        for chip in range(chips):
            there = pl.multiple_of((chip * 2 + 1 - core) * rows_own, rows_own)
            copy = remote(
                weight_s.at[pl.ds(there, rows_own)], right_s.at[pl.ds(chip * rows_own, rows_own)],
                pair_send.at[j, chip], pair_recv.at[j, chip], pair,
            )
            copy.start()
            pairs.append(copy)
    saves = []

    def pair_sums(j):
        weight_s, _, right_s = jobs[j]
        for chip in range(chips):
            pairs[j * chips + chip].wait()
            base = (chip * 2 + core) * rows_own

            def add(i, _):
                r = pl.ds(pl.multiple_of(base + i * 16, 16), 16)
                near = right_s[pl.ds(pl.multiple_of(chip * rows_own + i * 16, 16), 16)]
                weight_s[r] = (weight_s[r].astype(F32) + near.astype(F32)).astype(BF)
                return 0

            lax.fori_loop(0, rows_own // 16, add, 0)
            copy = pltpu.make_async_copy(
                weight_s.at[pl.ds(pl.multiple_of(base, rows_own), rows_own)], sum_o.at[(j + 2) % 3, chip], pair_save.at[j, chip]
            )
            copy.start()
            saves.append(copy)

    mix_a = jnp.zeros((8, width), F32)
    for block in range(blocks):
        rows = pl.ds(block * BLOCK, BLOCK)
        copies_d[block].wait()

        def last(r, i, total):
            states, ro, uo, rr, h1 = first_half(r)
            mix = mix_ref[0:1]
            dr1 = unit_back(rr, h1, dh_s[r] + (own_s[r].astype(F32) + got_d[r].astype(F32)))
            dh_s[r] = dr1 * (1.0 - mix)
            dm_s[r] = unit_back(ro, uo, mix * dr1).astype(BF)
            return total + fold(dr1 * (uo - states))

        mix_a = by_rows(block, last, mix_a)
        dy_o[rows] = dot_nn(dm_s[rows], wo_s[x]).astype(BF)
        if block < 3:
            pair_sums(block)
    ends = [
        pltpu.make_async_copy(dh_s, dri_o, load.at[3]),
        pltpu.make_async_copy(dm_s, do_o, load.at[4]),
    ]
    for copy in ends:
        copy.start()
    mix_o[0:1] = jnp.sum(mix_a, axis=0, keepdims=True)
    mix_o[1:2] = jnp.sum(mix_m, axis=0, keepdims=True)
    for copy in outs[-2:] + saves + ends:
        copy.wait()


def feed_forward(states, y, out_grad, mix, scales, attn_full, wo_peer, mlp_full, fsdp):
    chips = fsdp // 2
    length, width = states.shape
    cols, units = y.shape[2], scales.shape[1]
    vspec, anyspec = pl.BlockSpec(memory_space=VM), pl.BlockSpec(memory_space=pl.ANY)
    blocks = length // BLOCK
    sem = pltpu.SemaphoreType.DMA

    def low(*shape):
        return jax.ShapeDtypeStruct(shape, BF)

    def full(*shape):
        return jax.ShapeDtypeStruct(shape, F32)

    return pl.pallas_call(
        feed_kernel,
        out_shape=(
            full(length, width), full(length, width), low(length, width), low(length, cols),
            full(2, width), full(2, units), low(3, chips, width // fsdp, units),
        ),
        in_specs=[vspec] * 5 + [anyspec] * 3,
        out_specs=(anyspec, anyspec, anyspec, vspec, vspec, vspec, anyspec),
        scratch_shapes=[
            VM((2, width, cols), BF),
            VM((width, units), BF), VM((width, units), BF), VM((width, units), BF),
            VM((length, width), F32), VM((length, width), BF),
            VM((length, units), BF), VM((length, units), BF), VM((length, units), BF),
            VM((length, width), BF), VM((length, width), F32),
            VM((length, width), BF), VM((length, width), BF), VM((length, width), BF),
            VM((2, BLOCK, width), F32),
            sem((5,)), sem((blocks,)), sem((blocks,)), sem((blocks,)), sem((blocks,)), sem((blocks,)),
            pltpu.SemaphoreType.REGULAR((3,)), sem((3, chips)), sem((3, chips)), sem((3, chips)),
        ],
        compiler_params=pltpu.CompilerParams(collective_id=6, has_side_effects=True, vmem_limit_bytes=63 * MIB),
        name="feed_forward",
    )(states, y, out_grad, mix, scales, attn_full, wo_peer, mlp_full)


def local_fast(
    inputs, doc_ids, out_grad, attn_w, attn_mom, attn_avg, mlp_w, mlp_mom, mlp_avg,
    head_scale, head_mom, mix_rates, mix_mom, unit_scales, unit_mom,
):
    fsdp = lax.axis_size("fsdp")
    tokens = inputs.shape[0] * fsdp * inputs.shape[1]
    root_tokens = math.sqrt(tokens)
    width = inputs.shape[2]
    states = inputs[0]
    gain = head_scale[None]
    attn_full, mlp_full, wo_peer, q, k, v, rq, rk, y, start, cos, sin = attention_forward(
        attn_w, mlp_w, states, doc_ids, gain, fsdp
    )
    result, dri, do, dy, grad_mix, grad_units, sums = feed_forward(
        states, y, out_grad[0], mix_rates, unit_scales, attn_full, wo_peer, mlp_full, fsdp
    )
    input_low, grad_head, grad_attn, grad_mlp = attention_backward(
        states, attn_full, q, k, v, rq, rk, y, dy, do, dri, sums, cos, sin, gain, start, fsdp
    )
    input_grad = input_low.astype(F32)
    grad_head = grad_head[0]
    small = jnp.concatenate(
        [
            jnp.pad(grad_head, (0, D - grad_head.shape[0])),
            grad_mix.reshape(-1),
            grad_units.reshape(-1),
            jnp.zeros((D,), F32),
        ]
    ).reshape(8, D)
    attn_mom_new, attn_new, attn_avg_new, mlp_mom_new, mlp_new, mlp_avg_new, small = update(
        grad_attn, grad_mlp, small, attn_w, attn_mom, attn_avg, mlp_w, mlp_mom, mlp_avg,
        RATE_WEIGHT / root_tokens, width, fsdp,
    )
    grad_head, grad_mix, grad_units = small[0, : grad_head.shape[0]], small[1:3], small[3:7].reshape(2, -1)
    head_mom_new, head_new = nesterov(head_scale, head_mom, grad_head, RATE_HEAD / root_tokens)
    mix_mom_new, mix_new = nesterov(mix_rates, mix_mom, grad_mix, RATE_MIX / root_tokens)
    units_mom_new, units_new = nesterov(unit_scales, unit_mom, grad_units, RATE_UNITS / root_tokens)
    return (
        result[None], input_grad[None], attn_mom_new, attn_new, attn_avg_new, mlp_mom_new, mlp_new, mlp_avg_new,
        head_mom_new, head_new, mix_mom_new, mix_new, units_mom_new, units_new,
    )


def local(
    inputs,
    doc_ids,
    out_grad,
    attn_w,
    attn_mom,
    attn_avg,
    mlp_w,
    mlp_mom,
    mlp_avg,
    head_scale,
    head_mom,
    mix_rates,
    mix_mom,
    unit_scales,
    unit_mom,
):
    length = inputs.shape[1]
    model_width = inputs.shape[2]
    head_count = head_scale.shape[0] // HD
    block_rows = min(512, length)
    block_count = length // block_rows
    tokens = inputs.shape[0] * lax.axis_size("fsdp") * length
    doc_row = doc_ids[0]
    input_low = inputs[0]
    resid_in = input_low.astype(jnp.float32)
    cos_table, sin_table = rotary_tables(doc_row)
    position = jnp.arange(length, dtype=jnp.int32)
    attn_full = lax.all_gather(attn_w.astype(jnp.bfloat16), "fsdp", axis=1, tiled=True)
    projected = jnp.einsum(
        "sd,jdc->jsc", input_low, attn_full[:3], preferred_element_type=jnp.float32
    )
    head_gain = head_scale.reshape(head_count, HD)
    q_rot = rotate(projected[0].reshape(length, head_count, HD), cos_table, sin_table)
    k_rot = rotate(projected[1].reshape(length, head_count, HD), cos_table, sin_table)
    q_unit = rms_unit(q_rot)
    k_unit = rms_unit(k_rot)
    query_low = (head_gain * q_unit).astype(jnp.bfloat16)
    key_low = (head_gain * k_unit).astype(jnp.bfloat16)
    value_low = projected[2].reshape(length, head_count, HD).astype(jnp.bfloat16)

    def scores_of(row_first):
        query_blk = lax.dynamic_slice_in_dim(query_low, row_first, block_rows, 0)
        raw_scores = jnp.einsum(
            "qhe,khe->hqk", query_blk, key_low, preferred_element_type=jnp.float32
        )
        row_pos = lax.dynamic_slice_in_dim(position, row_first, block_rows, 0)
        row_docs = lax.dynamic_slice_in_dim(doc_row, row_first, block_rows, 0)
        allowed = (row_docs[:, None] == doc_row[None, :]) & (position[None, :] <= row_pos[:, None])
        return (jnp.where(allowed[None], raw_scores * HD ** (-0.5), NEG_FILL), query_blk)

    def attend(accums, blk_index):
        scores, query_blk = scores_of(blk_index * block_rows)
        peak_val = jnp.max(scores, axis=-1, keepdims=True)
        expo_vals = jnp.exp(scores - peak_val)
        row_total = jnp.sum(expo_vals, axis=-1, keepdims=True)
        probs_low = (expo_vals / row_total).astype(jnp.bfloat16)
        blk_out = jnp.einsum(
            "hqk,khe->qhe", probs_low, value_low, preferred_element_type=jnp.float32
        )
        return (accums, (blk_out, (peak_val + jnp.log(row_total))[..., 0]))

    _, (mixed_blocks, log_totals) = lax.scan(attend, None, jnp.arange(block_count))
    mixed_low = mixed_blocks.reshape(length, head_count * HD).astype(jnp.bfloat16)
    attn_part = jnp.einsum("sc,dc->sd", mixed_low, attn_full[3], preferred_element_type=jnp.float32)
    attn_out = lax.psum(attn_part, "mp")
    attn_unit = rms_unit(attn_out)
    resid_one = resid_in + mix_rates[0] * (attn_unit - resid_in)
    hidden_one = rms_unit(resid_one)
    hidden_low = hidden_one.astype(jnp.bfloat16)
    mlp_full = lax.all_gather(mlp_w.astype(jnp.bfloat16), "fsdp", axis=1, tiled=True)
    gates = jnp.einsum("sd,jdf->jsf", hidden_low, mlp_full[:2], preferred_element_type=jnp.float32)
    up_proj = gates[0]
    gate_proj = gates[1]
    gate_arg = unit_scales[1] * gate_proj * D ** (-0.5)
    gate_sig = jax.nn.sigmoid(gate_arg)
    gate_act = gate_arg * gate_sig
    units_low = (unit_scales[0] * up_proj * gate_act).astype(jnp.bfloat16)
    mlp_part = jnp.einsum("sf,df->sd", units_low, mlp_full[2], preferred_element_type=jnp.float32)
    mlp_out = lax.psum(mlp_part, "mp")
    mlp_unit = rms_unit(mlp_out)
    resid_two = hidden_one + mix_rates[1] * (mlp_unit - hidden_one)
    result = rms_unit(resid_two)
    cotangent = out_grad[0].astype(jnp.float32)
    d_resid_two = rms_back(resid_two, cotangent)
    grad_mix_mlp = jnp.sum(d_resid_two * (mlp_unit - hidden_one), axis=0)
    d_hidden_one = d_resid_two * (1.0 - mix_rates[1])
    d_mlp_low = rms_back(mlp_out, mix_rates[1] * d_resid_two).astype(jnp.bfloat16)
    mlp_back = lax.all_gather(mlp_w.astype(jnp.bfloat16), "fsdp", axis=1, tiled=True)
    d_units = jnp.einsum("sd,df->sf", d_mlp_low, mlp_back[2], preferred_element_type=jnp.float32)
    d_up = d_units * unit_scales[0] * gate_act
    d_arg = d_units * unit_scales[0] * up_proj * gate_sig * (1.0 + gate_arg * (1.0 - gate_sig))
    d_gate = d_arg * unit_scales[1] * D ** (-0.5)
    grad_units = jnp.stack(
        [
            jnp.sum(d_units * up_proj * gate_act, axis=0),
            jnp.sum(d_arg * gate_proj * D ** (-0.5), axis=0),
        ]
    )
    d_gates_low = jnp.stack([d_up, d_gate]).astype(jnp.bfloat16)
    mlp_back_part = jnp.einsum(
        "jsf,jdf->sd", d_gates_low, mlp_back[:2], preferred_element_type=jnp.float32
    )
    d_hidden_one = d_hidden_one + lax.psum(mlp_back_part, "mp")
    right_cols = d_mlp_low
    left_cols = hidden_low
    grad_mlp = jnp.transpose(
        lax.psum_scatter(
            jnp.concatenate(
                [
                    jnp.einsum(
                        "sd,jsf->djf", left_cols, d_gates_low, preferred_element_type=jnp.float32
                    ),
                    jnp.einsum(
                        "sd,sf->df", right_cols, units_low, preferred_element_type=jnp.float32
                    )[:, None, :],
                ],
                axis=1,
            ),
            "fsdp",
            scatter_dimension=0,
            tiled=True,
        ),
        (1, 0, 2),
    )
    d_resid_one = rms_back(resid_one, d_hidden_one)
    grad_mix_attn = jnp.sum(d_resid_one * (attn_unit - resid_in), axis=0)
    d_resid_in = d_resid_one * (1.0 - mix_rates[0])
    d_attn_low = rms_back(attn_out, mix_rates[0] * d_resid_one).astype(jnp.bfloat16)
    attn_back = lax.all_gather(attn_w.astype(jnp.bfloat16), "fsdp", axis=1, tiled=True)
    d_mixed = jnp.einsum("sd,dc->sc", d_attn_low, attn_back[3], preferred_element_type=jnp.float32)
    d_mixed = d_mixed.astype(jnp.bfloat16).reshape(length, head_count, HD)

    def attend_back(accums, blk_index):
        d_key, d_value = accums
        row_first = blk_index * block_rows
        scores, query_blk = scores_of(row_first)
        blk_total = lax.dynamic_index_in_dim(log_totals, blk_index, 0, keepdims=False)
        attn_probs = jnp.exp(scores - blk_total[..., None])
        d_out_blk = lax.dynamic_slice_in_dim(d_mixed, row_first, block_rows, 0)
        d_probs = jnp.einsum(
            "qhe,khe->hqk", d_out_blk, value_low, preferred_element_type=jnp.float32
        )
        d_scores = attn_probs * (d_probs - jnp.sum(attn_probs * d_probs, axis=-1, keepdims=True))
        d_raw_low = (d_scores * HD ** (-0.5)).astype(jnp.bfloat16)
        d_query = jnp.einsum("hqk,khe->qhe", d_raw_low, key_low, preferred_element_type=jnp.float32)
        d_key = d_key + jnp.einsum(
            "hqk,qhe->khe", d_raw_low, query_blk, preferred_element_type=jnp.float32
        )
        d_value = d_value + jnp.einsum(
            "hqk,qhe->khe",
            attn_probs.astype(jnp.bfloat16),
            d_out_blk,
            preferred_element_type=jnp.float32,
        )
        return ((d_key, d_value), d_query)

    zero_heads = jnp.zeros((length, head_count, HD), jnp.float32)
    (d_key_all, d_value_all), d_query_blocks = lax.scan(
        attend_back, (zero_heads, zero_heads), jnp.arange(block_count)
    )
    d_query_all = d_query_blocks.reshape(length, head_count, HD)
    grad_head = jnp.sum(d_query_all * q_unit + d_key_all * k_unit, axis=0).reshape(-1)
    d_query_raw = rotate_back(rms_back(q_rot, head_gain * d_query_all), cos_table, sin_table)
    d_key_raw = rotate_back(rms_back(k_rot, head_gain * d_key_all), cos_table, sin_table)
    d_proj_low = jnp.stack(
        [
            d_query_raw.reshape(length, -1),
            d_key_raw.reshape(length, -1),
            d_value_all.reshape(length, -1),
        ]
    ).astype(jnp.bfloat16)
    grad_mix = jnp.stack([grad_mix_attn, grad_mix_mlp])
    grad_head, grad_mix, grad_units = lax.psum((grad_head, grad_mix, grad_units), "fsdp")
    attn_back_part = jnp.einsum(
        "jsc,jdc->sd", d_proj_low, attn_back[:3], preferred_element_type=jnp.float32
    )
    input_grad = d_resid_in + lax.psum(attn_back_part.astype(jnp.bfloat16), "mp").astype(
        jnp.float32
    )
    left_cols = input_low
    right_cols = d_attn_low
    in_terms = jnp.einsum("sd,jsc->djc", left_cols, d_proj_low, preferred_element_type=jnp.float32)
    out_terms = jnp.einsum("sd,sc->dc", right_cols, mixed_low, preferred_element_type=jnp.float32)
    grad_attn = jnp.transpose(
        lax.psum_scatter(
            jnp.concatenate([in_terms, out_terms[:, None, :]], axis=1),
            "fsdp",
            scatter_dimension=0,
            tiled=True,
        ),
        (1, 0, 2),
    )
    root_tokens = math.sqrt(tokens)
    weight_rate = RATE_WEIGHT / root_tokens
    attn_mom_new, attn_step = nesterov(attn_w, attn_mom, grad_attn, weight_rate)
    mlp_mom_new, mlp_step = nesterov(mlp_w, mlp_mom, grad_mlp, weight_rate)
    attn_squares = jnp.sum(attn_step * attn_step, axis=1)
    mlp_squares = jnp.sum(mlp_step * mlp_step, axis=1)
    attn_squares, mlp_squares = lax.psum((attn_squares, mlp_squares), "fsdp")
    attn_new = attn_step * lax.rsqrt(attn_squares[:, None, :] / model_width + EPS)
    mlp_new = mlp_step * lax.rsqrt(mlp_squares[:, None, :] / model_width + EPS)
    head_mom_new, head_new = nesterov(head_scale, head_mom, grad_head, RATE_HEAD / root_tokens)
    mix_mom_new, mix_new = nesterov(mix_rates, mix_mom, grad_mix, RATE_MIX / root_tokens)
    units_mom_new, units_new = nesterov(unit_scales, unit_mom, grad_units, RATE_UNITS / root_tokens)
    return (
        result[None],
        input_grad[None],
        attn_mom_new,
        attn_new,
        AVERAGE * attn_avg + (1.0 - AVERAGE) * attn_new,
        mlp_mom_new,
        mlp_new,
        AVERAGE * mlp_avg + (1.0 - AVERAGE) * mlp_new,
        head_mom_new,
        head_new,
        mix_mom_new,
        mix_new,
        units_mom_new,
        units_new,
    )


def solution(mesh):
    fast = D // mesh.shape["fsdp"] % 16 == 0 and mesh.shape["fsdp"] % 8 == 0
    placed = (
        P("fsdp", None, None),
        P("fsdp", None),
        P("fsdp", None, None),
        P(None, "fsdp", "mp"),
        P(None, "fsdp", "mp"),
        P(None, "fsdp", "mp"),
        P(None, "fsdp", "mp"),
        P(None, "fsdp", "mp"),
        P(None, "fsdp", "mp"),
        P("mp"),
        P("mp"),
        P(),
        P(),
        P(None, "mp"),
        P(None, "mp"),
    )
    return jax.shard_map(
        local_fast if fast else local,
        mesh=mesh,
        in_specs=placed,
        out_specs=(
            P("fsdp", None, None),
            P("fsdp", None, None),
            P(None, "fsdp", "mp"),
            P(None, "fsdp", "mp"),
            P(None, "fsdp", "mp"),
            P(None, "fsdp", "mp"),
            P(None, "fsdp", "mp"),
            P(None, "fsdp", "mp"),
            P("mp"),
            P("mp"),
            P(),
            P(),
            P(None, "mp"),
            P(None, "mp"),
        ),
        check_vma=False,
    )
```

```python
import functools
import math

import jax
import jax.numpy as jnp
from jax import lax
from jax.experimental import pallas as pl
from jax.experimental.pallas import tpu as pltpu
from jax.sharding import PartitionSpec as P

D = 1024
HD = 64


EPS = 1e-06
MOMENTUM = 0.9
AVERAGE = 0.9
NEG_FILL = -1e30
THETA = 10000.0
RATE_WEIGHT = 50.0
RATE_HEAD = 0.08
RATE_MIX = 0.02
RATE_UNITS = 0.5


def rms_unit(vector):
    return vector * lax.rsqrt(jnp.mean(vector * vector, axis=-1, keepdims=True) + EPS)


def rms_back(vector, grad):
    factor = lax.rsqrt(jnp.mean(vector * vector, axis=-1, keepdims=True) + EPS)
    unit_vec = vector * factor
    return factor * (grad - unit_vec * jnp.mean(grad * unit_vec, axis=-1, keepdims=True))


def rotary_tables(doc_row):
    length = doc_row.shape[0]
    position = jnp.arange(length, dtype=jnp.int32)
    boundary = jnp.concatenate(
        [jnp.ones((1,), jnp.int32), (doc_row[1:] != doc_row[:-1]).astype(jnp.int32)]
    )
    doc_start = lax.cummax(jnp.where(boundary > 0, position, 0), axis=0)
    offset = (position - doc_start).astype(jnp.float32)
    freq = THETA ** (-2.0 * jnp.arange(HD // 2, dtype=jnp.float32) / HD)
    angle = offset[:, None] * freq[None, :]
    return (jnp.cos(angle), jnp.sin(angle))


def rotate(vector, cos_table, sin_table):
    half_dim = vector.shape[-1] // 2
    lower_half = vector[..., :half_dim]
    upper_half = vector[..., half_dim:]
    cos_part = cos_table[:, None, :]
    sin_part = sin_table[:, None, :]
    return jnp.concatenate(
        [
            lower_half * cos_part - upper_half * sin_part,
            lower_half * sin_part + upper_half * cos_part,
        ],
        axis=-1,
    )


def rotate_back(grad, cos_table, sin_table):
    half_dim = grad.shape[-1] // 2
    lower_half = grad[..., :half_dim]
    upper_half = grad[..., half_dim:]
    cos_part = cos_table[:, None, :]
    sin_part = sin_table[:, None, :]
    return jnp.concatenate(
        [
            lower_half * cos_part + upper_half * sin_part,
            upper_half * cos_part - lower_half * sin_part,
        ],
        axis=-1,
    )


def nesterov(param, moment, grad, step_rate):
    moment_new = MOMENTUM * moment + grad
    return (moment_new, param - step_rate * (grad + MOMENTUM * moment_new))


BF = jnp.bfloat16
F32 = jnp.float32
MESH = pl.DeviceIdType.MESH
VM = pltpu.VMEM
MIB = 1 << 20
BLOCK = 256
SPAN = 512
ROWS_STEP = 128
UNIT_STEP = 1024


def dot_nn(a, b):
    return lax.dot_general(a, b, (((1,), (0,)), ((), ())), preferred_element_type=F32)


def dot_nt(a, b):
    return lax.dot_general(a, b, (((1,), (1,)), ((), ())), preferred_element_type=F32)


def dot_tn(a, b):
    return lax.dot_general(a, b, (((0,), (0,)), ((), ())), preferred_element_type=F32)


def split_dot(a, ones):
    high = a.astype(BF)
    return dot_nn(high, ones) + dot_nn((a - high.astype(F32)).astype(BF), ones)


def ring_place(index, chips):
    z, y = index // 4, (index // 2) % 2
    return z + y * (chips - 1 - 2 * z), index % 2


def ring_device(place, core, chips):
    y = place // (chips // 2)
    return ((place + y * (chips - 1 - 2 * place)) * 2 + y) * 2 + core


def peers_of(chips):
    index, x = lax.axis_index("fsdp"), lax.axis_index("mp")
    place, core = ring_place(index, chips)
    right = (ring_device((place + 1) % chips, core, chips), x)
    left = (ring_device((place + chips - 1) % chips, core, chips), x)
    return index, x, place, core, right, left, (index + 1 - 2 * core, x), (index, 1 - x)


def greet(peers):
    barrier = pltpu.get_barrier_semaphore()
    for peer in peers:
        pl.semaphore_signal(barrier, inc=1, device_id=peer, device_id_type=MESH)
    pl.semaphore_wait(barrier, len(peers))


def remote(src, dst, send, recv, peer):
    return pltpu.make_async_remote_copy(
        src_ref=src, dst_ref=dst, send_sem=send, recv_sem=recv, device_id=peer, device_id_type=MESH
    )


def start_copy(src, dst, sem):
    copy = pltpu.make_async_copy(src, dst, sem)
    copy.start()
    return copy


def by_step(total, step, body):
    def run(i, _):
        body(pl.ds(pl.multiple_of(i * step, step), step))
        return 0

    lax.fori_loop(0, total // step, run, 0)


def add_all(dst, refs):
    if len(dst.shape) == 3:
        for j in range(dst.shape[0]):
            add_all(dst.at[j], [ref.at[j] for ref in refs])
        return

    def body(r):
        total = refs[0][r].astype(F32)
        for ref in refs[1:]:
            total = total + ref[r].astype(F32)
        dst[r] = total.astype(dst.dtype)

    by_step(dst.shape[0], 16, body)


def ring_hops(chips, group, long_right):
    pair_of = (chips // 2, chips - 1 - chips // 2)
    return pair_of if group in long_right else pair_of[::-1]


class Scatter:
    def __init__(self, chips, long_right, mine, slot, result, send, recv):
        _, _, self.place, self.core, self.right, self.left, _, _ = peers_of(chips)
        self.chips, self.long_right, self.mine, self.slot_at, self.result = chips, long_right, mine, slot, result
        self.send, self.recv, self.sent = send, recv, []

    def hops(self, group):
        return ring_hops(self.chips, group, self.long_right)

    def chip(self, way, count):
        step = count if way == 0 else self.chips - count
        return ring_device((self.place + step) % self.chips, self.core, self.chips) // 2

    def copy(self, group, way, hop, src):
        at = hop - 1 if way == 0 else self.hops(group)[0] + hop - 1
        peer = self.right if way == 0 else self.left
        return remote(src, self.slot_at(group, at), self.send.at[group, at], self.recv.at[group, at], peer)

    def slot(self, group, way, hop):
        return self.slot_at(group, hop - 1 if way == 0 else self.hops(group)[0] + hop - 1)

    def launch(self, group):
        for way in (0, 1):
            copy = self.copy(group, way, 1, self.mine(group, self.chip(way, self.hops(group)[way])))
            copy.start()
            self.sent.append(copy)

    def tick(self, group, hop):
        hops = self.hops(group)
        for way in (0, 1):
            if hop > hops[way]:
                continue
            here = self.slot(group, way, hop)
            self.copy(group, way, hop, here).wait_recv()
            if hop < hops[way]:
                add_all(here, [here, self.mine(group, self.chip(way, hops[way] - hop))])
                copy = self.copy(group, way, hop + 1, here)
                copy.start()
                self.sent.append(copy)
        if hop == self.chips // 2:
            ends = [self.slot(group, way, hops[way]) for way in (0, 1)]
            add_all(self.result(group), [self.mine(group, self.chip(0, 0))] + ends)

    def close(self):
        for copy in self.sent:
            copy.wait_send()


def head_ones():
    row = lax.broadcasted_iota(jnp.int32, (128, 128), 0) // HD
    col = lax.broadcasted_iota(jnp.int32, (128, 128), 1) // HD
    return jnp.where(row == col, 1.0, 0.0).astype(BF)


def half_of(rows, half):
    lane = lax.broadcasted_iota(jnp.int32, (rows, 128), 1)
    return jnp.where((lane < HD) == (half == 0), 1.0, 0.0).astype(BF)


def other_half(v):
    lane = lax.broadcasted_iota(jnp.int32, v.shape, 1)
    return jnp.where(lane % HD < HD // 2, pltpu.roll(v, 128 - HD // 2, 1), pltpu.roll(v, HD // 2, 1))


def first_key(block):
    return max(0, block * BLOCK - SPAN)


def low(*shape):
    return jax.ShapeDtypeStruct(shape, BF)


def full(*shape):
    return jax.ShapeDtypeStruct(shape, F32)


GATHER_GROUPS = ((0, 0, 3), (0, 3, 1), (1, 0, 1), (1, 1, 1), (1, 2, 1))
GATHER_LONG = (0, 2, 4)


def forward_kernel(
    chips, attn_ref, mlp_ref, x_hbm, doc_ref, gain_ref, freq_ref,
    attn_o, mlp_o, wo_o, q_o, k_o, v_o, rq_o, rk_o, y_o, start_o, cos_o, sin_o,
    attn_s, mlp_s, w_s, x_ref, q_s, k_s, v_s, rq_s, rk_s, y_s, cos_s, sin_s, start_s, bias,
    load, store, send, recv, ring_send, ring_recv, pair_send, pair_recv, own_sem, wo_send, wo_recv,
):
    index, x, place, core, right, left, pair, across = peers_of(chips)
    pair_index = pair[0]
    rows_own = attn_ref.shape[1]
    length, cols = q_s.shape
    blocks = length // BLOCK
    load_x = start_copy(x_hbm, x_ref, load)
    ins, outs = (attn_s, mlp_s), (w_s, mlp_o)

    def own(group):
        kind, first, count = GATHER_GROUPS[group]
        return ins[kind].at[pl.ds(first, count)]

    def block_of(group, dev):
        kind, first, count = GATHER_GROUPS[group]
        return outs[kind].at[pl.ds(first, count), pl.ds(pl.multiple_of(dev * rows_own, rows_own), rows_own)]

    def counts(group):
        return ring_hops(chips, group, GATHER_LONG)

    def origin(way, hop):
        there = (place + chips - hop) % chips if way == 0 else (place + hop) % chips
        return ring_device(there, core, chips)

    def ring_copy(group, way, hop, src, dst):
        return remote(
            src, dst, ring_send.at[group, way, hop - 1], ring_recv.at[group, way, hop - 1], right if way == 0 else left
        )

    def pair_copy(group, at, src, dev):
        return remote(src, block_of(group, dev), pair_send.at[group, at], pair_recv.at[group, at], pair)

    sends, owns = [], []

    def launch(group):
        for way in (0, 1):
            copy = ring_copy(group, way, 1, own(group), block_of(group, index))
            copy.start()
            sends.append(copy)
        copy = pair_copy(group, 0, own(group), index)
        copy.start()
        sends.append(copy)
        owns.append(start_copy(own(group), block_of(group, index), own_sem.at[group]))

    def tick(group, hop):
        for way in (0, 1):
            if hop > counts(group)[way]:
                continue
            dev = origin(way, hop)
            here = block_of(group, dev)
            ring_copy(group, way, hop, here, here).wait_recv()
            if hop < counts(group)[way]:
                copy = ring_copy(group, way, hop + 1, here, here)
                copy.start()
                sends.append(copy)
            copy = pair_copy(group, hop if way == 0 else counts(group)[0] + hop, here, dev)
            copy.start()
            sends.append(copy)

    def await_pair(group):
        here = block_of(group, pair_index)
        pair_copy(group, 0, here, pair_index).wait_recv()
        for way in (0, 1):
            for hop in range(1, counts(group)[way] + 1):
                dev = origin(way, hop) + 1 - 2 * core
                here = block_of(group, dev)
                pair_copy(group, hop if way == 0 else counts(group)[0] + hop, here, dev).wait_recv()

    attn_s[...] = attn_ref[...].astype(BF)
    greet((right, left, pair, across))
    launch(0)
    launch(1)
    mlp_s[...] = mlp_ref[...].astype(BF)
    launch(2)
    doc = doc_ref[...]
    start = jnp.zeros(doc.shape, F32)
    for number in range(3):
        count = jnp.sum(jnp.where(doc == number, 1.0, 0.0), axis=1, keepdims=True)
        start = start + jnp.where(doc > number, count, 0.0)
    start_o[...] = start.astype(jnp.int32)
    start_s[...] = jnp.transpose(jnp.broadcast_to(start, (128, length)))

    def tables(rows, first):
        position = (lax.broadcasted_iota(jnp.int32, (BLOCK, 128), 0) + first).astype(F32)
        angle = (position - start_s[rows]) * freq_ref[...]
        lane = lax.broadcasted_iota(jnp.int32, (BLOCK, 128), 1)
        cos_s[rows] = jnp.cos(angle)
        sin_s[rows] = jnp.where(lane % HD < HD // 2, -1.0, 1.0) * jnp.sin(angle)

    for block in range(blocks // 2):
        tables(pl.ds(block * BLOCK, BLOCK), block * BLOCK)
    tick(0, 1)
    tick(1, 1)
    for block in range(blocks // 2, blocks):
        tables(pl.ds(block * BLOCK, BLOCK), block * BLOCK)
    stores = [start_copy(cos_s, cos_o, store.at[0]), start_copy(sin_s, sin_o, store.at[1])]
    longest = chips // 2
    tick(2, 1)
    launch(3)
    for hop in range(2, longest + 1):
        tick(0, hop)
        tick(1, hop)
        if hop == longest:
            break
        tick(2, hop)
    tick(3, 1)
    launch(4)
    pending = [(2, longest), (4, 1)]
    for hop in range(2, longest + 1):
        pending += [(3, hop), (4, hop)]
    ones = head_ones()
    load_x.wait()
    owns[0].wait()
    await_pair(0)
    stores.append(start_copy(w_s.at[pl.ds(0, 3)], attn_o.at[pl.ds(0, 3)], store.at[2]))
    owns[1].wait()
    await_pair(1)
    wo_copy = remote(w_s.at[3], wo_o, wo_send, wo_recv, across)
    wo_copy.start()
    stores.append(start_copy(w_s.at[3], attn_o.at[3], store.at[3]))

    def project(i, _):
        rows = pl.ds(pl.multiple_of(i * BLOCK, BLOCK), BLOCK)
        states = x_ref[rows]
        cos, sin = cos_s[rows], sin_s[rows]
        for j, (out, factor_s, scale) in enumerate(((q_s, rq_s, HD**-0.5), (k_s, rk_s, 1.0))):
            raw = dot_nn(states, w_s[j])
            for c in range(0, cols, 128):
                part = raw[:, c : c + 128]
                factor = lax.rsqrt(split_dot(part * part, ones) * (1.0 / HD) + EPS)
                unit = (part * cos + other_half(part) * sin) * factor
                out[rows, c : c + 128] = ((gain_ref[:, c : c + 128] * unit).astype(BF).astype(F32) * scale).astype(BF)
                factor_s[rows, c : c + 128] = factor.astype(BF)
        v_s[rows] = dot_nn(states, w_s[2]).astype(BF)
        return 0

    lax.fori_loop(0, blocks // 2, project, 0)
    tick(*pending.pop(0))
    lax.fori_loop(blocks // 2, blocks, project, 0)
    tick(*pending.pop(0))
    for j, (src, dst) in enumerate(((q_s, q_o), (k_s, k_o), (v_s, v_o), (rq_s, rq_o), (rk_s, rk_o))):
        stores.append(start_copy(src, dst, store.at[4 + j]))
    copies = []
    for block in range(blocks):
        first = first_key(block)
        keys = (block + 1) * BLOCK - first
        rows = pl.ds(block * BLOCK, BLOCK)
        span = pl.ds(first, keys)
        kpos = (lax.broadcasted_iota(jnp.int32, (BLOCK, keys), 1) + first).astype(F32)
        qpos = (lax.broadcasted_iota(jnp.int32, (BLOCK, keys), 0) + block * BLOCK).astype(F32)
        allowed = (kpos >= start_s[rows, 0:1]) & (kpos <= qpos)
        bias[:, :keys] = jnp.where(allowed, 0.0, NEG_FILL)

        def heads(pair_of, _):
            c = pl.ds(pl.multiple_of(pair_of * 128, 128), 128)
            q, k, v = q_s[rows, c], k_s[span, c], v_s[span, c]
            results = []
            for half in (0, 1):
                scores = dot_nt(q * half_of(BLOCK, half), k)
                probs = jnp.exp(scores + bias[:, :keys]).astype(BF)
                results.append(dot_nn(probs, v * half_of(keys, half) + half_of(keys, 1 - half)))
            lane = lax.broadcasted_iota(jnp.int32, (BLOCK, 128), 1)
            total = pltpu.roll(jnp.where(lane < HD, results[1], results[0]), HD, 1)
            y_s[rows, c] = (jnp.where(lane < HD, results[0], results[1]) / total).astype(BF)
            return 0

        lax.fori_loop(0, cols // 128, heads, 0)
        copy = remote(y_s.at[rows], y_o.at[x, rows], send.at[block], recv.at[block], across)
        copy.start()
        copies.append(copy)
        stores.append(start_copy(y_s.at[rows], y_o.at[x, rows], store.at[9 + block]))
        tick(*pending.pop(0))
    while pending:
        tick(*pending.pop(0))
    for group in (2, 3, 4):
        await_pair(group)
    for copy in owns[2:] + stores:
        copy.wait()
    for copy in sends + copies:
        copy.wait_send()
    for block in range(blocks):
        there = y_o.at[1 - x, pl.ds(block * BLOCK, BLOCK)]
        remote(there, there, send.at[block], recv.at[block], across).wait_recv()
    wo_copy.wait()


def attention_forward(attn_w, mlp_w, states, doc, gain, fsdp):
    chips = fsdp // 2
    length, width = states.shape
    cols, units, rows = attn_w.shape[2], mlp_w.shape[2], attn_w.shape[1]
    vspec, anyspec = pl.BlockSpec(memory_space=VM), pl.BlockSpec(memory_space=pl.ANY)
    blocks = length // BLOCK
    square, table = VM((length, cols), BF), VM((length, 128), F32)
    sem = pltpu.SemaphoreType.DMA
    number = len(GATHER_GROUPS)
    freq = THETA ** (-2.0 * (jnp.arange(128, dtype=F32) % (HD // 2)) / HD)
    return pl.pallas_call(
        functools.partial(forward_kernel, chips),
        out_shape=(
            low(4, width, cols), low(3, width, units), low(width, cols),
            low(length, cols), low(length, cols), low(length, cols), low(length, cols), low(length, cols),
            low(2, length, cols), jax.ShapeDtypeStruct((1, length), jnp.int32), full(length, 128), full(length, 128),
        ),
        in_specs=[vspec, vspec, anyspec, vspec, vspec, vspec],
        out_specs=(anyspec,) * 9 + (vspec,) + (anyspec,) * 2,
        scratch_shapes=[
            VM((4, rows, cols), BF), VM((3, rows, units), BF), VM((4, width, cols), BF), VM((length, width), BF),
            square, square, square, square, square, square, table, table, table, VM((BLOCK, BLOCK + SPAN), F32),
            sem, sem((9 + blocks,)), sem((blocks,)), sem((blocks,)), sem((number, 2, chips // 2)),
            sem((number, 2, chips // 2)), sem((number, chips)), sem((number, chips)), sem((number,)), sem, sem,
        ],
        compiler_params=pltpu.CompilerParams(collective_id=4, has_side_effects=True, vmem_limit_bytes=60 * MIB),
        name="attention_forward",
    )(attn_w, mlp_w, states, doc, gain, freq[None])


def row_factor(v):
    return lax.rsqrt(jnp.mean(v * v, axis=-1, keepdims=True) + EPS)


def unit_back(factor, unit, grad):
    return factor * (grad - unit * jnp.mean(grad * unit, axis=-1, keepdims=True))


def fold(v):
    return jnp.sum(v.reshape(v.shape[0] // 8, 8, v.shape[1]), axis=0)


def feed_chunks(length):
    half = BLOCK // 2
    return [(0, half)] + [(start, BLOCK) for start in range(half, length - half, BLOCK)] + [(length - half, half)]


def feed_kernel(
    chips, x_hbm, y_hbm, og_hbm, mix_ref, us_ref, wo_own, wo_peer, w_hbm,
    out_o, dri_o, do_o, dy_o, mix_o, us_o, sum_o, gd_o,
    x_ref, y_ref, wo_s, wu_s, wg_s, wd_s, o_s, hb_s, u_s, g_s, hid_s, dm_s, dh_s, own_s, got_m, got_d, hout_s, dy_s,
    wd_g, ring_s,
    load, store, save, send_m, recv_m, send_d, recv_d, pair_free, pair_send, pair_recv, pair_save, ring_send, ring_recv,
):
    index, x, place, core, right, left, pair, across = peers_of(chips)
    length, width = x_ref.shape
    cols, units = wo_own.shape[2], us_ref.shape[1]
    rows_own = width // (2 * chips)
    chunks = feed_chunks(length)
    loads = [
        start_copy(src, dst, load.at[j])
        for j, (src, dst) in enumerate(
            (
                (wo_own.at[3], wo_s.at[x]), (wo_peer, wo_s.at[1 - x]), (y_hbm, y_ref), (x_hbm, x_ref),
                (w_hbm.at[0], wu_s), (w_hbm.at[1], wg_s), (w_hbm.at[2], wd_s), (og_hbm, dm_s),
            )
        )
    ]
    greet((right, left, pair, across))
    copies_m, copies_d, stores = {}, {}, []

    def first_half(r):
        states = x_ref[r].astype(F32)
        o = o_s[r]
        ro = row_factor(o)
        uo = o * ro
        mix = mix_ref[0:1]
        r1 = states + mix * (uo - states)
        rr = row_factor(r1)
        return states, ro, uo, rr, r1 * rr

    def by_rows(chunk, body, init):
        start, size = chunks[chunk]
        for i in range(size // ROWS_STEP):
            init = body(pl.ds(start + i * ROWS_STEP, ROWS_STEP), i * ROWS_STEP, init)
        return init

    def forward(chunk):
        start, size = chunks[chunk]
        rows = pl.ds(start, size)
        if chunk == 0:
            for copy in loads[:3]:
                copy.wait()

        def out_proj(c):
            o_s[rows, c] = dot_nt(y_ref[0, rows], wo_s[0, c]) + dot_nt(y_ref[1, rows], wo_s[1, c])

        by_step(width, 512, out_proj)
        if chunk == 0:
            loads[3].wait()

        def hidden(r, i, _):
            hb_s[r] = first_half(r)[4].astype(BF)
            return 0

        by_rows(chunk, hidden, 0)
        if chunk == 0:
            loads[4].wait()
            loads[5].wait()

        def gate(f):
            up = dot_nn(hb_s[rows], wu_s[:, f])
            gt = dot_nn(hb_s[rows], wg_s[:, f])
            arg = us_ref[1:2, f] * gt * D**-0.5
            sig = 1.0 / (1.0 + jnp.exp(-arg))
            u_s[rows, f] = up.astype(BF)
            g_s[rows, f] = gt.astype(BF)
            hid_s[rows, f] = (us_ref[0:1, f] * up * (arg * sig)).astype(BF)

        by_step(units, UNIT_STEP, gate)
        if chunk == 0:
            loads[6].wait()

        def down(c):
            own_s[rows, c] = dot_nt(hid_s[rows], wd_s[c]).astype(BF)

        by_step(width, 512, down)
        copy = remote(own_s.at[rows], got_m.at[rows], send_m.at[chunk], recv_m.at[chunk], across)
        copy.start()
        copies_m[chunk] = copy

    def turn(chunk, mix_m):
        start, size = chunks[chunk]
        copies_m[chunk].wait()
        if chunk == 0:
            loads[7].wait()
        if chunk >= 2:
            stores[chunk - 2].wait()

        def middle(r, i, total):
            h1 = first_half(r)[4]
            m = own_s[r].astype(F32) + got_m[r].astype(F32)
            rm = row_factor(m)
            um = m * rm
            mix = mix_ref[1:2]
            r2 = h1 + mix * (um - h1)
            rr = row_factor(r2)
            out = r2 * rr
            hout_s[chunk % 2, pl.ds(i, ROWS_STEP)] = out.astype(BF)
            dr2 = unit_back(rr, out, dm_s[r].astype(F32))
            dm_s[r] = unit_back(rm, um, mix * dr2).astype(BF)
            dh_s[r] = dr2 * (1.0 - mix)
            return total + fold(dr2 * (um - h1))

        mix_m = by_rows(chunk, middle, mix_m)
        stores.append(start_copy(hout_s.at[chunk % 2, pl.ds(0, size)], out_o.at[pl.ds(start, size)], store.at[chunk]))
        return mix_m

    def back(chunk):
        start, size = chunks[chunk]
        rows = pl.ds(start, size)

        def gate_back(f):
            dhid = dot_nn(dm_s[rows], wd_s[:, f])
            up, gt = u_s[rows, f].astype(F32), g_s[rows, f].astype(F32)
            su, sv = us_ref[0:1, f], us_ref[1:2, f]
            arg = sv * gt * D**-0.5
            sig = 1.0 / (1.0 + jnp.exp(-arg))
            act = dhid * (arg * sig)
            darg = dhid * su * up * sig * (1.0 + arg * (1.0 - sig))
            us_o[0:1, f] = us_o[0:1, f] + jnp.sum(act * up, axis=0, keepdims=True)
            us_o[1:2, f] = us_o[1:2, f] + jnp.sum(darg * gt, axis=0, keepdims=True) * D**-0.5
            u_s[rows, f] = (act * su).astype(BF)
            g_s[rows, f] = (darg * sv * D**-0.5).astype(BF)

        by_step(units, UNIT_STEP, gate_back)

        def up_back(c):
            own_s[rows, c] = (dot_nt(u_s[rows], wu_s[c]) + dot_nt(g_s[rows], wg_s[c])).astype(BF)

        by_step(width, 512, up_back)
        copy = remote(own_s.at[rows], got_d.at[rows], send_d.at[chunk], recv_d.at[chunk], across)
        copy.start()
        copies_d[chunk] = copy

    near_s = (u_s, g_s, hid_s)
    pairs = {}

    def weight_grads(j, weight_s, left_s):
        right_s = near_s[j]

        def grads(d):
            for u in range(0, units, 1024):
                f = pl.ds(u, 1024)
                weight_s[d, f] = dot_tn(left_s[:, d], right_s[:, f]).astype(BF)

        by_step(width, BLOCK, grads)
        pl.semaphore_signal(pair_free.at[j], inc=1, device_id=pair, device_id_type=MESH)
        pl.semaphore_wait(pair_free.at[j], 1)
        for chip in range(chips):
            there = pl.multiple_of((chip * 2 + 1 - core) * rows_own, rows_own)
            copy = remote(
                weight_s.at[pl.ds(there, rows_own)], right_s.at[pl.ds(chip * rows_own, rows_own)],
                pair_send.at[j, chip], pair_recv.at[j, chip], pair,
            )
            copy.start()
            pairs[j, chip] = copy

    def pair_sums(j, weight_s):
        for chip in range(chips):
            pairs[j, chip].wait()
            base = pl.multiple_of((chip * 2 + core) * rows_own, rows_own)
            here = near_s[j].at[pl.ds(chip * rows_own, rows_own)]
            add_all(here, [here, weight_s.at[pl.ds(base, rows_own)]])

    def last(chunk, mix_a):
        start, size = chunks[chunk]
        rows = pl.ds(start, size)
        copies_d[chunk].wait()

        def body(r, i, total):
            states, ro, uo, rr, h1 = first_half(r)
            mix = mix_ref[0:1]
            dr1 = unit_back(rr, h1, dh_s[r] + (own_s[r].astype(F32) + got_d[r].astype(F32)))
            dh_s[r] = dr1 * (1.0 - mix)
            dm_s[r] = unit_back(ro, uo, mix * dr1).astype(BF)
            return total + fold(dr1 * (uo - states))

        mix_a = by_rows(chunk, body, mix_a)
        dy_s[rows] = dot_nn(dm_s[rows], wo_s[x]).astype(BF)
        for j, (src, dst) in enumerate(((dy_s, dy_o), (dm_s, do_o), (dh_s, dri_o))):
            stores.append(start_copy(src.at[rows], dst.at[rows], save.at[j, chunk]))
        return mix_a

    number = len(chunks)
    for chunk in range(number):
        forward(chunk)
    mix_m = jnp.zeros((8, width), F32)
    us_o[...] = jnp.zeros_like(us_o)
    for chunk in range(number - 2):
        mix_m = turn(chunk, mix_m)
        back(chunk)
    mix_m = turn(number - 2, mix_m)
    mix_m = turn(number - 1, mix_m)
    mix_o[1:2] = jnp.sum(mix_m, axis=0, keepdims=True)
    scatter = Scatter(
        chips, (0,), lambda group, chip: near_s[2].at[pl.ds(pl.multiple_of(chip * rows_own, rows_own), rows_own)],
        lambda group, at: ring_s.at[at], lambda group: gd_o, ring_send, ring_recv,
    )
    weight_grads(2, wd_g, dm_s)
    back(number - 2)
    pair_sums(2, wd_g)
    scatter.launch(0)
    back(number - 1)
    weight_grads(0, wu_s, hb_s)
    scatter.tick(0, 1)
    weight_grads(1, wg_s, hb_s)
    scatter.tick(0, 2)
    mix_a = jnp.zeros((8, width), F32)
    for chunk in range(number):
        mix_a = last(chunk, mix_a)
        if chunk < 2:
            pair_sums(chunk, (wu_s, wg_s)[chunk])
            stores.append(
                start_copy(
                    near_s[chunk].at[pl.ds(0, chips * rows_own)], sum_o.at[chunk], pair_save.at[chunk]
                )
            )
        if chunk >= number - 3 and chunk < number - 1:
            scatter.tick(0, chunk - (number - 3) + 3)
    mix_o[0:1] = jnp.sum(mix_a, axis=0, keepdims=True)
    for copy in stores[number - 2 :]:
        copy.wait()
    scatter.close()


def feed_forward(states, y, out_grad, mix, scales, attn_full, wo_peer, mlp_full, fsdp):
    chips = fsdp // 2
    length, width = states.shape
    cols, units = y.shape[2], scales.shape[1]
    rows = width // fsdp
    vspec, anyspec = pl.BlockSpec(memory_space=VM), pl.BlockSpec(memory_space=pl.ANY)
    number = len(feed_chunks(length))
    sem = pltpu.SemaphoreType.DMA
    square, wide, weight = VM((length, width), BF), VM((length, units), BF), VM((width, units), BF)
    return pl.pallas_call(
        functools.partial(feed_kernel, chips),
        out_shape=(
            low(length, width), full(length, width), low(length, width), low(length, cols),
            full(2, width), full(2, units), low(2, chips * rows, units), full(rows, units),
        ),
        in_specs=[anyspec] * 3 + [vspec] * 2 + [anyspec] * 3,
        out_specs=(anyspec, anyspec, anyspec, anyspec, vspec, vspec, anyspec, vspec),
        scratch_shapes=[
            square, VM((2, length, cols), BF), VM((2, width, cols), BF), weight, weight, weight,
            VM((length, width), F32), square, wide, wide, wide, square, VM((length, width), F32),
            square, square, square, VM((2, BLOCK, width), BF), VM((length, cols), BF),
            weight, VM((chips - 1, rows, units), BF),
            sem((8,)), sem((number,)), sem((3, number)), sem((number,)), sem((number,)), sem((number,)), sem((number,)),
            pltpu.SemaphoreType.REGULAR((3,)), sem((3, chips)), sem((3, chips)), sem((2,)),
            sem((1, chips - 1)), sem((1, chips - 1)),
        ],
        compiler_params=pltpu.CompilerParams(collective_id=6, has_side_effects=True, vmem_limit_bytes=63 * MIB),
        name="feed_forward",
    )(states, y, out_grad, mix, scales, attn_full, wo_peer, mlp_full)


SCATTER_LONG = (0, 2)


def stepped(param, moment, grad, rate):
    moment_new = MOMENTUM * moment + grad
    return moment_new, param - rate * (grad + MOMENTUM * moment_new)


def backward_kernel(
    rate, x_hbm, w_hbm, q_hbm, k_hbm, v_hbm, rq_hbm, rk_hbm, y_hbm, dy_hbm, do_hbm, dri_hbm, sums_hbm, cos_hbm, sin_hbm,
    wa_hbm, ma_hbm, wm_hbm, mm_hbm, gain_ref, start_ref, gd_ref, mix_ref, us_ref,
    ig_o, ga_o, gm_o, sum_a_o, sum_m_o,
    x_ref, w_ref, q_ref, k_ref, v_ref, rq_ref, rk_ref, y_ref, dy_ref, do_ref, sums, cos_ref, sin_ref, dri_s,
    wa_ref, ma_ref, wm_ref, mm_ref,
    bias, dq_s, dk_s, dv_s, low_s, out_s, in_s, dw_s, near, ring_a, ring_m, head_s, mine_a, got_a, mine_m, got_m,
    load, load_dri, store, send, recv, pair_send, pair_recv, ring_send, ring_recv, all_send, all_recv,
):
    chips, rows_own = sums.shape[1:3]
    index, x, place, core, right, left, pair, across = peers_of(chips)
    length, cols = q_ref.shape
    width, units = x_ref.shape[1], sums.shape[3]
    blocks = length // BLOCK
    stages = got_a.shape[0]
    turns = [(index + (1 << s) * (1 - 2 * ((index // (1 << s)) % 2)), x) for s in range(stages)]
    pieces = (
        (sums_hbm, sums), (q_hbm, q_ref), (k_hbm, k_ref), (v_hbm, v_ref), (dy_hbm, dy_ref), (y_hbm.at[x], y_ref),
        (cos_hbm, cos_ref), (sin_hbm, sin_ref), (rq_hbm, rq_ref), (rk_hbm, rk_ref), (w_hbm.at[pl.ds(0, 3)], w_ref),
        (do_hbm, do_ref), (x_hbm, x_ref), (wm_hbm, wm_ref), (mm_hbm, mm_ref), (wa_hbm, wa_ref), (ma_hbm, ma_ref),
    )
    loads = [start_copy(src, dst, load.at[j]) for j, (src, dst) in enumerate(pieces)]
    greet([right, left, pair, across] + turns)

    def mine(group, chip):
        if group < 2:
            return sums.at[group, chip]
        return near.at[3, chip] if group == 2 else near.at[pl.ds(0, 3), chip]

    def slot(group, at):
        if group < 2:
            return ring_m.at[group, at]
        return ring_a.at[at, 3] if group == 2 else ring_a.at[at, pl.ds(0, 3)]

    def result(group):
        return gm_o.at[group] if group < 2 else ga_o.at[3] if group == 2 else ga_o.at[pl.ds(0, 3)]

    scatter = Scatter(chips, SCATTER_LONG, mine, slot, result, ring_send, ring_recv)
    tick, launch = scatter.tick, scatter.launch

    def send_pair(matrices, at):
        copies = []
        for chip in range(chips):
            there = pl.multiple_of((chip * 2 + 1 - core) * rows_own, rows_own)
            copy = remote(
                dw_s.at[matrices, pl.ds(there, rows_own)], near.at[matrices, chip],
                pair_send.at[at, chip], pair_recv.at[at, chip], pair,
            )
            copy.start()
            copies.append(copy)
        return copies

    def sum_pair(copies, matrices):
        for chip, copy in enumerate(copies):
            copy.wait()
            own = pl.ds(pl.multiple_of((chip * 2 + core) * rows_own, rows_own), rows_own)
            here = near.at[matrices, chip]
            add_all(here, [here, dw_s.at[matrices, own]])

    loads[0].wait()
    launch(0)
    launch(1)
    dk_s[...] = jnp.zeros_like(dk_s)
    dv_s[...] = jnp.zeros_like(dv_s)
    head_s[...] = jnp.zeros_like(head_s)
    ones = head_ones()
    copies, stores = {}, []

    def fetch_dri(block):
        return start_copy(dri_hbm.at[pl.ds(block * BLOCK, BLOCK)], dri_s.at[block % 2], load_dri.at[block])

    fetched = {block: fetch_dri(block) for block in (blocks - 1, blocks - 2)}

    def finish_input(block):
        copies[block].wait()
        fetched[block].wait()
        for i in range(0, BLOCK, 128):
            r = pl.ds(block * BLOCK + i, 128)
            total = out_s[r].astype(F32) + in_s[r].astype(F32)
            out_s[r] = (dri_s[block % 2, pl.ds(i, 128)] + total).astype(BF)
        rows = pl.ds(block * BLOCK, BLOCK)
        stores.append(start_copy(out_s.at[rows], ig_o.at[rows], store.at[block]))
        if block >= 2:
            fetched[block - 2] = fetch_dri(block - 2)

    for copy in loads[1:6]:
        copy.wait()

    def attend(block):
        first = first_key(block)
        keys = (block + 1) * BLOCK - first
        rows = pl.ds(block * BLOCK, BLOCK)
        span = pl.ds(first, keys)
        kpos = lax.broadcasted_iota(jnp.int32, (keys, BLOCK), 0) + first
        qpos = lax.broadcasted_iota(jnp.int32, (keys, BLOCK), 1) + block * BLOCK
        allowed = (kpos >= start_ref[:, block * BLOCK : (block + 1) * BLOCK]) & (kpos <= qpos)
        bias[:keys] = jnp.where(allowed, 0.0, NEG_FILL)

        def heads(pair_of, _):
            c = pl.ds(pl.multiple_of(pair_of * 128, 128), 128)
            q, k, v, dy = q_ref[rows, c], k_ref[span, c], v_ref[span, c], dy_ref[rows, c]
            prod = dy.astype(F32) * y_ref[rows, c].astype(F32)
            prod_high = prod.astype(BF)
            prod_low = (prod - prod_high.astype(F32)).astype(BF)
            dq = jnp.zeros((BLOCK, 128), F32)
            dk = jnp.zeros((keys, 128), F32)
            dv = jnp.zeros((keys, 128), F32)
            for half in (0, 1):
                mask, row = half_of(BLOCK, half), half_of(8, half)
                qm, dym, km = q * mask, dy * mask, k * half_of(keys, half)
                expo = jnp.exp(dot_nt(k, qm) + bias[:keys])
                probs = expo * (1.0 / jnp.sum(expo, axis=0, keepdims=True))
                delta = (dot_nt(row, prod_high) + dot_nt(row, prod_low))[0:1]
                dz = (probs * (dot_nt(v, dym) - delta)).astype(BF)
                dk = dk + dot_nn(dz, qm)
                dv = dv + dot_nn(probs.astype(BF), dym)
                dq = dq + dot_tn(dz, km)
            dq_s[rows, c] = dq * HD**-0.5
            dk_s[span, c] = dk_s[span, c] + dk
            dv_s[span, c] = dv_s[span, c] + dv
            return 0

        return heads

    def project_back(block):
        rows = pl.ds(block * BLOCK, BLOCK)
        cos, sin = cos_ref[rows], sin_ref[rows]
        for c in range(0, cols, 128):
            s = slice(c, c + 128)
            gain = gain_ref[:, s]
            head = jnp.zeros((BLOCK, 128), F32)
            for j, (grad_s, low_ref, factor_ref, scale) in enumerate(
                ((dq_s, q_ref, rq_ref, HD**0.5), (dk_s, k_ref, rk_ref, 1.0))
            ):
                grad = grad_s[rows, s]
                unit = low_ref[rows, s].astype(F32) * (scale / gain)
                head = head + grad * unit
                grad = grad * gain
                turned = factor_ref[rows, s].astype(F32) * (grad - unit * (split_dot(grad * unit, ones) * (1.0 / HD)))
                low_s[j, rows, s] = (turned * cos - other_half(turned) * sin).astype(BF)
            head_s[:, s] = head_s[:, s] + jnp.sum(head, axis=0, keepdims=True)
            low_s[2, rows, s] = dv_s[rows, s].astype(BF)
        for c in range(0, width, 512):
            part = sum(dot_nt(low_s[j, rows], w_ref[j, c : c + 512]) for j in range(3))
            out_s[rows, c : c + 512] = part.astype(BF)
        copy = remote(out_s.at[rows], in_s.at[rows], send.at[block], recv.at[block], across)
        copy.start()
        copies[block] = copy

    longest = chips // 2
    pending = [(group, hop) for hop in range(1, longest + 1) for group in (0, 1)]
    step_pairs = cols // 256
    for block in reversed(range(blocks)):
        heads = attend(block)
        lax.fori_loop(0, step_pairs, heads, 0)
        if block < blocks - 1:
            tick(*pending.pop(0))
        lax.fori_loop(step_pairs, 2 * step_pairs, heads, 0)
        if block == blocks - 1:
            for copy in loads[6:11]:
                copy.wait()
            tick(*pending.pop(0))
        project_back(block)
        if block == blocks - 1:
            for copy in loads[11:13]:
                copy.wait()
            by_step(width, BLOCK, lambda d: out_grad(d, dw_s, do_ref, y_ref))
            pair_out = send_pair(3, 0)
        if block == blocks - 2:
            tick(*pending.pop(0))
            sum_pair(pair_out, 3)
            launch(2)
    finish_input(blocks - 1)
    tick(2, 1)
    tick(*pending.pop(0))

    def in_grads(d):
        for j in range(3):
            dw_s[j, d] = dot_tn(x_ref[:, d], low_s[j]).astype(BF)

    by_step(width, BLOCK, in_grads)
    pair_in = send_pair(pl.ds(0, 3), 1)
    tick(2, 2)
    tick(*pending.pop(0))
    sum_pair(pair_in, pl.ds(0, 3))
    launch(3)
    tick(2, 3)
    while pending:
        tick(*pending.pop(0))
    tick(2, 4)

    def squares(g, w, m):
        count = g.shape[-1]

        def body(i, total):
            r = pl.ds(pl.multiple_of(i * 8, 8), 8)
            step = stepped(w[r], m[r], g[r], rate)[1]
            return total + step * step

        total = lax.fori_loop(0, rows_own // 8, body, jnp.zeros((8, count), F32))
        return jnp.sum(total, axis=0, keepdims=True)

    def exchange(own, got, kind, s):
        copy = remote(own.at[s], got.at[s], all_send.at[kind, s], all_recv.at[kind, s], turns[s])
        copy.start()
        return copy

    for copy in loads[13:]:
        copy.wait()
    lanes = mine_m.shape[2]
    mine_m[0] = jnp.zeros(mine_m.shape[1:], F32)
    row = 0

    def place_row(value):
        nonlocal row
        for c in range(0, value.shape[1], lanes):
            size = min(lanes, value.shape[1])
            mine_m[0, row : row + 1, 0:size] = value[:, c : c + size]
            row += 1

    for j in range(3):
        place_row(squares(gd_ref if j == 2 else gm_o.at[j], wm_ref.at[j], mm_ref.at[j]))
    place_row(head_s[...])
    for ref in (mix_ref, us_ref):
        for j in range(2):
            place_row(ref[j : j + 1])
    for s in range(stages):
        copy = exchange(mine_m, got_m, 0, s)
        if s < longest:
            tick(3, s + 1)
        if s == 0:
            finish_input(blocks - 2)
        copy.wait()
        mine_m[s + 1] = mine_m[s] + got_m[s]
    sum_m_o[...] = mine_m[stages]
    for hop in range(stages + 1, longest + 1):
        tick(3, hop)
    for j in range(4):
        mine_a[0, j : j + 1] = squares(ga_o.at[j], wa_ref.at[j], ma_ref.at[j])
    for s in range(stages):
        copy = exchange(mine_a, got_a, 1, s)
        if s == 0:
            for block in reversed(range(blocks - 2)):
                finish_input(block)
        copy.wait()
        mine_a[s + 1] = mine_a[s] + got_a[s]
    sum_a_o[...] = mine_a[stages]
    for copy in stores:
        copy.wait()
    scatter.close()


def out_grad(d, dw_s, do_ref, y_ref):
    dw_s[3, d] = dot_tn(do_ref[:, d], y_ref[...]).astype(BF)


def attention_backward(
    states, weights, q, k, v, rq, rk, y, dy, do, dri, sums, cos, sin, attn_w, attn_mom, mlp_w, mlp_mom,
    gain, start, grad_down, grad_mix, grad_units, rate, fsdp,
):
    length, width = states.shape
    cols = gain.shape[1]
    chips = fsdp // 2
    rows, units = sums.shape[2:]
    stages = fsdp.bit_length() - 1
    vspec, anyspec = pl.BlockSpec(memory_space=VM), pl.BlockSpec(memory_space=pl.ANY)
    blocks = length // BLOCK
    sem = pltpu.SemaphoreType.DMA
    square, table, full_square = VM((length, cols), BF), VM((length, 128), F32), VM((length, cols), F32)
    wide = VM((length, width), BF)
    a_rows, m_rows = 4, -(-(3 * (units // width) + 3 + 2 * (units // width)) // 8) * 8
    return pl.pallas_call(
        functools.partial(backward_kernel, rate),
        out_shape=(
            low(length, width), full(4, rows, cols), full(2, rows, units), full(a_rows, cols), full(m_rows, width),
        ),
        in_specs=[anyspec] * 18 + [vspec] * 5,
        out_specs=(anyspec, vspec, vspec, vspec, vspec),
        scratch_shapes=[
            wide, VM((3, width, cols), BF), square, square, square, square, square, square, square,
            wide, VM(sums.shape, BF), table, table, VM((2, BLOCK, width), F32),
            VM(attn_w.shape, F32), VM(attn_w.shape, F32), VM(mlp_w.shape, F32), VM(mlp_w.shape, F32),
            VM((BLOCK + SPAN, BLOCK), F32), full_square, full_square, full_square,
            VM((3, length, cols), BF), wide, wide, VM((4, width, cols), BF), VM((4, chips, rows, cols), BF),
            VM((chips - 1, 4, rows, cols), BF), VM((2, chips - 1, rows, units), BF), VM((1, cols), F32),
            VM((stages + 1, a_rows, cols), F32), VM((stages, a_rows, cols), F32),
            VM((stages + 1, m_rows, width), F32), VM((stages, m_rows, width), F32),
            sem((17,)), sem((blocks,)), sem((blocks,)), sem((blocks,)), sem((blocks,)),
            sem((2, chips)), sem((2, chips)), sem((4, chips - 1)), sem((4, chips - 1)), sem((2, stages)), sem((2, stages)),
        ],
        compiler_params=pltpu.CompilerParams(collective_id=5, has_side_effects=True, vmem_limit_bytes=63 * MIB),
        name="attention_backward",
    )(
        states, weights, q, k, v, rq, rk, y, dy, do, dri, sums, cos, sin, attn_w, attn_mom, mlp_w, mlp_mom,
        gain, start, grad_down, grad_mix, grad_units,
    )


def update_kernel(
    rates, width, ig, hid, ga, gm, gd, sa, sm, wa, ma, aa, wm, mm, am, hs, hm, mr, mo, us, um,
    hid_o, ig_o, ma_o, wa_o, aa_o, mm_o, wm_o, am_o, hm_o, hs_o, mo_o, mr_o, um_o, us_o,
):
    hid_o[0] = hid[...].astype(F32)
    ig_o[0] = ig[...].astype(F32)
    lanes = sm.shape[1]
    cols, units = wa.shape[2], wm.shape[2]

    def matrix(j, grad, total, refs, outs):
        w, m, a = (ref[j] for ref in refs)
        moment, step = stepped(w, m, grad, rates[0])
        new = step * lax.rsqrt(total / width + EPS)
        outs[0][j] = moment
        outs[1][j] = new
        outs[2][j] = AVERAGE * a + (1.0 - AVERAGE) * new

    def wide(row):
        return jnp.concatenate([sm[row + c : row + c + 1] for c in range(units // lanes)], axis=1)

    for j in range(4):
        matrix(j, ga[j], sa[j : j + 1], (wa, ma, aa), (ma_o, wa_o, aa_o))
    for j in range(3):
        matrix(j, gd[...] if j == 2 else gm[j], wide(j * (units // lanes)), (wm, mm, am), (mm_o, wm_o, am_o))

    @pl.when(pl.program_id(0) == 0)
    def _():
        row = 3 * (units // lanes)
        hm_o[...], hs_o[...] = stepped(hs[...], hm[...], sm[row : row + 1, :cols], rates[1])
        mo_o[...], mr_o[...] = stepped(mr[...], mo[...], sm[row + 1 : row + 3], rates[2])
        row += 3
        grad = jnp.concatenate([wide(row), wide(row + units // lanes)], axis=0)
        um_o[...], us_o[...] = stepped(us[...], um[...], grad, rates[3])


def update(input_low, hidden_low, ga, gm, gd, sa, sm, wa, ma, aa, wm, mm, am, hs, hm, mr, mo, us, um, rates):
    length, width = input_low.shape
    rows, cols, units = wa.shape[1], wa.shape[2], wm.shape[2]
    steps = rows // 8
    tall = length // steps

    def whole(shape):
        return pl.BlockSpec(shape, lambda i: (0,) * len(shape))

    state = pl.BlockSpec((tall, width), lambda i: (i, 0))
    state_o = pl.BlockSpec((1, tall, width), lambda i: (0, i, 0))
    attn = pl.BlockSpec((4, 8, cols), lambda i: (0, i, 0))
    mlp = pl.BlockSpec((3, 8, units), lambda i: (0, i, 0))
    small = [whole((1, cols))] * 2 + [whole(mr.shape)] * 2 + [whole(us.shape)] * 2
    return pl.pallas_call(
        functools.partial(update_kernel, rates, width),
        grid=(steps,),
        out_shape=(
            full(1, length, width), full(1, length, width), *(full(*wa.shape),) * 3, *(full(*wm.shape),) * 3,
            *(full(1, cols),) * 2, *(full(*mr.shape),) * 2, *(full(*us.shape),) * 2,
        ),
        in_specs=[
            state, state, attn, pl.BlockSpec((2, 8, units), lambda i: (0, i, 0)), pl.BlockSpec((8, units), lambda i: (i, 0)),
            whole(sa.shape), whole(sm.shape), attn, attn, attn, mlp, mlp, mlp, *small,
        ],
        out_specs=(state_o, state_o, attn, attn, attn, mlp, mlp, mlp, *small),
        compiler_params=pltpu.CompilerParams(vmem_limit_bytes=60 * MIB),
        name="update_weights",
    )(input_low, hidden_low, ga, gm, gd, sa, sm, wa, ma, aa, wm, mm, am, hs, hm, mr, mo, us, um)


def local_fast(
    inputs, doc_ids, out_grad, attn_w, attn_mom, attn_avg, mlp_w, mlp_mom, mlp_avg,
    head_scale, head_mom, mix_rates, mix_mom, unit_scales, unit_mom,
):
    fsdp = lax.axis_size("fsdp")
    root_tokens = math.sqrt(inputs.shape[0] * fsdp * inputs.shape[1])
    rates = tuple(rate / root_tokens for rate in (RATE_WEIGHT, RATE_HEAD, RATE_MIX, RATE_UNITS))
    states, gain = inputs[0], head_scale[None]
    attn_full, mlp_full, wo_peer, q, k, v, rq, rk, y, start, cos, sin = attention_forward(
        attn_w, mlp_w, states, doc_ids, gain, fsdp
    )
    hidden_low, dri, do, dy, grad_mix, grad_units, sums, grad_down = feed_forward(
        states, y, out_grad[0], mix_rates, unit_scales, attn_full, wo_peer, mlp_full, fsdp
    )
    rows, units = mlp_w.shape[1:]
    sums = sums.reshape(2, fsdp // 2, rows, units)
    input_low, grad_attn, grad_mlp, total_attn, total_rest = attention_backward(
        states, attn_full, q, k, v, rq, rk, y, dy, do, dri, sums, cos, sin, attn_w, attn_mom, mlp_w, mlp_mom,
        gain, start, grad_down, grad_mix, grad_units, rates[0], fsdp,
    )
    outs = update(
        input_low, hidden_low, grad_attn, grad_mlp, grad_down, total_attn, total_rest,
        attn_w, attn_mom, attn_avg, mlp_w, mlp_mom, mlp_avg,
        gain, head_mom[None], mix_rates, mix_mom, unit_scales, unit_mom, rates,
    )
    return (*outs[:8], outs[8][0], outs[9][0], *outs[10:])


def local(
    inputs,
    doc_ids,
    out_grad,
    attn_w,
    attn_mom,
    attn_avg,
    mlp_w,
    mlp_mom,
    mlp_avg,
    head_scale,
    head_mom,
    mix_rates,
    mix_mom,
    unit_scales,
    unit_mom,
):
    length = inputs.shape[1]
    model_width = inputs.shape[2]
    head_count = head_scale.shape[0] // HD
    block_rows = min(512, length)
    block_count = length // block_rows
    tokens = inputs.shape[0] * lax.axis_size("fsdp") * length
    doc_row = doc_ids[0]
    input_low = inputs[0]
    resid_in = input_low.astype(jnp.float32)
    cos_table, sin_table = rotary_tables(doc_row)
    position = jnp.arange(length, dtype=jnp.int32)
    attn_full = lax.all_gather(attn_w.astype(jnp.bfloat16), "fsdp", axis=1, tiled=True)
    projected = jnp.einsum(
        "sd,jdc->jsc", input_low, attn_full[:3], preferred_element_type=jnp.float32
    )
    head_gain = head_scale.reshape(head_count, HD)
    q_rot = rotate(projected[0].reshape(length, head_count, HD), cos_table, sin_table)
    k_rot = rotate(projected[1].reshape(length, head_count, HD), cos_table, sin_table)
    q_unit = rms_unit(q_rot)
    k_unit = rms_unit(k_rot)
    query_low = (head_gain * q_unit).astype(jnp.bfloat16)
    key_low = (head_gain * k_unit).astype(jnp.bfloat16)
    value_low = projected[2].reshape(length, head_count, HD).astype(jnp.bfloat16)

    def scores_of(row_first):
        query_blk = lax.dynamic_slice_in_dim(query_low, row_first, block_rows, 0)
        raw_scores = jnp.einsum(
            "qhe,khe->hqk", query_blk, key_low, preferred_element_type=jnp.float32
        )
        row_pos = lax.dynamic_slice_in_dim(position, row_first, block_rows, 0)
        row_docs = lax.dynamic_slice_in_dim(doc_row, row_first, block_rows, 0)
        allowed = (row_docs[:, None] == doc_row[None, :]) & (position[None, :] <= row_pos[:, None])
        return (jnp.where(allowed[None], raw_scores * HD ** (-0.5), NEG_FILL), query_blk)

    def attend(accums, blk_index):
        scores, query_blk = scores_of(blk_index * block_rows)
        peak_val = jnp.max(scores, axis=-1, keepdims=True)
        expo_vals = jnp.exp(scores - peak_val)
        row_total = jnp.sum(expo_vals, axis=-1, keepdims=True)
        probs_low = (expo_vals / row_total).astype(jnp.bfloat16)
        blk_out = jnp.einsum(
            "hqk,khe->qhe", probs_low, value_low, preferred_element_type=jnp.float32
        )
        return (accums, (blk_out, (peak_val + jnp.log(row_total))[..., 0]))

    _, (mixed_blocks, log_totals) = lax.scan(attend, None, jnp.arange(block_count))
    mixed_low = mixed_blocks.reshape(length, head_count * HD).astype(jnp.bfloat16)
    attn_part = jnp.einsum("sc,dc->sd", mixed_low, attn_full[3], preferred_element_type=jnp.float32)
    attn_out = lax.psum(attn_part, "mp")
    attn_unit = rms_unit(attn_out)
    resid_one = resid_in + mix_rates[0] * (attn_unit - resid_in)
    hidden_one = rms_unit(resid_one)
    hidden_low = hidden_one.astype(jnp.bfloat16)
    mlp_full = lax.all_gather(mlp_w.astype(jnp.bfloat16), "fsdp", axis=1, tiled=True)
    gates = jnp.einsum("sd,jdf->jsf", hidden_low, mlp_full[:2], preferred_element_type=jnp.float32)
    up_proj = gates[0]
    gate_proj = gates[1]
    gate_arg = unit_scales[1] * gate_proj * D ** (-0.5)
    gate_sig = jax.nn.sigmoid(gate_arg)
    gate_act = gate_arg * gate_sig
    units_low = (unit_scales[0] * up_proj * gate_act).astype(jnp.bfloat16)
    mlp_part = jnp.einsum("sf,df->sd", units_low, mlp_full[2], preferred_element_type=jnp.float32)
    mlp_out = lax.psum(mlp_part, "mp")
    mlp_unit = rms_unit(mlp_out)
    resid_two = hidden_one + mix_rates[1] * (mlp_unit - hidden_one)
    result = rms_unit(resid_two)
    cotangent = out_grad[0].astype(jnp.float32)
    d_resid_two = rms_back(resid_two, cotangent)
    grad_mix_mlp = jnp.sum(d_resid_two * (mlp_unit - hidden_one), axis=0)
    d_hidden_one = d_resid_two * (1.0 - mix_rates[1])
    d_mlp_low = rms_back(mlp_out, mix_rates[1] * d_resid_two).astype(jnp.bfloat16)
    mlp_back = lax.all_gather(mlp_w.astype(jnp.bfloat16), "fsdp", axis=1, tiled=True)
    d_units = jnp.einsum("sd,df->sf", d_mlp_low, mlp_back[2], preferred_element_type=jnp.float32)
    d_up = d_units * unit_scales[0] * gate_act
    d_arg = d_units * unit_scales[0] * up_proj * gate_sig * (1.0 + gate_arg * (1.0 - gate_sig))
    d_gate = d_arg * unit_scales[1] * D ** (-0.5)
    grad_units = jnp.stack(
        [
            jnp.sum(d_units * up_proj * gate_act, axis=0),
            jnp.sum(d_arg * gate_proj * D ** (-0.5), axis=0),
        ]
    )
    d_gates_low = jnp.stack([d_up, d_gate]).astype(jnp.bfloat16)
    mlp_back_part = jnp.einsum(
        "jsf,jdf->sd", d_gates_low, mlp_back[:2], preferred_element_type=jnp.float32
    )
    d_hidden_one = d_hidden_one + lax.psum(mlp_back_part, "mp")
    right_cols = d_mlp_low
    left_cols = hidden_low
    grad_mlp = jnp.transpose(
        lax.psum_scatter(
            jnp.concatenate(
                [
                    jnp.einsum(
                        "sd,jsf->djf", left_cols, d_gates_low, preferred_element_type=jnp.float32
                    ),
                    jnp.einsum(
                        "sd,sf->df", right_cols, units_low, preferred_element_type=jnp.float32
                    )[:, None, :],
                ],
                axis=1,
            ),
            "fsdp",
            scatter_dimension=0,
            tiled=True,
        ),
        (1, 0, 2),
    )
    d_resid_one = rms_back(resid_one, d_hidden_one)
    grad_mix_attn = jnp.sum(d_resid_one * (attn_unit - resid_in), axis=0)
    d_resid_in = d_resid_one * (1.0 - mix_rates[0])
    d_attn_low = rms_back(attn_out, mix_rates[0] * d_resid_one).astype(jnp.bfloat16)
    attn_back = lax.all_gather(attn_w.astype(jnp.bfloat16), "fsdp", axis=1, tiled=True)
    d_mixed = jnp.einsum("sd,dc->sc", d_attn_low, attn_back[3], preferred_element_type=jnp.float32)
    d_mixed = d_mixed.astype(jnp.bfloat16).reshape(length, head_count, HD)

    def attend_back(accums, blk_index):
        d_key, d_value = accums
        row_first = blk_index * block_rows
        scores, query_blk = scores_of(row_first)
        blk_total = lax.dynamic_index_in_dim(log_totals, blk_index, 0, keepdims=False)
        attn_probs = jnp.exp(scores - blk_total[..., None])
        d_out_blk = lax.dynamic_slice_in_dim(d_mixed, row_first, block_rows, 0)
        d_probs = jnp.einsum(
            "qhe,khe->hqk", d_out_blk, value_low, preferred_element_type=jnp.float32
        )
        d_scores = attn_probs * (d_probs - jnp.sum(attn_probs * d_probs, axis=-1, keepdims=True))
        d_raw_low = (d_scores * HD ** (-0.5)).astype(jnp.bfloat16)
        d_query = jnp.einsum("hqk,khe->qhe", d_raw_low, key_low, preferred_element_type=jnp.float32)
        d_key = d_key + jnp.einsum(
            "hqk,qhe->khe", d_raw_low, query_blk, preferred_element_type=jnp.float32
        )
        d_value = d_value + jnp.einsum(
            "hqk,qhe->khe",
            attn_probs.astype(jnp.bfloat16),
            d_out_blk,
            preferred_element_type=jnp.float32,
        )
        return ((d_key, d_value), d_query)

    zero_heads = jnp.zeros((length, head_count, HD), jnp.float32)
    (d_key_all, d_value_all), d_query_blocks = lax.scan(
        attend_back, (zero_heads, zero_heads), jnp.arange(block_count)
    )
    d_query_all = d_query_blocks.reshape(length, head_count, HD)
    grad_head = jnp.sum(d_query_all * q_unit + d_key_all * k_unit, axis=0).reshape(-1)
    d_query_raw = rotate_back(rms_back(q_rot, head_gain * d_query_all), cos_table, sin_table)
    d_key_raw = rotate_back(rms_back(k_rot, head_gain * d_key_all), cos_table, sin_table)
    d_proj_low = jnp.stack(
        [
            d_query_raw.reshape(length, -1),
            d_key_raw.reshape(length, -1),
            d_value_all.reshape(length, -1),
        ]
    ).astype(jnp.bfloat16)
    grad_mix = jnp.stack([grad_mix_attn, grad_mix_mlp])
    grad_head, grad_mix, grad_units = lax.psum((grad_head, grad_mix, grad_units), "fsdp")
    attn_back_part = jnp.einsum(
        "jsc,jdc->sd", d_proj_low, attn_back[:3], preferred_element_type=jnp.float32
    )
    input_grad = d_resid_in + lax.psum(attn_back_part.astype(jnp.bfloat16), "mp").astype(
        jnp.float32
    )
    left_cols = input_low
    right_cols = d_attn_low
    in_terms = jnp.einsum("sd,jsc->djc", left_cols, d_proj_low, preferred_element_type=jnp.float32)
    out_terms = jnp.einsum("sd,sc->dc", right_cols, mixed_low, preferred_element_type=jnp.float32)
    grad_attn = jnp.transpose(
        lax.psum_scatter(
            jnp.concatenate([in_terms, out_terms[:, None, :]], axis=1),
            "fsdp",
            scatter_dimension=0,
            tiled=True,
        ),
        (1, 0, 2),
    )
    root_tokens = math.sqrt(tokens)
    weight_rate = RATE_WEIGHT / root_tokens
    attn_mom_new, attn_step = nesterov(attn_w, attn_mom, grad_attn, weight_rate)
    mlp_mom_new, mlp_step = nesterov(mlp_w, mlp_mom, grad_mlp, weight_rate)
    attn_squares = jnp.sum(attn_step * attn_step, axis=1)
    mlp_squares = jnp.sum(mlp_step * mlp_step, axis=1)
    attn_squares, mlp_squares = lax.psum((attn_squares, mlp_squares), "fsdp")
    attn_new = attn_step * lax.rsqrt(attn_squares[:, None, :] / model_width + EPS)
    mlp_new = mlp_step * lax.rsqrt(mlp_squares[:, None, :] / model_width + EPS)
    head_mom_new, head_new = nesterov(head_scale, head_mom, grad_head, RATE_HEAD / root_tokens)
    mix_mom_new, mix_new = nesterov(mix_rates, mix_mom, grad_mix, RATE_MIX / root_tokens)
    units_mom_new, units_new = nesterov(unit_scales, unit_mom, grad_units, RATE_UNITS / root_tokens)
    return (
        result[None],
        input_grad[None],
        attn_mom_new,
        attn_new,
        AVERAGE * attn_avg + (1.0 - AVERAGE) * attn_new,
        mlp_mom_new,
        mlp_new,
        AVERAGE * mlp_avg + (1.0 - AVERAGE) * mlp_new,
        head_mom_new,
        head_new,
        mix_mom_new,
        mix_new,
        units_mom_new,
        units_new,
    )


def solution(mesh):
    fsdp = mesh.shape["fsdp"]
    fast = fsdp == 16 and D // fsdp % 16 == 0
    placed = (
        P("fsdp", None, None),
        P("fsdp", None),
        P("fsdp", None, None),
        P(None, "fsdp", "mp"),
        P(None, "fsdp", "mp"),
        P(None, "fsdp", "mp"),
        P(None, "fsdp", "mp"),
        P(None, "fsdp", "mp"),
        P(None, "fsdp", "mp"),
        P("mp"),
        P("mp"),
        P(),
        P(),
        P(None, "mp"),
        P(None, "mp"),
    )
    return jax.shard_map(
        local_fast if fast else local,
        mesh=mesh,
        in_specs=placed,
        out_specs=(
            P("fsdp", None, None),
            P("fsdp", None, None),
            P(None, "fsdp", "mp"),
            P(None, "fsdp", "mp"),
            P(None, "fsdp", "mp"),
            P(None, "fsdp", "mp"),
            P(None, "fsdp", "mp"),
            P(None, "fsdp", "mp"),
            P("mp"),
            P("mp"),
            P(),
            P(),
            P(None, "mp"),
            P(None, "mp"),
        ),
        check_vma=False,
    )
```

```python
import functools
import math

import jax
import jax.numpy as jnp
from jax import lax
from jax.experimental import pallas as pl
from jax.experimental.pallas import tpu as pltpu
from jax.sharding import PartitionSpec as P

D = 1024
HD = 64


EPS = 1e-06
MOMENTUM = 0.9
AVERAGE = 0.9
NEG_FILL = -1e30
THETA = 10000.0
RATE_WEIGHT = 50.0
RATE_HEAD = 0.08
RATE_MIX = 0.02
RATE_UNITS = 0.5


def rms_unit(vector):
    return vector * lax.rsqrt(jnp.mean(vector * vector, axis=-1, keepdims=True) + EPS)


def rms_back(vector, grad):
    factor = lax.rsqrt(jnp.mean(vector * vector, axis=-1, keepdims=True) + EPS)
    unit_vec = vector * factor
    return factor * (grad - unit_vec * jnp.mean(grad * unit_vec, axis=-1, keepdims=True))


def rotary_tables(doc_row):
    length = doc_row.shape[0]
    position = jnp.arange(length, dtype=jnp.int32)
    boundary = jnp.concatenate(
        [jnp.ones((1,), jnp.int32), (doc_row[1:] != doc_row[:-1]).astype(jnp.int32)]
    )
    doc_start = lax.cummax(jnp.where(boundary > 0, position, 0), axis=0)
    offset = (position - doc_start).astype(jnp.float32)
    freq = THETA ** (-2.0 * jnp.arange(HD // 2, dtype=jnp.float32) / HD)
    angle = offset[:, None] * freq[None, :]
    return (jnp.cos(angle), jnp.sin(angle))


def rotate(vector, cos_table, sin_table):
    half_dim = vector.shape[-1] // 2
    lower_half = vector[..., :half_dim]
    upper_half = vector[..., half_dim:]
    cos_part = cos_table[:, None, :]
    sin_part = sin_table[:, None, :]
    return jnp.concatenate(
        [
            lower_half * cos_part - upper_half * sin_part,
            lower_half * sin_part + upper_half * cos_part,
        ],
        axis=-1,
    )


def rotate_back(grad, cos_table, sin_table):
    half_dim = grad.shape[-1] // 2
    lower_half = grad[..., :half_dim]
    upper_half = grad[..., half_dim:]
    cos_part = cos_table[:, None, :]
    sin_part = sin_table[:, None, :]
    return jnp.concatenate(
        [
            lower_half * cos_part + upper_half * sin_part,
            upper_half * cos_part - lower_half * sin_part,
        ],
        axis=-1,
    )


def nesterov(param, moment, grad, step_rate):
    moment_new = MOMENTUM * moment + grad
    return (moment_new, param - step_rate * (grad + MOMENTUM * moment_new))


BF = jnp.bfloat16
F32 = jnp.float32
MESH = pl.DeviceIdType.MESH
VM = pltpu.VMEM
MIB = 1 << 20
BLOCK = 256
SPAN = 512
ROWS_STEP = 128
UNIT_STEP = 1024


def dot_nn(a, b):
    return lax.dot_general(a, b, (((1,), (0,)), ((), ())), preferred_element_type=F32)


def dot_nt(a, b):
    return lax.dot_general(a, b, (((1,), (1,)), ((), ())), preferred_element_type=F32)


def dot_tn(a, b):
    return lax.dot_general(a, b, (((0,), (0,)), ((), ())), preferred_element_type=F32)


def split_dot(a, ones):
    high = a.astype(BF)
    return dot_nn(high, ones) + dot_nn((a - high.astype(F32)).astype(BF), ones)


def ring_place(index, chips):
    z, y = index // 4, (index // 2) % 2
    return z + y * (chips - 1 - 2 * z), index % 2


def ring_device(place, core, chips):
    y = place // (chips // 2)
    return ((place + y * (chips - 1 - 2 * place)) * 2 + y) * 2 + core


def peers_of(chips):
    index, x = lax.axis_index("fsdp"), lax.axis_index("mp")
    place, core = ring_place(index, chips)
    right = (ring_device((place + 1) % chips, core, chips), x)
    left = (ring_device((place + chips - 1) % chips, core, chips), x)
    return index, x, place, core, right, left, (index + 1 - 2 * core, x), (index, 1 - x)


def greet(peers):
    barrier = pltpu.get_barrier_semaphore()
    for peer in peers:
        pl.semaphore_signal(barrier, inc=1, device_id=peer, device_id_type=MESH)
    pl.semaphore_wait(barrier, len(peers))


def remote(src, dst, send, recv, peer):
    return pltpu.make_async_remote_copy(
        src_ref=src, dst_ref=dst, send_sem=send, recv_sem=recv, device_id=peer, device_id_type=MESH
    )


def start_copy(src, dst, sem):
    copy = pltpu.make_async_copy(src, dst, sem)
    copy.start()
    return copy


def by_step(total, step, body, first=0):
    def run(i, _):
        body(pl.ds(pl.multiple_of(first + i * step, step), step))
        return 0

    lax.fori_loop(0, total // step, run, 0)


def add_all(dst, refs):
    if len(dst.shape) == 3:
        for j in range(dst.shape[0]):
            add_all(dst.at[j], [ref.at[j] for ref in refs])
        return

    def body(r):
        total = refs[0][r].astype(F32)
        for ref in refs[1:]:
            total = total + ref[r].astype(F32)
        dst[r] = total.astype(dst.dtype)

    by_step(dst.shape[0], 16, body)


def ring_hops(chips, group, long_right):
    pair_of = (chips // 2, chips - 1 - chips // 2)
    return pair_of if group in long_right else pair_of[::-1]


class Scatter:
    def __init__(self, chips, long_right, mine, slot, result, send, recv):
        _, _, self.place, self.core, self.right, self.left, _, _ = peers_of(chips)
        self.chips, self.long_right, self.mine, self.slot_at, self.result = chips, long_right, mine, slot, result
        self.send, self.recv, self.sent = send, recv, []

    def hops(self, group):
        return ring_hops(self.chips, group, self.long_right)

    def term(self, group, way, to_go):
        step = to_go if way == 0 else self.chips - to_go
        return self.mine(group, way, to_go, ring_device((self.place + step) % self.chips, self.core, self.chips) // 2)

    def at(self, group, way, hop):
        return hop - 1 if way == 0 else self.hops(group)[0] + hop - 1

    def slot(self, group, way, hop):
        return self.slot_at(group, self.at(group, way, hop))

    def copy(self, group, way, hop, src):
        at, peer = self.at(group, way, hop), self.right if way == 0 else self.left
        return remote(src, self.slot_at(group, at), self.send.at[group, at], self.recv.at[group, at], peer)

    def go(self, group, way, hop, src):
        copy = self.copy(group, way, hop, src)
        copy.start()
        self.sent.append(copy)

    def launch(self, group):
        for way in (0, 1):
            self.go(group, way, 1, self.term(group, way, self.hops(group)[way]))

    def take(self, group, way, hop):
        here = self.slot(group, way, hop)
        self.copy(group, way, hop, here).wait_recv()
        return here

    def tick(self, group, hop):
        hops = self.hops(group)
        for way in (0, 1):
            if hop > hops[way]:
                continue
            here = self.take(group, way, hop)
            if hop < hops[way]:
                add_all(here, [here, self.term(group, way, hops[way] - hop)])
                self.go(group, way, hop + 1, here)
        if hop == self.chips // 2:
            ends = [self.slot(group, way, hops[way]) for way in (0, 1)]
            add_all(self.result(group), [self.term(group, 0, 0)] + ends)

    def close(self):
        for copy in self.sent:
            copy.wait_send()


def head_ones():
    row = lax.broadcasted_iota(jnp.int32, (128, 128), 0) // HD
    col = lax.broadcasted_iota(jnp.int32, (128, 128), 1) // HD
    return jnp.where(row == col, 1.0, 0.0).astype(BF)


def half_of(rows, half):
    lane = lax.broadcasted_iota(jnp.int32, (rows, 128), 1)
    return jnp.where((lane < HD) == (half == 0), 1.0, 0.0).astype(BF)


def other_half(v):
    lane = lax.broadcasted_iota(jnp.int32, v.shape, 1)
    return jnp.where(lane % HD < HD // 2, pltpu.roll(v, 128 - HD // 2, 1), pltpu.roll(v, HD // 2, 1))


def first_key(block):
    return max(0, block * BLOCK - SPAN)


def low(*shape):
    return jax.ShapeDtypeStruct(shape, BF)


def full(*shape):
    return jax.ShapeDtypeStruct(shape, F32)


GATHER_LONG = (0, 2, 4)
FEED_LONG = (0, 1)


def row_factor(v):
    return lax.rsqrt(jnp.mean(v * v, axis=-1, keepdims=True) + EPS)


def unit_back(factor, unit, grad):
    return factor * (grad - unit * jnp.mean(grad * unit, axis=-1, keepdims=True))


def fold(v):
    return jnp.sum(v.reshape(v.shape[0] // 8, 8, v.shape[1]), axis=0)


def feed_chunks(length):
    half = BLOCK // 2
    return [(0, half)] + [(start, BLOCK) for start in range(half, length - half, BLOCK)] + [(length - half, half)]


def layer_kernel(
    chips, attn_hbm, mlp_hbm, x_hbm, og_hbm, doc_ref, gain_ref, freq_ref, mix_ref, us_ref,
    out_o, dri_o, do_o, dy_o, w_o, qkv_o, r_o, y_o, tables_o, carry_o, rest_o, start_o, mix_o, us_o, gd_o,
    start_s, mix_s, us_s, gd_s, x_ref, y_ref, wo_s, wu_s, wg_s, wd_s, o_s, hb_s, u_s, g_s, hid_s, dm_s, dh_s, own_s, got_m, got_d, wd_g, ring_d, ring_n,
    load, store, save, rest_save, small_save, send_y, recv_y, wo_send, wo_recv, wo_near, send_m, recv_m, send_d, recv_d,
    gather_send, gather_recv, near_send, near_recv, own_sem, pair_free, pair_send, pair_recv, ring_send, ring_recv,
):
    index, x, place, core, right, left, pair, across = peers_of(chips)
    pair_index = pair[0]
    length, width = x_ref.shape
    cols, units = y_ref.shape[2], us_ref.shape[1]
    rows_own = width // (2 * chips)
    blocks = length // BLOCK
    chunks = feed_chunks(length)
    number = len(chunks)
    longest = chips // 2

    wide = 3 * cols
    loads_attn = [
        start_copy(attn_hbm.at[j], o_s.at[pl.ds(j * rows_own, rows_own), pl.ds(0, cols)], load.at[j]) for j in range(4)
    ]
    halves = units // width
    loads_mlp = [
        start_copy(
            mlp_hbm.at[j, :, pl.ds(h * width, width)],
            o_s.at[pl.ds((4 + j * halves + h) * rows_own, rows_own)], load.at[4 + j * halves + h],
        )
        for j in range(3)
        for h in range(halves)
    ]
    load_x = start_copy(x_hbm, x_ref, load.at[4 + 3 * halves])
    load_og = start_copy(og_hbm, dm_s, load.at[5 + 3 * halves])

    def own(group):
        if group == 0:
            return wd_g.at[pl.ds(0, rows_own), pl.ds(0, wide)]
        if group == 1:
            return wd_g.at[pl.ds(0, rows_own), pl.ds(wide, cols)]
        return wd_g.at[pl.ds((group - 1) * rows_own, rows_own)]

    def block_of(group, dev):
        r = pl.ds(pl.multiple_of(dev * rows_own, rows_own), rows_own)
        if group == 0:
            return g_s.at[r, pl.ds(0, wide)]
        if group == 1:
            return wo_s.at[x, r]
        return (wu_s, wg_s, wd_s)[group - 2].at[r]

    def counts(group):
        return ring_hops(chips, group, GATHER_LONG)

    def origin(way, hop):
        there = (place + chips - hop) % chips if way == 0 else (place + hop) % chips
        return ring_device(there, core, chips)

    def gather_copy(group, way, hop, src, dst):
        peer = right if way == 0 else left
        return remote(src, dst, gather_send.at[group, way, hop - 1], gather_recv.at[group, way, hop - 1], peer)

    def near_copy(group, at, src, dev):
        return remote(src, block_of(group, dev), near_send.at[group, at], near_recv.at[group, at], pair)

    sends, owns = [[] for _ in range(5)], []

    def launch(group):
        for way in (0, 1):
            sends[group].append(gather_copy(group, way, 1, own(group), block_of(group, index)))
            sends[group][-1].start()
        sends[group].append(near_copy(group, 0, own(group), index))
        sends[group][-1].start()
        owns.append(start_copy(own(group), block_of(group, index), own_sem.at[group]))

    def tick(group, hop):
        for way in (0, 1):
            if hop > counts(group)[way]:
                continue
            dev = origin(way, hop)
            here = block_of(group, dev)
            gather_copy(group, way, hop, here, here).wait_recv()
            if hop < counts(group)[way]:
                sends[group].append(gather_copy(group, way, hop + 1, here, here))
                sends[group][-1].start()
            sends[group].append(near_copy(group, hop if way == 0 else counts(group)[0] + hop, here, dev))
            sends[group][-1].start()

    def await_all(group):
        owns[group].wait()
        near_copy(group, 0, block_of(group, pair_index), pair_index).wait_recv()
        for way in (0, 1):
            for hop in range(1, counts(group)[way] + 1):
                dev = origin(way, hop) + 1 - 2 * core
                at = hop if way == 0 else counts(group)[0] + hop
                near_copy(group, at, block_of(group, dev), dev).wait_recv()

    for j, copy in enumerate(loads_attn):
        copy.wait()
        wd_g[0:rows_own, j * cols : (j + 1) * cols] = o_s[j * rows_own : (j + 1) * rows_own, 0:cols].astype(BF)
    greet((right, left, pair, across))
    launch(0)
    launch(1)
    for j in range(3):
        for h in range(halves):
            loads_mlp[j * halves + h].wait()
            first = (4 + j * halves + h) * rows_own
            wd_g[(j + 1) * rows_own : (j + 2) * rows_own, h * width : (h + 1) * width] = o_s[
                first : first + rows_own
            ].astype(BF)
    doc = doc_ref[...]
    start = jnp.zeros(doc.shape, F32)
    for value in range(3):
        count = jnp.sum(jnp.where(doc == value, 1.0, 0.0), axis=1, keepdims=True)
        start = start + jnp.where(doc > value, count, 0.0)
    start_s[...] = start.astype(jnp.int32)
    dh_s[:, 256:384] = jnp.transpose(jnp.broadcast_to(start, (128, length)))

    def tables(block):
        rows = pl.ds(block * BLOCK, BLOCK)
        position = (lax.broadcasted_iota(jnp.int32, (BLOCK, 128), 0) + block * BLOCK).astype(F32)
        angle = (position - dh_s[rows, 256:384]) * freq_ref[...]
        lane = lax.broadcasted_iota(jnp.int32, (BLOCK, 128), 1)
        dh_s[rows, 0:128] = jnp.cos(angle)
        dh_s[rows, 128:256] = jnp.where(lane % HD < HD // 2, -1.0, 1.0) * jnp.sin(angle)

    for block in range(blocks // 2):
        tables(block)
    tick(0, 1)
    tick(1, 1)
    for block in range(blocks // 2, blocks):
        tables(block)
    stores = [start_copy(dh_s.at[:, pl.ds(0, 256)], tables_o, store.at[0])]
    stores.append(start_copy(start_s, start_o, small_save.at[0]))
    tick(0, 2)
    launch(2)
    tick(1, 2)
    tick(0, 3)
    tick(2, 1)
    tick(1, 3)
    launch(3)
    tick(0, 4)
    pending = [
        (2, 2), (1, 4), (3, 1), (2, 3), (4, 1), (3, 2), (2, 4), (4, 2), (3, 3), (4, 3), (3, 4), (4, 4),
    ]
    ones = head_ones()
    load_x.wait()
    await_all(0)
    held = [start_copy(g_s.at[:, pl.ds(0, wide)], w_o, store.at[1])]

    def project(i, _):
        rows = pl.ds(pl.multiple_of(i * BLOCK, BLOCK), BLOCK)
        states = x_ref[rows]
        cos, sin = dh_s[rows, 0:128], dh_s[rows, 128:256]
        for j, scale in enumerate((HD**-0.5, 1.0)):
            raw = dot_nn(states, g_s[:, j * cols : (j + 1) * cols])
            for c in range(0, cols, 128):
                part = raw[:, c : c + 128]
                factor = lax.rsqrt(split_dot(part * part, ones) * (1.0 / HD) + EPS)
                unit = (part * cos + other_half(part) * sin) * factor
                at = slice(j * cols + c, j * cols + c + 128)
                u_s[rows, at] = ((gain_ref[:, c : c + 128] * unit).astype(BF).astype(F32) * scale).astype(BF)
                hid_s[rows, at] = factor.astype(BF)
        u_s[rows, 2 * cols : wide] = dot_nn(states, g_s[:, 2 * cols : wide]).astype(BF)
        return 0

    lax.fori_loop(0, blocks // 2, project, 0)
    tick(*pending.pop(0))
    launch(4)
    tick(*pending.pop(0))
    await_all(1)
    part = width // 2

    def wo_half(half, side, send, recv, peer):
        there = wo_s.at[side, pl.ds(pl.multiple_of(half * part, part), part)]
        return remote(there, there, send, recv, peer)

    wo_copy = wo_half(core, x, wo_send, wo_recv, across)
    wo_copy.start()
    lax.fori_loop(blocks // 2, blocks, project, 0)
    held.append(start_copy(u_s.at[:, pl.ds(0, wide)], qkv_o, store.at[2]))
    held.append(start_copy(hid_s.at[:, pl.ds(0, 2 * cols)], r_o, store.at[3]))
    tick(*pending.pop(0))
    copies_y = []
    for block in range(blocks):
        first = first_key(block)
        keys = (block + 1) * BLOCK - first
        rows = pl.ds(block * BLOCK, BLOCK)
        span = pl.ds(first, keys)
        bias = o_s.at[pl.ds(0, BLOCK), pl.ds(0, keys)]
        kpos = (lax.broadcasted_iota(jnp.int32, (BLOCK, keys), 1) + first).astype(F32)
        qpos = (lax.broadcasted_iota(jnp.int32, (BLOCK, keys), 0) + block * BLOCK).astype(F32)
        allowed = (kpos >= dh_s[rows, 256:257]) & (kpos <= qpos)
        bias[...] = jnp.where(allowed, 0.0, NEG_FILL)

        def heads(pair_of, _):
            c = pl.multiple_of(pair_of * 128, 128)
            q = u_s[rows, pl.ds(c, 128)]
            k = u_s[span, pl.ds(cols + c, 128)]
            v = u_s[span, pl.ds(2 * cols + c, 128)]
            results = []
            for half in (0, 1):
                scores = dot_nt(q * half_of(BLOCK, half), k)
                probs = jnp.exp(scores + bias[...]).astype(BF)
                results.append(dot_nn(probs, v * half_of(keys, half) + half_of(keys, 1 - half)))
            lane = lax.broadcasted_iota(jnp.int32, (BLOCK, 128), 1)
            total = pltpu.roll(jnp.where(lane < HD, results[1], results[0]), HD, 1)
            y_ref[x, rows, pl.ds(c, 128)] = (jnp.where(lane < HD, results[0], results[1]) / total).astype(BF)
            return 0

        lax.fori_loop(0, cols // 128, heads, 0)
        copy = remote(y_ref.at[x, rows], y_ref.at[x, rows], send_y.at[block], recv_y.at[block], across)
        copy.start()
        copies_y.append(copy)
        stores.append(start_copy(y_ref.at[x, rows], y_o.at[rows], store.at[4 + block]))
        tick(*pending.pop(0))
        if block == 1:
            wo_half(core, 1 - x, wo_send, wo_recv, across).wait_recv()
            wo_pass = wo_half(core, 1 - x, wo_near.at[0], wo_near.at[1], pair)
            wo_pass.start()

    copies_m, copies_d = {}, {}
    here_y = []

    def await_y(rows_end):
        while len(here_y) * BLOCK < rows_end:
            block = len(here_y)
            there = y_ref.at[1 - x, pl.ds(block * BLOCK, BLOCK)]
            remote(there, there, send_y.at[block], recv_y.at[block], across).wait_recv()
            here_y.append(block)

    def first_half(r):
        states = x_ref[r].astype(F32)
        o = o_s[r]
        ro = row_factor(o)
        uo = o * ro
        mix = mix_ref[0:1]
        r1 = states + mix * (uo - states)
        rr = row_factor(r1)
        return states, ro, uo, rr, r1 * rr

    def by_rows(chunk, body, init):
        start, size = chunks[chunk]
        for i in range(size // ROWS_STEP):
            init = body(pl.ds(start + i * ROWS_STEP, ROWS_STEP), init)
        return init

    def mixed(chunk):
        start, size = chunks[chunk]
        rows = pl.ds(start, size)
        await_y(start + size)

        def out_proj(c):
            o_s[rows, c] = dot_nt(y_ref[0, rows], wo_s[0, c]) + dot_nt(y_ref[1, rows], wo_s[1, c])

        by_step(width, 512, out_proj)

        def hidden(r, _):
            hb_s[r] = first_half(r)[4].astype(BF)
            return 0

        by_rows(chunk, hidden, 0)

    def gates(chunk):
        rows = pl.ds(*chunks[chunk])

        def gate(f):
            up = dot_nn(hb_s[rows], wu_s[:, f])
            gt = dot_nn(hb_s[rows], wg_s[:, f])
            arg = us_ref[1:2, f] * gt * D**-0.5
            sig = 1.0 / (1.0 + jnp.exp(-arg))
            u_s[rows, f] = up.astype(BF)
            g_s[rows, f] = gt.astype(BF)
            hid_s[rows, f] = (us_ref[0:1, f] * up * (arg * sig)).astype(BF)

        by_step(units, UNIT_STEP, gate)

    def down(chunk):
        rows = pl.ds(*chunks[chunk])

        def body(c):
            own_s[rows, c] = dot_nt(hid_s[rows], wd_s[c]).astype(BF)

        by_step(width, 512, body)
        copies_m[chunk] = remote(own_s.at[rows], got_m.at[rows], send_m.at[chunk], recv_m.at[chunk], across)
        copies_m[chunk].start()

    def turn(chunk, mix_m):
        rows = pl.ds(*chunks[chunk])
        copies_m[chunk].wait()

        def middle(r, total):
            h1 = first_half(r)[4]
            m = own_s[r].astype(F32) + got_m[r].astype(F32)
            rm = row_factor(m)
            um = m * rm
            mix = mix_ref[1:2]
            r2 = h1 + mix * (um - h1)
            rr = row_factor(r2)
            out = r2 * rr
            got_m[r] = out.astype(BF)
            dr2 = unit_back(rr, out, dm_s[r].astype(F32))
            dm_s[r] = unit_back(rm, um, mix * dr2).astype(BF)
            dh_s[r] = dr2 * (1.0 - mix)
            return total + fold(dr2 * (um - h1))

        mix_m = by_rows(chunk, middle, mix_m)
        stores.append(start_copy(got_m.at[rows], out_o.at[rows], save.at[3, chunk]))
        return mix_m

    def gates_back(chunk):
        rows = pl.ds(*chunks[chunk])

        def gate_back(f):
            dhid = dot_nn(dm_s[rows], wd_s[:, f])
            up, gt = u_s[rows, f].astype(F32), g_s[rows, f].astype(F32)
            su, sv = us_ref[0:1, f], us_ref[1:2, f]
            arg = sv * gt * D**-0.5
            sig = 1.0 / (1.0 + jnp.exp(-arg))
            act = dhid * (arg * sig)
            darg = dhid * su * up * sig * (1.0 + arg * (1.0 - sig))
            us_s[0:1, f] = us_s[0:1, f] + jnp.sum(act * up, axis=0, keepdims=True)
            us_s[1:2, f] = us_s[1:2, f] + jnp.sum(darg * gt, axis=0, keepdims=True) * D**-0.5
            u_s[rows, f] = (act * su).astype(BF)
            g_s[rows, f] = (darg * sv * D**-0.5).astype(BF)

        by_step(units, UNIT_STEP, gate_back)

    def ups_back(chunk):
        rows = pl.ds(*chunks[chunk])

        def up_back(c):
            own_s[rows, c] = (dot_nt(u_s[rows], wu_s[c]) + dot_nt(g_s[rows], wg_s[c])).astype(BF)

        by_step(width, 512, up_back)
        copies_d[chunk] = remote(own_s.at[rows], got_d.at[rows], send_d.at[chunk], recv_d.at[chunk], across)
        copies_d[chunk].start()

    def back(chunk):
        gates_back(chunk)
        ups_back(chunk)

    near_s = (hid_s, u_s, g_s)
    pairs = {}

    def weight_grads(j, weight_s, left_s, midway=None):
        right_s = near_s[j]

        def grads(d):
            for u in range(0, units, 1024):
                f = pl.ds(u, 1024)
                weight_s[d, f] = dot_tn(left_s[:, d], right_s[:, f]).astype(BF)

        by_step(width // 2, BLOCK, grads)
        if midway is not None:
            midway()
        by_step(width // 2, BLOCK, grads, width // 2)
        pl.semaphore_signal(pair_free.at[j], inc=1, device_id=pair, device_id_type=MESH)
        pl.semaphore_wait(pair_free.at[j], 1)
        for chip in range(chips):
            there = pl.multiple_of((chip * 2 + 1 - core) * rows_own, rows_own)
            copy = remote(
                weight_s.at[pl.ds(there, rows_own)], right_s.at[pl.ds(chip * rows_own, rows_own)],
                pair_send.at[j, chip], pair_recv.at[j, chip], pair,
            )
            copy.start()
            pairs[j, chip] = copy

    def pair_sums(j, weight_s):
        for chip in range(chips):
            pairs[j, chip].wait()
            base = pl.multiple_of((chip * 2 + core) * rows_own, rows_own)
            here = near_s[j].at[pl.ds(chip * rows_own, rows_own)]
            add_all(here, [here, weight_s.at[pl.ds(base, rows_own)]])

    def summed(group, way, to_go, chip):
        return near_s[group].at[pl.ds(pl.multiple_of(chip * rows_own, rows_own), rows_own)]

    def ring_slot(group, at):
        return ring_d.at[at] if group == 0 else ring_n.at[group - 1, 0 if at == 0 else 1]

    scatter = Scatter(chips, FEED_LONG, summed, ring_slot, lambda group: gd_s, ring_send, ring_recv)

    def hand_on(group):
        for way in (0, 1):
            here = scatter.take(group, way, 1)
            to_go = scatter.hops(group)[way] - 1
            add_all(here, [here, scatter.term(group, way, to_go)])
            stores.append(start_copy(here, carry_o.at[group - 1, way], rest_save.at[group - 1, way]))

    def hand_rest(group):
        hops = scatter.hops(group)
        wide_way = 0 if hops[0] > hops[1] else 1
        for at, (way, to_go) in enumerate(((wide_way, 2), (wide_way, 1), (1 - wide_way, 1), (0, 0))):
            stores.append(start_copy(scatter.term(group, way, to_go), rest_o.at[group - 1, at], rest_save.at[group - 1, 2 + at]))

    def last(chunk, mix_a):
        rows = pl.ds(*chunks[chunk])
        copies_d[chunk].wait()

        def body(r, total):
            states, ro, uo, rr, h1 = first_half(r)
            mix = mix_ref[0:1]
            dr1 = unit_back(rr, h1, dh_s[r] + (own_s[r].astype(F32) + got_d[r].astype(F32)))
            dh_s[r] = dr1 * (1.0 - mix)
            dm_s[r] = unit_back(ro, uo, mix * dr1).astype(BF)
            return total + fold(dr1 * (uo - states))

        mix_a = by_rows(chunk, body, mix_a)
        y_ref[1 - x, rows] = dot_nn(dm_s[rows], wo_s[x]).astype(BF)
        for j, (src, dst) in enumerate(((y_ref.at[1 - x], dy_o), (dm_s, do_o), (dh_s, dri_o))):
            stores.append(start_copy(src.at[rows], dst.at[rows], save.at[j, chunk]))
        return mix_a

    wo_half(1 - core, 1 - x, wo_near.at[0], wo_near.at[1], pair).wait_recv()
    for chunk in range(number):
        mixed(chunk)
        if len(pending) > 2:
            tick(*pending.pop(0))
    for copy in held:
        copy.wait()
    for copy in sends[0]:
        copy.wait_send()
    while len(pending) > 1:
        tick(*pending.pop(0))
    await_all(2)
    await_all(3)
    gates(0)
    tick(*pending.pop(0))
    await_all(4)
    for chunk in range(number):
        down(chunk)
        if chunk < number - 1:
            gates(chunk + 1)
        if chunk == 0:
            for group in range(1, 5):
                for copy in sends[group]:
                    copy.wait_send()
    mix_m = jnp.zeros((8, width), F32)
    us_s[...] = jnp.zeros_like(us_s)
    load_og.wait()
    stores[0].wait()
    for chunk in range(number - 2):
        mix_m = turn(chunk, mix_m)
        back(chunk)
    mix_m = turn(number - 2, mix_m)
    mix_m = turn(number - 1, mix_m)
    mix_s[1:2] = jnp.sum(mix_m, axis=0, keepdims=True)
    weight_grads(0, wd_g, dm_s)
    gates_back(number - 2)
    pair_sums(0, wd_g)
    scatter.launch(0)
    ups_back(number - 2)
    back(number - 1)
    stores.append(start_copy(us_s, us_o, small_save.at[1]))
    weight_grads(1, wu_s, hb_s, lambda: scatter.tick(0, 1))

    def up_ring():
        scatter.tick(0, 2)
        pair_sums(1, wu_s)
        scatter.launch(1)
        hand_rest(1)

    weight_grads(2, wg_s, hb_s, up_ring)
    wo_copy.wait_send()
    wo_pass.wait_send()
    for copy in copies_y:
        copy.wait_send()
    mix_a = jnp.zeros((8, width), F32)
    for chunk in range(number):
        mix_a = last(chunk, mix_a)
        if chunk == 1:
            scatter.tick(0, 3)
            pair_sums(2, wg_s)
            scatter.launch(2)
            hand_rest(2)
        if chunk == number - 3:
            hand_on(1)
        if chunk == number - 2:
            hand_on(2)
            scatter.tick(0, 4)
            stores.append(start_copy(gd_s, gd_o, small_save.at[2]))
    mix_s[0:1] = jnp.sum(mix_a, axis=0, keepdims=True)
    stores.append(start_copy(mix_s, mix_o, small_save.at[3]))
    for copy in stores[1:]:
        copy.wait()
    scatter.close()


def layer(attn_w, mlp_w, states, out_grad, doc, gain, mix, scales, fsdp):
    chips = fsdp // 2
    length, width = states.shape
    cols, units, rows = attn_w.shape[2], mlp_w.shape[2], attn_w.shape[1]
    vspec, anyspec = pl.BlockSpec(memory_space=VM), pl.BlockSpec(memory_space=pl.ANY)
    blocks, number = length // BLOCK, len(feed_chunks(length))
    sem = pltpu.SemaphoreType.DMA
    freq = THETA ** (-2.0 * (jnp.arange(128, dtype=F32) % (HD // 2)) / HD)
    square, wide, weight, tall = VM((length, width), BF), VM((length, units), BF), VM((width, units), BF), VM((length, width), F32)
    return pl.pallas_call(
        functools.partial(layer_kernel, chips),
        out_shape=(
            low(length, width), full(length, width), low(length, width), low(length, cols),
            low(width, 3 * cols), low(length, 3 * cols), low(length, 2 * cols), low(length, cols), full(length, 256),
            low(2, 2, rows, units), low(2, 4, rows, units),
            jax.ShapeDtypeStruct((1, length), jnp.int32), full(2, width), full(2, units), full(rows, units),
        ),
        in_specs=[anyspec] * 4 + [vspec] * 5,
        out_specs=(anyspec,) * 15,
        scratch_shapes=[
            VM((1, length), jnp.int32), VM((2, width), F32), VM((2, units), F32), VM((rows, units), F32),
            square, VM((2, length, cols), BF), VM((2, width, cols), BF), weight, weight, weight,
            tall, square, wide, wide, wide, square, tall, square, square, square, weight,
            VM((chips - 1, rows, units), BF), VM((2, 2, rows, units), BF),
            sem((6 + 3 * (units // width),)), sem((4 + blocks,)), sem((4, number)), sem((2, 6)),
            sem((4,)), sem((blocks,)), sem((blocks,)), sem, sem, sem((2,)), sem((number,)), sem((number,)), sem((number,)), sem((number,)),
            sem((5, 2, chips // 2)), sem((5, 2, chips // 2)), sem((5, chips)), sem((5, chips)), sem((5,)),
            pltpu.SemaphoreType.REGULAR((3,)), sem((3, chips)), sem((3, chips)), sem((3, chips - 1)), sem((3, chips - 1)),
        ],
        compiler_params=pltpu.CompilerParams(collective_id=6, has_side_effects=True, vmem_limit_bytes=63 * MIB),
        name="layer",
    )(attn_w, mlp_w, states, out_grad, doc, gain, freq[None], mix, scales)


SCATTER_LONG = (0, 3, 5)
MATRIX_OF = {2: 3, 3: 2, 4: 1, 5: 0}


def stepped(param, moment, grad, rate):
    moment_new = MOMENTUM * moment + grad
    return moment_new, param - rate * (grad + MOMENTUM * moment_new)


def backward_kernel(
    rate, x_hbm, w_hbm, qkv_hbm, r_hbm, y_hbm, dy_hbm, do_hbm, dri_hbm, carry_hbm, rest_hbm, tables_hbm,
    wa_hbm, ma_hbm, wm_hbm, mm_hbm, gain_ref, start_ref, gd_ref, mix_ref, us_ref,
    ig_o, ga_o, gm_o, sum_a_o, sum_m_o,
    ga_s, gm_s, x_ref, w_ref, qkv_ref, r_ref, y_ref, dy_ref, do_ref, carry, rest, tables_ref, dri_s,
    wa_ref, ma_ref, wm_ref, mm_ref,
    bias, dq_s, dk_s, dv_s, low_s, out_s, in_s, dw_s, near, ring_a, ring_m, head_s, mine_a, got_a, mine_m, got_m,
    load, load_dri, store, save, send, recv, pair_send, pair_recv, ring_send, ring_recv, all_send, all_recv,
):
    chips, rows_own = near.shape[1:3]
    index, x, place, core, right, left, pair, across = peers_of(chips)
    length, cols = y_ref.shape
    width = x_ref.shape[1]
    blocks = length // BLOCK
    stages = got_a.shape[0]
    turns = [(index + (1 << s) * (1 - 2 * ((index // (1 << s)) % 2)), x) for s in range(stages)]
    pieces = (
        (carry_hbm, carry), (qkv_hbm, qkv_ref), (dy_hbm, dy_ref), (y_hbm, y_ref),
        (tables_hbm, tables_ref), (r_hbm, r_ref), (w_hbm, w_ref), (rest_hbm, rest),
        (do_hbm, do_ref), (x_hbm, x_ref), (wm_hbm, wm_ref), (mm_hbm, mm_ref), (wa_hbm, wa_ref), (ma_hbm, ma_ref),
    )
    loads = [start_copy(src, dst, load.at[j]) for j, (src, dst) in enumerate(pieces)]
    greet([right, left, pair, across] + turns)

    def mine(group, way, to_go, chip):
        if group < 2:
            wide_way = 0 if group in SCATTER_LONG else 1
            return rest.at[group, 3 if to_go == 0 else 2 - to_go if way == wide_way else 2]
        return near.at[MATRIX_OF[group], chip]

    def slot(group, at):
        if group < 2:
            return ring_m.at[group, at]
        return ring_a.at[at, MATRIX_OF[group]]

    def result(group):
        return gm_s.at[group] if group < 2 else ga_s.at[MATRIX_OF[group]]

    scatter = Scatter(chips, SCATTER_LONG, mine, slot, result, ring_send, ring_recv)
    tick, launch = scatter.tick, scatter.launch

    def send_pair(j):
        copies = []
        for chip in range(chips):
            there = pl.multiple_of((chip * 2 + 1 - core) * rows_own, rows_own)
            copy = remote(
                dw_s.at[j, pl.ds(there, rows_own)], near.at[j, chip], pair_send.at[j, chip], pair_recv.at[j, chip], pair
            )
            copy.start()
            copies.append(copy)
        return copies

    def sum_pair(copies, j):
        for chip, copy in enumerate(copies):
            copy.wait()
            own = pl.ds(pl.multiple_of((chip * 2 + core) * rows_own, rows_own), rows_own)
            here = near.at[j, chip]
            add_all(here, [here, dw_s.at[j, own]])

    loads[0].wait()
    for group in (0, 1):
        for way in (0, 1):
            scatter.go(group, way, 2, carry.at[group, way])
    dk_s[...] = jnp.zeros_like(dk_s)
    dv_s[...] = jnp.zeros_like(dv_s)
    head_s[...] = jnp.zeros_like(head_s)
    ones = head_ones()
    copies, stores = {}, []

    def fetch_dri(block):
        return start_copy(dri_hbm.at[pl.ds(block * BLOCK, BLOCK)], dri_s.at[block % 2], load_dri.at[block])

    fetched = {block: fetch_dri(block) for block in (blocks - 1, blocks - 2)}

    def finish_input(block):
        copies[block].wait()
        fetched[block].wait()
        for i in range(0, BLOCK, 128):
            r = pl.ds(block * BLOCK + i, 128)
            total = out_s[r].astype(F32) + in_s[r].astype(F32)
            out_s[r] = (dri_s[block % 2, pl.ds(i, 128)] + total).astype(BF)
        rows = pl.ds(block * BLOCK, BLOCK)
        stores.append(start_copy(out_s.at[rows], ig_o.at[rows], store.at[block]))
        if block >= 2:
            fetched[block - 2] = fetch_dri(block - 2)

    for copy in loads[1:4]:
        copy.wait()

    def attend(block):
        first = first_key(block)
        keys = (block + 1) * BLOCK - first
        rows = pl.ds(block * BLOCK, BLOCK)
        span = pl.ds(first, keys)
        kpos = lax.broadcasted_iota(jnp.int32, (keys, BLOCK), 0) + first
        qpos = lax.broadcasted_iota(jnp.int32, (keys, BLOCK), 1) + block * BLOCK
        allowed = (kpos >= start_ref[:, block * BLOCK : (block + 1) * BLOCK]) & (kpos <= qpos)
        bias[:keys] = jnp.where(allowed, 0.0, NEG_FILL)

        def heads(pair_of, _):
            at = pl.multiple_of(pair_of * 128, 128)
            c = pl.ds(at, 128)
            q, dy = qkv_ref[rows, c], dy_ref[rows, c]
            k, v = qkv_ref[span, pl.ds(cols + at, 128)], qkv_ref[span, pl.ds(2 * cols + at, 128)]
            prod = dy.astype(F32) * y_ref[rows, c].astype(F32)
            prod_high = prod.astype(BF)
            prod_low = (prod - prod_high.astype(F32)).astype(BF)
            dq = jnp.zeros((BLOCK, 128), F32)
            dk = jnp.zeros((keys, 128), F32)
            dv = jnp.zeros((keys, 128), F32)
            for half in (0, 1):
                mask, row = half_of(BLOCK, half), half_of(8, half)
                qm, dym, km = q * mask, dy * mask, k * half_of(keys, half)
                expo = jnp.exp(dot_nt(k, qm) + bias[:keys])
                probs = expo * (1.0 / jnp.sum(expo, axis=0, keepdims=True))
                delta = (dot_nt(row, prod_high) + dot_nt(row, prod_low))[0:1]
                dz = (probs * (dot_nt(v, dym) - delta)).astype(BF)
                dk = dk + dot_nn(dz, qm)
                dv = dv + dot_nn(probs.astype(BF), dym)
                dq = dq + dot_tn(dz, km)
            dq_s[rows, c] = dq * HD**-0.5
            dk_s[span, c] = dk_s[span, c] + dk
            dv_s[span, c] = dv_s[span, c] + dv
            return 0

        return heads

    def project_back(block):
        rows = pl.ds(block * BLOCK, BLOCK)
        cos, sin = tables_ref[rows, 0:128], tables_ref[rows, 128:256]
        for c in range(0, cols, 128):
            s = slice(c, c + 128)
            gain = gain_ref[:, s]
            head = jnp.zeros((BLOCK, 128), F32)
            for j, (grad_s, scale) in enumerate(((dq_s, HD**0.5), (dk_s, 1.0))):
                at = slice(j * cols + c, j * cols + c + 128)
                grad = grad_s[rows, s]
                unit = qkv_ref[rows, at].astype(F32) * (scale / gain)
                head = head + grad * unit
                grad = grad * gain
                turned = r_ref[rows, at].astype(F32) * (grad - unit * (split_dot(grad * unit, ones) * (1.0 / HD)))
                low_s[j, rows, s] = (turned * cos - other_half(turned) * sin).astype(BF)
            head_s[:, s] = head_s[:, s] + jnp.sum(head, axis=0, keepdims=True)
            low_s[2, rows, s] = dv_s[rows, s].astype(BF)
        for c in range(0, width, 512):
            part = sum(dot_nt(low_s[j, rows], w_ref[c : c + 512, j * cols : (j + 1) * cols]) for j in range(3))
            out_s[rows, c : c + 512] = part.astype(BF)
        copy = remote(out_s.at[rows], in_s.at[rows], send.at[block], recv.at[block], across)
        copy.start()
        copies[block] = copy

    longest = chips // 2
    pending = [(group, hop) for hop in range(2, longest + 1) for group in (0, 1)]
    step_pairs = cols // 256
    def weight_grad(j, d, left, right):
        dw_s[j, d] = dot_tn(left, right).astype(BF)

    for block in reversed(range(blocks)):
        heads = attend(block)
        lax.fori_loop(0, step_pairs, heads, 0)
        if block == blocks - 2:
            tick(*pending.pop(0))
        lax.fori_loop(step_pairs, 2 * step_pairs, heads, 0)
        if block == blocks - 1:
            for copy in loads[4:8]:
                copy.wait()
        if block in (blocks - 1, 1, 0):
            tick(*pending.pop(0))
        project_back(block)
        if block == blocks - 1:
            for copy in loads[8:10]:
                copy.wait()
            by_step(width, BLOCK, lambda d: weight_grad(3, d, do_ref[:, d], y_ref[...]))
            pair_out = send_pair(3)
        if block == blocks - 2:
            tick(*pending.pop(0))
            sum_pair(pair_out, 3)
            launch(2)
    tick(*pending.pop(0))
    assert not pending
    pairs = {}
    for group in (3, 4, 5):
        j = MATRIX_OF[group]
        by_step(width, BLOCK, lambda d: weight_grad(j, d, x_ref[:, d], low_s[j]))
        pairs[group] = send_pair(j)
        tick(2, group - 2)
        if group > 3:
            sum_pair(pairs[group - 1], MATRIX_OF[group - 1])
            launch(group - 1)
    sum_pair(pairs[5], MATRIX_OF[5])
    launch(5)
    tick(2, 4)

    def squares(g, w, m):
        count = g.shape[-1]

        def body(i, total):
            r = pl.ds(pl.multiple_of(i * 8, 8), 8)
            step = stepped(w[r], m[r], g[r], rate)[1]
            return total + step * step

        total = lax.fori_loop(0, rows_own // 8, body, jnp.zeros((8, count), F32))
        return jnp.sum(total, axis=0, keepdims=True)

    def exchange(own, got, kind, s):
        copy = remote(own.at[s], got.at[s], all_send.at[kind, s], all_recv.at[kind, s], turns[s])
        copy.start()
        return copy

    for copy in loads[10:]:
        copy.wait()
    lanes = mine_m.shape[2]
    mine_m[0] = jnp.zeros(mine_m.shape[1:], F32)
    row = 0

    def place_row(value):
        nonlocal row
        for c in range(0, value.shape[1], lanes):
            size = min(lanes, value.shape[1])
            mine_m[0, row : row + 1, 0:size] = value[:, c : c + size]
            row += 1

    for j in range(3):
        place_row(squares(gd_ref if j == 2 else gm_s.at[j], wm_ref.at[j], mm_ref.at[j]))
    place_row(head_s[...])
    for ref in (mix_ref, us_ref):
        for j in range(2):
            place_row(ref[j : j + 1])
    def attn_squares(j):
        mine_a[0, j : j + 1] = squares(ga_s.at[j], wa_ref.at[j], ma_ref.at[j])

    stores.append(start_copy(gm_s, gm_o, save.at[0]))
    attn_squares(3)
    for hop in range(1, max(stages, longest) + 1):
        if hop <= stages:
            copy = exchange(mine_m, got_m, 0, hop - 1)
        if hop == 1:
            finish_input(blocks - 1)
        if hop == 2:
            finish_input(blocks - 2)
        if hop <= longest:
            for group in (3, 4, 5):
                tick(group, hop)
                if hop == longest:
                    attn_squares(MATRIX_OF[group])
        if hop == max(stages, longest):
            last = exchange(mine_a, got_a, 1, 0)
            stores.append(start_copy(ga_s, ga_o, save.at[1]))
        if hop <= stages:
            copy.wait()
            mine_m[hop] = mine_m[hop - 1] + got_m[hop - 1]
    stores.append(start_copy(mine_m.at[stages], sum_m_o, save.at[2]))
    for s in range(stages):
        copy = last if s == 0 else exchange(mine_a, got_a, 1, s)
        if s < blocks - 2:
            finish_input(blocks - 3 - s)
        copy.wait()
        mine_a[s + 1] = mine_a[s] + got_a[s]
    stores.append(start_copy(mine_a.at[stages], sum_a_o, save.at[3]))
    for copy in stores:
        copy.wait()
    scatter.close()


def attention_backward(
    states, weights, qkv, factors, y, dy, do, dri, carry, rest, tables, attn_w, attn_mom, mlp_w, mlp_mom,
    gain, start, grad_down, grad_mix, grad_units, rate, fsdp,
):
    length, width = states.shape
    cols = gain.shape[1]
    chips = fsdp // 2
    rows, units = rest.shape[2:]
    stages = fsdp.bit_length() - 1
    vspec, anyspec = pl.BlockSpec(memory_space=VM), pl.BlockSpec(memory_space=pl.ANY)
    blocks = length // BLOCK
    sem = pltpu.SemaphoreType.DMA
    square, full_square = VM((length, cols), BF), VM((length, cols), F32)
    wide = VM((length, width), BF)
    a_rows, m_rows = 4, -(-(3 * (units // width) + 3 + 2 * (units // width)) // 8) * 8
    return pl.pallas_call(
        functools.partial(backward_kernel, rate),
        out_shape=(
            low(length, width), full(4, rows, cols), full(2, rows, units), full(a_rows, cols), full(m_rows, width),
        ),
        in_specs=[anyspec] * 15 + [vspec] * 5,
        out_specs=(anyspec,) * 5,
        scratch_shapes=[
            VM((4, rows, cols), F32), VM((2, rows, units), F32), wide, VM(weights.shape, BF), VM(qkv.shape, BF), VM(factors.shape, BF), square, square,
            wide, VM(carry.shape, BF), VM(rest.shape, BF), VM(tables.shape, F32), VM((2, BLOCK, width), F32),
            VM(attn_w.shape, F32), VM(attn_w.shape, F32), VM(mlp_w.shape, F32), VM(mlp_w.shape, F32),
            VM((BLOCK + SPAN, BLOCK), F32), full_square, full_square, full_square,
            VM((3, length, cols), BF), wide, wide, VM((4, width, cols), BF), VM((4, chips, rows, cols), BF),
            VM((chips - 1, 4, rows, cols), BF), VM((2, chips - 1, rows, units), BF), VM((1, cols), F32),
            VM((stages + 1, a_rows, cols), F32), VM((stages, a_rows, cols), F32),
            VM((stages + 1, m_rows, width), F32), VM((stages, m_rows, width), F32),
            sem((14,)), sem((blocks,)), sem((blocks,)), sem((4,)), sem((blocks,)), sem((blocks,)),
            sem((4, chips)), sem((4, chips)), sem((6, chips - 1)), sem((6, chips - 1)), sem((2, stages)), sem((2, stages)),
        ],
        compiler_params=pltpu.CompilerParams(collective_id=5, has_side_effects=True, vmem_limit_bytes=63 * MIB),
        name="attention_backward",
    )(
        states, weights, qkv, factors, y, dy, do, dri, carry, rest, tables, attn_w, attn_mom, mlp_w, mlp_mom,
        gain, start, grad_down, grad_mix, grad_units,
    )


def update_kernel(
    rates, width, ig, hid, ga, gm, gd, sa, sm, wa, ma, aa, wm, mm, am, hs, hm, mr, mo, us, um,
    hid_o, ig_o, ma_o, wa_o, aa_o, mm_o, wm_o, am_o, hm_o, hs_o, mo_o, mr_o, um_o, us_o,
):
    hid_o[0] = hid[...].astype(F32)
    ig_o[0] = ig[...].astype(F32)
    lanes = sm.shape[1]
    cols, units = wa.shape[2], wm.shape[2]

    def matrix(j, grad, total, refs, outs):
        w, m, a = (ref[j] for ref in refs)
        moment, step = stepped(w, m, grad, rates[0])
        new = step * lax.rsqrt(total / width + EPS)
        outs[0][j] = moment
        outs[1][j] = new
        outs[2][j] = AVERAGE * a + (1.0 - AVERAGE) * new

    def wide(row):
        return jnp.concatenate([sm[row + c : row + c + 1] for c in range(units // lanes)], axis=1)

    for j in range(4):
        matrix(j, ga[j], sa[j : j + 1], (wa, ma, aa), (ma_o, wa_o, aa_o))
    for j in range(3):
        matrix(j, gd[...] if j == 2 else gm[j], wide(j * (units // lanes)), (wm, mm, am), (mm_o, wm_o, am_o))

    @pl.when(pl.program_id(0) == 0)
    def _():
        row = 3 * (units // lanes)
        hm_o[...], hs_o[...] = stepped(hs[...], hm[...], sm[row : row + 1, :cols], rates[1])
        mo_o[...], mr_o[...] = stepped(mr[...], mo[...], sm[row + 1 : row + 3], rates[2])
        row += 3
        grad = jnp.concatenate([wide(row), wide(row + units // lanes)], axis=0)
        um_o[...], us_o[...] = stepped(us[...], um[...], grad, rates[3])


def update(input_low, hidden_low, ga, gm, gd, sa, sm, wa, ma, aa, wm, mm, am, hs, hm, mr, mo, us, um, rates):
    length, width = input_low.shape
    rows, cols, units = wa.shape[1], wa.shape[2], wm.shape[2]
    steps = rows // 8
    tall = length // steps

    def whole(shape):
        return pl.BlockSpec(shape, lambda i: (0,) * len(shape))

    state = pl.BlockSpec((tall, width), lambda i: (i, 0))
    state_o = pl.BlockSpec((1, tall, width), lambda i: (0, i, 0))
    attn = pl.BlockSpec((4, 8, cols), lambda i: (0, i, 0))
    mlp = pl.BlockSpec((3, 8, units), lambda i: (0, i, 0))
    small = [whole((1, cols))] * 2 + [whole(mr.shape)] * 2 + [whole(us.shape)] * 2
    return pl.pallas_call(
        functools.partial(update_kernel, rates, width),
        grid=(steps,),
        out_shape=(
            full(1, length, width), full(1, length, width), *(full(*wa.shape),) * 3, *(full(*wm.shape),) * 3,
            *(full(1, cols),) * 2, *(full(*mr.shape),) * 2, *(full(*us.shape),) * 2,
        ),
        in_specs=[
            state, state, attn, pl.BlockSpec((2, 8, units), lambda i: (0, i, 0)), pl.BlockSpec((8, units), lambda i: (i, 0)),
            whole(sa.shape), whole(sm.shape), attn, attn, attn, mlp, mlp, mlp, *small,
        ],
        out_specs=(state_o, state_o, attn, attn, attn, mlp, mlp, mlp, *small),
        compiler_params=pltpu.CompilerParams(vmem_limit_bytes=60 * MIB),
        name="update_weights",
    )(input_low, hidden_low, ga, gm, gd, sa, sm, wa, ma, aa, wm, mm, am, hs, hm, mr, mo, us, um)


def local_fast(
    inputs, doc_ids, out_grad, attn_w, attn_mom, attn_avg, mlp_w, mlp_mom, mlp_avg,
    head_scale, head_mom, mix_rates, mix_mom, unit_scales, unit_mom,
):
    fsdp = lax.axis_size("fsdp")
    root_tokens = math.sqrt(inputs.shape[0] * fsdp * inputs.shape[1])
    rates = tuple(rate / root_tokens for rate in (RATE_WEIGHT, RATE_HEAD, RATE_MIX, RATE_UNITS))
    states, gain = inputs[0], head_scale[None]
    hidden_low, dri, do, dy, w_in, qkv, factors, y, tables, carry, rest, start, grad_mix, grad_units, grad_down = layer(
        attn_w, mlp_w, states, out_grad[0], doc_ids, gain, mix_rates, unit_scales, fsdp
    )
    input_low, grad_attn, grad_mlp, total_attn, total_rest = attention_backward(
        states, w_in, qkv, factors, y, dy, do, dri, carry, rest, tables, attn_w, attn_mom, mlp_w, mlp_mom,
        gain, start, grad_down, grad_mix, grad_units, rates[0], fsdp,
    )
    outs = update(
        input_low, hidden_low, grad_attn, grad_mlp, grad_down, total_attn, total_rest,
        attn_w, attn_mom, attn_avg, mlp_w, mlp_mom, mlp_avg,
        gain, head_mom[None], mix_rates, mix_mom, unit_scales, unit_mom, rates,
    )
    return (*outs[:8], outs[8][0], outs[9][0], *outs[10:])


def local(
    inputs,
    doc_ids,
    out_grad,
    attn_w,
    attn_mom,
    attn_avg,
    mlp_w,
    mlp_mom,
    mlp_avg,
    head_scale,
    head_mom,
    mix_rates,
    mix_mom,
    unit_scales,
    unit_mom,
):
    length = inputs.shape[1]
    model_width = inputs.shape[2]
    head_count = head_scale.shape[0] // HD
    block_rows = min(512, length)
    block_count = length // block_rows
    tokens = inputs.shape[0] * lax.axis_size("fsdp") * length
    doc_row = doc_ids[0]
    input_low = inputs[0]
    resid_in = input_low.astype(jnp.float32)
    cos_table, sin_table = rotary_tables(doc_row)
    position = jnp.arange(length, dtype=jnp.int32)
    attn_full = lax.all_gather(attn_w.astype(jnp.bfloat16), "fsdp", axis=1, tiled=True)
    projected = jnp.einsum(
        "sd,jdc->jsc", input_low, attn_full[:3], preferred_element_type=jnp.float32
    )
    head_gain = head_scale.reshape(head_count, HD)
    q_rot = rotate(projected[0].reshape(length, head_count, HD), cos_table, sin_table)
    k_rot = rotate(projected[1].reshape(length, head_count, HD), cos_table, sin_table)
    q_unit = rms_unit(q_rot)
    k_unit = rms_unit(k_rot)
    query_low = (head_gain * q_unit).astype(jnp.bfloat16)
    key_low = (head_gain * k_unit).astype(jnp.bfloat16)
    value_low = projected[2].reshape(length, head_count, HD).astype(jnp.bfloat16)

    def scores_of(row_first):
        query_blk = lax.dynamic_slice_in_dim(query_low, row_first, block_rows, 0)
        raw_scores = jnp.einsum(
            "qhe,khe->hqk", query_blk, key_low, preferred_element_type=jnp.float32
        )
        row_pos = lax.dynamic_slice_in_dim(position, row_first, block_rows, 0)
        row_docs = lax.dynamic_slice_in_dim(doc_row, row_first, block_rows, 0)
        allowed = (row_docs[:, None] == doc_row[None, :]) & (position[None, :] <= row_pos[:, None])
        return (jnp.where(allowed[None], raw_scores * HD ** (-0.5), NEG_FILL), query_blk)

    def attend(accums, blk_index):
        scores, query_blk = scores_of(blk_index * block_rows)
        peak_val = jnp.max(scores, axis=-1, keepdims=True)
        expo_vals = jnp.exp(scores - peak_val)
        row_total = jnp.sum(expo_vals, axis=-1, keepdims=True)
        probs_low = (expo_vals / row_total).astype(jnp.bfloat16)
        blk_out = jnp.einsum(
            "hqk,khe->qhe", probs_low, value_low, preferred_element_type=jnp.float32
        )
        return (accums, (blk_out, (peak_val + jnp.log(row_total))[..., 0]))

    _, (mixed_blocks, log_totals) = lax.scan(attend, None, jnp.arange(block_count))
    mixed_low = mixed_blocks.reshape(length, head_count * HD).astype(jnp.bfloat16)
    attn_part = jnp.einsum("sc,dc->sd", mixed_low, attn_full[3], preferred_element_type=jnp.float32)
    attn_out = lax.psum(attn_part, "mp")
    attn_unit = rms_unit(attn_out)
    resid_one = resid_in + mix_rates[0] * (attn_unit - resid_in)
    hidden_one = rms_unit(resid_one)
    hidden_low = hidden_one.astype(jnp.bfloat16)
    mlp_full = lax.all_gather(mlp_w.astype(jnp.bfloat16), "fsdp", axis=1, tiled=True)
    gates = jnp.einsum("sd,jdf->jsf", hidden_low, mlp_full[:2], preferred_element_type=jnp.float32)
    up_proj = gates[0]
    gate_proj = gates[1]
    gate_arg = unit_scales[1] * gate_proj * D ** (-0.5)
    gate_sig = jax.nn.sigmoid(gate_arg)
    gate_act = gate_arg * gate_sig
    units_low = (unit_scales[0] * up_proj * gate_act).astype(jnp.bfloat16)
    mlp_part = jnp.einsum("sf,df->sd", units_low, mlp_full[2], preferred_element_type=jnp.float32)
    mlp_out = lax.psum(mlp_part, "mp")
    mlp_unit = rms_unit(mlp_out)
    resid_two = hidden_one + mix_rates[1] * (mlp_unit - hidden_one)
    result = rms_unit(resid_two)
    cotangent = out_grad[0].astype(jnp.float32)
    d_resid_two = rms_back(resid_two, cotangent)
    grad_mix_mlp = jnp.sum(d_resid_two * (mlp_unit - hidden_one), axis=0)
    d_hidden_one = d_resid_two * (1.0 - mix_rates[1])
    d_mlp_low = rms_back(mlp_out, mix_rates[1] * d_resid_two).astype(jnp.bfloat16)
    mlp_back = lax.all_gather(mlp_w.astype(jnp.bfloat16), "fsdp", axis=1, tiled=True)
    d_units = jnp.einsum("sd,df->sf", d_mlp_low, mlp_back[2], preferred_element_type=jnp.float32)
    d_up = d_units * unit_scales[0] * gate_act
    d_arg = d_units * unit_scales[0] * up_proj * gate_sig * (1.0 + gate_arg * (1.0 - gate_sig))
    d_gate = d_arg * unit_scales[1] * D ** (-0.5)
    grad_units = jnp.stack(
        [
            jnp.sum(d_units * up_proj * gate_act, axis=0),
            jnp.sum(d_arg * gate_proj * D ** (-0.5), axis=0),
        ]
    )
    d_gates_low = jnp.stack([d_up, d_gate]).astype(jnp.bfloat16)
    mlp_back_part = jnp.einsum(
        "jsf,jdf->sd", d_gates_low, mlp_back[:2], preferred_element_type=jnp.float32
    )
    d_hidden_one = d_hidden_one + lax.psum(mlp_back_part, "mp")
    right_cols = d_mlp_low
    left_cols = hidden_low
    grad_mlp = jnp.transpose(
        lax.psum_scatter(
            jnp.concatenate(
                [
                    jnp.einsum(
                        "sd,jsf->djf", left_cols, d_gates_low, preferred_element_type=jnp.float32
                    ),
                    jnp.einsum(
                        "sd,sf->df", right_cols, units_low, preferred_element_type=jnp.float32
                    )[:, None, :],
                ],
                axis=1,
            ),
            "fsdp",
            scatter_dimension=0,
            tiled=True,
        ),
        (1, 0, 2),
    )
    d_resid_one = rms_back(resid_one, d_hidden_one)
    grad_mix_attn = jnp.sum(d_resid_one * (attn_unit - resid_in), axis=0)
    d_resid_in = d_resid_one * (1.0 - mix_rates[0])
    d_attn_low = rms_back(attn_out, mix_rates[0] * d_resid_one).astype(jnp.bfloat16)
    attn_back = lax.all_gather(attn_w.astype(jnp.bfloat16), "fsdp", axis=1, tiled=True)
    d_mixed = jnp.einsum("sd,dc->sc", d_attn_low, attn_back[3], preferred_element_type=jnp.float32)
    d_mixed = d_mixed.astype(jnp.bfloat16).reshape(length, head_count, HD)

    def attend_back(accums, blk_index):
        d_key, d_value = accums
        row_first = blk_index * block_rows
        scores, query_blk = scores_of(row_first)
        blk_total = lax.dynamic_index_in_dim(log_totals, blk_index, 0, keepdims=False)
        attn_probs = jnp.exp(scores - blk_total[..., None])
        d_out_blk = lax.dynamic_slice_in_dim(d_mixed, row_first, block_rows, 0)
        d_probs = jnp.einsum(
            "qhe,khe->hqk", d_out_blk, value_low, preferred_element_type=jnp.float32
        )
        d_scores = attn_probs * (d_probs - jnp.sum(attn_probs * d_probs, axis=-1, keepdims=True))
        d_raw_low = (d_scores * HD ** (-0.5)).astype(jnp.bfloat16)
        d_query = jnp.einsum("hqk,khe->qhe", d_raw_low, key_low, preferred_element_type=jnp.float32)
        d_key = d_key + jnp.einsum(
            "hqk,qhe->khe", d_raw_low, query_blk, preferred_element_type=jnp.float32
        )
        d_value = d_value + jnp.einsum(
            "hqk,qhe->khe",
            attn_probs.astype(jnp.bfloat16),
            d_out_blk,
            preferred_element_type=jnp.float32,
        )
        return ((d_key, d_value), d_query)

    zero_heads = jnp.zeros((length, head_count, HD), jnp.float32)
    (d_key_all, d_value_all), d_query_blocks = lax.scan(
        attend_back, (zero_heads, zero_heads), jnp.arange(block_count)
    )
    d_query_all = d_query_blocks.reshape(length, head_count, HD)
    grad_head = jnp.sum(d_query_all * q_unit + d_key_all * k_unit, axis=0).reshape(-1)
    d_query_raw = rotate_back(rms_back(q_rot, head_gain * d_query_all), cos_table, sin_table)
    d_key_raw = rotate_back(rms_back(k_rot, head_gain * d_key_all), cos_table, sin_table)
    d_proj_low = jnp.stack(
        [
            d_query_raw.reshape(length, -1),
            d_key_raw.reshape(length, -1),
            d_value_all.reshape(length, -1),
        ]
    ).astype(jnp.bfloat16)
    grad_mix = jnp.stack([grad_mix_attn, grad_mix_mlp])
    grad_head, grad_mix, grad_units = lax.psum((grad_head, grad_mix, grad_units), "fsdp")
    attn_back_part = jnp.einsum(
        "jsc,jdc->sd", d_proj_low, attn_back[:3], preferred_element_type=jnp.float32
    )
    input_grad = d_resid_in + lax.psum(attn_back_part.astype(jnp.bfloat16), "mp").astype(
        jnp.float32
    )
    left_cols = input_low
    right_cols = d_attn_low
    in_terms = jnp.einsum("sd,jsc->djc", left_cols, d_proj_low, preferred_element_type=jnp.float32)
    out_terms = jnp.einsum("sd,sc->dc", right_cols, mixed_low, preferred_element_type=jnp.float32)
    grad_attn = jnp.transpose(
        lax.psum_scatter(
            jnp.concatenate([in_terms, out_terms[:, None, :]], axis=1),
            "fsdp",
            scatter_dimension=0,
            tiled=True,
        ),
        (1, 0, 2),
    )
    root_tokens = math.sqrt(tokens)
    weight_rate = RATE_WEIGHT / root_tokens
    attn_mom_new, attn_step = nesterov(attn_w, attn_mom, grad_attn, weight_rate)
    mlp_mom_new, mlp_step = nesterov(mlp_w, mlp_mom, grad_mlp, weight_rate)
    attn_squares = jnp.sum(attn_step * attn_step, axis=1)
    mlp_squares = jnp.sum(mlp_step * mlp_step, axis=1)
    attn_squares, mlp_squares = lax.psum((attn_squares, mlp_squares), "fsdp")
    attn_new = attn_step * lax.rsqrt(attn_squares[:, None, :] / model_width + EPS)
    mlp_new = mlp_step * lax.rsqrt(mlp_squares[:, None, :] / model_width + EPS)
    head_mom_new, head_new = nesterov(head_scale, head_mom, grad_head, RATE_HEAD / root_tokens)
    mix_mom_new, mix_new = nesterov(mix_rates, mix_mom, grad_mix, RATE_MIX / root_tokens)
    units_mom_new, units_new = nesterov(unit_scales, unit_mom, grad_units, RATE_UNITS / root_tokens)
    return (
        result[None],
        input_grad[None],
        attn_mom_new,
        attn_new,
        AVERAGE * attn_avg + (1.0 - AVERAGE) * attn_new,
        mlp_mom_new,
        mlp_new,
        AVERAGE * mlp_avg + (1.0 - AVERAGE) * mlp_new,
        head_mom_new,
        head_new,
        mix_mom_new,
        mix_new,
        units_mom_new,
        units_new,
    )


def solution(mesh):
    fsdp = mesh.shape["fsdp"]
    fast = fsdp == 16 and D // fsdp % 16 == 0
    placed = (
        P("fsdp", None, None),
        P("fsdp", None),
        P("fsdp", None, None),
        P(None, "fsdp", "mp"),
        P(None, "fsdp", "mp"),
        P(None, "fsdp", "mp"),
        P(None, "fsdp", "mp"),
        P(None, "fsdp", "mp"),
        P(None, "fsdp", "mp"),
        P("mp"),
        P("mp"),
        P(),
        P(),
        P(None, "mp"),
        P(None, "mp"),
    )
    return jax.shard_map(
        local_fast if fast else local,
        mesh=mesh,
        in_specs=placed,
        out_specs=(
            P("fsdp", None, None),
            P("fsdp", None, None),
            P(None, "fsdp", "mp"),
            P(None, "fsdp", "mp"),
            P(None, "fsdp", "mp"),
            P(None, "fsdp", "mp"),
            P(None, "fsdp", "mp"),
            P(None, "fsdp", "mp"),
            P("mp"),
            P("mp"),
            P(),
            P(),
            P(None, "mp"),
            P(None, "mp"),
        ),
        check_vma=False,
    )
```

```python
import functools
import math

import jax
import jax.numpy as jnp
import numpy as np
from jax import lax
from jax.experimental import pallas as pl
from jax.experimental.pallas import tpu as pltpu
from jax.sharding import PartitionSpec as P

D = 1024
HD = 64


EPS = 1e-06
MOMENTUM = 0.9
AVERAGE = 0.9
NEG_FILL = -1e30
THETA = 10000.0
RATE_WEIGHT = 50.0
RATE_HEAD = 0.08
RATE_MIX = 0.02
RATE_UNITS = 0.5


def rms_unit(vector):
    return vector * lax.rsqrt(jnp.mean(vector * vector, axis=-1, keepdims=True) + EPS)


def rms_back(vector, grad):
    factor = lax.rsqrt(jnp.mean(vector * vector, axis=-1, keepdims=True) + EPS)
    unit_vec = vector * factor
    return factor * (grad - unit_vec * jnp.mean(grad * unit_vec, axis=-1, keepdims=True))


def rotary_tables(doc_row):
    length = doc_row.shape[0]
    position = jnp.arange(length, dtype=jnp.int32)
    boundary = jnp.concatenate(
        [jnp.ones((1,), jnp.int32), (doc_row[1:] != doc_row[:-1]).astype(jnp.int32)]
    )
    doc_start = lax.cummax(jnp.where(boundary > 0, position, 0), axis=0)
    offset = (position - doc_start).astype(jnp.float32)
    freq = THETA ** (-2.0 * jnp.arange(HD // 2, dtype=jnp.float32) / HD)
    angle = offset[:, None] * freq[None, :]
    return (jnp.cos(angle), jnp.sin(angle))


def rotate(vector, cos_table, sin_table):
    half_dim = vector.shape[-1] // 2
    lower_half = vector[..., :half_dim]
    upper_half = vector[..., half_dim:]
    cos_part = cos_table[:, None, :]
    sin_part = sin_table[:, None, :]
    return jnp.concatenate(
        [
            lower_half * cos_part - upper_half * sin_part,
            lower_half * sin_part + upper_half * cos_part,
        ],
        axis=-1,
    )


def rotate_back(grad, cos_table, sin_table):
    half_dim = grad.shape[-1] // 2
    lower_half = grad[..., :half_dim]
    upper_half = grad[..., half_dim:]
    cos_part = cos_table[:, None, :]
    sin_part = sin_table[:, None, :]
    return jnp.concatenate(
        [
            lower_half * cos_part + upper_half * sin_part,
            upper_half * cos_part - lower_half * sin_part,
        ],
        axis=-1,
    )


def nesterov(param, moment, grad, step_rate):
    moment_new = MOMENTUM * moment + grad
    return (moment_new, param - step_rate * (grad + MOMENTUM * moment_new))


BF = jnp.bfloat16
F32 = jnp.float32
MESH = pl.DeviceIdType.MESH
VM = pltpu.VMEM
MIB = 1 << 20
BLOCK = 256
SPAN = 512
ROWS_STEP = 128
UNIT_STEP = 1024


def dot_nn(a, b):
    return lax.dot_general(a, b, (((1,), (0,)), ((), ())), preferred_element_type=F32)


def dot_nt(a, b):
    return lax.dot_general(a, b, (((1,), (1,)), ((), ())), preferred_element_type=F32)


def dot_tn(a, b):
    return lax.dot_general(a, b, (((0,), (0,)), ((), ())), preferred_element_type=F32)


def split_dot(a, ones):
    high = a.astype(BF)
    return dot_nn(high, ones) + dot_nn((a - high.astype(F32)).astype(BF), ones)


def ring_place(index, chips):
    z, y = index // 4, (index // 2) % 2
    return z + y * (chips - 1 - 2 * z), index % 2


def ring_device(place, core, chips):
    y = place // (chips // 2)
    return ((place + y * (chips - 1 - 2 * place)) * 2 + y) * 2 + core


def peers_of(chips):
    index, x = lax.axis_index("fsdp"), lax.axis_index("mp")
    place, core = ring_place(index, chips)
    right = (ring_device((place + 1) % chips, core, chips), x)
    left = (ring_device((place + chips - 1) % chips, core, chips), x)
    return index, x, place, core, right, left, (index + 1 - 2 * core, x), (index, 1 - x)


def greet(peers):
    barrier = pltpu.get_barrier_semaphore()
    for peer in peers:
        pl.semaphore_signal(barrier, inc=1, device_id=peer, device_id_type=MESH)
    pl.semaphore_wait(barrier, len(peers))


def remote(src, dst, send, recv, peer):
    return pltpu.make_async_remote_copy(
        src_ref=src, dst_ref=dst, send_sem=send, recv_sem=recv, device_id=peer, device_id_type=MESH
    )


def start_copy(src, dst, sem):
    copy = pltpu.make_async_copy(src, dst, sem)
    copy.start()
    return copy


def by_step(total, step, body, first=0):
    def run(i, _):
        body(pl.ds(pl.multiple_of(first + i * step, step), step))
        return 0

    lax.fori_loop(0, total // step, run, 0)


def add_all(dst, refs):
    if len(dst.shape) == 3:
        for j in range(dst.shape[0]):
            add_all(dst.at[j], [ref.at[j] for ref in refs])
        return

    def body(r):
        total = refs[0][r].astype(F32)
        for ref in refs[1:]:
            total = total + ref[r].astype(F32)
        dst[r] = total.astype(dst.dtype)

    by_step(dst.shape[0], 16, body)


def ring_hops(chips, group, long_right):
    pair_of = (chips // 2, chips - 1 - chips // 2)
    return pair_of if group in long_right else pair_of[::-1]


class Scatter:
    def __init__(self, chips, long_right, mine, slot, result, sent, send, recv):
        _, _, self.place, self.core, self.right, self.left, _, _ = peers_of(chips)
        self.chips, self.long_right, self.mine, self.slot_at, self.result = chips, long_right, mine, slot, result
        self.send, self.recv, self.sent = send, recv, sent

    def hops(self, group):
        return ring_hops(self.chips, group, self.long_right)

    def term(self, group, way, to_go):
        step = to_go if way == 0 else self.chips - to_go
        return self.mine(group, way, to_go, ring_device((self.place + step) % self.chips, self.core, self.chips) // 2)

    def at(self, group, way, hop):
        return hop - 1 if way == 0 else self.hops(group)[0] + hop - 1

    def slot(self, group, way, hop):
        return self.slot_at(group, self.at(group, way, hop))

    def copy(self, group, way, hop, src):
        at, peer = self.at(group, way, hop), self.right if way == 0 else self.left
        return remote(src, self.slot_at(group, at), self.send.at[group], self.recv.at[group, at], peer)

    def go(self, group, way, hop, src):
        self.copy(group, way, hop, src).start()

    def launch(self, group):
        for way in (0, 1):
            self.go(group, way, 1, self.term(group, way, self.hops(group)[way]))

    def take(self, group, way, hop):
        here = self.slot(group, way, hop)
        self.copy(group, way, hop, here).wait_recv()
        return here

    def tick(self, group, hop):
        hops = self.hops(group)
        for way in (0, 1):
            if hop > hops[way]:
                continue
            here = self.take(group, way, hop)
            if hop < hops[way]:
                add_all(here, [here, self.term(group, way, hops[way] - hop)])
                self.go(group, way, hop + 1, here)
        if hop == self.chips // 2:
            ends = [self.slot(group, way, hops[way]) for way in (0, 1)]
            add_all(self.result(group), [self.term(group, 0, 0)] + ends)

    def close(self):
        for group in range(self.send.shape[0]):
            ref = self.sent(group)
            remote(ref, ref, self.send.at[group], self.send.at[group], self.right).wait_send()


def head_ones():
    row = lax.broadcasted_iota(jnp.int32, (128, 128), 0) // HD
    col = lax.broadcasted_iota(jnp.int32, (128, 128), 1) // HD
    return jnp.where(row == col, 1.0, 0.0).astype(BF)


def half_of(rows, half):
    lane = lax.broadcasted_iota(jnp.int32, (rows, 128), 1)
    return jnp.where((lane < HD) == (half == 0), 1.0, 0.0).astype(BF)


def other_half(v):
    lane = lax.broadcasted_iota(jnp.int32, v.shape, 1)
    return jnp.where(lane % HD < HD // 2, pltpu.roll(v, 128 - HD // 2, 1), pltpu.roll(v, HD // 2, 1))


def first_key(block):
    return max(0, block * BLOCK - SPAN)


def low(*shape):
    return jax.ShapeDtypeStruct(shape, BF)


def full(*shape):
    return jax.ShapeDtypeStruct(shape, F32)


GATHER_LONG = (0, 2, 4)
FEED_LONG = (0, 1)


def row_factor(v):
    return lax.rsqrt(jnp.mean(v * v, axis=-1, keepdims=True) + EPS)


def unit_back(factor, unit, grad):
    return factor * (grad - unit * jnp.mean(grad * unit, axis=-1, keepdims=True))


def fold(v):
    return jnp.sum(v.reshape(v.shape[0] // 8, 8, v.shape[1]), axis=0)


def feed_chunks(length):
    half = BLOCK // 2
    return [(0, half)] + [(start, BLOCK) for start in range(half, length - half, BLOCK)] + [(length - half, half)]


def layer_kernel(
    chips, attn_hbm, mlp_hbm, x_hbm, og_hbm, doc_ref, gain_ref, freq_ref, mix_ref, us_ref,
    out_o, dri_o, do_o, dy_o, w_o, qkv_o, r_o, y_o, tables_o, carry_o, rest_o, start_o, mix_o, us_o, gd_o,
    start_s, mix_s, us_s, gd_s, x_ref, y_ref, wo_s, wu_s, wg_s, wd_s, o_s, hb_s, u_s, g_s, hid_s, dm_s, dh_s, own_s, got_m, got_d, wd_g, ring_d, ring_n,
    load, store, save, rest_save, small_save, send_y, recv_y, wo_send, wo_recv, wo_near, send_m, recv_m, send_d, recv_d,
    gather_send, gather_recv, near_send, near_recv, own_sem, pair_free, pair_send, pair_recv, ring_send, ring_recv,
):
    index, x, place, core, right, left, pair, across = peers_of(chips)
    pair_index = pair[0]
    length, width = x_ref.shape
    cols, units = y_ref.shape[2], us_ref.shape[1]
    rows_own = width // (2 * chips)
    blocks = length // BLOCK
    chunks = feed_chunks(length)
    number = len(chunks)
    longest = chips // 2

    wide = 3 * cols
    loads_attn = [
        start_copy(attn_hbm.at[j], o_s.at[pl.ds(j * rows_own, rows_own), pl.ds(0, cols)], load.at[j]) for j in range(4)
    ]
    halves = units // width
    loads_mlp = [
        start_copy(
            mlp_hbm.at[j, :, pl.ds(h * width, width)],
            o_s.at[pl.ds((4 + j * halves + h) * rows_own, rows_own)], load.at[4 + j * halves + h],
        )
        for j in range(3)
        for h in range(halves)
    ]
    load_x = start_copy(x_hbm, x_ref, load.at[4 + 3 * halves])
    load_og = start_copy(og_hbm, dm_s, load.at[5 + 3 * halves])

    def own(group):
        if group == 0:
            return wd_g.at[pl.ds(0, rows_own), pl.ds(0, wide)]
        if group == 1:
            return wd_g.at[pl.ds(0, rows_own), pl.ds(wide, cols)]
        return wd_g.at[pl.ds((group - 1) * rows_own, rows_own)]

    def block_of(group, dev):
        r = pl.ds(pl.multiple_of(dev * rows_own, rows_own), rows_own)
        if group == 0:
            return g_s.at[r, pl.ds(0, wide)]
        if group == 1:
            return wo_s.at[x, r]
        return (wu_s, wg_s, wd_s)[group - 2].at[r]

    def counts(group):
        return ring_hops(chips, group, GATHER_LONG)

    def origin(way, hop):
        there = (place + chips - hop) % chips if way == 0 else (place + hop) % chips
        return ring_device(there, core, chips)

    def gather_copy(group, way, hop, src, dst):
        peer = right if way == 0 else left
        return remote(src, dst, gather_send.at[group], gather_recv.at[group, way, hop - 1], peer)

    def near_copy(group, src, dev):
        return remote(src, block_of(group, dev), near_send.at[group], near_recv.at[group], pair)

    def blocks_of(group, count):
        r = pl.ds(0, count * rows_own)
        if group == 0:
            return g_s.at[r, pl.ds(0, wide)]
        return wo_s.at[x, r] if group == 1 else (wu_s, wg_s, wd_s)[group - 2].at[r]

    owns = []

    def launch(group):
        for way in (0, 1):
            gather_copy(group, way, 1, own(group), block_of(group, index)).start()
        near_copy(group, own(group), index).start()
        owns.append(start_copy(own(group), block_of(group, index), own_sem.at[group]))

    def tick(group, hop):
        for way in (0, 1):
            if hop > counts(group)[way]:
                continue
            dev = origin(way, hop)
            here = block_of(group, dev)
            gather_copy(group, way, hop, here, here).wait_recv()
            if hop < counts(group)[way]:
                gather_copy(group, way, hop + 1, here, here).start()
            near_copy(group, here, dev).start()

    def await_all(group):
        owns[group].wait()
        ref = blocks_of(group, chips)
        remote(ref, ref, near_send.at[group], near_recv.at[group], pair).wait_recv()

    def await_sends(group):
        ref = blocks_of(group, chips - 1)
        remote(ref, ref, gather_send.at[group], gather_send.at[group], right).wait_send()
        ref = blocks_of(group, chips)
        remote(ref, ref, near_send.at[group], near_recv.at[group], pair).wait_send()

    for j, copy in enumerate(loads_attn):
        copy.wait()
        wd_g[0:rows_own, j * cols : (j + 1) * cols] = o_s[j * rows_own : (j + 1) * rows_own, 0:cols].astype(BF)
    greet((right, left, pair, across))
    launch(0)
    launch(1)
    for j in range(3):
        for h in range(halves):
            loads_mlp[j * halves + h].wait()
            first = (4 + j * halves + h) * rows_own
            wd_g[(j + 1) * rows_own : (j + 2) * rows_own, h * width : (h + 1) * width] = o_s[
                first : first + rows_own
            ].astype(BF)
    doc = doc_ref[...]
    start = jnp.zeros(doc.shape, F32)
    for value in range(3):
        count = jnp.sum(jnp.where(doc == value, 1.0, 0.0), axis=1, keepdims=True)
        start = start + jnp.where(doc > value, count, 0.0)
    start_s[...] = start.astype(jnp.int32)
    dh_s[:, 256:384] = jnp.transpose(jnp.broadcast_to(start, (128, length)))

    def tables(block):
        rows = pl.ds(block * BLOCK, BLOCK)
        position = (lax.broadcasted_iota(jnp.int32, (BLOCK, 128), 0) + block * BLOCK).astype(F32)
        angle = (position - dh_s[rows, 256:384]) * freq_ref[...]
        lane = lax.broadcasted_iota(jnp.int32, (BLOCK, 128), 1)
        dh_s[rows, 0:128] = jnp.cos(angle)
        dh_s[rows, 128:256] = jnp.where(lane % HD < HD // 2, -1.0, 1.0) * jnp.sin(angle)

    for block in range(blocks // 2):
        tables(block)
    tick(0, 1)
    tick(1, 1)
    for block in range(blocks // 2, blocks):
        tables(block)
    stores = [start_copy(dh_s.at[:, pl.ds(0, 256)], tables_o, store.at[0])]
    stores.append(start_copy(start_s, start_o, small_save.at[0]))
    tick(0, 2)
    launch(2)
    tick(1, 2)
    tick(0, 3)
    tick(2, 1)
    tick(1, 3)
    launch(3)
    tick(0, 4)
    pending = [
        (2, 2), (1, 4), (3, 1), (2, 3), (4, 1), (3, 2), (2, 4), (4, 2), (3, 3), (4, 3), (3, 4), (4, 4),
    ]
    ones = head_ones()
    load_x.wait()
    await_all(0)
    held = [start_copy(g_s.at[:, pl.ds(0, wide)], w_o, store.at[1])]

    def project(i, _):
        rows = pl.ds(pl.multiple_of(i * BLOCK, BLOCK), BLOCK)
        states = x_ref[rows]
        cos, sin = dh_s[rows, 0:128], dh_s[rows, 128:256]
        for j, scale in enumerate((HD**-0.5, 1.0)):
            raw = dot_nn(states, g_s[:, j * cols : (j + 1) * cols])
            for c in range(0, cols, 128):
                part = raw[:, c : c + 128]
                factor = lax.rsqrt(split_dot(part * part, ones) * (1.0 / HD) + EPS)
                unit = (part * cos + other_half(part) * sin) * factor
                at = slice(j * cols + c, j * cols + c + 128)
                u_s[rows, at] = ((gain_ref[:, c : c + 128] * unit).astype(BF).astype(F32) * scale).astype(BF)
                hid_s[rows, at] = factor.astype(BF)
        u_s[rows, 2 * cols : wide] = dot_nn(states, g_s[:, 2 * cols : wide]).astype(BF)
        return 0

    lax.fori_loop(0, blocks // 2, project, 0)
    tick(*pending.pop(0))
    launch(4)
    tick(*pending.pop(0))
    await_all(1)
    part = width // 2

    def wo_half(half, side, send, recv, peer):
        there = wo_s.at[side, pl.ds(pl.multiple_of(half * part, part), part)]
        return remote(there, there, send, recv, peer)

    wo_copy = wo_half(core, x, wo_send, wo_recv, across)
    wo_copy.start()
    lax.fori_loop(blocks // 2, blocks, project, 0)
    held.append(start_copy(u_s.at[:, pl.ds(0, wide)], qkv_o, store.at[2]))
    held.append(start_copy(hid_s.at[:, pl.ds(0, 2 * cols)], r_o, store.at[3]))
    tick(*pending.pop(0))
    copies_y = []
    for block in range(blocks):
        first = first_key(block)
        keys = (block + 1) * BLOCK - first
        rows = pl.ds(block * BLOCK, BLOCK)
        span = pl.ds(first, keys)
        bias = o_s.at[pl.ds(0, BLOCK), pl.ds(0, keys)]
        kpos = (lax.broadcasted_iota(jnp.int32, (BLOCK, keys), 1) + first).astype(F32)
        qpos = (lax.broadcasted_iota(jnp.int32, (BLOCK, keys), 0) + block * BLOCK).astype(F32)
        allowed = (kpos >= dh_s[rows, 256:257]) & (kpos <= qpos)
        bias[...] = jnp.where(allowed, 0.0, NEG_FILL)

        def heads(pair_of, _):
            c = pl.multiple_of(pair_of * 128, 128)
            q = u_s[rows, pl.ds(c, 128)]
            k = u_s[span, pl.ds(cols + c, 128)]
            v = u_s[span, pl.ds(2 * cols + c, 128)]
            results = []
            for half in (0, 1):
                scores = dot_nt(q * half_of(BLOCK, half), k)
                probs = jnp.exp(scores + bias[...]).astype(BF)
                results.append(dot_nn(probs, v * half_of(keys, half) + half_of(keys, 1 - half)))
            lane = lax.broadcasted_iota(jnp.int32, (BLOCK, 128), 1)
            total = pltpu.roll(jnp.where(lane < HD, results[1], results[0]), HD, 1)
            y_ref[x, rows, pl.ds(c, 128)] = (jnp.where(lane < HD, results[0], results[1]) / total).astype(BF)
            return 0

        lax.fori_loop(0, cols // 128, heads, 0)
        copy = remote(y_ref.at[x, rows], y_ref.at[x, rows], send_y.at[block], recv_y.at[block], across)
        copy.start()
        copies_y.append(copy)
        stores.append(start_copy(y_ref.at[x, rows], y_o.at[rows], store.at[4 + block]))
        tick(*pending.pop(0))
        if block == 1:
            wo_half(core, 1 - x, wo_send, wo_recv, across).wait_recv()
            wo_pass = wo_half(core, 1 - x, wo_near.at[0], wo_near.at[1], pair)
            wo_pass.start()

    copies_m, copies_d = {}, {}
    here_y = []

    def await_y(rows_end):
        while len(here_y) * BLOCK < rows_end:
            block = len(here_y)
            there = y_ref.at[1 - x, pl.ds(block * BLOCK, BLOCK)]
            remote(there, there, send_y.at[block], recv_y.at[block], across).wait_recv()
            here_y.append(block)

    def first_half(r):
        states = x_ref[r].astype(F32)
        o = o_s[r]
        ro = row_factor(o)
        uo = o * ro
        mix = mix_ref[0:1]
        r1 = states + mix * (uo - states)
        rr = row_factor(r1)
        return states, ro, uo, rr, r1 * rr

    def by_rows(chunk, body, init):
        start, size = chunks[chunk]
        for i in range(size // ROWS_STEP):
            init = body(pl.ds(start + i * ROWS_STEP, ROWS_STEP), init)
        return init

    def mixed(chunk):
        start, size = chunks[chunk]
        rows = pl.ds(start, size)
        await_y(start + size)

        def out_proj(c):
            o_s[rows, c] = dot_nt(y_ref[0, rows], wo_s[0, c]) + dot_nt(y_ref[1, rows], wo_s[1, c])

        by_step(width, 512, out_proj)

        def hidden(r, _):
            hb_s[r] = first_half(r)[4].astype(BF)
            return 0

        by_rows(chunk, hidden, 0)

    def gates(chunk):
        rows = pl.ds(*chunks[chunk])

        def gate(f):
            up = dot_nn(hb_s[rows], wu_s[:, f])
            gt = dot_nn(hb_s[rows], wg_s[:, f])
            arg = us_ref[1:2, f] * gt * D**-0.5
            sig = 1.0 / (1.0 + jnp.exp(-arg))
            u_s[rows, f] = up.astype(BF)
            g_s[rows, f] = gt.astype(BF)
            hid_s[rows, f] = (us_ref[0:1, f] * up * (arg * sig)).astype(BF)

        by_step(units, UNIT_STEP, gate)

    def down(chunk):
        rows = pl.ds(*chunks[chunk])

        def body(c):
            own_s[rows, c] = dot_nt(hid_s[rows], wd_s[c]).astype(BF)

        by_step(width, 512, body)
        copies_m[chunk] = remote(own_s.at[rows], got_m.at[rows], send_m.at[chunk], recv_m.at[chunk], across)
        copies_m[chunk].start()

    def turn(chunk, mix_m):
        rows = pl.ds(*chunks[chunk])
        copies_m[chunk].wait()

        def middle(r, total):
            h1 = first_half(r)[4]
            m = own_s[r].astype(F32) + got_m[r].astype(F32)
            rm = row_factor(m)
            um = m * rm
            mix = mix_ref[1:2]
            r2 = h1 + mix * (um - h1)
            rr = row_factor(r2)
            out = r2 * rr
            got_m[r] = out.astype(BF)
            dr2 = unit_back(rr, out, dm_s[r].astype(F32))
            dm_s[r] = unit_back(rm, um, mix * dr2).astype(BF)
            dh_s[r] = dr2 * (1.0 - mix)
            return total + fold(dr2 * (um - h1))

        mix_m = by_rows(chunk, middle, mix_m)
        start_copy(got_m.at[rows], out_o.at[rows], save.at[3])
        return mix_m

    def gates_back(chunk):
        rows = pl.ds(*chunks[chunk])

        def gate_back(f):
            dhid = dot_nn(dm_s[rows], wd_s[:, f])
            up, gt = u_s[rows, f].astype(F32), g_s[rows, f].astype(F32)
            su, sv = us_ref[0:1, f], us_ref[1:2, f]
            arg = sv * gt * D**-0.5
            sig = 1.0 / (1.0 + jnp.exp(-arg))
            act = dhid * (arg * sig)
            darg = dhid * su * up * sig * (1.0 + arg * (1.0 - sig))
            us_s[0:1, f] = us_s[0:1, f] + jnp.sum(act * up, axis=0, keepdims=True)
            us_s[1:2, f] = us_s[1:2, f] + jnp.sum(darg * gt, axis=0, keepdims=True) * D**-0.5
            u_s[rows, f] = (act * su).astype(BF)
            g_s[rows, f] = (darg * sv * D**-0.5).astype(BF)

        by_step(units, UNIT_STEP, gate_back)

    def ups_back(chunk):
        rows = pl.ds(*chunks[chunk])

        def up_back(c):
            own_s[rows, c] = (dot_nt(u_s[rows], wu_s[c]) + dot_nt(g_s[rows], wg_s[c])).astype(BF)

        by_step(width, 512, up_back)
        copies_d[chunk] = remote(own_s.at[rows], got_d.at[rows], send_d.at[chunk], recv_d.at[chunk], across)
        copies_d[chunk].start()

    def back(chunk):
        gates_back(chunk)
        ups_back(chunk)

    near_s = (hid_s, u_s, g_s)

    def grads_of(j, weight_s, left_s, first, rows):
        tokens = pl.ds(first, rows)

        def grads(d):
            for u in range(0, units, 1024):
                f = pl.ds(u, 1024)
                total = dot_tn(left_s[tokens, d], near_s[j][tokens, f])
                if first:
                    total = total + weight_s[d, f].astype(F32)
                weight_s[d, f] = total.astype(BF)

        return grads

    def weight_grads(j, weight_s, left_s, midway=None, first=0):
        right_s = near_s[j]
        grads = grads_of(j, weight_s, left_s, first, length - first)
        by_step(width // 2, BLOCK, grads)
        if midway is not None:
            midway()
        by_step(width // 2, BLOCK, grads, width // 2)
        pl.semaphore_signal(pair_free.at[j], inc=1, device_id=pair, device_id_type=MESH)
        pl.semaphore_wait(pair_free.at[j], 1)
        for chip in range(chips):
            there = pl.multiple_of((chip * 2 + 1 - core) * rows_own, rows_own)
            copy = remote(
                weight_s.at[pl.ds(there, rows_own)], right_s.at[pl.ds(chip * rows_own, rows_own)],
                pair_send.at[j], pair_recv.at[j], pair,
            )
            copy.start()

    def pair_sums(j, weight_s):
        ref = near_s[j].at[pl.ds(0, chips * rows_own)]
        remote(ref, ref, pair_send.at[j], pair_recv.at[j], pair).wait()
        for chip in range(chips):
            base = pl.multiple_of((chip * 2 + core) * rows_own, rows_own)
            here = near_s[j].at[pl.ds(chip * rows_own, rows_own)]
            add_all(here, [here, weight_s.at[pl.ds(base, rows_own)]])

    def summed(group, way, to_go, chip):
        return near_s[group].at[pl.ds(pl.multiple_of(chip * rows_own, rows_own), rows_own)]

    def ring_slot(group, at):
        return ring_d.at[at] if group == 0 else ring_n.at[0 if at == 0 else 1]

    scatter = Scatter(
        chips, FEED_LONG, summed, ring_slot, lambda group: gd_s,
        lambda group: ring_d if group == 0 else ring_n, ring_send, ring_recv,
    )

    def hand_on():
        for way in (0, 1):
            here = scatter.take(1, way, 1)
            add_all(here, [here, scatter.term(1, way, scatter.hops(1)[way] - 1)])
            start_copy(here, carry_o.at[0, way], rest_save.at[0, 0])

    def hand_rest(group):
        hops = scatter.hops(group)
        far = 0 if hops[0] > hops[1] else 1
        for at, (way, to_go) in enumerate(((far, 1), (far, 2), (far, 3), (1 - far, 1), (1 - far, 2), (0, 0))):
            start_copy(scatter.term(group, way, to_go), rest_o.at[group - 1, at], rest_save.at[1, group - 1])
        if group == 2:
            for way in (0, 1):
                start_copy(scatter.term(group, way, hops[way]), carry_o.at[1, way], rest_save.at[0, 1])

    def last(chunk, mix_a):
        rows = pl.ds(*chunks[chunk])
        copies_d[chunk].wait()

        def body(r, total):
            states, ro, uo, rr, h1 = first_half(r)
            mix = mix_ref[0:1]
            dr1 = unit_back(rr, h1, dh_s[r] + (own_s[r].astype(F32) + got_d[r].astype(F32)))
            dh_s[r] = dr1 * (1.0 - mix)
            dm_s[r] = unit_back(ro, uo, mix * dr1).astype(BF)
            return total + fold(dr1 * (uo - states))

        mix_a = by_rows(chunk, body, mix_a)
        y_ref[1 - x, rows] = dot_nn(dm_s[rows], wo_s[x]).astype(BF)
        for j, (src, dst) in enumerate(((y_ref.at[1 - x], dy_o), (dm_s, do_o), (dh_s, dri_o))):
            start_copy(src.at[rows], dst.at[rows], save.at[j])
        return mix_a

    wo_half(1 - core, 1 - x, wo_near.at[0], wo_near.at[1], pair).wait_recv()
    for chunk in range(number):
        mixed(chunk)
        if len(pending) > 2:
            tick(*pending.pop(0))
    for copy in held:
        copy.wait()
    await_sends(0)
    while len(pending) > 1:
        tick(*pending.pop(0))
    await_all(2)
    await_all(3)
    gates(0)
    tick(*pending.pop(0))
    await_all(4)
    for chunk in range(number):
        down(chunk)
        if chunk < number - 1:
            gates(chunk + 1)
        if chunk == 0:
            for group in range(1, 5):
                await_sends(group)
    mix_m = jnp.zeros((8, width), F32)
    us_s[...] = jnp.zeros_like(us_s)
    load_og.wait()
    stores[0].wait()
    for chunk in range(number - 2):
        mix_m = turn(chunk, mix_m)
        back(chunk)
    here = chunks[number - 2][0]
    by_step(width, BLOCK, grads_of(0, wd_g, dm_s, 0, here))
    mix_m = turn(number - 2, mix_m)
    mix_m = turn(number - 1, mix_m)
    mix_s[1:2] = jnp.sum(mix_m, axis=0, keepdims=True)
    weight_grads(0, wd_g, dm_s, None, here)
    gates_back(number - 2)
    pair_sums(0, wd_g)
    scatter.launch(0)
    ups_back(number - 2)
    back(number - 1)
    stores.append(start_copy(us_s, us_o, small_save.at[1]))
    scatter.tick(0, 1)
    weight_grads(1, wu_s, hb_s)

    def up_ring():
        scatter.tick(0, 2)
        pair_sums(1, wu_s)
        scatter.launch(1)
        hand_rest(1)

    weight_grads(2, wg_s, hb_s, up_ring)
    wo_copy.wait_send()
    wo_pass.wait_send()
    for copy in copies_y:
        copy.wait_send()
    mix_a = jnp.zeros((8, width), F32)
    for chunk in range(number):
        mix_a = last(chunk, mix_a)
        if chunk == 1:
            scatter.tick(0, 3)
            pair_sums(2, wg_s)
            hand_rest(2)
        if chunk == number - 3:
            hand_on()
        if chunk == number - 2:
            scatter.tick(0, 4)
            stores.append(start_copy(gd_s, gd_o, small_save.at[2]))
    mix_s[0:1] = jnp.sum(mix_a, axis=0, keepdims=True)
    stores.append(start_copy(mix_s, mix_o, small_save.at[3]))
    for copy in stores[1:]:
        copy.wait()
    for j, (src, dst) in enumerate(((y_ref.at[1 - x], dy_o), (dm_s, do_o), (dh_s, dri_o), (got_m, out_o))):
        pltpu.make_async_copy(src, dst, save.at[j]).wait()
    for j in range(2):
        pltpu.make_async_copy(carry_o.at[j], carry_o.at[j], rest_save.at[0, j]).wait()
        pltpu.make_async_copy(rest_o.at[j], rest_o.at[j], rest_save.at[1, j]).wait()
    scatter.close()


def layer(attn_w, mlp_w, states, out_grad, doc, gain, mix, scales, fsdp):
    chips = fsdp // 2
    length, width = states.shape
    cols, units, rows = attn_w.shape[2], mlp_w.shape[2], attn_w.shape[1]
    vspec, anyspec = pl.BlockSpec(memory_space=VM), pl.BlockSpec(memory_space=pl.ANY)
    blocks, number = length // BLOCK, len(feed_chunks(length))
    sem = pltpu.SemaphoreType.DMA
    freq = np.asarray(THETA ** (-2.0 * (np.arange(128) % (HD // 2)) / HD), np.float32)
    square, wide, weight, tall = VM((length, width), BF), VM((length, units), BF), VM((width, units), BF), VM((length, width), F32)
    return pl.pallas_call(
        functools.partial(layer_kernel, chips),
        out_shape=(
            low(length, width), full(length, width), low(length, width), low(length, cols),
            low(width, 3 * cols), low(length, 3 * cols), low(length, 2 * cols), low(length, cols), full(length, 256),
            low(2, 2, rows, units), low(2, 6, rows, units),
            jax.ShapeDtypeStruct((1, length), jnp.int32), full(2, width), full(2, units), full(rows, units),
        ),
        in_specs=[anyspec] * 4 + [vspec] * 5,
        out_specs=(anyspec,) * 15,
        scratch_shapes=[
            VM((1, length), jnp.int32), VM((2, width), F32), VM((2, units), F32), VM((rows, units), F32),
            square, VM((2, length, cols), BF), VM((2, width, cols), BF), weight, weight, weight,
            tall, square, wide, wide, wide, square, tall, square, square, square, weight,
            VM((chips - 1, rows, units), BF), VM((2, rows, units), BF),
            sem((6 + 3 * (units // width),)), sem((4 + blocks,)), sem((4,)), sem((2, 2)),
            sem((4,)), sem((blocks,)), sem((blocks,)), sem, sem, sem((2,)), sem((number,)), sem((number,)), sem((number,)), sem((number,)),
            sem((5,)), sem((5, 2, chips // 2)), sem((5,)), sem((5,)), sem((5,)),
            pltpu.SemaphoreType.REGULAR((3,)), sem((3,)), sem((3,)), sem((2,)), sem((2, chips - 1)),
        ],
        compiler_params=pltpu.CompilerParams(collective_id=6, has_side_effects=True, vmem_limit_bytes=63 * MIB),
        name="layer",
    )(attn_w, mlp_w, states, out_grad, doc, gain, freq[None], mix, scales)


SCATTER_LONG = (0, 3, 5)
MATRIX_OF = {2: 3, 3: 2, 4: 1, 5: 0}


def back_pieces(length):
    half = BLOCK // 2
    return [(length - half, half), (length - BLOCK, half)] + [(start, BLOCK) for start in range(length - 2 * BLOCK, -1, -BLOCK)]


def stepped(param, moment, grad, rate):
    moment_new = MOMENTUM * moment + grad
    return moment_new, param - rate * (grad + MOMENTUM * moment_new)


def backward_kernel(
    rate, x_hbm, w_hbm, qkv_hbm, r_hbm, y_hbm, dy_hbm, do_hbm, dri_hbm, carry_hbm, rest_hbm, tables_hbm,
    wa_hbm, ma_hbm, wm_hbm, mm_hbm, gain_ref, start_ref, gd_ref, mix_ref, us_ref,
    ig_o, ga_o, gm_o, sum_a_o, sum_m_o,
    ga_s, gm_s, x_ref, w_ref, qkv_ref, r_ref, y_ref, dy_ref, do_ref, carry, rest, tables_ref, dri_s,
    wa_ref, ma_ref, wm_ref, mm_ref,
    bias, dq_s, dk_s, dv_s, low_s, out_s, in_s, dw_s, near, ring_a, ring_m, head_s, mine_a, got_a, mine_m, got_m,
    load, load_dri, store, save, send, recv, pair_send, pair_recv, ring_send, ring_recv, all_send, all_recv,
):
    chips, rows_own = near.shape[1:3]
    index, x, place, core, right, left, pair, across = peers_of(chips)
    length, cols = y_ref.shape
    width = x_ref.shape[1]
    parts = back_pieces(length)
    blocks = len(parts)
    stages = got_m.shape[0]
    others = [(ring_device((place + d) % chips, core, chips), x) for d in range(1, chips)]
    turns = [(index + (1 << s) * (1 - 2 * ((index // (1 << s)) % 2)), x) for s in range(stages)]
    pieces = (
        (carry_hbm, carry), (qkv_hbm, qkv_ref), (dy_hbm, dy_ref), (y_hbm, y_ref),
        (tables_hbm, tables_ref), (r_hbm, r_ref), (w_hbm, w_ref), (rest_hbm, rest),
        (do_hbm, do_ref), (x_hbm, x_ref), (wm_hbm, wm_ref), (mm_hbm, mm_ref), (wa_hbm, wa_ref), (ma_hbm, ma_ref),
    )
    loads = [start_copy(src, dst, load.at[j]) for j, (src, dst) in enumerate(pieces)]
    greet([pair, across] + others)

    def mine(group, way, to_go, chip):
        if group < 2:
            wide_way = 0 if group in SCATTER_LONG else 1
            return rest.at[group, 5 if to_go == 0 else to_go - 1 if way == wide_way else 2 + to_go]
        return near.at[MATRIX_OF[group], chip]

    def slot(group, at):
        if group < 2:
            return ring_m.at[group, at]
        return ring_a.at[at, MATRIX_OF[group]]

    def result(group):
        return gm_s.at[group] if group < 2 else ga_s.at[MATRIX_OF[group]]

    def sent(group):
        return ring_m.at[group, pl.ds(0, chips - 3 + 2 * group)] if group < 2 else ring_a.at[:, MATRIX_OF[group]]

    scatter = Scatter(chips, SCATTER_LONG, mine, slot, result, sent, ring_send, ring_recv)
    tick, launch = scatter.tick, scatter.launch

    def send_pair(j):
        for chip in range(chips):
            there = pl.multiple_of((chip * 2 + 1 - core) * rows_own, rows_own)
            remote(dw_s.at[j, pl.ds(there, rows_own)], near.at[j, chip], pair_send.at[j], pair_recv.at[j], pair).start()

    def sum_pair(j):
        remote(near.at[j], near.at[j], pair_send.at[j], pair_recv.at[j], pair).wait()
        for chip in range(chips):
            own = pl.ds(pl.multiple_of((chip * 2 + core) * rows_own, rows_own), rows_own)
            here = near.at[j, chip]
            add_all(here, [here, dw_s.at[j, own]])

    loads[0].wait()
    for group in (0, 1):
        for way in (0, 1):
            scatter.go(group, way, 2 - group, carry.at[group, way])
    dk_s[...] = jnp.zeros_like(dk_s)
    dv_s[...] = jnp.zeros_like(dv_s)
    head_s[...] = jnp.zeros_like(head_s)
    ones = head_ones()
    copies, stores = {}, []

    def fetch_dri(block):
        start, size = parts[block]
        return start_copy(dri_hbm.at[pl.ds(start, size)], dri_s.at[block % 2, pl.ds(0, size)], load_dri.at[block])

    fetched = {block: fetch_dri(block) for block in (0, 1)}

    def finish_input(block):
        start, size = parts[block]
        copies[block].wait()
        fetched[block].wait()
        for i in range(0, size, 128):
            r = pl.ds(start + i, 128)
            total = out_s[r].astype(F32) + in_s[r].astype(F32)
            out_s[r] = (dri_s[block % 2, pl.ds(i, 128)] + total).astype(BF)
        rows = pl.ds(start, size)
        stores.append(start_copy(out_s.at[rows], ig_o.at[rows], store.at[block]))
        if block + 2 < blocks:
            fetched[block + 2] = fetch_dri(block + 2)

    for copy in loads[1:4]:
        copy.wait()

    def attend(block):
        start, size = parts[block]
        first = max(0, start - SPAN)
        keys = start + size - first
        rows = pl.ds(start, size)
        span = pl.ds(first, keys)
        kpos = lax.broadcasted_iota(jnp.int32, (keys, size), 0) + first
        qpos = lax.broadcasted_iota(jnp.int32, (keys, size), 1) + start
        allowed = (kpos >= start_ref[:, start : start + size]) & (kpos <= qpos)
        bias[:keys, :size] = jnp.where(allowed, 0.0, NEG_FILL)

        def heads(pair_of, _):
            at = pl.multiple_of(pair_of * 128, 128)
            c = pl.ds(at, 128)
            q, dy = qkv_ref[rows, c], dy_ref[rows, c]
            k, v = qkv_ref[span, pl.ds(cols + at, 128)], qkv_ref[span, pl.ds(2 * cols + at, 128)]
            prod = dy.astype(F32) * y_ref[rows, c].astype(F32)
            prod_high = prod.astype(BF)
            prod_low = (prod - prod_high.astype(F32)).astype(BF)
            dq = jnp.zeros((size, 128), F32)
            dk = jnp.zeros((keys, 128), F32)
            dv = jnp.zeros((keys, 128), F32)
            for half in (0, 1):
                mask, row = half_of(size, half), half_of(8, half)
                qm, dym, km = q * mask, dy * mask, k * half_of(keys, half)
                expo = jnp.exp(dot_nt(k, qm) + bias[:keys, :size])
                probs = expo * (1.0 / jnp.sum(expo, axis=0, keepdims=True))
                delta = (dot_nt(row, prod_high) + dot_nt(row, prod_low))[0:1]
                dz = (probs * (dot_nt(v, dym) - delta)).astype(BF)
                dk = dk + dot_nn(dz, qm)
                dv = dv + dot_nn(probs.astype(BF), dym)
                dq = dq + dot_tn(dz, km)
            dq_s[rows, c] = dq * HD**-0.5
            dk_s[span, c] = dk_s[span, c] + dk
            dv_s[span, c] = dv_s[span, c] + dv
            return 0

        return heads

    def project_back(block):
        start, size = parts[block]
        rows = pl.ds(start, size)
        cos, sin = tables_ref[rows, 0:128], tables_ref[rows, 128:256]
        for c in range(0, cols, 128):
            s = slice(c, c + 128)
            gain = gain_ref[:, s]
            head = jnp.zeros((size, 128), F32)
            for j, (grad_s, scale) in enumerate(((dq_s, HD**0.5), (dk_s, 1.0))):
                at = slice(j * cols + c, j * cols + c + 128)
                grad = grad_s[rows, s]
                unit = qkv_ref[rows, at].astype(F32) * (scale / gain)
                head = head + grad * unit
                grad = grad * gain
                turned = r_ref[rows, at].astype(F32) * (grad - unit * (split_dot(grad * unit, ones) * (1.0 / HD)))
                low_s[j, rows, s] = (turned * cos - other_half(turned) * sin).astype(BF)
            head_s[:, s] = head_s[:, s] + jnp.sum(head, axis=0, keepdims=True)
            low_s[2, rows, s] = dv_s[rows, s].astype(BF)
        for c in range(0, width, 512):
            part = sum(dot_nt(low_s[j, rows], w_ref[c : c + 512, j * cols : (j + 1) * cols]) for j in range(3))
            out_s[rows, c : c + 512] = part.astype(BF)
        copy = remote(out_s.at[rows], in_s.at[rows], send.at[block], recv.at[block], across)
        copy.start()
        copies[block] = copy

    longest = chips // 2
    pending = [(0, 2), (1, 1)]
    for hop in range(3, longest + 1):
        pending += [(0, hop), (1, hop - 1)]
    pending.append((1, longest))
    step_pairs = cols // 256
    def weight_grad(j, d, left, right):
        dw_s[j, d] = dot_tn(left, right).astype(BF)

    for block in range(blocks):
        heads = attend(block)
        lax.fori_loop(0, step_pairs, heads, 0)
        if block == 2:
            tick(*pending.pop(0))
        lax.fori_loop(step_pairs, 2 * step_pairs, heads, 0)
        if block == 0:
            for copy in loads[4:8]:
                copy.wait()
        if block > 2:
            tick(*pending.pop(0))
        project_back(block)
        if block == 1:
            tick(*pending.pop(0))
            for copy in loads[8:10]:
                copy.wait()
            by_step(width, BLOCK, lambda d: weight_grad(3, d, do_ref[:, d], y_ref[...]))
            send_pair(3)
        if block == 2:
            tick(*pending.pop(0))
            sum_pair(3)
            launch(2)
    for group in (3, 4, 5):
        j = MATRIX_OF[group]
        by_step(width, BLOCK, lambda d: weight_grad(j, d, x_ref[:, d], low_s[j]))
        send_pair(j)
        if group == 4:
            tick(*pending.pop(0))
        if group > 3:
            sum_pair(MATRIX_OF[group - 1])
            launch(group - 1)
        if group == 4:
            tick(2, 1)
    sum_pair(MATRIX_OF[5])
    launch(5)
    tick(*pending.pop(0))
    assert not pending

    def squares(g, w, m):
        count = g.shape[-1]

        def body(i, total):
            r = pl.ds(pl.multiple_of(i * 8, 8), 8)
            step = stepped(w[r], m[r], g[r], rate)[1]
            return total + step * step

        total = lax.fori_loop(0, rows_own // 8, body, jnp.zeros((8, count), F32))
        return jnp.sum(total, axis=0, keepdims=True)

    def exchange(s):
        copy = remote(mine_m.at[s], got_m.at[s], all_send.at[0, s], all_recv.at[0, s], turns[s])
        copy.start()
        return copy

    for copy in loads[10:]:
        copy.wait()
    lanes = mine_m.shape[2]
    mine_m[0] = jnp.zeros(mine_m.shape[1:], F32)
    row = 0

    def place_row(value):
        nonlocal row
        for c in range(0, value.shape[1], lanes):
            size = min(lanes, value.shape[1])
            mine_m[0, row : row + 1, 0:size] = value[:, c : c + size]
            row += 1

    for j in range(3):
        place_row(squares(gd_ref if j == 2 else gm_s.at[j], wm_ref.at[j], mm_ref.at[j]))
    place_row(head_s[...])
    for ref in (mix_ref, us_ref):
        for j in range(2):
            place_row(ref[j : j + 1])
    def attn_squares(j):
        mine_a[0, j : j + 1] = squares(ga_s.at[j], wa_ref.at[j], ma_ref.at[j])

    stores.append(start_copy(gm_s, gm_o, save.at[0]))
    def settle(s, copy):
        copy.wait()
        mine_m[s + 1] = mine_m[s] + got_m[s]

    copy = exchange(0)
    finish_input(0)
    finish_input(1)
    settle(0, copy)
    for hop in range(1, longest + 1):
        if hop < stages:
            copy = exchange(hop)
        if hop == 2:
            finish_input(2)
        for group in (3, 4, 5):
            tick(group, hop)
            if hop == longest:
                attn_squares(MATRIX_OF[group])
        if hop < longest:
            tick(2, hop + 1)
            if hop + 1 == longest:
                attn_squares(3)
        if hop < stages:
            settle(hop, copy)
    for hop in range(longest + 1, stages):
        settle(hop, exchange(hop))
    last = remote(mine_a.at[0], got_a.at[0], all_send.at[1, 0], all_recv.at[1, 0], pair)
    last.start()
    stores.append(start_copy(ga_s, ga_o, save.at[1]))
    stores.append(start_copy(mine_m.at[stages], sum_m_o, save.at[2]))
    last.wait()
    mine_a[1] = mine_a[0] + got_a[0]
    for d, peer in enumerate(others):
        remote(mine_a.at[1], got_a.at[1 + d], all_send.at[1, 1], all_recv.at[1, 1], peer).start()
    for block in range(3, blocks):
        finish_input(block)
    every = got_a.at[pl.ds(1, chips - 1)]
    remote(every, every, all_send.at[1, 1], all_recv.at[1, 1], pair).wait()
    total = mine_a[1]
    for d in range(1, chips):
        total = total + got_a[d]
    mine_a[2] = total
    stores.append(start_copy(mine_a.at[2], sum_a_o, save.at[3]))
    for copy in stores:
        copy.wait()
    scatter.close()


def attention_backward(
    states, weights, qkv, factors, y, dy, do, dri, carry, rest, tables, attn_w, attn_mom, mlp_w, mlp_mom,
    gain, start, grad_down, grad_mix, grad_units, rate, fsdp,
):
    length, width = states.shape
    cols = gain.shape[1]
    chips = fsdp // 2
    rows, units = rest.shape[2:]
    stages = fsdp.bit_length() - 1
    vspec, anyspec = pl.BlockSpec(memory_space=VM), pl.BlockSpec(memory_space=pl.ANY)
    blocks = len(back_pieces(length))
    sem = pltpu.SemaphoreType.DMA
    square, full_square = VM((length, cols), BF), VM((length, cols), F32)
    wide = VM((length, width), BF)
    a_rows, m_rows = 4, -(-(3 * (units // width) + 3 + 2 * (units // width)) // 8) * 8
    return pl.pallas_call(
        functools.partial(backward_kernel, rate),
        out_shape=(
            low(length, width), full(4, rows, cols), full(2, rows, units), full(a_rows, cols), full(m_rows, width),
        ),
        in_specs=[anyspec] * 15 + [vspec] * 5,
        out_specs=(anyspec,) * 5,
        scratch_shapes=[
            VM((4, rows, cols), F32), VM((2, rows, units), F32), wide, VM(weights.shape, BF), VM(qkv.shape, BF), VM(factors.shape, BF), square, square,
            wide, VM(carry.shape, BF), VM(rest.shape, BF), VM(tables.shape, F32), VM((2, BLOCK, width), F32),
            VM(attn_w.shape, F32), VM(attn_w.shape, F32), VM(mlp_w.shape, F32), VM(mlp_w.shape, F32),
            VM((BLOCK + SPAN, BLOCK), F32), full_square, full_square, full_square,
            VM((3, length, cols), BF), wide, wide, VM((4, width, cols), BF), VM((4, chips, rows, cols), BF),
            VM((chips - 1, 4, rows, cols), BF), VM((2, chips - 1, rows, units), BF), VM((1, cols), F32),
            VM((3, a_rows, cols), F32), VM((chips, a_rows, cols), F32),
            VM((stages + 1, m_rows, width), F32), VM((stages, m_rows, width), F32),
            sem((14,)), sem((blocks,)), sem((blocks,)), sem((4,)), sem((blocks,)), sem((blocks,)),
            sem((4,)), sem((4,)), sem((6,)), sem((6, chips - 1)), sem((2, stages)), sem((2, stages)),
        ],
        compiler_params=pltpu.CompilerParams(collective_id=5, has_side_effects=True, vmem_limit_bytes=63 * MIB),
        name="attention_backward",
    )(
        states, weights, qkv, factors, y, dy, do, dri, carry, rest, tables, attn_w, attn_mom, mlp_w, mlp_mom,
        gain, start, grad_down, grad_mix, grad_units,
    )


def update_kernel(
    rates, width, ig, hid, ga, gm, gd, sa, sm, wa, ma, aa, wm, mm, am, hs, hm, mr, mo, us, um,
    hid_o, ig_o, ma_o, wa_o, aa_o, mm_o, wm_o, am_o, hm_o, hs_o, mo_o, mr_o, um_o, us_o,
):
    hid_o[0] = hid[...].astype(F32)
    ig_o[0] = ig[...].astype(F32)
    lanes = sm.shape[1]
    cols, units = wa.shape[2], wm.shape[2]

    def matrix(j, grad, total, refs, outs):
        w, m, a = (ref[j] for ref in refs)
        moment, step = stepped(w, m, grad, rates[0])
        new = step * lax.rsqrt(total / width + EPS)
        outs[0][j] = moment
        outs[1][j] = new
        outs[2][j] = AVERAGE * a + (1.0 - AVERAGE) * new

    def wide(row):
        return jnp.concatenate([sm[row + c : row + c + 1] for c in range(units // lanes)], axis=1)

    for j in range(4):
        matrix(j, ga[j], sa[j : j + 1], (wa, ma, aa), (ma_o, wa_o, aa_o))
    for j in range(3):
        matrix(j, gd[...] if j == 2 else gm[j], wide(j * (units // lanes)), (wm, mm, am), (mm_o, wm_o, am_o))

    @pl.when(pl.program_id(0) == 0)
    def _():
        row = 3 * (units // lanes)
        hm_o[...], hs_o[...] = stepped(hs[...], hm[...], sm[row : row + 1, :cols], rates[1])
        mo_o[...], mr_o[...] = stepped(mr[...], mo[...], sm[row + 1 : row + 3], rates[2])
        row += 3
        grad = jnp.concatenate([wide(row), wide(row + units // lanes)], axis=0)
        um_o[...], us_o[...] = stepped(us[...], um[...], grad, rates[3])


def update(input_low, hidden_low, ga, gm, gd, sa, sm, wa, ma, aa, wm, mm, am, hs, hm, mr, mo, us, um, rates):
    length, width = input_low.shape
    rows, cols, units = wa.shape[1], wa.shape[2], wm.shape[2]
    steps, block = rows // 16, 16
    tall = length // steps

    def whole(shape):
        return pl.BlockSpec(shape, lambda i: (0,) * len(shape))

    state = pl.BlockSpec((tall, width), lambda i: (i, 0))
    state_o = pl.BlockSpec((1, tall, width), lambda i: (0, i, 0))
    attn = pl.BlockSpec((4, block, cols), lambda i: (0, i, 0))
    mlp = pl.BlockSpec((3, block, units), lambda i: (0, i, 0))
    small = [whole((1, cols))] * 2 + [whole(mr.shape)] * 2 + [whole(us.shape)] * 2
    return pl.pallas_call(
        functools.partial(update_kernel, rates, width),
        grid=(steps,),
        out_shape=(
            full(1, length, width), full(1, length, width), *(full(*wa.shape),) * 3, *(full(*wm.shape),) * 3,
            *(full(1, cols),) * 2, *(full(*mr.shape),) * 2, *(full(*us.shape),) * 2,
        ),
        in_specs=[
            state, state, attn, pl.BlockSpec((2, block, units), lambda i: (0, i, 0)), pl.BlockSpec((block, units), lambda i: (i, 0)),
            whole(sa.shape), whole(sm.shape), attn, attn, attn, mlp, mlp, mlp, *small,
        ],
        out_specs=(state_o, state_o, attn, attn, attn, mlp, mlp, mlp, *small),
        compiler_params=pltpu.CompilerParams(vmem_limit_bytes=60 * MIB),
        name="update_weights",
    )(input_low, hidden_low, ga, gm, gd, sa, sm, wa, ma, aa, wm, mm, am, hs, hm, mr, mo, us, um)


def local_fast(
    inputs, doc_ids, out_grad, attn_w, attn_mom, attn_avg, mlp_w, mlp_mom, mlp_avg,
    head_scale, head_mom, mix_rates, mix_mom, unit_scales, unit_mom,
):
    fsdp = lax.axis_size("fsdp")
    root_tokens = math.sqrt(inputs.shape[0] * fsdp * inputs.shape[1])
    rates = tuple(rate / root_tokens for rate in (RATE_WEIGHT, RATE_HEAD, RATE_MIX, RATE_UNITS))
    states, gain = inputs[0], head_scale[None]
    hidden_low, dri, do, dy, w_in, qkv, factors, y, tables, carry, rest, start, grad_mix, grad_units, grad_down = layer(
        attn_w, mlp_w, states, out_grad[0], doc_ids, gain, mix_rates, unit_scales, fsdp
    )
    input_low, grad_attn, grad_mlp, total_attn, total_rest = attention_backward(
        states, w_in, qkv, factors, y, dy, do, dri, carry, rest, tables, attn_w, attn_mom, mlp_w, mlp_mom,
        gain, start, grad_down, grad_mix, grad_units, rates[0], fsdp,
    )
    outs = update(
        input_low, hidden_low, grad_attn, grad_mlp, grad_down, total_attn, total_rest,
        attn_w, attn_mom, attn_avg, mlp_w, mlp_mom, mlp_avg,
        gain, head_mom[None], mix_rates, mix_mom, unit_scales, unit_mom, rates,
    )
    return (*outs[:8], outs[8][0], outs[9][0], *outs[10:])


def local(
    inputs,
    doc_ids,
    out_grad,
    attn_w,
    attn_mom,
    attn_avg,
    mlp_w,
    mlp_mom,
    mlp_avg,
    head_scale,
    head_mom,
    mix_rates,
    mix_mom,
    unit_scales,
    unit_mom,
):
    length = inputs.shape[1]
    model_width = inputs.shape[2]
    head_count = head_scale.shape[0] // HD
    block_rows = min(512, length)
    block_count = length // block_rows
    tokens = inputs.shape[0] * lax.axis_size("fsdp") * length
    doc_row = doc_ids[0]
    input_low = inputs[0]
    resid_in = input_low.astype(jnp.float32)
    cos_table, sin_table = rotary_tables(doc_row)
    position = jnp.arange(length, dtype=jnp.int32)
    attn_full = lax.all_gather(attn_w.astype(jnp.bfloat16), "fsdp", axis=1, tiled=True)
    projected = jnp.einsum(
        "sd,jdc->jsc", input_low, attn_full[:3], preferred_element_type=jnp.float32
    )
    head_gain = head_scale.reshape(head_count, HD)
    q_rot = rotate(projected[0].reshape(length, head_count, HD), cos_table, sin_table)
    k_rot = rotate(projected[1].reshape(length, head_count, HD), cos_table, sin_table)
    q_unit = rms_unit(q_rot)
    k_unit = rms_unit(k_rot)
    query_low = (head_gain * q_unit).astype(jnp.bfloat16)
    key_low = (head_gain * k_unit).astype(jnp.bfloat16)
    value_low = projected[2].reshape(length, head_count, HD).astype(jnp.bfloat16)

    def scores_of(row_first):
        query_blk = lax.dynamic_slice_in_dim(query_low, row_first, block_rows, 0)
        raw_scores = jnp.einsum(
            "qhe,khe->hqk", query_blk, key_low, preferred_element_type=jnp.float32
        )
        row_pos = lax.dynamic_slice_in_dim(position, row_first, block_rows, 0)
        row_docs = lax.dynamic_slice_in_dim(doc_row, row_first, block_rows, 0)
        allowed = (row_docs[:, None] == doc_row[None, :]) & (position[None, :] <= row_pos[:, None])
        return (jnp.where(allowed[None], raw_scores * HD ** (-0.5), NEG_FILL), query_blk)

    def attend(accums, blk_index):
        scores, query_blk = scores_of(blk_index * block_rows)
        peak_val = jnp.max(scores, axis=-1, keepdims=True)
        expo_vals = jnp.exp(scores - peak_val)
        row_total = jnp.sum(expo_vals, axis=-1, keepdims=True)
        probs_low = (expo_vals / row_total).astype(jnp.bfloat16)
        blk_out = jnp.einsum(
            "hqk,khe->qhe", probs_low, value_low, preferred_element_type=jnp.float32
        )
        return (accums, (blk_out, (peak_val + jnp.log(row_total))[..., 0]))

    _, (mixed_blocks, log_totals) = lax.scan(attend, None, jnp.arange(block_count))
    mixed_low = mixed_blocks.reshape(length, head_count * HD).astype(jnp.bfloat16)
    attn_part = jnp.einsum("sc,dc->sd", mixed_low, attn_full[3], preferred_element_type=jnp.float32)
    attn_out = lax.psum(attn_part, "mp")
    attn_unit = rms_unit(attn_out)
    resid_one = resid_in + mix_rates[0] * (attn_unit - resid_in)
    hidden_one = rms_unit(resid_one)
    hidden_low = hidden_one.astype(jnp.bfloat16)
    mlp_full = lax.all_gather(mlp_w.astype(jnp.bfloat16), "fsdp", axis=1, tiled=True)
    gates = jnp.einsum("sd,jdf->jsf", hidden_low, mlp_full[:2], preferred_element_type=jnp.float32)
    up_proj = gates[0]
    gate_proj = gates[1]
    gate_arg = unit_scales[1] * gate_proj * D ** (-0.5)
    gate_sig = jax.nn.sigmoid(gate_arg)
    gate_act = gate_arg * gate_sig
    units_low = (unit_scales[0] * up_proj * gate_act).astype(jnp.bfloat16)
    mlp_part = jnp.einsum("sf,df->sd", units_low, mlp_full[2], preferred_element_type=jnp.float32)
    mlp_out = lax.psum(mlp_part, "mp")
    mlp_unit = rms_unit(mlp_out)
    resid_two = hidden_one + mix_rates[1] * (mlp_unit - hidden_one)
    result = rms_unit(resid_two)
    cotangent = out_grad[0].astype(jnp.float32)
    d_resid_two = rms_back(resid_two, cotangent)
    grad_mix_mlp = jnp.sum(d_resid_two * (mlp_unit - hidden_one), axis=0)
    d_hidden_one = d_resid_two * (1.0 - mix_rates[1])
    d_mlp_low = rms_back(mlp_out, mix_rates[1] * d_resid_two).astype(jnp.bfloat16)
    mlp_back = lax.all_gather(mlp_w.astype(jnp.bfloat16), "fsdp", axis=1, tiled=True)
    d_units = jnp.einsum("sd,df->sf", d_mlp_low, mlp_back[2], preferred_element_type=jnp.float32)
    d_up = d_units * unit_scales[0] * gate_act
    d_arg = d_units * unit_scales[0] * up_proj * gate_sig * (1.0 + gate_arg * (1.0 - gate_sig))
    d_gate = d_arg * unit_scales[1] * D ** (-0.5)
    grad_units = jnp.stack(
        [
            jnp.sum(d_units * up_proj * gate_act, axis=0),
            jnp.sum(d_arg * gate_proj * D ** (-0.5), axis=0),
        ]
    )
    d_gates_low = jnp.stack([d_up, d_gate]).astype(jnp.bfloat16)
    mlp_back_part = jnp.einsum(
        "jsf,jdf->sd", d_gates_low, mlp_back[:2], preferred_element_type=jnp.float32
    )
    d_hidden_one = d_hidden_one + lax.psum(mlp_back_part, "mp")
    right_cols = d_mlp_low
    left_cols = hidden_low
    grad_mlp = jnp.transpose(
        lax.psum_scatter(
            jnp.concatenate(
                [
                    jnp.einsum(
                        "sd,jsf->djf", left_cols, d_gates_low, preferred_element_type=jnp.float32
                    ),
                    jnp.einsum(
                        "sd,sf->df", right_cols, units_low, preferred_element_type=jnp.float32
                    )[:, None, :],
                ],
                axis=1,
            ),
            "fsdp",
            scatter_dimension=0,
            tiled=True,
        ),
        (1, 0, 2),
    )
    d_resid_one = rms_back(resid_one, d_hidden_one)
    grad_mix_attn = jnp.sum(d_resid_one * (attn_unit - resid_in), axis=0)
    d_resid_in = d_resid_one * (1.0 - mix_rates[0])
    d_attn_low = rms_back(attn_out, mix_rates[0] * d_resid_one).astype(jnp.bfloat16)
    attn_back = lax.all_gather(attn_w.astype(jnp.bfloat16), "fsdp", axis=1, tiled=True)
    d_mixed = jnp.einsum("sd,dc->sc", d_attn_low, attn_back[3], preferred_element_type=jnp.float32)
    d_mixed = d_mixed.astype(jnp.bfloat16).reshape(length, head_count, HD)

    def attend_back(accums, blk_index):
        d_key, d_value = accums
        row_first = blk_index * block_rows
        scores, query_blk = scores_of(row_first)
        blk_total = lax.dynamic_index_in_dim(log_totals, blk_index, 0, keepdims=False)
        attn_probs = jnp.exp(scores - blk_total[..., None])
        d_out_blk = lax.dynamic_slice_in_dim(d_mixed, row_first, block_rows, 0)
        d_probs = jnp.einsum(
            "qhe,khe->hqk", d_out_blk, value_low, preferred_element_type=jnp.float32
        )
        d_scores = attn_probs * (d_probs - jnp.sum(attn_probs * d_probs, axis=-1, keepdims=True))
        d_raw_low = (d_scores * HD ** (-0.5)).astype(jnp.bfloat16)
        d_query = jnp.einsum("hqk,khe->qhe", d_raw_low, key_low, preferred_element_type=jnp.float32)
        d_key = d_key + jnp.einsum(
            "hqk,qhe->khe", d_raw_low, query_blk, preferred_element_type=jnp.float32
        )
        d_value = d_value + jnp.einsum(
            "hqk,qhe->khe",
            attn_probs.astype(jnp.bfloat16),
            d_out_blk,
            preferred_element_type=jnp.float32,
        )
        return ((d_key, d_value), d_query)

    zero_heads = jnp.zeros((length, head_count, HD), jnp.float32)
    (d_key_all, d_value_all), d_query_blocks = lax.scan(
        attend_back, (zero_heads, zero_heads), jnp.arange(block_count)
    )
    d_query_all = d_query_blocks.reshape(length, head_count, HD)
    grad_head = jnp.sum(d_query_all * q_unit + d_key_all * k_unit, axis=0).reshape(-1)
    d_query_raw = rotate_back(rms_back(q_rot, head_gain * d_query_all), cos_table, sin_table)
    d_key_raw = rotate_back(rms_back(k_rot, head_gain * d_key_all), cos_table, sin_table)
    d_proj_low = jnp.stack(
        [
            d_query_raw.reshape(length, -1),
            d_key_raw.reshape(length, -1),
            d_value_all.reshape(length, -1),
        ]
    ).astype(jnp.bfloat16)
    grad_mix = jnp.stack([grad_mix_attn, grad_mix_mlp])
    grad_head, grad_mix, grad_units = lax.psum((grad_head, grad_mix, grad_units), "fsdp")
    attn_back_part = jnp.einsum(
        "jsc,jdc->sd", d_proj_low, attn_back[:3], preferred_element_type=jnp.float32
    )
    input_grad = d_resid_in + lax.psum(attn_back_part.astype(jnp.bfloat16), "mp").astype(
        jnp.float32
    )
    left_cols = input_low
    right_cols = d_attn_low
    in_terms = jnp.einsum("sd,jsc->djc", left_cols, d_proj_low, preferred_element_type=jnp.float32)
    out_terms = jnp.einsum("sd,sc->dc", right_cols, mixed_low, preferred_element_type=jnp.float32)
    grad_attn = jnp.transpose(
        lax.psum_scatter(
            jnp.concatenate([in_terms, out_terms[:, None, :]], axis=1),
            "fsdp",
            scatter_dimension=0,
            tiled=True,
        ),
        (1, 0, 2),
    )
    root_tokens = math.sqrt(tokens)
    weight_rate = RATE_WEIGHT / root_tokens
    attn_mom_new, attn_step = nesterov(attn_w, attn_mom, grad_attn, weight_rate)
    mlp_mom_new, mlp_step = nesterov(mlp_w, mlp_mom, grad_mlp, weight_rate)
    attn_squares = jnp.sum(attn_step * attn_step, axis=1)
    mlp_squares = jnp.sum(mlp_step * mlp_step, axis=1)
    attn_squares, mlp_squares = lax.psum((attn_squares, mlp_squares), "fsdp")
    attn_new = attn_step * lax.rsqrt(attn_squares[:, None, :] / model_width + EPS)
    mlp_new = mlp_step * lax.rsqrt(mlp_squares[:, None, :] / model_width + EPS)
    head_mom_new, head_new = nesterov(head_scale, head_mom, grad_head, RATE_HEAD / root_tokens)
    mix_mom_new, mix_new = nesterov(mix_rates, mix_mom, grad_mix, RATE_MIX / root_tokens)
    units_mom_new, units_new = nesterov(unit_scales, unit_mom, grad_units, RATE_UNITS / root_tokens)
    return (
        result[None],
        input_grad[None],
        attn_mom_new,
        attn_new,
        AVERAGE * attn_avg + (1.0 - AVERAGE) * attn_new,
        mlp_mom_new,
        mlp_new,
        AVERAGE * mlp_avg + (1.0 - AVERAGE) * mlp_new,
        head_mom_new,
        head_new,
        mix_mom_new,
        mix_new,
        units_mom_new,
        units_new,
    )


def solution(mesh):
    fsdp = mesh.shape["fsdp"]
    fast = fsdp == 16 and D // fsdp % 16 == 0
    placed = (
        P("fsdp", None, None),
        P("fsdp", None),
        P("fsdp", None, None),
        P(None, "fsdp", "mp"),
        P(None, "fsdp", "mp"),
        P(None, "fsdp", "mp"),
        P(None, "fsdp", "mp"),
        P(None, "fsdp", "mp"),
        P(None, "fsdp", "mp"),
        P("mp"),
        P("mp"),
        P(),
        P(),
        P(None, "mp"),
        P(None, "mp"),
    )
    return jax.shard_map(
        local_fast if fast else local,
        mesh=mesh,
        in_specs=placed,
        out_specs=(
            P("fsdp", None, None),
            P("fsdp", None, None),
            P(None, "fsdp", "mp"),
            P(None, "fsdp", "mp"),
            P(None, "fsdp", "mp"),
            P(None, "fsdp", "mp"),
            P(None, "fsdp", "mp"),
            P(None, "fsdp", "mp"),
            P("mp"),
            P("mp"),
            P(),
            P(),
            P(None, "mp"),
            P(None, "mp"),
        ),
        check_vma=False,
    )
```

```python
import functools
import math

import jax
import jax.numpy as jnp
import numpy as np
from jax import lax
from jax.experimental import pallas as pl
from jax.experimental.pallas import tpu as pltpu
from jax.sharding import PartitionSpec as P

D = 1024
HD = 64


EPS = 1e-06
MOMENTUM = 0.9
AVERAGE = 0.9
NEG_FILL = -1e30
THETA = 10000.0
RATE_WEIGHT = 50.0
RATE_HEAD = 0.08
RATE_MIX = 0.02
RATE_UNITS = 0.5


def rms_unit(vector):
    return vector * lax.rsqrt(jnp.mean(vector * vector, axis=-1, keepdims=True) + EPS)


def rms_back(vector, grad):
    factor = lax.rsqrt(jnp.mean(vector * vector, axis=-1, keepdims=True) + EPS)
    unit_vec = vector * factor
    return factor * (grad - unit_vec * jnp.mean(grad * unit_vec, axis=-1, keepdims=True))


def rotary_tables(doc_row):
    length = doc_row.shape[0]
    position = jnp.arange(length, dtype=jnp.int32)
    boundary = jnp.concatenate(
        [jnp.ones((1,), jnp.int32), (doc_row[1:] != doc_row[:-1]).astype(jnp.int32)]
    )
    doc_start = lax.cummax(jnp.where(boundary > 0, position, 0), axis=0)
    offset = (position - doc_start).astype(jnp.float32)
    freq = THETA ** (-2.0 * jnp.arange(HD // 2, dtype=jnp.float32) / HD)
    angle = offset[:, None] * freq[None, :]
    return (jnp.cos(angle), jnp.sin(angle))


def rotate(vector, cos_table, sin_table):
    half_dim = vector.shape[-1] // 2
    lower_half = vector[..., :half_dim]
    upper_half = vector[..., half_dim:]
    cos_part = cos_table[:, None, :]
    sin_part = sin_table[:, None, :]
    return jnp.concatenate(
        [
            lower_half * cos_part - upper_half * sin_part,
            lower_half * sin_part + upper_half * cos_part,
        ],
        axis=-1,
    )


def rotate_back(grad, cos_table, sin_table):
    half_dim = grad.shape[-1] // 2
    lower_half = grad[..., :half_dim]
    upper_half = grad[..., half_dim:]
    cos_part = cos_table[:, None, :]
    sin_part = sin_table[:, None, :]
    return jnp.concatenate(
        [
            lower_half * cos_part + upper_half * sin_part,
            upper_half * cos_part - lower_half * sin_part,
        ],
        axis=-1,
    )


def nesterov(param, moment, grad, step_rate):
    moment_new = MOMENTUM * moment + grad
    return (moment_new, param - step_rate * (grad + MOMENTUM * moment_new))


BF = jnp.bfloat16
F32 = jnp.float32
MESH = pl.DeviceIdType.MESH
VM = pltpu.VMEM
MIB = 1 << 20
BLOCK = 256
SPAN = 512
ROWS_STEP = 128
UNIT_STEP = 1024


def dot_nn(a, b):
    return lax.dot_general(a, b, (((1,), (0,)), ((), ())), preferred_element_type=F32)


def dot_nt(a, b):
    return lax.dot_general(a, b, (((1,), (1,)), ((), ())), preferred_element_type=F32)


def dot_tn(a, b):
    return lax.dot_general(a, b, (((0,), (0,)), ((), ())), preferred_element_type=F32)


def split_dot(a, ones):
    high = a.astype(BF)
    return dot_nn(high, ones) + dot_nn((a - high.astype(F32)).astype(BF), ones)


def ring_place(index, chips):
    z, y = index // 4, (index // 2) % 2
    return z + y * (chips - 1 - 2 * z), index % 2


def ring_device(place, core, chips):
    y = place // (chips // 2)
    return ((place + y * (chips - 1 - 2 * place)) * 2 + y) * 2 + core


def peers_of(chips):
    index, x = lax.axis_index("fsdp"), lax.axis_index("mp")
    place, core = ring_place(index, chips)
    right = (ring_device((place + 1) % chips, core, chips), x)
    left = (ring_device((place + chips - 1) % chips, core, chips), x)
    return index, x, place, core, right, left, (index + 1 - 2 * core, x), (index, 1 - x)


def greet(peers):
    barrier = pltpu.get_barrier_semaphore()
    for peer in peers:
        pl.semaphore_signal(barrier, inc=1, device_id=peer, device_id_type=MESH)
    pl.semaphore_wait(barrier, len(peers))


def remote(src, dst, send, recv, peer):
    return pltpu.make_async_remote_copy(
        src_ref=src, dst_ref=dst, send_sem=send, recv_sem=recv, device_id=peer, device_id_type=MESH
    )


def start_copy(src, dst, sem):
    copy = pltpu.make_async_copy(src, dst, sem)
    copy.start()
    return copy


def by_step(total, step, body, first=0):
    def run(i, _):
        body(pl.ds(pl.multiple_of(first + i * step, step), step))
        return 0

    lax.fori_loop(0, total // step, run, 0)


def add_all(dst, refs):
    if len(dst.shape) == 3:
        for j in range(dst.shape[0]):
            add_all(dst.at[j], [ref.at[j] for ref in refs])
        return

    def body(r):
        total = refs[0][r].astype(F32)
        for ref in refs[1:]:
            total = total + ref[r].astype(F32)
        dst[r] = total.astype(dst.dtype)

    by_step(dst.shape[0], 16, body)


def ring_hops(chips, group, long_right):
    pair_of = (chips // 2, chips - 1 - chips // 2)
    return pair_of if group in long_right else pair_of[::-1]


class Scatter:
    def __init__(self, chips, long_right, mine, slot, result, sent, send, recv):
        _, _, self.place, self.core, self.right, self.left, _, _ = peers_of(chips)
        self.chips, self.long_right, self.mine, self.slot_at, self.result = chips, long_right, mine, slot, result
        self.send, self.recv, self.sent = send, recv, sent

    def hops(self, group):
        return ring_hops(self.chips, group, self.long_right)

    def term(self, group, way, to_go):
        step = to_go if way == 0 else self.chips - to_go
        return self.mine(group, way, to_go, ring_device((self.place + step) % self.chips, self.core, self.chips) // 2)

    def at(self, group, way, hop):
        return hop - 1 if way == 0 else self.hops(group)[0] + hop - 1

    def slot(self, group, way, hop):
        return self.slot_at(group, self.at(group, way, hop))

    def copy(self, group, way, hop, src):
        at, peer = self.at(group, way, hop), self.right if way == 0 else self.left
        return remote(src, self.slot_at(group, at), self.send.at[group], self.recv.at[group, at], peer)

    def go(self, group, way, hop, src):
        self.copy(group, way, hop, src).start()

    def launch(self, group):
        for way in (0, 1):
            self.go(group, way, 1, self.term(group, way, self.hops(group)[way]))

    def take(self, group, way, hop):
        here = self.slot(group, way, hop)
        self.copy(group, way, hop, here).wait_recv()
        return here

    def tick(self, group, hop):
        hops = self.hops(group)
        for way in (0, 1):
            if hop > hops[way]:
                continue
            here = self.take(group, way, hop)
            if hop < hops[way]:
                add_all(here, [here, self.term(group, way, hops[way] - hop)])
                self.go(group, way, hop + 1, here)
        if hop == self.chips // 2:
            ends = [self.slot(group, way, hops[way]) for way in (0, 1)]
            add_all(self.result(group), [self.term(group, 0, 0)] + ends)

    def close(self):
        for group in range(self.send.shape[0]):
            ref = self.sent(group)
            remote(ref, ref, self.send.at[group], self.send.at[group], self.right).wait_send()


def head_ones():
    row = lax.broadcasted_iota(jnp.int32, (128, 128), 0) // HD
    col = lax.broadcasted_iota(jnp.int32, (128, 128), 1) // HD
    return jnp.where(row == col, 1.0, 0.0).astype(BF)


def half_of(rows, half):
    lane = lax.broadcasted_iota(jnp.int32, (rows, 128), 1)
    return jnp.where((lane < HD) == (half == 0), 1.0, 0.0).astype(BF)


def other_half(v):
    lane = lax.broadcasted_iota(jnp.int32, v.shape, 1)
    return jnp.where(lane % HD < HD // 2, pltpu.roll(v, 128 - HD // 2, 1), pltpu.roll(v, HD // 2, 1))


def first_key(block):
    return max(0, block * BLOCK - SPAN)


def low(*shape):
    return jax.ShapeDtypeStruct(shape, BF)


def full(*shape):
    return jax.ShapeDtypeStruct(shape, F32)


GATHER_LONG = (0, 2, 4)
FEED_LONG = (0, 1)


def row_factor(v):
    return lax.rsqrt(jnp.mean(v * v, axis=-1, keepdims=True) + EPS)


def unit_back(factor, unit, grad):
    return factor * (grad - unit * jnp.mean(grad * unit, axis=-1, keepdims=True))


def fold(v):
    return jnp.sum(v.reshape(v.shape[0] // 8, 8, v.shape[1]), axis=0)


def feed_chunks(length):
    half = BLOCK // 2
    return [(0, half)] + [(start, BLOCK) for start in range(half, length - half, BLOCK)] + [(length - half, half)]


def layer_kernel(
    chips, attn_hbm, mlp_hbm, x_hbm, og_hbm, doc_ref, gain_ref, freq_ref, mix_ref, us_ref,
    out_o, dri_o, do_o, dy_o, w_o, qkv_o, r_o, y_o, tables_o, carry_o, rest_o, start_o, mix_o, us_o, gd_o,
    start_s, mix_s, us_s, gd_s, x_ref, y_ref, wo_s, wu_s, wg_s, wd_s, o_s, hb_s, u_s, g_s, hid_s, dm_s, dh_s, own_s, got_m, got_d, wd_g, ring_d, ring_n,
    load, store, save, rest_save, small_save, send_y, recv_y, wo_send, wo_recv, wo_near, send_m, recv_m, send_d, recv_d,
    gather_send, gather_recv, near_send, near_recv, own_sem, pair_free, pair_send, pair_recv, ring_send, ring_recv,
):
    index, x, place, core, right, left, pair, across = peers_of(chips)
    pair_index = pair[0]
    length, width = x_ref.shape
    cols, units = y_ref.shape[2], us_ref.shape[1]
    rows_own = width // (2 * chips)
    blocks = length // BLOCK
    chunks = feed_chunks(length)
    number = len(chunks)
    longest = chips // 2

    wide = 3 * cols
    loads_attn = [
        start_copy(attn_hbm.at[j], o_s.at[pl.ds(j * rows_own, rows_own), pl.ds(0, cols)], load.at[j]) for j in range(4)
    ]
    halves = units // width
    loads_mlp = [
        start_copy(
            mlp_hbm.at[j, :, pl.ds(h * width, width)],
            o_s.at[pl.ds((4 + j * halves + h) * rows_own, rows_own)], load.at[4 + j * halves + h],
        )
        for j in range(3)
        for h in range(halves)
    ]
    load_x = start_copy(x_hbm, x_ref, load.at[4 + 3 * halves])
    load_og = start_copy(og_hbm, dm_s, load.at[5 + 3 * halves])

    def own(group):
        if group == 0:
            return wd_g.at[pl.ds(0, rows_own), pl.ds(0, wide)]
        if group == 1:
            return wd_g.at[pl.ds(0, rows_own), pl.ds(wide, cols)]
        return wd_g.at[pl.ds((group - 1) * rows_own, rows_own)]

    def block_of(group, dev):
        r = pl.ds(pl.multiple_of(dev * rows_own, rows_own), rows_own)
        if group == 0:
            return g_s.at[r, pl.ds(0, wide)]
        if group == 1:
            return wo_s.at[x, r]
        return (wu_s, wg_s, wd_s)[group - 2].at[r]

    def counts(group):
        return ring_hops(chips, group, GATHER_LONG)

    def origin(way, hop):
        there = (place + chips - hop) % chips if way == 0 else (place + hop) % chips
        return ring_device(there, core, chips)

    def gather_copy(group, way, hop, src, dst):
        peer = right if way == 0 else left
        return remote(src, dst, gather_send.at[group], gather_recv.at[group, way, hop - 1], peer)

    def near_copy(group, src, dev):
        return remote(src, block_of(group, dev), near_send.at[group], near_recv.at[group], pair)

    def blocks_of(group, count):
        r = pl.ds(0, count * rows_own)
        if group == 0:
            return g_s.at[r, pl.ds(0, wide)]
        return wo_s.at[x, r] if group == 1 else (wu_s, wg_s, wd_s)[group - 2].at[r]

    owns = []

    def launch(group):
        for way in (0, 1):
            gather_copy(group, way, 1, own(group), block_of(group, index)).start()
        near_copy(group, own(group), index).start()
        owns.append(start_copy(own(group), block_of(group, index), own_sem.at[group]))

    def tick(group, hop):
        for way in (0, 1):
            if hop > counts(group)[way]:
                continue
            dev = origin(way, hop)
            here = block_of(group, dev)
            gather_copy(group, way, hop, here, here).wait_recv()
            if hop < counts(group)[way]:
                gather_copy(group, way, hop + 1, here, here).start()
            near_copy(group, here, dev).start()

    def await_all(group):
        owns[group].wait()
        ref = blocks_of(group, chips)
        remote(ref, ref, near_send.at[group], near_recv.at[group], pair).wait_recv()

    def await_sends(group):
        ref = blocks_of(group, chips - 1)
        remote(ref, ref, gather_send.at[group], gather_send.at[group], right).wait_send()
        ref = blocks_of(group, chips)
        remote(ref, ref, near_send.at[group], near_recv.at[group], pair).wait_send()

    for j, copy in enumerate(loads_attn):
        copy.wait()
        wd_g[0:rows_own, j * cols : (j + 1) * cols] = o_s[j * rows_own : (j + 1) * rows_own, 0:cols].astype(BF)
    greet((right, left, pair, across))
    launch(0)
    launch(1)
    for j in range(3):
        for h in range(halves):
            loads_mlp[j * halves + h].wait()
            first = (4 + j * halves + h) * rows_own
            wd_g[(j + 1) * rows_own : (j + 2) * rows_own, h * width : (h + 1) * width] = o_s[
                first : first + rows_own
            ].astype(BF)
    doc = doc_ref[...]
    start = jnp.zeros(doc.shape, F32)
    for value in range(3):
        count = jnp.sum(jnp.where(doc == value, 1.0, 0.0), axis=1, keepdims=True)
        start = start + jnp.where(doc > value, count, 0.0)
    start_s[...] = start.astype(jnp.int32)
    dh_s[:, 256:384] = jnp.transpose(jnp.broadcast_to(start, (128, length)))

    def tables(block):
        rows = pl.ds(block * BLOCK, BLOCK)
        position = (lax.broadcasted_iota(jnp.int32, (BLOCK, 128), 0) + block * BLOCK).astype(F32)
        angle = (position - dh_s[rows, 256:384]) * freq_ref[...]
        lane = lax.broadcasted_iota(jnp.int32, (BLOCK, 128), 1)
        dh_s[rows, 0:128] = jnp.cos(angle)
        dh_s[rows, 128:256] = jnp.where(lane % HD < HD // 2, -1.0, 1.0) * jnp.sin(angle)

    for block in range(blocks // 2):
        tables(block)
    tick(0, 1)
    tick(1, 1)
    for block in range(blocks // 2, blocks):
        tables(block)
    stores = [start_copy(dh_s.at[:, pl.ds(0, 256)], tables_o, store.at[0])]
    stores.append(start_copy(start_s, start_o, small_save.at[0]))
    tick(0, 2)
    launch(2)
    tick(1, 2)
    tick(0, 3)
    tick(2, 1)
    tick(1, 3)
    launch(3)
    tick(0, 4)
    pending = [
        (2, 2), (1, 4), (3, 1), (2, 3), (4, 1), (3, 2), (2, 4), (4, 2), (3, 3), (4, 3), (3, 4), (4, 4),
    ]
    ones = head_ones()
    load_x.wait()
    await_all(0)
    held = [start_copy(g_s.at[:, pl.ds(0, wide)], w_o, store.at[1])]

    def project(i, _):
        rows = pl.ds(pl.multiple_of(i * BLOCK, BLOCK), BLOCK)
        states = x_ref[rows]
        cos, sin = dh_s[rows, 0:128], dh_s[rows, 128:256]
        for j, scale in enumerate((HD**-0.5, 1.0)):
            raw = dot_nn(states, g_s[:, j * cols : (j + 1) * cols])
            for c in range(0, cols, 128):
                part = raw[:, c : c + 128]
                factor = lax.rsqrt(split_dot(part * part, ones) * (1.0 / HD) + EPS)
                unit = (part * cos + other_half(part) * sin) * factor
                at = slice(j * cols + c, j * cols + c + 128)
                u_s[rows, at] = ((gain_ref[:, c : c + 128] * unit).astype(BF).astype(F32) * scale).astype(BF)
                hid_s[rows, at] = factor.astype(BF)
        u_s[rows, 2 * cols : wide] = dot_nn(states, g_s[:, 2 * cols : wide]).astype(BF)
        return 0

    lax.fori_loop(0, blocks // 2, project, 0)
    tick(*pending.pop(0))
    launch(4)
    tick(*pending.pop(0))
    await_all(1)
    part = width // 2

    def wo_half(half, side, send, recv, peer):
        there = wo_s.at[side, pl.ds(pl.multiple_of(half * part, part), part)]
        return remote(there, there, send, recv, peer)

    wo_copy = wo_half(core, x, wo_send, wo_recv, across)
    wo_copy.start()
    lax.fori_loop(blocks // 2, blocks, project, 0)
    held.append(start_copy(u_s.at[:, pl.ds(0, wide)], qkv_o, store.at[2]))
    held.append(start_copy(hid_s.at[:, pl.ds(0, 2 * cols)], r_o, store.at[3]))
    tick(*pending.pop(0))
    copies_y = []
    for block in range(blocks):
        first = first_key(block)
        keys = (block + 1) * BLOCK - first
        rows = pl.ds(block * BLOCK, BLOCK)
        span = pl.ds(first, keys)
        bias = o_s.at[pl.ds(0, BLOCK), pl.ds(0, keys)]
        kpos = (lax.broadcasted_iota(jnp.int32, (BLOCK, keys), 1) + first).astype(F32)
        qpos = (lax.broadcasted_iota(jnp.int32, (BLOCK, keys), 0) + block * BLOCK).astype(F32)
        allowed = (kpos >= dh_s[rows, 256:257]) & (kpos <= qpos)
        bias[...] = jnp.where(allowed, 0.0, NEG_FILL)

        def heads(pair_of, _):
            c = pl.multiple_of(pair_of * 128, 128)
            q = u_s[rows, pl.ds(c, 128)]
            k = u_s[span, pl.ds(cols + c, 128)]
            v = u_s[span, pl.ds(2 * cols + c, 128)]
            results = []
            for half in (0, 1):
                scores = dot_nt(q * half_of(BLOCK, half), k)
                probs = jnp.exp(scores + bias[...]).astype(BF)
                results.append(dot_nn(probs, v * half_of(keys, half) + half_of(keys, 1 - half)))
            lane = lax.broadcasted_iota(jnp.int32, (BLOCK, 128), 1)
            total = pltpu.roll(jnp.where(lane < HD, results[1], results[0]), HD, 1)
            y_ref[x, rows, pl.ds(c, 128)] = (jnp.where(lane < HD, results[0], results[1]) / total).astype(BF)
            return 0

        lax.fori_loop(0, cols // 128, heads, 0)
        copy = remote(y_ref.at[x, rows], y_ref.at[x, rows], send_y.at[block], recv_y.at[block], across)
        copy.start()
        copies_y.append(copy)
        stores.append(start_copy(y_ref.at[x, rows], y_o.at[rows], store.at[4 + block]))
        tick(*pending.pop(0))
        if block == 1:
            wo_half(core, 1 - x, wo_send, wo_recv, across).wait_recv()
            wo_pass = wo_half(core, 1 - x, wo_near.at[0], wo_near.at[1], pair)
            wo_pass.start()

    copies_m, copies_d = {}, {}
    here_y = []

    def await_y(rows_end):
        while len(here_y) * BLOCK < rows_end:
            block = len(here_y)
            there = y_ref.at[1 - x, pl.ds(block * BLOCK, BLOCK)]
            remote(there, there, send_y.at[block], recv_y.at[block], across).wait_recv()
            here_y.append(block)

    def first_half(r):
        states = x_ref[r].astype(F32)
        o = o_s[r]
        ro = row_factor(o)
        uo = o * ro
        mix = mix_ref[0:1]
        r1 = states + mix * (uo - states)
        rr = row_factor(r1)
        return states, ro, uo, rr, r1 * rr

    def by_rows(chunk, body, init):
        start, size = chunks[chunk]
        for i in range(size // ROWS_STEP):
            init = body(pl.ds(start + i * ROWS_STEP, ROWS_STEP), init)
        return init

    def mixed(chunk):
        start, size = chunks[chunk]
        rows = pl.ds(start, size)
        await_y(start + size)

        def out_proj(c):
            o_s[rows, c] = dot_nt(y_ref[0, rows], wo_s[0, c]) + dot_nt(y_ref[1, rows], wo_s[1, c])

        by_step(width, 512, out_proj)

        def hidden(r, _):
            hb_s[r] = first_half(r)[4].astype(BF)
            return 0

        by_rows(chunk, hidden, 0)

    def gates(chunk):
        rows = pl.ds(*chunks[chunk])

        def gate(f):
            up = dot_nn(hb_s[rows], wu_s[:, f])
            gt = dot_nn(hb_s[rows], wg_s[:, f])
            arg = us_ref[1:2, f] * gt * D**-0.5
            sig = 1.0 / (1.0 + jnp.exp(-arg))
            u_s[rows, f] = up.astype(BF)
            g_s[rows, f] = gt.astype(BF)
            hid_s[rows, f] = (us_ref[0:1, f] * up * (arg * sig)).astype(BF)

        by_step(units, UNIT_STEP, gate)

    def down(chunk):
        rows = pl.ds(*chunks[chunk])

        def body(c):
            own_s[rows, c] = dot_nt(hid_s[rows], wd_s[c]).astype(BF)

        by_step(width, 512, body)
        copies_m[chunk] = remote(own_s.at[rows], got_m.at[rows], send_m.at[chunk], recv_m.at[chunk], across)
        copies_m[chunk].start()

    def turn(chunk, mix_m):
        rows = pl.ds(*chunks[chunk])
        copies_m[chunk].wait()

        def middle(r, total):
            h1 = first_half(r)[4]
            m = own_s[r].astype(F32) + got_m[r].astype(F32)
            rm = row_factor(m)
            um = m * rm
            mix = mix_ref[1:2]
            r2 = h1 + mix * (um - h1)
            rr = row_factor(r2)
            out = r2 * rr
            got_m[r] = out.astype(BF)
            dr2 = unit_back(rr, out, dm_s[r].astype(F32))
            dm_s[r] = unit_back(rm, um, mix * dr2).astype(BF)
            dh_s[r] = dr2 * (1.0 - mix)
            return total + fold(dr2 * (um - h1))

        mix_m = by_rows(chunk, middle, mix_m)
        start_copy(got_m.at[rows], out_o.at[rows], save.at[3])
        return mix_m

    def gates_back(chunk):
        rows = pl.ds(*chunks[chunk])

        def gate_back(f):
            dhid = dot_nn(dm_s[rows], wd_s[:, f])
            up, gt = u_s[rows, f].astype(F32), g_s[rows, f].astype(F32)
            su, sv = us_ref[0:1, f], us_ref[1:2, f]
            arg = sv * gt * D**-0.5
            sig = 1.0 / (1.0 + jnp.exp(-arg))
            act = dhid * (arg * sig)
            darg = dhid * su * up * sig * (1.0 + arg * (1.0 - sig))
            us_s[0:1, f] = us_s[0:1, f] + jnp.sum(act * up, axis=0, keepdims=True)
            us_s[1:2, f] = us_s[1:2, f] + jnp.sum(darg * gt, axis=0, keepdims=True) * D**-0.5
            u_s[rows, f] = (act * su).astype(BF)
            g_s[rows, f] = (darg * sv * D**-0.5).astype(BF)

        by_step(units, UNIT_STEP, gate_back)

    def ups_back(chunk):
        rows = pl.ds(*chunks[chunk])

        def up_back(c):
            own_s[rows, c] = (dot_nt(u_s[rows], wu_s[c]) + dot_nt(g_s[rows], wg_s[c])).astype(BF)

        by_step(width, 512, up_back)
        copies_d[chunk] = remote(own_s.at[rows], got_d.at[rows], send_d.at[chunk], recv_d.at[chunk], across)
        copies_d[chunk].start()

    def back(chunk):
        gates_back(chunk)
        ups_back(chunk)

    near_s = (hid_s, u_s, g_s)

    def grads_of(j, weight_s, left_s, first, rows):
        tokens = pl.ds(first, rows)

        def grads(d):
            for u in range(0, units, 1024):
                f = pl.ds(u, 1024)
                total = dot_tn(left_s[tokens, d], near_s[j][tokens, f])
                if first:
                    total = total + weight_s[d, f].astype(F32)
                weight_s[d, f] = total.astype(BF)

        return grads

    def weight_grads(j, weight_s, left_s, midway=None, first=0):
        right_s = near_s[j]
        grads = grads_of(j, weight_s, left_s, first, length - first)
        by_step(width // 2, BLOCK, grads)
        if midway is not None:
            midway()
        by_step(width // 2, BLOCK, grads, width // 2)
        pl.semaphore_signal(pair_free.at[j], inc=1, device_id=pair, device_id_type=MESH)
        pl.semaphore_wait(pair_free.at[j], 1)
        for chip in range(chips):
            there = pl.multiple_of((chip * 2 + 1 - core) * rows_own, rows_own)
            copy = remote(
                weight_s.at[pl.ds(there, rows_own)], right_s.at[pl.ds(chip * rows_own, rows_own)],
                pair_send.at[j], pair_recv.at[j], pair,
            )
            copy.start()

    def pair_sums(j, weight_s):
        ref = near_s[j].at[pl.ds(0, chips * rows_own)]
        remote(ref, ref, pair_send.at[j], pair_recv.at[j], pair).wait()
        for chip in range(chips):
            base = pl.multiple_of((chip * 2 + core) * rows_own, rows_own)
            here = near_s[j].at[pl.ds(chip * rows_own, rows_own)]
            add_all(here, [here, weight_s.at[pl.ds(base, rows_own)]])

    def summed(group, way, to_go, chip):
        return near_s[group].at[pl.ds(pl.multiple_of(chip * rows_own, rows_own), rows_own)]

    def ring_slot(group, at):
        return ring_d.at[at] if group == 0 else ring_n.at[0 if at == 0 else 1]

    scatter = Scatter(
        chips, FEED_LONG, summed, ring_slot, lambda group: gd_s,
        lambda group: ring_d if group == 0 else ring_n, ring_send, ring_recv,
    )

    def hand_on():
        for way in (0, 1):
            here = scatter.take(1, way, 1)
            add_all(here, [here, scatter.term(1, way, scatter.hops(1)[way] - 1)])
            start_copy(here, carry_o.at[0, way], rest_save.at[0, 0])

    def hand_rest(group):
        hops = scatter.hops(group)
        far = 0 if hops[0] > hops[1] else 1
        for at, (way, to_go) in enumerate(((far, 1), (far, 2), (far, 3), (1 - far, 1), (1 - far, 2), (0, 0))):
            start_copy(scatter.term(group, way, to_go), rest_o.at[group - 1, at], rest_save.at[1, group - 1])
        if group == 2:
            for way in (0, 1):
                start_copy(scatter.term(group, way, hops[way]), carry_o.at[1, way], rest_save.at[0, 1])

    def last(chunk, mix_a):
        rows = pl.ds(*chunks[chunk])
        copies_d[chunk].wait()

        def body(r, total):
            states, ro, uo, rr, h1 = first_half(r)
            mix = mix_ref[0:1]
            dr1 = unit_back(rr, h1, dh_s[r] + (own_s[r].astype(F32) + got_d[r].astype(F32)))
            dh_s[r] = dr1 * (1.0 - mix)
            dm_s[r] = unit_back(ro, uo, mix * dr1).astype(BF)
            return total + fold(dr1 * (uo - states))

        mix_a = by_rows(chunk, body, mix_a)
        y_ref[1 - x, rows] = dot_nn(dm_s[rows], wo_s[x]).astype(BF)
        for j, (src, dst) in enumerate(((y_ref.at[1 - x], dy_o), (dm_s, do_o), (dh_s, dri_o))):
            start_copy(src.at[rows], dst.at[rows], save.at[j])
        return mix_a

    wo_half(1 - core, 1 - x, wo_near.at[0], wo_near.at[1], pair).wait_recv()
    for chunk in range(number):
        mixed(chunk)
        if len(pending) > 2:
            tick(*pending.pop(0))
    for copy in held:
        copy.wait()
    await_sends(0)
    while len(pending) > 1:
        tick(*pending.pop(0))
    await_all(2)
    await_all(3)
    gates(0)
    tick(*pending.pop(0))
    await_all(4)
    for chunk in range(number):
        down(chunk)
        if chunk < number - 1:
            gates(chunk + 1)
        if chunk == 0:
            for group in range(1, 5):
                await_sends(group)
    mix_m = jnp.zeros((8, width), F32)
    us_s[...] = jnp.zeros_like(us_s)
    load_og.wait()
    stores[0].wait()
    for chunk in range(number - 2):
        mix_m = turn(chunk, mix_m)
        back(chunk)
    here = chunks[number - 2][0]
    by_step(width, BLOCK, grads_of(0, wd_g, dm_s, 0, here))
    mix_m = turn(number - 2, mix_m)
    mix_m = turn(number - 1, mix_m)
    mix_s[1:2] = jnp.sum(mix_m, axis=0, keepdims=True)
    weight_grads(0, wd_g, dm_s, None, here)
    gates_back(number - 2)
    pair_sums(0, wd_g)
    scatter.launch(0)
    ups_back(number - 2)
    back(number - 1)
    stores.append(start_copy(us_s, us_o, small_save.at[1]))
    scatter.tick(0, 1)
    weight_grads(1, wu_s, hb_s)

    def up_ring():
        scatter.tick(0, 2)
        pair_sums(1, wu_s)
        scatter.launch(1)
        hand_rest(1)

    weight_grads(2, wg_s, hb_s, up_ring)
    wo_copy.wait_send()
    wo_pass.wait_send()
    for copy in copies_y:
        copy.wait_send()
    mix_a = jnp.zeros((8, width), F32)
    for chunk in range(number):
        mix_a = last(chunk, mix_a)
        if chunk == 1:
            scatter.tick(0, 3)
            pair_sums(2, wg_s)
            hand_rest(2)
        if chunk == number - 3:
            hand_on()
        if chunk == number - 2:
            scatter.tick(0, 4)
            stores.append(start_copy(gd_s, gd_o, small_save.at[2]))
    mix_s[0:1] = jnp.sum(mix_a, axis=0, keepdims=True)
    stores.append(start_copy(mix_s, mix_o, small_save.at[3]))
    for copy in stores[1:]:
        copy.wait()
    for j, (src, dst) in enumerate(((y_ref.at[1 - x], dy_o), (dm_s, do_o), (dh_s, dri_o), (got_m, out_o))):
        pltpu.make_async_copy(src, dst, save.at[j]).wait()
    for j in range(2):
        pltpu.make_async_copy(carry_o.at[j], carry_o.at[j], rest_save.at[0, j]).wait()
        pltpu.make_async_copy(rest_o.at[j], rest_o.at[j], rest_save.at[1, j]).wait()
    scatter.close()


def layer(attn_w, mlp_w, states, out_grad, doc, gain, mix, scales, fsdp):
    chips = fsdp // 2
    length, width = states.shape
    cols, units, rows = attn_w.shape[2], mlp_w.shape[2], attn_w.shape[1]
    vspec, anyspec = pl.BlockSpec(memory_space=VM), pl.BlockSpec(memory_space=pl.ANY)
    blocks, number = length // BLOCK, len(feed_chunks(length))
    sem = pltpu.SemaphoreType.DMA
    freq = np.asarray(THETA ** (-2.0 * (np.arange(128) % (HD // 2)) / HD), np.float32)
    square, wide, weight, tall = VM((length, width), BF), VM((length, units), BF), VM((width, units), BF), VM((length, width), F32)
    return pl.pallas_call(
        functools.partial(layer_kernel, chips),
        out_shape=(
            low(length, width), full(length, width), low(length, width), low(length, cols),
            low(width, 3 * cols), low(length, 3 * cols), low(length, 2 * cols), low(length, cols), full(length, 256),
            low(2, 2, rows, units), low(2, 6, rows, units),
            jax.ShapeDtypeStruct((1, length), jnp.int32), full(2, width), full(2, units), full(rows, units),
        ),
        in_specs=[anyspec] * 4 + [vspec] * 5,
        out_specs=(anyspec,) * 15,
        scratch_shapes=[
            VM((1, length), jnp.int32), VM((2, width), F32), VM((2, units), F32), VM((rows, units), F32),
            square, VM((2, length, cols), BF), VM((2, width, cols), BF), weight, weight, weight,
            tall, square, wide, wide, wide, square, tall, square, square, square, weight,
            VM((chips - 1, rows, units), BF), VM((2, rows, units), BF),
            sem((6 + 3 * (units // width),)), sem((4 + blocks,)), sem((4,)), sem((2, 2)),
            sem((4,)), sem((blocks,)), sem((blocks,)), sem, sem, sem((2,)), sem((number,)), sem((number,)), sem((number,)), sem((number,)),
            sem((5,)), sem((5, 2, chips // 2)), sem((5,)), sem((5,)), sem((5,)),
            pltpu.SemaphoreType.REGULAR((3,)), sem((3,)), sem((3,)), sem((2,)), sem((2, chips - 1)),
        ],
        compiler_params=pltpu.CompilerParams(collective_id=6, has_side_effects=True, vmem_limit_bytes=63 * MIB),
        name="layer",
    )(attn_w, mlp_w, states, out_grad, doc, gain, freq[None], mix, scales)


SCATTER_LONG = (0, 3, 5)
MATRIX_OF = {2: 3, 3: 2, 4: 1, 5: 0}


def back_pieces(length):
    half = BLOCK // 2
    return [(length - half, half), (length - BLOCK, half)] + [(start, BLOCK) for start in range(length - 2 * BLOCK, -1, -BLOCK)]


def stepped(param, moment, grad, rate):
    moment_new = MOMENTUM * moment + grad
    return moment_new, param - rate * (grad + MOMENTUM * moment_new)


def backward_kernel(
    rate, x_hbm, w_hbm, qkv_hbm, r_hbm, y_hbm, dy_hbm, do_hbm, dri_hbm, carry_hbm, rest_hbm, tables_hbm,
    wa_hbm, ma_hbm, wm_hbm, mm_hbm, gain_ref, start_ref, gd_ref, mix_ref, us_ref,
    ig_o, ga_o, gm_o, sum_a_o, sum_m_o,
    ga_s, gm_s, x_ref, w_ref, qkv_ref, r_ref, y_ref, dy_ref, do_ref, carry, rest, tables_ref, dri_s,
    wa_ref, ma_ref, wm_ref, mm_ref,
    bias, dq_s, dk_s, dv_s, low_s, out_s, in_s, dw_s, near, ring_a, ring_m, head_s, mine_a, got_a, mine_m, got_m,
    load, load_dri, store, save, send, recv, pair_send, pair_recv, ring_send, ring_recv, all_send, all_recv,
):
    chips, rows_own = near.shape[1:3]
    index, x, place, core, right, left, pair, across = peers_of(chips)
    length, cols = y_ref.shape
    width = x_ref.shape[1]
    parts = back_pieces(length)
    blocks = len(parts)
    stages = got_m.shape[0]
    others = [(ring_device((place + d) % chips, core, chips), x) for d in range(1, chips)]
    turns = [(index + (1 << s) * (1 - 2 * ((index // (1 << s)) % 2)), x) for s in range(stages)]
    pieces = (
        (carry_hbm, carry), (qkv_hbm, qkv_ref), (dy_hbm, dy_ref), (y_hbm, y_ref),
        (tables_hbm, tables_ref), (r_hbm, r_ref), (w_hbm, w_ref), (rest_hbm, rest),
        (do_hbm, do_ref), (x_hbm, x_ref), (wm_hbm, wm_ref), (mm_hbm, mm_ref), (wa_hbm, wa_ref), (ma_hbm, ma_ref),
    )
    loads = [start_copy(src, dst, load.at[j]) for j, (src, dst) in enumerate(pieces)]
    greet([pair, across] + others)

    def mine(group, way, to_go, chip):
        if group < 2:
            wide_way = 0 if group in SCATTER_LONG else 1
            return rest.at[group, 5 if to_go == 0 else to_go - 1 if way == wide_way else 2 + to_go]
        return near.at[MATRIX_OF[group], chip]

    def slot(group, at):
        if group < 2:
            return ring_m.at[group, at]
        return ring_a.at[at, MATRIX_OF[group]]

    def result(group):
        return gm_s.at[group] if group < 2 else ga_s.at[MATRIX_OF[group]]

    def sent(group):
        return ring_m.at[group, pl.ds(0, chips - 3 + 2 * group)] if group < 2 else ring_a.at[:, MATRIX_OF[group]]

    scatter = Scatter(chips, SCATTER_LONG, mine, slot, result, sent, ring_send, ring_recv)
    tick, launch = scatter.tick, scatter.launch

    def send_pair(j):
        for chip in range(chips):
            there = pl.multiple_of((chip * 2 + 1 - core) * rows_own, rows_own)
            remote(dw_s.at[j, pl.ds(there, rows_own)], near.at[j, chip], pair_send.at[j], pair_recv.at[j], pair).start()

    def sum_pair(j):
        remote(near.at[j], near.at[j], pair_send.at[j], pair_recv.at[j], pair).wait()
        for chip in range(chips):
            own = pl.ds(pl.multiple_of((chip * 2 + core) * rows_own, rows_own), rows_own)
            here = near.at[j, chip]
            add_all(here, [here, dw_s.at[j, own]])

    loads[0].wait()
    for group, hop in ((1, 1), (0, 2)):
        for way in (0, 1):
            scatter.go(group, way, hop, carry.at[group, way])
    dk_s[...] = jnp.zeros_like(dk_s)
    dv_s[...] = jnp.zeros_like(dv_s)
    head_s[...] = jnp.zeros_like(head_s)
    ones = head_ones()
    copies, stores = {}, []

    def fetch_dri(block):
        start, size = parts[block]
        return start_copy(dri_hbm.at[pl.ds(start, size)], dri_s.at[block % 2, pl.ds(0, size)], load_dri.at[block])

    fetched = {block: fetch_dri(block) for block in (0, 1)}

    def finish_input(block):
        start, size = parts[block]
        copies[block].wait()
        fetched[block].wait()
        for i in range(0, size, 128):
            r = pl.ds(start + i, 128)
            total = out_s[r].astype(F32) + in_s[r].astype(F32)
            out_s[r] = (dri_s[block % 2, pl.ds(i, 128)] + total).astype(BF)
        rows = pl.ds(start, size)
        stores.append(start_copy(out_s.at[rows], ig_o.at[rows], store.at[block]))
        if block + 2 < blocks:
            fetched[block + 2] = fetch_dri(block + 2)

    for copy in loads[1:4]:
        copy.wait()

    def attend(block):
        start, size = parts[block]
        first = max(0, start - SPAN)
        keys = start + size - first
        rows = pl.ds(start, size)
        span = pl.ds(first, keys)
        kpos = lax.broadcasted_iota(jnp.int32, (keys, size), 0) + first
        qpos = lax.broadcasted_iota(jnp.int32, (keys, size), 1) + start
        allowed = (kpos >= start_ref[:, start : start + size]) & (kpos <= qpos)
        bias[:keys, :size] = jnp.where(allowed, 0.0, NEG_FILL)

        def heads(pair_of, _):
            at = pl.multiple_of(pair_of * 128, 128)
            c = pl.ds(at, 128)
            q, dy = qkv_ref[rows, c], dy_ref[rows, c]
            k, v = qkv_ref[span, pl.ds(cols + at, 128)], qkv_ref[span, pl.ds(2 * cols + at, 128)]
            prod = dy.astype(F32) * y_ref[rows, c].astype(F32)
            prod_high = prod.astype(BF)
            prod_low = (prod - prod_high.astype(F32)).astype(BF)
            dq = jnp.zeros((size, 128), F32)
            dk = jnp.zeros((keys, 128), F32)
            dv = jnp.zeros((keys, 128), F32)
            for half in (0, 1):
                mask, row = half_of(size, half), half_of(8, half)
                qm, dym, km = q * mask, dy * mask, k * half_of(keys, half)
                expo = jnp.exp(dot_nt(k, qm) + bias[:keys, :size])
                probs = expo * (1.0 / jnp.sum(expo, axis=0, keepdims=True))
                delta = (dot_nt(row, prod_high) + dot_nt(row, prod_low))[0:1]
                dz = (probs * (dot_nt(v, dym) - delta)).astype(BF)
                dk = dk + dot_nn(dz, qm)
                dv = dv + dot_nn(probs.astype(BF), dym)
                dq = dq + dot_tn(dz, km)
            dq_s[rows, c] = dq * HD**-0.5
            dk_s[span, c] = dk_s[span, c] + dk
            dv_s[span, c] = dv_s[span, c] + dv
            return 0

        return heads

    def project_back(block):
        start, size = parts[block]
        rows = pl.ds(start, size)
        cos, sin = tables_ref[rows, 0:128], tables_ref[rows, 128:256]
        for c in range(0, cols, 128):
            s = slice(c, c + 128)
            gain = gain_ref[:, s]
            head = jnp.zeros((size, 128), F32)
            for j, (grad_s, scale) in enumerate(((dq_s, HD**0.5), (dk_s, 1.0))):
                at = slice(j * cols + c, j * cols + c + 128)
                grad = grad_s[rows, s]
                unit = qkv_ref[rows, at].astype(F32) * (scale / gain)
                head = head + grad * unit
                grad = grad * gain
                turned = r_ref[rows, at].astype(F32) * (grad - unit * (split_dot(grad * unit, ones) * (1.0 / HD)))
                low_s[j, rows, s] = (turned * cos - other_half(turned) * sin).astype(BF)
            head_s[:, s] = head_s[:, s] + jnp.sum(head, axis=0, keepdims=True)
            low_s[2, rows, s] = dv_s[rows, s].astype(BF)
        for c in range(0, width, 512):
            part = sum(dot_nt(low_s[j, rows], w_ref[c : c + 512, j * cols : (j + 1) * cols]) for j in range(3))
            out_s[rows, c : c + 512] = part.astype(BF)
        copy = remote(out_s.at[rows], in_s.at[rows], send.at[block], recv.at[block], across)
        copy.start()
        copies[block] = copy

    longest = chips // 2
    pending = [(1, 1), (0, 2), (1, 2), (0, 3), (1, 3), (0, 4), (1, 4)]
    step_pairs = cols // 256
    def weight_grad(j, d, left, right):
        dw_s[j, d] = dot_tn(left, right).astype(BF)

    for block in range(blocks):
        heads = attend(block)
        lax.fori_loop(0, step_pairs, heads, 0)
        if block == 2:
            tick(*pending.pop(0))
        lax.fori_loop(step_pairs, 2 * step_pairs, heads, 0)
        if block == 0:
            for copy in loads[4:8]:
                copy.wait()
        if block == 3:
            tick(*pending.pop(0))
        project_back(block)
        if block == blocks - 1:
            tick(*pending.pop(0))
            tick(2, 1)
        if block == 1:
            tick(*pending.pop(0))
            for copy in loads[8:10]:
                copy.wait()
            by_step(width, BLOCK, lambda d: weight_grad(3, d, do_ref[:, d], y_ref[...]))
            send_pair(3)
        if block == 2:
            tick(*pending.pop(0))
            sum_pair(3)
            launch(2)
    for group in (3, 4, 5):
        j = MATRIX_OF[group]
        by_step(width, BLOCK, lambda d: weight_grad(j, d, x_ref[:, d], low_s[j]))
        send_pair(j)
        if group > 3:
            sum_pair(MATRIX_OF[group - 1])
            launch(group - 1)
    sum_pair(MATRIX_OF[5])
    launch(5)
    tick(*pending.pop(0))
    tick(*pending.pop(0))
    tick(2, 2)
    assert not pending

    def squares(g, w, m):
        count = g.shape[-1]

        def body(i, total):
            r = pl.ds(pl.multiple_of(i * 8, 8), 8)
            step = stepped(w[r], m[r], g[r], rate)[1]
            return total + step * step

        total = lax.fori_loop(0, rows_own // 8, body, jnp.zeros((8, count), F32))
        return jnp.sum(total, axis=0, keepdims=True)

    def exchange(s):
        copy = remote(mine_m.at[s], got_m.at[s], all_send.at[0, s], all_recv.at[0, s], turns[s])
        copy.start()
        return copy

    for copy in loads[10:]:
        copy.wait()
    lanes = mine_m.shape[2]
    mine_m[0] = jnp.zeros(mine_m.shape[1:], F32)
    row = 0

    def place_row(value):
        nonlocal row
        for c in range(0, value.shape[1], lanes):
            size = min(lanes, value.shape[1])
            mine_m[0, row : row + 1, 0:size] = value[:, c : c + size]
            row += 1

    for j in range(3):
        place_row(squares(gd_ref if j == 2 else gm_s.at[j], wm_ref.at[j], mm_ref.at[j]))
    place_row(head_s[...])
    for ref in (mix_ref, us_ref):
        for j in range(2):
            place_row(ref[j : j + 1])
    def attn_squares(j):
        mine_a[0, j : j + 1] = squares(ga_s.at[j], wa_ref.at[j], ma_ref.at[j])

    stores.append(start_copy(gm_s, gm_o, save.at[0]))
    def settle(s, copy):
        copy.wait()
        mine_m[s + 1] = mine_m[s] + got_m[s]

    copy = exchange(0)
    finish_input(0)
    finish_input(1)
    settle(0, copy)
    for hop in range(1, longest + 1):
        if hop < stages:
            copy = exchange(hop)
        if hop == 2:
            finish_input(2)
        for group in (3, 4, 5):
            tick(group, hop)
            if hop == longest:
                attn_squares(MATRIX_OF[group])
        if hop + 2 <= longest:
            tick(2, hop + 2)
            if hop + 2 == longest:
                attn_squares(3)
        if hop < stages:
            settle(hop, copy)
    for hop in range(longest + 1, stages):
        settle(hop, exchange(hop))
    last = remote(mine_a.at[0], got_a.at[0], all_send.at[1, 0], all_recv.at[1, 0], pair)
    last.start()
    stores.append(start_copy(ga_s, ga_o, save.at[1]))
    stores.append(start_copy(mine_m.at[stages], sum_m_o, save.at[2]))
    last.wait()
    mine_a[1] = mine_a[0] + got_a[0]
    for d, peer in enumerate(others):
        remote(mine_a.at[1], got_a.at[1 + d], all_send.at[1, 1], all_recv.at[1, 1], peer).start()
    for block in range(3, blocks):
        finish_input(block)
    every = got_a.at[pl.ds(1, chips - 1)]
    remote(every, every, all_send.at[1, 1], all_recv.at[1, 1], pair).wait()
    total = mine_a[1]
    for d in range(1, chips):
        total = total + got_a[d]
    mine_a[2] = total
    stores.append(start_copy(mine_a.at[2], sum_a_o, save.at[3]))
    for copy in stores:
        copy.wait()
    scatter.close()


def attention_backward(
    states, weights, qkv, factors, y, dy, do, dri, carry, rest, tables, attn_w, attn_mom, mlp_w, mlp_mom,
    gain, start, grad_down, grad_mix, grad_units, rate, fsdp,
):
    length, width = states.shape
    cols = gain.shape[1]
    chips = fsdp // 2
    rows, units = rest.shape[2:]
    stages = fsdp.bit_length() - 1
    vspec, anyspec = pl.BlockSpec(memory_space=VM), pl.BlockSpec(memory_space=pl.ANY)
    blocks = len(back_pieces(length))
    sem = pltpu.SemaphoreType.DMA
    square, full_square = VM((length, cols), BF), VM((length, cols), F32)
    wide = VM((length, width), BF)
    a_rows, m_rows = 4, -(-(3 * (units // width) + 3 + 2 * (units // width)) // 8) * 8
    return pl.pallas_call(
        functools.partial(backward_kernel, rate),
        out_shape=(
            low(length, width), full(4, rows, cols), full(2, rows, units), full(a_rows, cols), full(m_rows, width),
        ),
        in_specs=[anyspec] * 15 + [vspec] * 5,
        out_specs=(anyspec,) * 5,
        scratch_shapes=[
            VM((4, rows, cols), F32), VM((2, rows, units), F32), wide, VM(weights.shape, BF), VM(qkv.shape, BF), VM(factors.shape, BF), square, square,
            wide, VM(carry.shape, BF), VM(rest.shape, BF), VM(tables.shape, F32), VM((2, BLOCK, width), F32),
            VM(attn_w.shape, F32), VM(attn_w.shape, F32), VM(mlp_w.shape, F32), VM(mlp_w.shape, F32),
            VM((BLOCK + SPAN, BLOCK), F32), full_square, full_square, full_square,
            VM((3, length, cols), BF), wide, wide, VM((4, width, cols), BF), VM((4, chips, rows, cols), BF),
            VM((chips - 1, 4, rows, cols), BF), VM((2, chips - 1, rows, units), BF), VM((1, cols), F32),
            VM((3, a_rows, cols), F32), VM((chips, a_rows, cols), F32),
            VM((stages + 1, m_rows, width), F32), VM((stages, m_rows, width), F32),
            sem((14,)), sem((blocks,)), sem((blocks,)), sem((4,)), sem((blocks,)), sem((blocks,)),
            sem((4,)), sem((4,)), sem((6,)), sem((6, chips - 1)), sem((2, stages)), sem((2, stages)),
        ],
        compiler_params=pltpu.CompilerParams(collective_id=5, has_side_effects=True, vmem_limit_bytes=63 * MIB),
        name="attention_backward",
    )(
        states, weights, qkv, factors, y, dy, do, dri, carry, rest, tables, attn_w, attn_mom, mlp_w, mlp_mom,
        gain, start, grad_down, grad_mix, grad_units,
    )


def update_kernel(
    rates, width, ig, hid, ga, gm, gd, sa, sm, wa, ma, aa, wm, mm, am, hs, hm, mr, mo, us, um,
    hid_o, ig_o, ma_o, wa_o, aa_o, mm_o, wm_o, am_o, hm_o, hs_o, mo_o, mr_o, um_o, us_o,
):
    hid_o[0] = hid[...].astype(F32)
    ig_o[0] = ig[...].astype(F32)
    lanes = sm.shape[1]
    cols, units = wa.shape[2], wm.shape[2]

    def matrix(j, grad, total, refs, outs):
        w, m, a = (ref[j] for ref in refs)
        moment, step = stepped(w, m, grad, rates[0])
        new = step * lax.rsqrt(total / width + EPS)
        outs[0][j] = moment
        outs[1][j] = new
        outs[2][j] = AVERAGE * a + (1.0 - AVERAGE) * new

    def wide(row):
        return jnp.concatenate([sm[row + c : row + c + 1] for c in range(units // lanes)], axis=1)

    for j in range(4):
        matrix(j, ga[j], sa[j : j + 1], (wa, ma, aa), (ma_o, wa_o, aa_o))
    for j in range(3):
        matrix(j, gd[...] if j == 2 else gm[j], wide(j * (units // lanes)), (wm, mm, am), (mm_o, wm_o, am_o))

    @pl.when(pl.program_id(0) == 0)
    def _():
        row = 3 * (units // lanes)
        hm_o[...], hs_o[...] = stepped(hs[...], hm[...], sm[row : row + 1, :cols], rates[1])
        mo_o[...], mr_o[...] = stepped(mr[...], mo[...], sm[row + 1 : row + 3], rates[2])
        row += 3
        grad = jnp.concatenate([wide(row), wide(row + units // lanes)], axis=0)
        um_o[...], us_o[...] = stepped(us[...], um[...], grad, rates[3])


def update(input_low, hidden_low, ga, gm, gd, sa, sm, wa, ma, aa, wm, mm, am, hs, hm, mr, mo, us, um, rates):
    length, width = input_low.shape
    rows, cols, units = wa.shape[1], wa.shape[2], wm.shape[2]
    steps, block = rows // 16, 16
    tall = length // steps

    def whole(shape):
        return pl.BlockSpec(shape, lambda i: (0,) * len(shape))

    state = pl.BlockSpec((tall, width), lambda i: (i, 0))
    state_o = pl.BlockSpec((1, tall, width), lambda i: (0, i, 0))
    attn = pl.BlockSpec((4, block, cols), lambda i: (0, i, 0))
    mlp = pl.BlockSpec((3, block, units), lambda i: (0, i, 0))
    small = [whole((1, cols))] * 2 + [whole(mr.shape)] * 2 + [whole(us.shape)] * 2
    return pl.pallas_call(
        functools.partial(update_kernel, rates, width),
        grid=(steps,),
        out_shape=(
            full(1, length, width), full(1, length, width), *(full(*wa.shape),) * 3, *(full(*wm.shape),) * 3,
            *(full(1, cols),) * 2, *(full(*mr.shape),) * 2, *(full(*us.shape),) * 2,
        ),
        in_specs=[
            state, state, attn, pl.BlockSpec((2, block, units), lambda i: (0, i, 0)), pl.BlockSpec((block, units), lambda i: (i, 0)),
            whole(sa.shape), whole(sm.shape), attn, attn, attn, mlp, mlp, mlp, *small,
        ],
        out_specs=(state_o, state_o, attn, attn, attn, mlp, mlp, mlp, *small),
        compiler_params=pltpu.CompilerParams(vmem_limit_bytes=60 * MIB),
        name="update_weights",
    )(input_low, hidden_low, ga, gm, gd, sa, sm, wa, ma, aa, wm, mm, am, hs, hm, mr, mo, us, um)


def local_fast(
    inputs, doc_ids, out_grad, attn_w, attn_mom, attn_avg, mlp_w, mlp_mom, mlp_avg,
    head_scale, head_mom, mix_rates, mix_mom, unit_scales, unit_mom,
):
    fsdp = lax.axis_size("fsdp")
    root_tokens = math.sqrt(inputs.shape[0] * fsdp * inputs.shape[1])
    rates = tuple(rate / root_tokens for rate in (RATE_WEIGHT, RATE_HEAD, RATE_MIX, RATE_UNITS))
    states, gain = inputs[0], head_scale[None]
    hidden_low, dri, do, dy, w_in, qkv, factors, y, tables, carry, rest, start, grad_mix, grad_units, grad_down = layer(
        attn_w, mlp_w, states, out_grad[0], doc_ids, gain, mix_rates, unit_scales, fsdp
    )
    input_low, grad_attn, grad_mlp, total_attn, total_rest = attention_backward(
        states, w_in, qkv, factors, y, dy, do, dri, carry, rest, tables, attn_w, attn_mom, mlp_w, mlp_mom,
        gain, start, grad_down, grad_mix, grad_units, rates[0], fsdp,
    )
    outs = update(
        input_low, hidden_low, grad_attn, grad_mlp, grad_down, total_attn, total_rest,
        attn_w, attn_mom, attn_avg, mlp_w, mlp_mom, mlp_avg,
        gain, head_mom[None], mix_rates, mix_mom, unit_scales, unit_mom, rates,
    )
    return (*outs[:8], outs[8][0], outs[9][0], *outs[10:])


def local(
    inputs,
    doc_ids,
    out_grad,
    attn_w,
    attn_mom,
    attn_avg,
    mlp_w,
    mlp_mom,
    mlp_avg,
    head_scale,
    head_mom,
    mix_rates,
    mix_mom,
    unit_scales,
    unit_mom,
):
    length = inputs.shape[1]
    model_width = inputs.shape[2]
    head_count = head_scale.shape[0] // HD
    block_rows = min(512, length)
    block_count = length // block_rows
    tokens = inputs.shape[0] * lax.axis_size("fsdp") * length
    doc_row = doc_ids[0]
    input_low = inputs[0]
    resid_in = input_low.astype(jnp.float32)
    cos_table, sin_table = rotary_tables(doc_row)
    position = jnp.arange(length, dtype=jnp.int32)
    attn_full = lax.all_gather(attn_w.astype(jnp.bfloat16), "fsdp", axis=1, tiled=True)
    projected = jnp.einsum(
        "sd,jdc->jsc", input_low, attn_full[:3], preferred_element_type=jnp.float32
    )
    head_gain = head_scale.reshape(head_count, HD)
    q_rot = rotate(projected[0].reshape(length, head_count, HD), cos_table, sin_table)
    k_rot = rotate(projected[1].reshape(length, head_count, HD), cos_table, sin_table)
    q_unit = rms_unit(q_rot)
    k_unit = rms_unit(k_rot)
    query_low = (head_gain * q_unit).astype(jnp.bfloat16)
    key_low = (head_gain * k_unit).astype(jnp.bfloat16)
    value_low = projected[2].reshape(length, head_count, HD).astype(jnp.bfloat16)

    def scores_of(row_first):
        query_blk = lax.dynamic_slice_in_dim(query_low, row_first, block_rows, 0)
        raw_scores = jnp.einsum(
            "qhe,khe->hqk", query_blk, key_low, preferred_element_type=jnp.float32
        )
        row_pos = lax.dynamic_slice_in_dim(position, row_first, block_rows, 0)
        row_docs = lax.dynamic_slice_in_dim(doc_row, row_first, block_rows, 0)
        allowed = (row_docs[:, None] == doc_row[None, :]) & (position[None, :] <= row_pos[:, None])
        return (jnp.where(allowed[None], raw_scores * HD ** (-0.5), NEG_FILL), query_blk)

    def attend(accums, blk_index):
        scores, query_blk = scores_of(blk_index * block_rows)
        peak_val = jnp.max(scores, axis=-1, keepdims=True)
        expo_vals = jnp.exp(scores - peak_val)
        row_total = jnp.sum(expo_vals, axis=-1, keepdims=True)
        probs_low = (expo_vals / row_total).astype(jnp.bfloat16)
        blk_out = jnp.einsum(
            "hqk,khe->qhe", probs_low, value_low, preferred_element_type=jnp.float32
        )
        return (accums, (blk_out, (peak_val + jnp.log(row_total))[..., 0]))

    _, (mixed_blocks, log_totals) = lax.scan(attend, None, jnp.arange(block_count))
    mixed_low = mixed_blocks.reshape(length, head_count * HD).astype(jnp.bfloat16)
    attn_part = jnp.einsum("sc,dc->sd", mixed_low, attn_full[3], preferred_element_type=jnp.float32)
    attn_out = lax.psum(attn_part, "mp")
    attn_unit = rms_unit(attn_out)
    resid_one = resid_in + mix_rates[0] * (attn_unit - resid_in)
    hidden_one = rms_unit(resid_one)
    hidden_low = hidden_one.astype(jnp.bfloat16)
    mlp_full = lax.all_gather(mlp_w.astype(jnp.bfloat16), "fsdp", axis=1, tiled=True)
    gates = jnp.einsum("sd,jdf->jsf", hidden_low, mlp_full[:2], preferred_element_type=jnp.float32)
    up_proj = gates[0]
    gate_proj = gates[1]
    gate_arg = unit_scales[1] * gate_proj * D ** (-0.5)
    gate_sig = jax.nn.sigmoid(gate_arg)
    gate_act = gate_arg * gate_sig
    units_low = (unit_scales[0] * up_proj * gate_act).astype(jnp.bfloat16)
    mlp_part = jnp.einsum("sf,df->sd", units_low, mlp_full[2], preferred_element_type=jnp.float32)
    mlp_out = lax.psum(mlp_part, "mp")
    mlp_unit = rms_unit(mlp_out)
    resid_two = hidden_one + mix_rates[1] * (mlp_unit - hidden_one)
    result = rms_unit(resid_two)
    cotangent = out_grad[0].astype(jnp.float32)
    d_resid_two = rms_back(resid_two, cotangent)
    grad_mix_mlp = jnp.sum(d_resid_two * (mlp_unit - hidden_one), axis=0)
    d_hidden_one = d_resid_two * (1.0 - mix_rates[1])
    d_mlp_low = rms_back(mlp_out, mix_rates[1] * d_resid_two).astype(jnp.bfloat16)
    mlp_back = lax.all_gather(mlp_w.astype(jnp.bfloat16), "fsdp", axis=1, tiled=True)
    d_units = jnp.einsum("sd,df->sf", d_mlp_low, mlp_back[2], preferred_element_type=jnp.float32)
    d_up = d_units * unit_scales[0] * gate_act
    d_arg = d_units * unit_scales[0] * up_proj * gate_sig * (1.0 + gate_arg * (1.0 - gate_sig))
    d_gate = d_arg * unit_scales[1] * D ** (-0.5)
    grad_units = jnp.stack(
        [
            jnp.sum(d_units * up_proj * gate_act, axis=0),
            jnp.sum(d_arg * gate_proj * D ** (-0.5), axis=0),
        ]
    )
    d_gates_low = jnp.stack([d_up, d_gate]).astype(jnp.bfloat16)
    mlp_back_part = jnp.einsum(
        "jsf,jdf->sd", d_gates_low, mlp_back[:2], preferred_element_type=jnp.float32
    )
    d_hidden_one = d_hidden_one + lax.psum(mlp_back_part, "mp")
    right_cols = d_mlp_low
    left_cols = hidden_low
    grad_mlp = jnp.transpose(
        lax.psum_scatter(
            jnp.concatenate(
                [
                    jnp.einsum(
                        "sd,jsf->djf", left_cols, d_gates_low, preferred_element_type=jnp.float32
                    ),
                    jnp.einsum(
                        "sd,sf->df", right_cols, units_low, preferred_element_type=jnp.float32
                    )[:, None, :],
                ],
                axis=1,
            ),
            "fsdp",
            scatter_dimension=0,
            tiled=True,
        ),
        (1, 0, 2),
    )
    d_resid_one = rms_back(resid_one, d_hidden_one)
    grad_mix_attn = jnp.sum(d_resid_one * (attn_unit - resid_in), axis=0)
    d_resid_in = d_resid_one * (1.0 - mix_rates[0])
    d_attn_low = rms_back(attn_out, mix_rates[0] * d_resid_one).astype(jnp.bfloat16)
    attn_back = lax.all_gather(attn_w.astype(jnp.bfloat16), "fsdp", axis=1, tiled=True)
    d_mixed = jnp.einsum("sd,dc->sc", d_attn_low, attn_back[3], preferred_element_type=jnp.float32)
    d_mixed = d_mixed.astype(jnp.bfloat16).reshape(length, head_count, HD)

    def attend_back(accums, blk_index):
        d_key, d_value = accums
        row_first = blk_index * block_rows
        scores, query_blk = scores_of(row_first)
        blk_total = lax.dynamic_index_in_dim(log_totals, blk_index, 0, keepdims=False)
        attn_probs = jnp.exp(scores - blk_total[..., None])
        d_out_blk = lax.dynamic_slice_in_dim(d_mixed, row_first, block_rows, 0)
        d_probs = jnp.einsum(
            "qhe,khe->hqk", d_out_blk, value_low, preferred_element_type=jnp.float32
        )
        d_scores = attn_probs * (d_probs - jnp.sum(attn_probs * d_probs, axis=-1, keepdims=True))
        d_raw_low = (d_scores * HD ** (-0.5)).astype(jnp.bfloat16)
        d_query = jnp.einsum("hqk,khe->qhe", d_raw_low, key_low, preferred_element_type=jnp.float32)
        d_key = d_key + jnp.einsum(
            "hqk,qhe->khe", d_raw_low, query_blk, preferred_element_type=jnp.float32
        )
        d_value = d_value + jnp.einsum(
            "hqk,qhe->khe",
            attn_probs.astype(jnp.bfloat16),
            d_out_blk,
            preferred_element_type=jnp.float32,
        )
        return ((d_key, d_value), d_query)

    zero_heads = jnp.zeros((length, head_count, HD), jnp.float32)
    (d_key_all, d_value_all), d_query_blocks = lax.scan(
        attend_back, (zero_heads, zero_heads), jnp.arange(block_count)
    )
    d_query_all = d_query_blocks.reshape(length, head_count, HD)
    grad_head = jnp.sum(d_query_all * q_unit + d_key_all * k_unit, axis=0).reshape(-1)
    d_query_raw = rotate_back(rms_back(q_rot, head_gain * d_query_all), cos_table, sin_table)
    d_key_raw = rotate_back(rms_back(k_rot, head_gain * d_key_all), cos_table, sin_table)
    d_proj_low = jnp.stack(
        [
            d_query_raw.reshape(length, -1),
            d_key_raw.reshape(length, -1),
            d_value_all.reshape(length, -1),
        ]
    ).astype(jnp.bfloat16)
    grad_mix = jnp.stack([grad_mix_attn, grad_mix_mlp])
    grad_head, grad_mix, grad_units = lax.psum((grad_head, grad_mix, grad_units), "fsdp")
    attn_back_part = jnp.einsum(
        "jsc,jdc->sd", d_proj_low, attn_back[:3], preferred_element_type=jnp.float32
    )
    input_grad = d_resid_in + lax.psum(attn_back_part.astype(jnp.bfloat16), "mp").astype(
        jnp.float32
    )
    left_cols = input_low
    right_cols = d_attn_low
    in_terms = jnp.einsum("sd,jsc->djc", left_cols, d_proj_low, preferred_element_type=jnp.float32)
    out_terms = jnp.einsum("sd,sc->dc", right_cols, mixed_low, preferred_element_type=jnp.float32)
    grad_attn = jnp.transpose(
        lax.psum_scatter(
            jnp.concatenate([in_terms, out_terms[:, None, :]], axis=1),
            "fsdp",
            scatter_dimension=0,
            tiled=True,
        ),
        (1, 0, 2),
    )
    root_tokens = math.sqrt(tokens)
    weight_rate = RATE_WEIGHT / root_tokens
    attn_mom_new, attn_step = nesterov(attn_w, attn_mom, grad_attn, weight_rate)
    mlp_mom_new, mlp_step = nesterov(mlp_w, mlp_mom, grad_mlp, weight_rate)
    attn_squares = jnp.sum(attn_step * attn_step, axis=1)
    mlp_squares = jnp.sum(mlp_step * mlp_step, axis=1)
    attn_squares, mlp_squares = lax.psum((attn_squares, mlp_squares), "fsdp")
    attn_new = attn_step * lax.rsqrt(attn_squares[:, None, :] / model_width + EPS)
    mlp_new = mlp_step * lax.rsqrt(mlp_squares[:, None, :] / model_width + EPS)
    head_mom_new, head_new = nesterov(head_scale, head_mom, grad_head, RATE_HEAD / root_tokens)
    mix_mom_new, mix_new = nesterov(mix_rates, mix_mom, grad_mix, RATE_MIX / root_tokens)
    units_mom_new, units_new = nesterov(unit_scales, unit_mom, grad_units, RATE_UNITS / root_tokens)
    return (
        result[None],
        input_grad[None],
        attn_mom_new,
        attn_new,
        AVERAGE * attn_avg + (1.0 - AVERAGE) * attn_new,
        mlp_mom_new,
        mlp_new,
        AVERAGE * mlp_avg + (1.0 - AVERAGE) * mlp_new,
        head_mom_new,
        head_new,
        mix_mom_new,
        mix_new,
        units_mom_new,
        units_new,
    )


def solution(mesh):
    fsdp = mesh.shape["fsdp"]
    fast = fsdp == 16 and D // fsdp % 16 == 0
    placed = (
        P("fsdp", None, None),
        P("fsdp", None),
        P("fsdp", None, None),
        P(None, "fsdp", "mp"),
        P(None, "fsdp", "mp"),
        P(None, "fsdp", "mp"),
        P(None, "fsdp", "mp"),
        P(None, "fsdp", "mp"),
        P(None, "fsdp", "mp"),
        P("mp"),
        P("mp"),
        P(),
        P(),
        P(None, "mp"),
        P(None, "mp"),
    )
    return jax.shard_map(
        local_fast if fast else local,
        mesh=mesh,
        in_specs=placed,
        out_specs=(
            P("fsdp", None, None),
            P("fsdp", None, None),
            P(None, "fsdp", "mp"),
            P(None, "fsdp", "mp"),
            P(None, "fsdp", "mp"),
            P(None, "fsdp", "mp"),
            P(None, "fsdp", "mp"),
            P(None, "fsdp", "mp"),
            P("mp"),
            P("mp"),
            P(),
            P(),
            P(None, "mp"),
            P(None, "mp"),
        ),
        check_vma=False,
    )
```

```python
import functools
import math

import jax
import jax.numpy as jnp
import numpy as np
from jax import lax
from jax.experimental import pallas as pl
from jax.experimental.pallas import tpu as pltpu
from jax.sharding import PartitionSpec as P

D = 1024
HD = 64


EPS = 1e-06
MOMENTUM = 0.9
AVERAGE = 0.9
NEG_FILL = -1e30
THETA = 10000.0
RATE_WEIGHT = 50.0
RATE_HEAD = 0.08
RATE_MIX = 0.02
RATE_UNITS = 0.5


def rms_unit(vector):
    return vector * lax.rsqrt(jnp.mean(vector * vector, axis=-1, keepdims=True) + EPS)


def rms_back(vector, grad):
    factor = lax.rsqrt(jnp.mean(vector * vector, axis=-1, keepdims=True) + EPS)
    unit_vec = vector * factor
    return factor * (grad - unit_vec * jnp.mean(grad * unit_vec, axis=-1, keepdims=True))


def rotary_tables(doc_row):
    length = doc_row.shape[0]
    position = jnp.arange(length, dtype=jnp.int32)
    boundary = jnp.concatenate(
        [jnp.ones((1,), jnp.int32), (doc_row[1:] != doc_row[:-1]).astype(jnp.int32)]
    )
    doc_start = lax.cummax(jnp.where(boundary > 0, position, 0), axis=0)
    offset = (position - doc_start).astype(jnp.float32)
    freq = THETA ** (-2.0 * jnp.arange(HD // 2, dtype=jnp.float32) / HD)
    angle = offset[:, None] * freq[None, :]
    return (jnp.cos(angle), jnp.sin(angle))


def rotate(vector, cos_table, sin_table):
    half_dim = vector.shape[-1] // 2
    lower_half = vector[..., :half_dim]
    upper_half = vector[..., half_dim:]
    cos_part = cos_table[:, None, :]
    sin_part = sin_table[:, None, :]
    return jnp.concatenate(
        [
            lower_half * cos_part - upper_half * sin_part,
            lower_half * sin_part + upper_half * cos_part,
        ],
        axis=-1,
    )


def rotate_back(grad, cos_table, sin_table):
    half_dim = grad.shape[-1] // 2
    lower_half = grad[..., :half_dim]
    upper_half = grad[..., half_dim:]
    cos_part = cos_table[:, None, :]
    sin_part = sin_table[:, None, :]
    return jnp.concatenate(
        [
            lower_half * cos_part + upper_half * sin_part,
            upper_half * cos_part - lower_half * sin_part,
        ],
        axis=-1,
    )


def nesterov(param, moment, grad, step_rate):
    moment_new = MOMENTUM * moment + grad
    return (moment_new, param - step_rate * (grad + MOMENTUM * moment_new))


BF = jnp.bfloat16
F32 = jnp.float32
MESH = pl.DeviceIdType.MESH
VM = pltpu.VMEM
MIB = 1 << 20
BLOCK = 256
SPAN = 512
ROWS_STEP = 128
UNIT_STEP = 1024


def dot_nn(a, b):
    return lax.dot_general(a, b, (((1,), (0,)), ((), ())), preferred_element_type=F32)


def dot_nt(a, b):
    return lax.dot_general(a, b, (((1,), (1,)), ((), ())), preferred_element_type=F32)


def dot_tn(a, b):
    return lax.dot_general(a, b, (((0,), (0,)), ((), ())), preferred_element_type=F32)


def split_dot(a, ones):
    high = a.astype(BF)
    return dot_nn(high, ones) + dot_nn((a - high.astype(F32)).astype(BF), ones)


def ring_place(index, chips):
    z, y = index // 4, (index // 2) % 2
    return z + y * (chips - 1 - 2 * z), index % 2


def ring_device(place, core, chips):
    y = place // (chips // 2)
    return ((place + y * (chips - 1 - 2 * place)) * 2 + y) * 2 + core


def peers_of(chips):
    index, x = lax.axis_index("fsdp"), lax.axis_index("mp")
    place, core = ring_place(index, chips)
    right = (ring_device((place + 1) % chips, core, chips), x)
    left = (ring_device((place + chips - 1) % chips, core, chips), x)
    return index, x, place, core, right, left, (index + 1 - 2 * core, x), (index, 1 - x)


def greet(peers):
    barrier = pltpu.get_barrier_semaphore()
    for peer in peers:
        pl.semaphore_signal(barrier, inc=1, device_id=peer, device_id_type=MESH)
    pl.semaphore_wait(barrier, len(peers))


def remote(src, dst, send, recv, peer):
    return pltpu.make_async_remote_copy(
        src_ref=src, dst_ref=dst, send_sem=send, recv_sem=recv, device_id=peer, device_id_type=MESH
    )


def start_copy(src, dst, sem):
    copy = pltpu.make_async_copy(src, dst, sem)
    copy.start()
    return copy


def by_step(total, step, body, first=0):
    def run(i, _):
        body(pl.ds(pl.multiple_of(first + i * step, step), step))
        return 0

    lax.fori_loop(0, total // step, run, 0)


def add_all(dst, refs):
    if len(dst.shape) == 3:
        for j in range(dst.shape[0]):
            add_all(dst.at[j], [ref.at[j] for ref in refs])
        return

    def body(r):
        total = refs[0][r].astype(F32)
        for ref in refs[1:]:
            total = total + ref[r].astype(F32)
        dst[r] = total.astype(dst.dtype)

    by_step(dst.shape[0], 16, body)


def ring_hops(chips, group, long_right):
    pair_of = (chips // 2, chips - 1 - chips // 2)
    return pair_of if group in long_right else pair_of[::-1]


class Scatter:
    def __init__(self, chips, long_right, mine, slot, result, sent, send, recv):
        _, _, self.place, self.core, self.right, self.left, _, _ = peers_of(chips)
        self.chips, self.long_right, self.mine, self.slot_at, self.result = chips, long_right, mine, slot, result
        self.send, self.recv, self.sent = send, recv, sent

    def hops(self, group):
        return ring_hops(self.chips, group, self.long_right)

    def term(self, group, way, to_go):
        step = to_go if way == 0 else self.chips - to_go
        return self.mine(group, way, to_go, ring_device((self.place + step) % self.chips, self.core, self.chips) // 2)

    def at(self, group, way, hop):
        return hop - 1 if way == 0 else self.hops(group)[0] + hop - 1

    def slot(self, group, way, hop):
        return self.slot_at(group, self.at(group, way, hop))

    def copy(self, group, way, hop, src):
        at, peer = self.at(group, way, hop), self.right if way == 0 else self.left
        return remote(src, self.slot_at(group, at), self.send.at[group], self.recv.at[group, at], peer)

    def go(self, group, way, hop, src):
        self.copy(group, way, hop, src).start()

    def launch(self, group):
        for way in (0, 1):
            self.go(group, way, 1, self.term(group, way, self.hops(group)[way]))

    def take(self, group, way, hop):
        here = self.slot(group, way, hop)
        self.copy(group, way, hop, here).wait_recv()
        return here

    def tick(self, group, hop):
        hops = self.hops(group)
        for way in (0, 1):
            if hop > hops[way]:
                continue
            here = self.take(group, way, hop)
            if hop < hops[way]:
                add_all(here, [here, self.term(group, way, hops[way] - hop)])
                self.go(group, way, hop + 1, here)
        if hop == self.chips // 2:
            ends = [self.slot(group, way, hops[way]) for way in (0, 1)]
            add_all(self.result(group), [self.term(group, 0, 0)] + ends)

    def close(self):
        for group in range(self.send.shape[0]):
            ref = self.sent(group)
            remote(ref, ref, self.send.at[group], self.send.at[group], self.right).wait_send()


def head_ones():
    row = lax.broadcasted_iota(jnp.int32, (128, 128), 0) // HD
    col = lax.broadcasted_iota(jnp.int32, (128, 128), 1) // HD
    return jnp.where(row == col, 1.0, 0.0).astype(BF)


def half_of(rows, half):
    lane = lax.broadcasted_iota(jnp.int32, (rows, 128), 1)
    return jnp.where((lane < HD) == (half == 0), 1.0, 0.0).astype(BF)


def other_half(v):
    lane = lax.broadcasted_iota(jnp.int32, v.shape, 1)
    return jnp.where(lane % HD < HD // 2, pltpu.roll(v, 128 - HD // 2, 1), pltpu.roll(v, HD // 2, 1))


def first_key(block):
    return max(0, block * BLOCK - SPAN)


def low(*shape):
    return jax.ShapeDtypeStruct(shape, BF)


def full(*shape):
    return jax.ShapeDtypeStruct(shape, F32)


GATHER_LONG = (0, 2, 4)
FEED_LONG = (0, 1)


def row_factor(v):
    return lax.rsqrt(jnp.mean(v * v, axis=-1, keepdims=True) + EPS)


def unit_back(factor, unit, grad):
    return factor * (grad - unit * jnp.mean(grad * unit, axis=-1, keepdims=True))


def fold(v):
    return jnp.sum(v.reshape(v.shape[0] // 8, 8, v.shape[1]), axis=0)


def feed_chunks(length):
    half = BLOCK // 2
    return [(0, half)] + [(start, BLOCK) for start in range(half, length - half, BLOCK)] + [(length - half, half)]


def layer_kernel(
    chips, attn_hbm, mlp_hbm, x_hbm, og_hbm, doc_ref, gain_ref, freq_ref, mix_ref, us_ref,
    out_o, dri_o, do_o, dy_o, w_o, qkv_o, r_o, y_o, tables_o, carry_o, rest_o, start_o, mix_o, us_o, gd_o,
    start_s, mix_s, us_s, gd_s, x_ref, y_ref, wo_s, wu_s, wg_s, wd_s, o_s, hb_s, u_s, g_s, hid_s, dm_s, dh_s, own_s, got_m, got_d, wd_g, ring_d, ring_n,
    load, store, save, rest_save, small_save, send_y, recv_y, wo_send, wo_recv, wo_near, send_m, recv_m, send_d, recv_d,
    gather_send, gather_recv, near_send, near_recv, own_sem, pair_free, pair_send, pair_recv, ring_send, ring_recv,
):
    index, x, place, core, right, left, pair, across = peers_of(chips)
    pair_index = pair[0]
    length, width = x_ref.shape
    cols, units = y_ref.shape[2], us_ref.shape[1]
    rows_own = width // (2 * chips)
    blocks = length // BLOCK
    chunks = feed_chunks(length)
    number = len(chunks)
    longest = chips // 2

    wide = 3 * cols
    loads_attn = [
        start_copy(attn_hbm.at[j], o_s.at[pl.ds(j * rows_own, rows_own), pl.ds(0, cols)], load.at[j]) for j in range(4)
    ]
    halves = units // width
    loads_mlp = [
        start_copy(
            mlp_hbm.at[j, :, pl.ds(h * width, width)],
            o_s.at[pl.ds((4 + j * halves + h) * rows_own, rows_own)], load.at[4 + j * halves + h],
        )
        for j in range(3)
        for h in range(halves)
    ]
    load_x = start_copy(x_hbm, x_ref, load.at[4 + 3 * halves])
    load_og = start_copy(og_hbm, dm_s, load.at[5 + 3 * halves])

    def own(group):
        if group == 0:
            return wd_g.at[pl.ds(0, rows_own), pl.ds(0, wide)]
        if group == 1:
            return wd_g.at[pl.ds(0, rows_own), pl.ds(wide, cols)]
        return wd_g.at[pl.ds((group - 1) * rows_own, rows_own)]

    def block_of(group, dev):
        r = pl.ds(pl.multiple_of(dev * rows_own, rows_own), rows_own)
        if group == 0:
            return g_s.at[r, pl.ds(0, wide)]
        if group == 1:
            return wo_s.at[x, r]
        return (wu_s, wg_s, wd_s)[group - 2].at[r]

    def counts(group):
        return ring_hops(chips, group, GATHER_LONG)

    def origin(way, hop):
        there = (place + chips - hop) % chips if way == 0 else (place + hop) % chips
        return ring_device(there, core, chips)

    def gather_copy(group, way, hop, src, dst):
        peer = right if way == 0 else left
        return remote(src, dst, gather_send.at[group], gather_recv.at[group, way, hop - 1], peer)

    def near_copy(group, src, dev):
        return remote(src, block_of(group, dev), near_send.at[group], near_recv.at[group], pair)

    def blocks_of(group, count):
        r = pl.ds(0, count * rows_own)
        if group == 0:
            return g_s.at[r, pl.ds(0, wide)]
        return wo_s.at[x, r] if group == 1 else (wu_s, wg_s, wd_s)[group - 2].at[r]

    owns = []

    def launch(group):
        for way in (0, 1):
            gather_copy(group, way, 1, own(group), block_of(group, index)).start()
        near_copy(group, own(group), index).start()
        owns.append(start_copy(own(group), block_of(group, index), own_sem.at[group]))

    def tick(group, hop):
        for way in (0, 1):
            if hop > counts(group)[way]:
                continue
            dev = origin(way, hop)
            here = block_of(group, dev)
            gather_copy(group, way, hop, here, here).wait_recv()
            if hop < counts(group)[way]:
                gather_copy(group, way, hop + 1, here, here).start()
            near_copy(group, here, dev).start()

    def await_all(group):
        owns[group].wait()
        ref = blocks_of(group, chips)
        remote(ref, ref, near_send.at[group], near_recv.at[group], pair).wait_recv()

    def await_sends(group):
        ref = blocks_of(group, chips - 1)
        remote(ref, ref, gather_send.at[group], gather_send.at[group], right).wait_send()
        ref = blocks_of(group, chips)
        remote(ref, ref, near_send.at[group], near_recv.at[group], pair).wait_send()

    for j, copy in enumerate(loads_attn):
        copy.wait()
        wd_g[0:rows_own, j * cols : (j + 1) * cols] = o_s[j * rows_own : (j + 1) * rows_own, 0:cols].astype(BF)
    greet((right, left, pair, across))
    launch(0)
    launch(1)
    for j in range(3):
        for h in range(halves):
            loads_mlp[j * halves + h].wait()
            first = (4 + j * halves + h) * rows_own
            wd_g[(j + 1) * rows_own : (j + 2) * rows_own, h * width : (h + 1) * width] = o_s[
                first : first + rows_own
            ].astype(BF)
    doc = doc_ref[...]
    start = jnp.zeros(doc.shape, F32)
    for value in range(3):
        count = jnp.sum(jnp.where(doc == value, 1.0, 0.0), axis=1, keepdims=True)
        start = start + jnp.where(doc > value, count, 0.0)
    start_s[...] = start.astype(jnp.int32)
    dh_s[:, 256:384] = jnp.transpose(jnp.broadcast_to(start, (128, length)))

    def tables(block):
        rows = pl.ds(block * BLOCK, BLOCK)
        position = (lax.broadcasted_iota(jnp.int32, (BLOCK, 128), 0) + block * BLOCK).astype(F32)
        angle = (position - dh_s[rows, 256:384]) * freq_ref[...]
        lane = lax.broadcasted_iota(jnp.int32, (BLOCK, 128), 1)
        dh_s[rows, 0:128] = jnp.cos(angle)
        dh_s[rows, 128:256] = jnp.where(lane % HD < HD // 2, -1.0, 1.0) * jnp.sin(angle)

    for block in range(blocks // 2):
        tables(block)
    tick(0, 1)
    tick(1, 1)
    for block in range(blocks // 2, blocks):
        tables(block)
    stores = [start_copy(dh_s.at[:, pl.ds(0, 256)], tables_o, store.at[0])]
    stores.append(start_copy(start_s, start_o, small_save.at[0]))
    tick(0, 2)
    launch(2)
    tick(1, 2)
    tick(0, 3)
    tick(2, 1)
    tick(1, 3)
    launch(3)
    tick(0, 4)
    pending = [
        (2, 2), (1, 4), (3, 1), (2, 3), (4, 1), (3, 2), (2, 4), (4, 2), (3, 3), (4, 3), (3, 4), (4, 4),
    ]
    ones = head_ones()
    load_x.wait()
    await_all(0)
    held = [start_copy(g_s.at[:, pl.ds(0, wide)], w_o, store.at[1])]

    def project(i, _):
        rows = pl.ds(pl.multiple_of(i * BLOCK, BLOCK), BLOCK)
        states = x_ref[rows]
        cos, sin = dh_s[rows, 0:128], dh_s[rows, 128:256]
        for j, scale in enumerate((HD**-0.5, 1.0)):
            raw = dot_nn(states, g_s[:, j * cols : (j + 1) * cols])
            for c in range(0, cols, 128):
                part = raw[:, c : c + 128]
                factor = lax.rsqrt(split_dot(part * part, ones) * (1.0 / HD) + EPS)
                unit = (part * cos + other_half(part) * sin) * factor
                at = slice(j * cols + c, j * cols + c + 128)
                u_s[rows, at] = ((gain_ref[:, c : c + 128] * unit).astype(BF).astype(F32) * scale).astype(BF)
                hid_s[rows, at] = factor.astype(BF)
        u_s[rows, 2 * cols : wide] = dot_nn(states, g_s[:, 2 * cols : wide]).astype(BF)
        return 0

    lax.fori_loop(0, blocks // 2, project, 0)
    tick(*pending.pop(0))
    launch(4)
    tick(*pending.pop(0))
    await_all(1)
    part = width // 2

    def wo_half(half, side, send, recv, peer):
        there = wo_s.at[side, pl.ds(pl.multiple_of(half * part, part), part)]
        return remote(there, there, send, recv, peer)

    wo_copy = wo_half(core, x, wo_send, wo_recv, across)
    wo_copy.start()
    lax.fori_loop(blocks // 2, blocks, project, 0)
    held.append(start_copy(u_s.at[:, pl.ds(0, wide)], qkv_o, store.at[2]))
    held.append(start_copy(hid_s.at[:, pl.ds(0, 2 * cols)], r_o, store.at[3]))
    tick(*pending.pop(0))
    copies_y = []
    for block in range(blocks):
        first = first_key(block)
        keys = (block + 1) * BLOCK - first
        rows = pl.ds(block * BLOCK, BLOCK)
        span = pl.ds(first, keys)
        bias = o_s.at[pl.ds(0, BLOCK), pl.ds(0, keys)]
        kpos = (lax.broadcasted_iota(jnp.int32, (BLOCK, keys), 1) + first).astype(F32)
        qpos = (lax.broadcasted_iota(jnp.int32, (BLOCK, keys), 0) + block * BLOCK).astype(F32)
        allowed = (kpos >= dh_s[rows, 256:257]) & (kpos <= qpos)
        bias[...] = jnp.where(allowed, 0.0, NEG_FILL)

        def heads(pair_of, _):
            c = pl.multiple_of(pair_of * 128, 128)
            q = u_s[rows, pl.ds(c, 128)]
            k = u_s[span, pl.ds(cols + c, 128)]
            v = u_s[span, pl.ds(2 * cols + c, 128)]
            results = []
            for half in (0, 1):
                scores = dot_nt(q * half_of(BLOCK, half), k)
                probs = jnp.exp(scores + bias[...]).astype(BF)
                results.append(dot_nn(probs, v * half_of(keys, half) + half_of(keys, 1 - half)))
            lane = lax.broadcasted_iota(jnp.int32, (BLOCK, 128), 1)
            total = pltpu.roll(jnp.where(lane < HD, results[1], results[0]), HD, 1)
            y_ref[x, rows, pl.ds(c, 128)] = (jnp.where(lane < HD, results[0], results[1]) / total).astype(BF)
            return 0

        lax.fori_loop(0, cols // 128, heads, 0)
        copy = remote(y_ref.at[x, rows], y_ref.at[x, rows], send_y.at[block], recv_y.at[block], across)
        copy.start()
        copies_y.append(copy)
        stores.append(start_copy(y_ref.at[x, rows], y_o.at[rows], store.at[4 + block]))
        tick(*pending.pop(0))
        if block == 1:
            wo_half(core, 1 - x, wo_send, wo_recv, across).wait_recv()
            wo_pass = wo_half(core, 1 - x, wo_near.at[0], wo_near.at[1], pair)
            wo_pass.start()

    copies_m, copies_d = {}, {}
    here_y = []

    def await_y(rows_end):
        while len(here_y) * BLOCK < rows_end:
            block = len(here_y)
            there = y_ref.at[1 - x, pl.ds(block * BLOCK, BLOCK)]
            remote(there, there, send_y.at[block], recv_y.at[block], across).wait_recv()
            here_y.append(block)

    def first_half(r):
        states = x_ref[r].astype(F32)
        o = o_s[r]
        ro = row_factor(o)
        uo = o * ro
        mix = mix_ref[0:1]
        r1 = states + mix * (uo - states)
        rr = row_factor(r1)
        return states, ro, uo, rr, r1 * rr

    def by_rows(chunk, body, init):
        start, size = chunks[chunk]
        for i in range(size // ROWS_STEP):
            init = body(pl.ds(start + i * ROWS_STEP, ROWS_STEP), init)
        return init

    def mixed(chunk):
        start, size = chunks[chunk]
        rows = pl.ds(start, size)
        await_y(start + size)

        def out_proj(c):
            o_s[rows, c] = dot_nt(y_ref[0, rows], wo_s[0, c]) + dot_nt(y_ref[1, rows], wo_s[1, c])

        by_step(width, 512, out_proj)

        def hidden(r, _):
            hb_s[r] = first_half(r)[4].astype(BF)
            return 0

        by_rows(chunk, hidden, 0)

    def gates(chunk):
        rows = pl.ds(*chunks[chunk])

        def gate(f):
            up = dot_nn(hb_s[rows], wu_s[:, f])
            gt = dot_nn(hb_s[rows], wg_s[:, f])
            arg = us_ref[1:2, f] * gt * D**-0.5
            sig = 1.0 / (1.0 + jnp.exp(-arg))
            u_s[rows, f] = up.astype(BF)
            g_s[rows, f] = gt.astype(BF)
            hid_s[rows, f] = (us_ref[0:1, f] * up * (arg * sig)).astype(BF)

        by_step(units, UNIT_STEP, gate)

    def down(chunk):
        rows = pl.ds(*chunks[chunk])

        def body(c):
            own_s[rows, c] = dot_nt(hid_s[rows], wd_s[c]).astype(BF)

        by_step(width, 512, body)
        copies_m[chunk] = remote(own_s.at[rows], got_m.at[rows], send_m.at[chunk], recv_m.at[chunk], across)
        copies_m[chunk].start()

    def turn(chunk, mix_m):
        rows = pl.ds(*chunks[chunk])
        copies_m[chunk].wait()

        def middle(r, total):
            h1 = first_half(r)[4]
            m = own_s[r].astype(F32) + got_m[r].astype(F32)
            rm = row_factor(m)
            um = m * rm
            mix = mix_ref[1:2]
            r2 = h1 + mix * (um - h1)
            rr = row_factor(r2)
            out = r2 * rr
            got_m[r] = out.astype(BF)
            dr2 = unit_back(rr, out, dm_s[r].astype(F32))
            dm_s[r] = unit_back(rm, um, mix * dr2).astype(BF)
            dh_s[r] = dr2 * (1.0 - mix)
            return total + fold(dr2 * (um - h1))

        mix_m = by_rows(chunk, middle, mix_m)
        start_copy(got_m.at[rows], out_o.at[rows], save.at[3])
        return mix_m

    def gates_back(chunk):
        rows = pl.ds(*chunks[chunk])

        def gate_back(f):
            dhid = dot_nn(dm_s[rows], wd_s[:, f])
            up, gt = u_s[rows, f].astype(F32), g_s[rows, f].astype(F32)
            su, sv = us_ref[0:1, f], us_ref[1:2, f]
            arg = sv * gt * D**-0.5
            sig = 1.0 / (1.0 + jnp.exp(-arg))
            act = dhid * (arg * sig)
            darg = dhid * su * up * sig * (1.0 + arg * (1.0 - sig))
            us_s[0:1, f] = us_s[0:1, f] + jnp.sum(act * up, axis=0, keepdims=True)
            us_s[1:2, f] = us_s[1:2, f] + jnp.sum(darg * gt, axis=0, keepdims=True) * D**-0.5
            u_s[rows, f] = (act * su).astype(BF)
            g_s[rows, f] = (darg * sv * D**-0.5).astype(BF)

        by_step(units, UNIT_STEP, gate_back)

    def ups_back(chunk):
        rows = pl.ds(*chunks[chunk])

        def up_back(c):
            own_s[rows, c] = (dot_nt(u_s[rows], wu_s[c]) + dot_nt(g_s[rows], wg_s[c])).astype(BF)

        by_step(width, 512, up_back)
        copies_d[chunk] = remote(own_s.at[rows], got_d.at[rows], send_d.at[chunk], recv_d.at[chunk], across)
        copies_d[chunk].start()

    def back(chunk):
        gates_back(chunk)
        ups_back(chunk)

    near_s = (hid_s, u_s, g_s)

    def grads_of(j, weight_s, left_s, first, rows):
        tokens = pl.ds(first, rows)

        def grads(d):
            for u in range(0, units, 1024):
                f = pl.ds(u, 1024)
                total = dot_tn(left_s[tokens, d], near_s[j][tokens, f])
                if first:
                    total = total + weight_s[d, f].astype(F32)
                weight_s[d, f] = total.astype(BF)

        return grads

    def weight_grads(j, weight_s, left_s, midway=None, first=0):
        right_s = near_s[j]
        grads = grads_of(j, weight_s, left_s, first, length - first)
        by_step(width // 2, BLOCK, grads)
        if midway is not None:
            midway()
        by_step(width // 2, BLOCK, grads, width // 2)
        pl.semaphore_signal(pair_free.at[j], inc=1, device_id=pair, device_id_type=MESH)
        pl.semaphore_wait(pair_free.at[j], 1)
        for chip in range(chips):
            there = pl.multiple_of((chip * 2 + 1 - core) * rows_own, rows_own)
            copy = remote(
                weight_s.at[pl.ds(there, rows_own)], right_s.at[pl.ds(chip * rows_own, rows_own)],
                pair_send.at[j], pair_recv.at[j], pair,
            )
            copy.start()

    def pair_sums(j, weight_s):
        ref = near_s[j].at[pl.ds(0, chips * rows_own)]
        remote(ref, ref, pair_send.at[j], pair_recv.at[j], pair).wait()
        for chip in range(chips):
            base = pl.multiple_of((chip * 2 + core) * rows_own, rows_own)
            here = near_s[j].at[pl.ds(chip * rows_own, rows_own)]
            add_all(here, [here, weight_s.at[pl.ds(base, rows_own)]])

    def summed(group, way, to_go, chip):
        return near_s[group].at[pl.ds(pl.multiple_of(chip * rows_own, rows_own), rows_own)]

    def ring_slot(group, at):
        return ring_d.at[at] if group == 0 else ring_n.at[0 if at == 0 else 1]

    scatter = Scatter(
        chips, FEED_LONG, summed, ring_slot, lambda group: gd_s,
        lambda group: ring_d if group == 0 else ring_n, ring_send, ring_recv,
    )

    def hand_on():
        for way in (0, 1):
            here = scatter.take(1, way, 1)
            add_all(here, [here, scatter.term(1, way, scatter.hops(1)[way] - 1)])
            start_copy(here, carry_o.at[0, way], rest_save.at[0, 0])

    def hand_rest(group):
        hops = scatter.hops(group)
        far = 0 if hops[0] > hops[1] else 1
        for at, (way, to_go) in enumerate(((far, 1), (far, 2), (far, 3), (1 - far, 1), (1 - far, 2), (0, 0))):
            start_copy(scatter.term(group, way, to_go), rest_o.at[group - 1, at], rest_save.at[1, group - 1])
        if group == 2:
            for way in (0, 1):
                start_copy(scatter.term(group, way, hops[way]), carry_o.at[1, way], rest_save.at[0, 1])

    def last(chunk, mix_a):
        rows = pl.ds(*chunks[chunk])
        copies_d[chunk].wait()

        def body(r, total):
            states, ro, uo, rr, h1 = first_half(r)
            mix = mix_ref[0:1]
            dr1 = unit_back(rr, h1, dh_s[r] + (own_s[r].astype(F32) + got_d[r].astype(F32)))
            dh_s[r] = dr1 * (1.0 - mix)
            dm_s[r] = unit_back(ro, uo, mix * dr1).astype(BF)
            return total + fold(dr1 * (uo - states))

        mix_a = by_rows(chunk, body, mix_a)
        y_ref[1 - x, rows] = dot_nn(dm_s[rows], wo_s[x]).astype(BF)
        for j, (src, dst) in enumerate(((y_ref.at[1 - x], dy_o), (dm_s, do_o), (dh_s, dri_o))):
            start_copy(src.at[rows], dst.at[rows], save.at[j])
        return mix_a

    wo_half(1 - core, 1 - x, wo_near.at[0], wo_near.at[1], pair).wait_recv()
    for chunk in range(number):
        mixed(chunk)
        if len(pending) > 2:
            tick(*pending.pop(0))
    for copy in held:
        copy.wait()
    await_sends(0)
    while len(pending) > 1:
        tick(*pending.pop(0))
    await_all(2)
    await_all(3)
    gates(0)
    tick(*pending.pop(0))
    await_all(4)
    for chunk in range(number):
        down(chunk)
        if chunk < number - 1:
            gates(chunk + 1)
        if chunk == 0:
            for group in range(1, 5):
                await_sends(group)
    mix_m = jnp.zeros((8, width), F32)
    us_s[...] = jnp.zeros_like(us_s)
    load_og.wait()
    stores[0].wait()
    for chunk in range(number - 2):
        mix_m = turn(chunk, mix_m)
        back(chunk)
    here = chunks[number - 2][0]
    by_step(width, BLOCK, grads_of(0, wd_g, dm_s, 0, here))
    mix_m = turn(number - 2, mix_m)
    mix_m = turn(number - 1, mix_m)
    mix_s[1:2] = jnp.sum(mix_m, axis=0, keepdims=True)
    weight_grads(0, wd_g, dm_s, None, here)
    gates_back(number - 2)
    pair_sums(0, wd_g)
    scatter.launch(0)
    ups_back(number - 2)
    back(number - 1)
    stores.append(start_copy(us_s, us_o, small_save.at[1]))
    scatter.tick(0, 1)
    weight_grads(1, wu_s, hb_s)

    def up_ring():
        scatter.tick(0, 2)
        pair_sums(1, wu_s)
        scatter.launch(1)
        hand_rest(1)

    weight_grads(2, wg_s, hb_s, up_ring)
    wo_copy.wait_send()
    wo_pass.wait_send()
    for copy in copies_y:
        copy.wait_send()
    mix_a = jnp.zeros((8, width), F32)
    for chunk in range(number):
        mix_a = last(chunk, mix_a)
        if chunk == 1:
            scatter.tick(0, 3)
            pair_sums(2, wg_s)
            hand_rest(2)
        if chunk == number - 3:
            hand_on()
        if chunk == number - 2:
            scatter.tick(0, 4)
            stores.append(start_copy(gd_s, gd_o, small_save.at[2]))
    mix_s[0:1] = jnp.sum(mix_a, axis=0, keepdims=True)
    stores.append(start_copy(mix_s, mix_o, small_save.at[3]))
    for copy in stores[1:]:
        copy.wait()
    for j, (src, dst) in enumerate(((y_ref.at[1 - x], dy_o), (dm_s, do_o), (dh_s, dri_o), (got_m, out_o))):
        pltpu.make_async_copy(src, dst, save.at[j]).wait()
    for j in range(2):
        pltpu.make_async_copy(carry_o.at[j], carry_o.at[j], rest_save.at[0, j]).wait()
        pltpu.make_async_copy(rest_o.at[j], rest_o.at[j], rest_save.at[1, j]).wait()
    scatter.close()


def layer(attn_w, mlp_w, states, out_grad, doc, gain, mix, scales, fsdp):
    chips = fsdp // 2
    length, width = states.shape
    cols, units, rows = attn_w.shape[2], mlp_w.shape[2], attn_w.shape[1]
    vspec, anyspec = pl.BlockSpec(memory_space=VM), pl.BlockSpec(memory_space=pl.ANY)
    blocks, number = length // BLOCK, len(feed_chunks(length))
    sem = pltpu.SemaphoreType.DMA
    freq = np.asarray(THETA ** (-2.0 * (np.arange(128) % (HD // 2)) / HD), np.float32)
    square, wide, weight, tall = VM((length, width), BF), VM((length, units), BF), VM((width, units), BF), VM((length, width), F32)
    return pl.pallas_call(
        functools.partial(layer_kernel, chips),
        out_shape=(
            low(length, width), full(length, width), low(length, width), low(length, cols),
            low(width, 3 * cols), low(length, 3 * cols), low(length, 2 * cols), low(length, cols), full(length, 256),
            low(2, 2, rows, units), low(2, 6, rows, units),
            jax.ShapeDtypeStruct((1, length), jnp.int32), full(2, width), full(2, units), full(rows, units),
        ),
        in_specs=[anyspec] * 4 + [vspec] * 5,
        out_specs=(anyspec,) * 15,
        scratch_shapes=[
            VM((1, length), jnp.int32), VM((2, width), F32), VM((2, units), F32), VM((rows, units), F32),
            square, VM((2, length, cols), BF), VM((2, width, cols), BF), weight, weight, weight,
            tall, square, wide, wide, wide, square, tall, square, square, square, weight,
            VM((chips - 1, rows, units), BF), VM((2, rows, units), BF),
            sem((6 + 3 * (units // width),)), sem((4 + blocks,)), sem((4,)), sem((2, 2)),
            sem((4,)), sem((blocks,)), sem((blocks,)), sem, sem, sem((2,)), sem((number,)), sem((number,)), sem((number,)), sem((number,)),
            sem((5,)), sem((5, 2, chips // 2)), sem((5,)), sem((5,)), sem((5,)),
            pltpu.SemaphoreType.REGULAR((3,)), sem((3,)), sem((3,)), sem((2,)), sem((2, chips - 1)),
        ],
        compiler_params=pltpu.CompilerParams(collective_id=6, has_side_effects=True, vmem_limit_bytes=63 * MIB),
        name="layer",
    )(attn_w, mlp_w, states, out_grad, doc, gain, freq[None], mix, scales)


SCATTER_LONG = (0, 3, 5)
MATRIX_OF = {2: 3, 3: 2, 4: 1, 5: 0}


def back_pieces(length):
    half = BLOCK // 2
    return [(length - half, half), (length - BLOCK, half)] + [(start, BLOCK) for start in range(length - 2 * BLOCK, -1, -BLOCK)]


def stepped(param, moment, grad, rate):
    moment_new = MOMENTUM * moment + grad
    return moment_new, param - rate * (grad + MOMENTUM * moment_new)


def backward_kernel(
    rate, x_hbm, w_hbm, qkv_hbm, r_hbm, y_hbm, dy_hbm, do_hbm, dri_hbm, carry_hbm, rest_hbm, tables_hbm,
    wa_hbm, ma_hbm, wm_hbm, mm_hbm, gain_ref, start_ref, gd_ref, mix_ref, us_ref,
    ig_o, ga_o, gm_o, sum_a_o, sum_m_o,
    ga_s, gm_s, x_ref, w_ref, qkv_ref, r_ref, y_ref, dy_ref, do_ref, carry, rest, tables_ref, dri_s,
    wa_ref, ma_ref, wm_ref, mm_ref,
    bias, dq_s, dk_s, dv_s, low_s, out_s, in_s, dw_s, near, ring_a, ring_m, head_s, mine_a, got_a, mine_m, got_m,
    load, load_dri, store, save, send, recv, pair_send, pair_recv, ring_send, ring_recv, all_send, all_recv,
):
    chips, rows_own = near.shape[1:3]
    index, x, place, core, right, left, pair, across = peers_of(chips)
    length, cols = y_ref.shape
    width = x_ref.shape[1]
    parts = back_pieces(length)
    blocks = len(parts)
    stages = got_m.shape[0]
    others = [(ring_device((place + d) % chips, core, chips), x) for d in range(1, chips)]
    turns = [(index + (1 << s) * (1 - 2 * ((index // (1 << s)) % 2)), x) for s in range(stages)]
    pieces = (
        (carry_hbm, carry), (qkv_hbm, qkv_ref), (dy_hbm, dy_ref), (y_hbm, y_ref),
        (tables_hbm, tables_ref), (r_hbm, r_ref), (w_hbm, w_ref), (rest_hbm, rest),
        (do_hbm, do_ref), (x_hbm, x_ref), (wm_hbm, wm_ref), (mm_hbm, mm_ref), (wa_hbm, wa_ref), (ma_hbm, ma_ref),
    )
    loads = [start_copy(src, dst, load.at[j]) for j, (src, dst) in enumerate(pieces)]
    greet([pair, across] + others)

    def mine(group, way, to_go, chip):
        if group < 2:
            wide_way = 0 if group in SCATTER_LONG else 1
            return rest.at[group, 5 if to_go == 0 else to_go - 1 if way == wide_way else 2 + to_go]
        return near.at[MATRIX_OF[group], chip]

    def slot(group, at):
        if group < 2:
            return ring_m.at[group, at]
        return ring_a.at[at, MATRIX_OF[group]]

    def result(group):
        return gm_s.at[group] if group < 2 else ga_s.at[MATRIX_OF[group]]

    def sent(group):
        return ring_m.at[group, pl.ds(0, chips - 3 + 2 * group)] if group < 2 else ring_a.at[:, MATRIX_OF[group]]

    scatter = Scatter(chips, SCATTER_LONG, mine, slot, result, sent, ring_send, ring_recv)
    tick, launch = scatter.tick, scatter.launch

    def send_pair(j):
        for chip in range(chips):
            there = pl.multiple_of((chip * 2 + 1 - core) * rows_own, rows_own)
            remote(dw_s.at[j, pl.ds(there, rows_own)], near.at[j, chip], pair_send.at[j], pair_recv.at[j], pair).start()

    def sum_pair(j):
        remote(near.at[j], near.at[j], pair_send.at[j], pair_recv.at[j], pair).wait()
        for chip in range(chips):
            own = pl.ds(pl.multiple_of((chip * 2 + core) * rows_own, rows_own), rows_own)
            here = near.at[j, chip]
            add_all(here, [here, dw_s.at[j, own]])

    loads[0].wait()
    for group, hop in ((1, 1), (0, 2)):
        for way in (0, 1):
            scatter.go(group, way, hop, carry.at[group, way])
    dk_s[...] = jnp.zeros_like(dk_s)
    dv_s[...] = jnp.zeros_like(dv_s)
    head_s[...] = jnp.zeros_like(head_s)
    ones = head_ones()
    copies, stores = {}, []

    def fetch_dri(block):
        start, size = parts[block]
        return start_copy(dri_hbm.at[pl.ds(start, size)], dri_s.at[block % 2, pl.ds(0, size)], load_dri.at[block])

    fetched = {block: fetch_dri(block) for block in (0, 1)}

    def finish_input(block):
        start, size = parts[block]
        copies[block].wait()
        fetched[block].wait()
        for i in range(0, size, 128):
            r = pl.ds(start + i, 128)
            total = out_s[r].astype(F32) + in_s[r].astype(F32)
            out_s[r] = (dri_s[block % 2, pl.ds(i, 128)] + total).astype(BF)
        rows = pl.ds(start, size)
        stores.append(start_copy(out_s.at[rows], ig_o.at[rows], store.at[block]))
        if block + 2 < blocks:
            fetched[block + 2] = fetch_dri(block + 2)

    for copy in loads[1:4]:
        copy.wait()

    def attend(block):
        start, size = parts[block]
        first = max(0, start - SPAN)
        keys = start + size - first
        rows = pl.ds(start, size)
        span = pl.ds(first, keys)
        kpos = lax.broadcasted_iota(jnp.int32, (keys, size), 0) + first
        qpos = lax.broadcasted_iota(jnp.int32, (keys, size), 1) + start
        allowed = (kpos >= start_ref[:, start : start + size]) & (kpos <= qpos)
        bias[:keys, :size] = jnp.where(allowed, 0.0, NEG_FILL)

        def heads(pair_of, _):
            at = pl.multiple_of(pair_of * 128, 128)
            c = pl.ds(at, 128)
            q, dy = qkv_ref[rows, c], dy_ref[rows, c]
            k, v = qkv_ref[span, pl.ds(cols + at, 128)], qkv_ref[span, pl.ds(2 * cols + at, 128)]
            prod = dy.astype(F32) * y_ref[rows, c].astype(F32)
            prod_high = prod.astype(BF)
            prod_low = (prod - prod_high.astype(F32)).astype(BF)
            dq = jnp.zeros((size, 128), F32)
            dk = jnp.zeros((keys, 128), F32)
            dv = jnp.zeros((keys, 128), F32)
            for half in (0, 1):
                mask, row = half_of(size, half), half_of(8, half)
                qm, dym, km = q * mask, dy * mask, k * half_of(keys, half)
                expo = jnp.exp(dot_nt(k, qm) + bias[:keys, :size])
                probs = expo * (1.0 / jnp.sum(expo, axis=0, keepdims=True))
                delta = (dot_nt(row, prod_high) + dot_nt(row, prod_low))[0:1]
                dz = (probs * (dot_nt(v, dym) - delta)).astype(BF)
                dk = dk + dot_nn(dz, qm)
                dv = dv + dot_nn(probs.astype(BF), dym)
                dq = dq + dot_tn(dz, km)
            dq_s[rows, c] = dq * HD**-0.5
            dk_s[span, c] = dk_s[span, c] + dk
            dv_s[span, c] = dv_s[span, c] + dv
            return 0

        return heads

    def project_back(block):
        start, size = parts[block]
        rows = pl.ds(start, size)
        cos, sin = tables_ref[rows, 0:128], tables_ref[rows, 128:256]
        for c in range(0, cols, 128):
            s = slice(c, c + 128)
            gain = gain_ref[:, s]
            head = jnp.zeros((size, 128), F32)
            for j, (grad_s, scale) in enumerate(((dq_s, HD**0.5), (dk_s, 1.0))):
                at = slice(j * cols + c, j * cols + c + 128)
                grad = grad_s[rows, s]
                unit = qkv_ref[rows, at].astype(F32) * (scale / gain)
                head = head + grad * unit
                grad = grad * gain
                turned = r_ref[rows, at].astype(F32) * (grad - unit * (split_dot(grad * unit, ones) * (1.0 / HD)))
                low_s[j, rows, s] = (turned * cos - other_half(turned) * sin).astype(BF)
            head_s[:, s] = head_s[:, s] + jnp.sum(head, axis=0, keepdims=True)
            low_s[2, rows, s] = dv_s[rows, s].astype(BF)
        for c in range(0, width, 512):
            part = sum(dot_nt(low_s[j, rows], w_ref[c : c + 512, j * cols : (j + 1) * cols]) for j in range(3))
            out_s[rows, c : c + 512] = part.astype(BF)
        copy = remote(out_s.at[rows], in_s.at[rows], send.at[block], recv.at[block], across)
        copy.start()
        copies[block] = copy

    longest = chips // 2
    pending = [(1, 1), (0, 2), (1, 2), (0, 3), (1, 3), (0, 4), (1, 4)]
    step_pairs = cols // 256
    def weight_grad(j, d, left, right):
        dw_s[j, d] = dot_tn(left, right).astype(BF)

    for block in range(blocks):
        heads = attend(block)
        lax.fori_loop(0, step_pairs, heads, 0)
        if block == 2:
            tick(*pending.pop(0))
        lax.fori_loop(step_pairs, 2 * step_pairs, heads, 0)
        if block == 0:
            for copy in loads[4:8]:
                copy.wait()
        if block == 3:
            tick(*pending.pop(0))
        project_back(block)
        if block == blocks - 1:
            tick(*pending.pop(0))
            tick(2, 1)
        if block == 1:
            tick(*pending.pop(0))
            for copy in loads[8:10]:
                copy.wait()
            by_step(width, BLOCK, lambda d: weight_grad(3, d, do_ref[:, d], y_ref[...]))
            send_pair(3)
        if block == 2:
            tick(*pending.pop(0))
            sum_pair(3)
            launch(2)
    for group in (3, 4, 5):
        j = MATRIX_OF[group]
        by_step(width, BLOCK, lambda d: weight_grad(j, d, x_ref[:, d], low_s[j]))
        send_pair(j)
        if group > 3:
            sum_pair(MATRIX_OF[group - 1])
            launch(group - 1)
    sum_pair(MATRIX_OF[5])
    launch(5)
    tick(*pending.pop(0))
    tick(*pending.pop(0))
    tick(2, 2)
    assert not pending

    def squares(g, w, m):
        count = g.shape[-1]

        def body(i, total):
            r = pl.ds(pl.multiple_of(i * 8, 8), 8)
            step = stepped(w[r], m[r], g[r], rate)[1]
            return total + step * step

        total = lax.fori_loop(0, rows_own // 8, body, jnp.zeros((8, count), F32))
        return jnp.sum(total, axis=0, keepdims=True)

    def exchange(s):
        copy = remote(mine_m.at[s], got_m.at[s], all_send.at[0, s], all_recv.at[0, s], turns[s])
        copy.start()
        return copy

    for copy in loads[10:]:
        copy.wait()
    lanes = mine_m.shape[2]
    mine_m[0] = jnp.zeros(mine_m.shape[1:], F32)
    row = 0

    def place_row(value):
        nonlocal row
        for c in range(0, value.shape[1], lanes):
            size = min(lanes, value.shape[1])
            mine_m[0, row : row + 1, 0:size] = value[:, c : c + size]
            row += 1

    for j in range(3):
        place_row(squares(gd_ref if j == 2 else gm_s.at[j], wm_ref.at[j], mm_ref.at[j]))
    place_row(head_s[...])
    for ref in (mix_ref, us_ref):
        for j in range(2):
            place_row(ref[j : j + 1])
    def attn_squares(j):
        mine_a[0, j : j + 1] = squares(ga_s.at[j], wa_ref.at[j], ma_ref.at[j])

    stores.append(start_copy(gm_s, gm_o, save.at[0]))
    def settle(s, copy):
        copy.wait()
        mine_m[s + 1] = mine_m[s] + got_m[s]

    copy = exchange(0)
    finish_input(0)
    finish_input(1)
    settle(0, copy)
    copy = None
    for hop in range(1, longest + 1):
        if hop == 2:
            finish_input(2)
        for group in (3, 4, 5):
            tick(group, hop)
            if hop == longest:
                attn_squares(MATRIX_OF[group])
            if group == 3 and hop <= stages:
                if copy is not None:
                    settle(hop - 1, copy)
                copy = exchange(hop) if hop < stages else None
        if hop + 2 <= longest:
            tick(2, hop + 2)
            if hop + 2 == longest:
                attn_squares(3)
    if copy is not None:
        settle(longest, copy)
    for hop in range(longest + 1, stages):
        settle(hop, exchange(hop))
    last = remote(mine_a.at[0], got_a.at[0], all_send.at[1, 0], all_recv.at[1, 0], pair)
    last.start()
    stores.append(start_copy(ga_s, ga_o, save.at[1]))
    stores.append(start_copy(mine_m.at[stages], sum_m_o, save.at[2]))
    last.wait()
    mine_a[1] = mine_a[0] + got_a[0]
    for d, peer in enumerate(others):
        remote(mine_a.at[1], got_a.at[1 + d], all_send.at[1, 1], all_recv.at[1, 1], peer).start()
    for block in range(3, blocks):
        finish_input(block)
    every = got_a.at[pl.ds(1, chips - 1)]
    remote(every, every, all_send.at[1, 1], all_recv.at[1, 1], pair).wait()
    total = mine_a[1]
    for d in range(1, chips):
        total = total + got_a[d]
    mine_a[2] = total
    stores.append(start_copy(mine_a.at[2], sum_a_o, save.at[3]))
    for copy in stores:
        copy.wait()
    scatter.close()


def attention_backward(
    states, weights, qkv, factors, y, dy, do, dri, carry, rest, tables, attn_w, attn_mom, mlp_w, mlp_mom,
    gain, start, grad_down, grad_mix, grad_units, rate, fsdp,
):
    length, width = states.shape
    cols = gain.shape[1]
    chips = fsdp // 2
    rows, units = rest.shape[2:]
    stages = fsdp.bit_length() - 1
    vspec, anyspec = pl.BlockSpec(memory_space=VM), pl.BlockSpec(memory_space=pl.ANY)
    blocks = len(back_pieces(length))
    sem = pltpu.SemaphoreType.DMA
    square, full_square = VM((length, cols), BF), VM((length, cols), F32)
    wide = VM((length, width), BF)
    a_rows, m_rows = 4, -(-(3 * (units // width) + 3 + 2 * (units // width)) // 8) * 8
    return pl.pallas_call(
        functools.partial(backward_kernel, rate),
        out_shape=(
            low(length, width), full(4, rows, cols), full(2, rows, units), full(a_rows, cols), full(m_rows, width),
        ),
        in_specs=[anyspec] * 15 + [vspec] * 5,
        out_specs=(anyspec,) * 5,
        scratch_shapes=[
            VM((4, rows, cols), F32), VM((2, rows, units), F32), wide, VM(weights.shape, BF), VM(qkv.shape, BF), VM(factors.shape, BF), square, square,
            wide, VM(carry.shape, BF), VM(rest.shape, BF), VM(tables.shape, F32), VM((2, BLOCK, width), F32),
            VM(attn_w.shape, F32), VM(attn_w.shape, F32), VM(mlp_w.shape, F32), VM(mlp_w.shape, F32),
            VM((BLOCK + SPAN, BLOCK), F32), full_square, full_square, full_square,
            VM((3, length, cols), BF), wide, wide, VM((4, width, cols), BF), VM((4, chips, rows, cols), BF),
            VM((chips - 1, 4, rows, cols), BF), VM((2, chips - 1, rows, units), BF), VM((1, cols), F32),
            VM((3, a_rows, cols), F32), VM((chips, a_rows, cols), F32),
            VM((stages + 1, m_rows, width), F32), VM((stages, m_rows, width), F32),
            sem((14,)), sem((blocks,)), sem((blocks,)), sem((4,)), sem((blocks,)), sem((blocks,)),
            sem((4,)), sem((4,)), sem((6,)), sem((6, chips - 1)), sem((2, stages)), sem((2, stages)),
        ],
        compiler_params=pltpu.CompilerParams(collective_id=5, has_side_effects=True, vmem_limit_bytes=63 * MIB),
        name="attention_backward",
    )(
        states, weights, qkv, factors, y, dy, do, dri, carry, rest, tables, attn_w, attn_mom, mlp_w, mlp_mom,
        gain, start, grad_down, grad_mix, grad_units,
    )


def update_kernel(
    rates, width, ig, hid, ga, gm, gd, sa, sm, wa, ma, aa, wm, mm, am, hs, hm, mr, mo, us, um,
    hid_o, ig_o, ma_o, wa_o, aa_o, mm_o, wm_o, am_o, hm_o, hs_o, mo_o, mr_o, um_o, us_o,
):
    hid_o[0] = hid[...].astype(F32)
    ig_o[0] = ig[...].astype(F32)
    lanes = sm.shape[1]
    cols, units = wa.shape[2], wm.shape[2]

    def matrix(j, grad, total, refs, outs):
        w, m, a = (ref[j] for ref in refs)
        moment, step = stepped(w, m, grad, rates[0])
        new = step * lax.rsqrt(total / width + EPS)
        outs[0][j] = moment
        outs[1][j] = new
        outs[2][j] = AVERAGE * a + (1.0 - AVERAGE) * new

    def wide(row):
        return jnp.concatenate([sm[row + c : row + c + 1] for c in range(units // lanes)], axis=1)

    for j in range(4):
        matrix(j, ga[j], sa[j : j + 1], (wa, ma, aa), (ma_o, wa_o, aa_o))
    for j in range(3):
        matrix(j, gd[...] if j == 2 else gm[j], wide(j * (units // lanes)), (wm, mm, am), (mm_o, wm_o, am_o))

    @pl.when(pl.program_id(0) == 0)
    def _():
        row = 3 * (units // lanes)
        hm_o[...], hs_o[...] = stepped(hs[...], hm[...], sm[row : row + 1, :cols], rates[1])
        mo_o[...], mr_o[...] = stepped(mr[...], mo[...], sm[row + 1 : row + 3], rates[2])
        row += 3
        grad = jnp.concatenate([wide(row), wide(row + units // lanes)], axis=0)
        um_o[...], us_o[...] = stepped(us[...], um[...], grad, rates[3])


def update(input_low, hidden_low, ga, gm, gd, sa, sm, wa, ma, aa, wm, mm, am, hs, hm, mr, mo, us, um, rates):
    length, width = input_low.shape
    rows, cols, units = wa.shape[1], wa.shape[2], wm.shape[2]
    steps, block = rows // 16, 16
    tall = length // steps

    def whole(shape):
        return pl.BlockSpec(shape, lambda i: (0,) * len(shape))

    state = pl.BlockSpec((tall, width), lambda i: (i, 0))
    state_o = pl.BlockSpec((1, tall, width), lambda i: (0, i, 0))
    attn = pl.BlockSpec((4, block, cols), lambda i: (0, i, 0))
    mlp = pl.BlockSpec((3, block, units), lambda i: (0, i, 0))
    small = [whole((1, cols))] * 2 + [whole(mr.shape)] * 2 + [whole(us.shape)] * 2
    return pl.pallas_call(
        functools.partial(update_kernel, rates, width),
        grid=(steps,),
        out_shape=(
            full(1, length, width), full(1, length, width), *(full(*wa.shape),) * 3, *(full(*wm.shape),) * 3,
            *(full(1, cols),) * 2, *(full(*mr.shape),) * 2, *(full(*us.shape),) * 2,
        ),
        in_specs=[
            state, state, attn, pl.BlockSpec((2, block, units), lambda i: (0, i, 0)), pl.BlockSpec((block, units), lambda i: (i, 0)),
            whole(sa.shape), whole(sm.shape), attn, attn, attn, mlp, mlp, mlp, *small,
        ],
        out_specs=(state_o, state_o, attn, attn, attn, mlp, mlp, mlp, *small),
        compiler_params=pltpu.CompilerParams(vmem_limit_bytes=60 * MIB),
        name="update_weights",
    )(input_low, hidden_low, ga, gm, gd, sa, sm, wa, ma, aa, wm, mm, am, hs, hm, mr, mo, us, um)


def local_fast(
    inputs, doc_ids, out_grad, attn_w, attn_mom, attn_avg, mlp_w, mlp_mom, mlp_avg,
    head_scale, head_mom, mix_rates, mix_mom, unit_scales, unit_mom,
):
    fsdp = lax.axis_size("fsdp")
    root_tokens = math.sqrt(inputs.shape[0] * fsdp * inputs.shape[1])
    rates = tuple(rate / root_tokens for rate in (RATE_WEIGHT, RATE_HEAD, RATE_MIX, RATE_UNITS))
    states, gain = inputs[0], head_scale[None]
    hidden_low, dri, do, dy, w_in, qkv, factors, y, tables, carry, rest, start, grad_mix, grad_units, grad_down = layer(
        attn_w, mlp_w, states, out_grad[0], doc_ids, gain, mix_rates, unit_scales, fsdp
    )
    input_low, grad_attn, grad_mlp, total_attn, total_rest = attention_backward(
        states, w_in, qkv, factors, y, dy, do, dri, carry, rest, tables, attn_w, attn_mom, mlp_w, mlp_mom,
        gain, start, grad_down, grad_mix, grad_units, rates[0], fsdp,
    )
    outs = update(
        input_low, hidden_low, grad_attn, grad_mlp, grad_down, total_attn, total_rest,
        attn_w, attn_mom, attn_avg, mlp_w, mlp_mom, mlp_avg,
        gain, head_mom[None], mix_rates, mix_mom, unit_scales, unit_mom, rates,
    )
    return (*outs[:8], outs[8][0], outs[9][0], *outs[10:])


def local(
    inputs,
    doc_ids,
    out_grad,
    attn_w,
    attn_mom,
    attn_avg,
    mlp_w,
    mlp_mom,
    mlp_avg,
    head_scale,
    head_mom,
    mix_rates,
    mix_mom,
    unit_scales,
    unit_mom,
):
    length = inputs.shape[1]
    model_width = inputs.shape[2]
    head_count = head_scale.shape[0] // HD
    block_rows = min(512, length)
    block_count = length // block_rows
    tokens = inputs.shape[0] * lax.axis_size("fsdp") * length
    doc_row = doc_ids[0]
    input_low = inputs[0]
    resid_in = input_low.astype(jnp.float32)
    cos_table, sin_table = rotary_tables(doc_row)
    position = jnp.arange(length, dtype=jnp.int32)
    attn_full = lax.all_gather(attn_w.astype(jnp.bfloat16), "fsdp", axis=1, tiled=True)
    projected = jnp.einsum(
        "sd,jdc->jsc", input_low, attn_full[:3], preferred_element_type=jnp.float32
    )
    head_gain = head_scale.reshape(head_count, HD)
    q_rot = rotate(projected[0].reshape(length, head_count, HD), cos_table, sin_table)
    k_rot = rotate(projected[1].reshape(length, head_count, HD), cos_table, sin_table)
    q_unit = rms_unit(q_rot)
    k_unit = rms_unit(k_rot)
    query_low = (head_gain * q_unit).astype(jnp.bfloat16)
    key_low = (head_gain * k_unit).astype(jnp.bfloat16)
    value_low = projected[2].reshape(length, head_count, HD).astype(jnp.bfloat16)

    def scores_of(row_first):
        query_blk = lax.dynamic_slice_in_dim(query_low, row_first, block_rows, 0)
        raw_scores = jnp.einsum(
            "qhe,khe->hqk", query_blk, key_low, preferred_element_type=jnp.float32
        )
        row_pos = lax.dynamic_slice_in_dim(position, row_first, block_rows, 0)
        row_docs = lax.dynamic_slice_in_dim(doc_row, row_first, block_rows, 0)
        allowed = (row_docs[:, None] == doc_row[None, :]) & (position[None, :] <= row_pos[:, None])
        return (jnp.where(allowed[None], raw_scores * HD ** (-0.5), NEG_FILL), query_blk)

    def attend(accums, blk_index):
        scores, query_blk = scores_of(blk_index * block_rows)
        peak_val = jnp.max(scores, axis=-1, keepdims=True)
        expo_vals = jnp.exp(scores - peak_val)
        row_total = jnp.sum(expo_vals, axis=-1, keepdims=True)
        probs_low = (expo_vals / row_total).astype(jnp.bfloat16)
        blk_out = jnp.einsum(
            "hqk,khe->qhe", probs_low, value_low, preferred_element_type=jnp.float32
        )
        return (accums, (blk_out, (peak_val + jnp.log(row_total))[..., 0]))

    _, (mixed_blocks, log_totals) = lax.scan(attend, None, jnp.arange(block_count))
    mixed_low = mixed_blocks.reshape(length, head_count * HD).astype(jnp.bfloat16)
    attn_part = jnp.einsum("sc,dc->sd", mixed_low, attn_full[3], preferred_element_type=jnp.float32)
    attn_out = lax.psum(attn_part, "mp")
    attn_unit = rms_unit(attn_out)
    resid_one = resid_in + mix_rates[0] * (attn_unit - resid_in)
    hidden_one = rms_unit(resid_one)
    hidden_low = hidden_one.astype(jnp.bfloat16)
    mlp_full = lax.all_gather(mlp_w.astype(jnp.bfloat16), "fsdp", axis=1, tiled=True)
    gates = jnp.einsum("sd,jdf->jsf", hidden_low, mlp_full[:2], preferred_element_type=jnp.float32)
    up_proj = gates[0]
    gate_proj = gates[1]
    gate_arg = unit_scales[1] * gate_proj * D ** (-0.5)
    gate_sig = jax.nn.sigmoid(gate_arg)
    gate_act = gate_arg * gate_sig
    units_low = (unit_scales[0] * up_proj * gate_act).astype(jnp.bfloat16)
    mlp_part = jnp.einsum("sf,df->sd", units_low, mlp_full[2], preferred_element_type=jnp.float32)
    mlp_out = lax.psum(mlp_part, "mp")
    mlp_unit = rms_unit(mlp_out)
    resid_two = hidden_one + mix_rates[1] * (mlp_unit - hidden_one)
    result = rms_unit(resid_two)
    cotangent = out_grad[0].astype(jnp.float32)
    d_resid_two = rms_back(resid_two, cotangent)
    grad_mix_mlp = jnp.sum(d_resid_two * (mlp_unit - hidden_one), axis=0)
    d_hidden_one = d_resid_two * (1.0 - mix_rates[1])
    d_mlp_low = rms_back(mlp_out, mix_rates[1] * d_resid_two).astype(jnp.bfloat16)
    mlp_back = lax.all_gather(mlp_w.astype(jnp.bfloat16), "fsdp", axis=1, tiled=True)
    d_units = jnp.einsum("sd,df->sf", d_mlp_low, mlp_back[2], preferred_element_type=jnp.float32)
    d_up = d_units * unit_scales[0] * gate_act
    d_arg = d_units * unit_scales[0] * up_proj * gate_sig * (1.0 + gate_arg * (1.0 - gate_sig))
    d_gate = d_arg * unit_scales[1] * D ** (-0.5)
    grad_units = jnp.stack(
        [
            jnp.sum(d_units * up_proj * gate_act, axis=0),
            jnp.sum(d_arg * gate_proj * D ** (-0.5), axis=0),
        ]
    )
    d_gates_low = jnp.stack([d_up, d_gate]).astype(jnp.bfloat16)
    mlp_back_part = jnp.einsum(
        "jsf,jdf->sd", d_gates_low, mlp_back[:2], preferred_element_type=jnp.float32
    )
    d_hidden_one = d_hidden_one + lax.psum(mlp_back_part, "mp")
    right_cols = d_mlp_low
    left_cols = hidden_low
    grad_mlp = jnp.transpose(
        lax.psum_scatter(
            jnp.concatenate(
                [
                    jnp.einsum(
                        "sd,jsf->djf", left_cols, d_gates_low, preferred_element_type=jnp.float32
                    ),
                    jnp.einsum(
                        "sd,sf->df", right_cols, units_low, preferred_element_type=jnp.float32
                    )[:, None, :],
                ],
                axis=1,
            ),
            "fsdp",
            scatter_dimension=0,
            tiled=True,
        ),
        (1, 0, 2),
    )
    d_resid_one = rms_back(resid_one, d_hidden_one)
    grad_mix_attn = jnp.sum(d_resid_one * (attn_unit - resid_in), axis=0)
    d_resid_in = d_resid_one * (1.0 - mix_rates[0])
    d_attn_low = rms_back(attn_out, mix_rates[0] * d_resid_one).astype(jnp.bfloat16)
    attn_back = lax.all_gather(attn_w.astype(jnp.bfloat16), "fsdp", axis=1, tiled=True)
    d_mixed = jnp.einsum("sd,dc->sc", d_attn_low, attn_back[3], preferred_element_type=jnp.float32)
    d_mixed = d_mixed.astype(jnp.bfloat16).reshape(length, head_count, HD)

    def attend_back(accums, blk_index):
        d_key, d_value = accums
        row_first = blk_index * block_rows
        scores, query_blk = scores_of(row_first)
        blk_total = lax.dynamic_index_in_dim(log_totals, blk_index, 0, keepdims=False)
        attn_probs = jnp.exp(scores - blk_total[..., None])
        d_out_blk = lax.dynamic_slice_in_dim(d_mixed, row_first, block_rows, 0)
        d_probs = jnp.einsum(
            "qhe,khe->hqk", d_out_blk, value_low, preferred_element_type=jnp.float32
        )
        d_scores = attn_probs * (d_probs - jnp.sum(attn_probs * d_probs, axis=-1, keepdims=True))
        d_raw_low = (d_scores * HD ** (-0.5)).astype(jnp.bfloat16)
        d_query = jnp.einsum("hqk,khe->qhe", d_raw_low, key_low, preferred_element_type=jnp.float32)
        d_key = d_key + jnp.einsum(
            "hqk,qhe->khe", d_raw_low, query_blk, preferred_element_type=jnp.float32
        )
        d_value = d_value + jnp.einsum(
            "hqk,qhe->khe",
            attn_probs.astype(jnp.bfloat16),
            d_out_blk,
            preferred_element_type=jnp.float32,
        )
        return ((d_key, d_value), d_query)

    zero_heads = jnp.zeros((length, head_count, HD), jnp.float32)
    (d_key_all, d_value_all), d_query_blocks = lax.scan(
        attend_back, (zero_heads, zero_heads), jnp.arange(block_count)
    )
    d_query_all = d_query_blocks.reshape(length, head_count, HD)
    grad_head = jnp.sum(d_query_all * q_unit + d_key_all * k_unit, axis=0).reshape(-1)
    d_query_raw = rotate_back(rms_back(q_rot, head_gain * d_query_all), cos_table, sin_table)
    d_key_raw = rotate_back(rms_back(k_rot, head_gain * d_key_all), cos_table, sin_table)
    d_proj_low = jnp.stack(
        [
            d_query_raw.reshape(length, -1),
            d_key_raw.reshape(length, -1),
            d_value_all.reshape(length, -1),
        ]
    ).astype(jnp.bfloat16)
    grad_mix = jnp.stack([grad_mix_attn, grad_mix_mlp])
    grad_head, grad_mix, grad_units = lax.psum((grad_head, grad_mix, grad_units), "fsdp")
    attn_back_part = jnp.einsum(
        "jsc,jdc->sd", d_proj_low, attn_back[:3], preferred_element_type=jnp.float32
    )
    input_grad = d_resid_in + lax.psum(attn_back_part.astype(jnp.bfloat16), "mp").astype(
        jnp.float32
    )
    left_cols = input_low
    right_cols = d_attn_low
    in_terms = jnp.einsum("sd,jsc->djc", left_cols, d_proj_low, preferred_element_type=jnp.float32)
    out_terms = jnp.einsum("sd,sc->dc", right_cols, mixed_low, preferred_element_type=jnp.float32)
    grad_attn = jnp.transpose(
        lax.psum_scatter(
            jnp.concatenate([in_terms, out_terms[:, None, :]], axis=1),
            "fsdp",
            scatter_dimension=0,
            tiled=True,
        ),
        (1, 0, 2),
    )
    root_tokens = math.sqrt(tokens)
    weight_rate = RATE_WEIGHT / root_tokens
    attn_mom_new, attn_step = nesterov(attn_w, attn_mom, grad_attn, weight_rate)
    mlp_mom_new, mlp_step = nesterov(mlp_w, mlp_mom, grad_mlp, weight_rate)
    attn_squares = jnp.sum(attn_step * attn_step, axis=1)
    mlp_squares = jnp.sum(mlp_step * mlp_step, axis=1)
    attn_squares, mlp_squares = lax.psum((attn_squares, mlp_squares), "fsdp")
    attn_new = attn_step * lax.rsqrt(attn_squares[:, None, :] / model_width + EPS)
    mlp_new = mlp_step * lax.rsqrt(mlp_squares[:, None, :] / model_width + EPS)
    head_mom_new, head_new = nesterov(head_scale, head_mom, grad_head, RATE_HEAD / root_tokens)
    mix_mom_new, mix_new = nesterov(mix_rates, mix_mom, grad_mix, RATE_MIX / root_tokens)
    units_mom_new, units_new = nesterov(unit_scales, unit_mom, grad_units, RATE_UNITS / root_tokens)
    return (
        result[None],
        input_grad[None],
        attn_mom_new,
        attn_new,
        AVERAGE * attn_avg + (1.0 - AVERAGE) * attn_new,
        mlp_mom_new,
        mlp_new,
        AVERAGE * mlp_avg + (1.0 - AVERAGE) * mlp_new,
        head_mom_new,
        head_new,
        mix_mom_new,
        mix_new,
        units_mom_new,
        units_new,
    )


def solution(mesh):
    fsdp = mesh.shape["fsdp"]
    fast = fsdp == 16 and D // fsdp % 16 == 0
    placed = (
        P("fsdp", None, None),
        P("fsdp", None),
        P("fsdp", None, None),
        P(None, "fsdp", "mp"),
        P(None, "fsdp", "mp"),
        P(None, "fsdp", "mp"),
        P(None, "fsdp", "mp"),
        P(None, "fsdp", "mp"),
        P(None, "fsdp", "mp"),
        P("mp"),
        P("mp"),
        P(),
        P(),
        P(None, "mp"),
        P(None, "mp"),
    )
    return jax.shard_map(
        local_fast if fast else local,
        mesh=mesh,
        in_specs=placed,
        out_specs=(
            P("fsdp", None, None),
            P("fsdp", None, None),
            P(None, "fsdp", "mp"),
            P(None, "fsdp", "mp"),
            P(None, "fsdp", "mp"),
            P(None, "fsdp", "mp"),
            P(None, "fsdp", "mp"),
            P(None, "fsdp", "mp"),
            P("mp"),
            P("mp"),
            P(),
            P(),
            P(None, "mp"),
            P(None, "mp"),
        ),
        check_vma=False,
    )
```
